32 devices in a mesh: dp: 16 (over z, x, core), tensor: 2 (over y).
Axes of the slice: x: 2, y: 2, z: 4, core: 2. Of those that a mesh axis runs over, the one named last changes fastest.
Arguments:
- tokens: bfloat16 [5120, 2048], P('dp'), may hold values from -6 to 6
- cotangent: bfloat16 [5120, 2048], P('dp'), may hold values from -6 to 6
- route_ids: int32 [5120, 6], P('dp'), may hold values from 0 to 15, all different within a row; in each aligned block of 320 rows (0 to 319, 320 to 639, ...) at most 160 rows name the same one
- route_gates: float32 [5120, 6], P('dp'), may hold values from 0.08 to 0.32
- gain_first: bfloat16 [2048], P('dp'), may hold values from 0.5 to 1.5
- w_query: bfloat16 [2048, 2048], P('dp', 'tensor'), may hold values from -0.125 to 0.125
- w_key: bfloat16 [2048, 2048], P('dp', 'tensor'), may hold values from -0.125 to 0.125
- w_value: bfloat16 [2048, 2048], P('dp', 'tensor'), may hold values from -0.125 to 0.125
- w_output: bfloat16 [2048, 2048], P('dp', 'tensor'), may hold values from -0.5 to 0.5
- gain_second: bfloat16 [2048], P('dp'), may hold values from 0.5 to 1.5
- shared_gate: bfloat16 [2048, 2816], P('dp', 'tensor'), may hold values from -0.125 to 0.125
- shared_up: bfloat16 [2048, 2816], P('dp', 'tensor'), may hold values from -0.125 to 0.125
- shared_down: bfloat16 [2048, 2816], P('dp', 'tensor'), may hold values from -0.109375 to 0.109375
- expert_gate: bfloat16 [16, 2048, 1408], P('dp', None, 'tensor'), may hold values from -0.125 to 0.125
- expert_up: bfloat16 [16, 2048, 1408], P('dp', None, 'tensor'), may hold values from -0.125 to 0.125
- expert_down: bfloat16 [16, 1408, 2048], P('dp', 'tensor'), may hold values from -0.15625 to 0.15625
Outputs:
- layer_out: bfloat16 [5120, 2048], P('dp')
- tokens_grad: bfloat16 [5120, 2048], P('dp')
- gain_first_grad: float32 [2048], P('dp')
- query_grad: float32 [2048, 2048], P('dp', 'tensor')
- key_grad: float32 [2048, 2048], P('dp', 'tensor')
- value_grad: float32 [2048, 2048], P('dp', 'tensor')
- output_grad: float32 [2048, 2048], P('dp', 'tensor')
- gain_second_grad: float32 [2048], P('dp')
- shared_gate_grad: float32 [2048, 2816], P('dp', 'tensor')
- shared_up_grad: float32 [2048, 2816], P('dp', 'tensor')
- shared_down_grad: float32 [2048, 2816], P('dp', 'tensor')
- expert_gate_grad: float32 [16, 2048, 1408], P('dp', None, 'tensor')
- expert_up_grad: float32 [16, 2048, 1408], P('dp', None, 'tensor')
- expert_down_grad: float32 [16, 1408, 2048], P('dp', 'tensor')
The draws below stay inside these ranges and needn't reach their ends.
Inputs may be any that keep to these rules, and one draw needn't show every extreme that they name: `route_ids`: each row names 6 different experts. Among the 320 rows of one index of dp no expert is named by more than 160 rows, and in the rows of some index one expert is named by exactly 160.
All inputs are finite; a program needn't handle non-finite values.
Results may differ from the reference program's by a relative error of at most 0.014.
Values may be sent and summed in bfloat16 or wider, within the bound.
A program may use at most 320 MiB of HBM per device.

```python
import math
import jax
import jax.numpy as jnp
import numpy as np
from jax import lax

D = 2048
HEADS = 16
HD = 128
FF_E = 1408
FF_S = 2816
TOPK = 6
TOK_DEV = 320
EXPERTS = 16
CAP = 160
TOKENS = 5120


def strengthened(values, stream_key, source, target, blocks, factor):
    owner, partner = [(jnp.arange(values.shape[position]) // (values.shape[position] // blocks)).reshape([-1 if axis == position else 1 for axis in range(values.ndim)]) for position in (source, target)]
    chosen = jax.random.permutation(stream_key, blocks)[partner]
    strong = (owner == chosen) | (owner == (partner + blocks // 2) % blocks)
    return jnp.where(strong, factor * values, values)


def shard_levels(rng, shape, shards, low, top_value):
    level = 1.0
    for position, parts in shards:
        steps = jax.random.uniform(jax.random.fold_in(jax.random.fold_in(rng, 6), position), (parts,), jnp.float32, low / len(shards), top_value / len(shards))
        level = level * jnp.repeat(jnp.exp(steps), shape[position] // parts).reshape((-1,) + (1,) * (len(shape) - 1 - position))
    return level


def assign_block(rng, own, number, rows, amount, top, reach, lean):
    ranking = jax.random.permutation(rng, amount)
    heavy_load, ordinary = load_shares(amount, rows * top, reach, lean, True), load_shares(amount, rows * top, reach, lean, False)
    places = jnp.arange(amount)

    def named(sizes, rotation):
        used = int((sizes > 0).sum())
        fixed = max(1, used // 4)
        moved = fixed + (places - fixed + rotation * (used - fixed)) % max(1, amount - fixed)
        return jnp.zeros((amount,), jnp.int32).at[ranking[jnp.where(places < fixed, places, moved)]].set(jnp.asarray(sizes, jnp.int32))

    sizes = jnp.where(number % 4 == 0, named(heavy_load, number // 4), named(ordinary, number - number // 4 - 1))
    mixed = jax.random.permutation(jax.random.fold_in(own, 3), amount)
    donor, taker = mixed[0:amount // 2 * 2:2], mixed[1:amount // 2 * 2:2]
    margin = jnp.minimum(sizes[donor] - 1, reach - sizes[taker]) // 2
    margin = jnp.where((donor == ranking[0]) | (taker == ranking[0]) | (sizes[taker] == 0), 0, jnp.maximum(margin, 0))
    moved = jax.random.randint(jax.random.fold_in(own, 4), (amount // 2,), 0, 1 << 20) % (margin + 1)
    sizes = sizes.at[donor].add(-moved).at[taker].add(moved)
    items = jnp.searchsorted(jnp.cumsum(sizes), jnp.arange(rows * top), side="right").astype(jnp.int32)
    grid = items.reshape(top, rows).T
    grid = grid[jax.random.permutation(jax.random.fold_in(own, 1), rows)]
    rotation = jax.random.randint(jax.random.fold_in(own, 2), (rows, 1), 0, top)
    return jnp.take_along_axis(grid, (jnp.arange(top)[None, :] + rotation) % top, axis=1)


def load_shares(number_of, total, limit, lean, full):
    weights = [(1 << 20) // math.isqrt(standing ** lean) + 1 for standing in range(1, number_of + 1)]
    largest = limit if full else min(limit, max(-(-total // number_of), total * weights[0] // sum(weights)))
    least = 1 if total - largest >= number_of - 1 else 0
    holding, spare = [largest] + [least] * (number_of - 1), total - largest - least * (number_of - 1)
    while spare > 0:
        movable = [i for i in range(1, number_of) if holding[i] < largest] or [i for i in range(1, number_of) if holding[i] < limit]
        whole, left = sum([weights[i] for i in movable]), spare
        for i in movable:
            extra = min(limit - holding[i], max(1, left * weights[i] // whole), spare)
            holding[i] = holding[i] + extra
            spare = spare - extra
    return np.array(holding)


def gaussian(key, dims, deviation, most, shards=(), kind=jnp.bfloat16):
    level = shard_levels(key, dims, shards, -0.22, 0.18) if shards else 1.0
    values = jax.random.normal(key, dims, jnp.float32) * deviation * level
    return jnp.minimum(jnp.maximum(values, -most), most).astype(kind)


def noise_with(rng, dims, scale, reach, cuts, heavy, kind=jnp.bfloat16):
    entries = scale * jax.random.normal(rng, dims, jnp.float32)
    if cuts:
        entries = entries * shard_levels(rng, dims, cuts, -0.22, 0.18)
    return jnp.clip(strengthened(entries, jax.random.fold_in(rng, 3), *heavy), -reach, reach).astype(kind)


def setup_inputs(seed: int = 0) -> dict:
    keys = jax.random.split(jax.random.key(seed), 17)
    tokens = noise_with(keys[0], (TOKENS, D), 1.0, 6.0, ((0, 16),), (0, 1, 16, 2.0))
    cotangent = noise_with(keys[1], (TOKENS, D), 1.0, 6.0, ((0, 16),), (0, 1, 16, 2.0))
    route_ids_keys = jax.random.split(jax.random.fold_in(keys[2], 1), TOKENS // TOK_DEV)
    route_ids_turns = jax.random.permutation(jax.random.fold_in(keys[2], 3), TOKENS // TOK_DEV)
    route_ids = jax.vmap(lambda own, number: assign_block(jax.random.fold_in(keys[2], 2), own, number, TOK_DEV, EXPERTS, TOPK, CAP, 1))(route_ids_keys, route_ids_turns).reshape((TOKENS, TOPK))
    route_gates = jnp.clip(0.08 + 0.24 * jax.random.uniform(keys[3], (TOKENS, TOPK), jnp.float32) ** shard_levels(keys[3], (TOKENS, TOPK), ((0, 16),), -0.2, 0.2), 0.08, 0.32)
    gain_first = jnp.clip(1.0 + 0.1 * jax.random.normal(keys[4], (D,), jnp.float32), 0.5, 1.5).astype(jnp.bfloat16)
    w_query = gaussian(keys[5], (D, HEADS * HD), D ** -0.5, 0.125, ((0, 16), (1, 2)))
    w_key = gaussian(keys[6], (D, HEADS * HD), D ** -0.5, 0.125, ((0, 16), (1, 2)))
    w_value = gaussian(keys[7], (D, HEADS * HD), D ** -0.5, 0.125, ((0, 16), (1, 2)))
    w_output = gaussian(keys[8], (D, HEADS * HD), (HEADS * HD // 16) ** -0.5, 0.5, ((0, 16), (1, 2)))
    gain_second = jnp.clip(1.0 + 0.1 * jax.random.normal(keys[9], (D,), jnp.float32), 0.5, 1.5).astype(jnp.bfloat16)
    shared_gate = gaussian(keys[10], (D, FF_S), D ** -0.5, 0.125, ((0, 16), (1, 2)))
    shared_up = gaussian(keys[11], (D, FF_S), D ** -0.5, 0.125, ((0, 16), (1, 2)))
    shared_down = gaussian(keys[12], (D, FF_S), FF_S ** -0.5, 0.109375, ((0, 16), (1, 2)))
    expert_gate = gaussian(keys[13], (EXPERTS, D, FF_E), D ** -0.5, 0.125, ((0, 16), (2, 2)))
    expert_up = gaussian(keys[14], (EXPERTS, D, FF_E), D ** -0.5, 0.125, ((0, 16), (2, 2)))
    expert_down = gaussian(keys[15], (EXPERTS, FF_E, D), FF_E ** -0.5, 0.15625, ((0, 16), (1, 2)))
    return {"tokens": tokens, "cotangent": cotangent, "route_ids": route_ids, "route_gates": route_gates, "gain_first": gain_first, "w_query": w_query, "w_key": w_key, "w_value": w_value, "w_output": w_output, "gain_second": gain_second, "shared_gate": shared_gate, "shared_up": shared_up, "shared_down": shared_down, "expert_gate": expert_gate, "expert_up": expert_up, "expert_down": expert_down}


EPS = 1e-06
HIGH = lax.Precision.HIGHEST

@jax.custom_vjp
def low(v):
    return lax.optimization_barrier(v.astype(jnp.bfloat16)).astype(jnp.float32)

@jax.custom_vjp
def low_back(v):
    return v

def low_keep(v):
    return (low(v), None)

def low_pass(kept, grad):
    return (grad,)

def back_keep(v):
    return (v, None)

def back_low(kept, grad):
    return (low(grad),)
low.defvjp(low_keep, low_pass)
low_back.defvjp(back_keep, back_low)

def rms_norm(values, gain):
    mean_square = lax.optimization_barrier(jnp.mean(values * values, axis=-1, keepdims=True))
    return values * lax.rsqrt(mean_square + EPS) * gain

def rotate(values, positions):
    head = values.shape[-1]
    half = head // 2
    freqs = 10000.0 ** (-2.0 * jnp.arange(half, dtype=jnp.float32) / head)
    angles = positions[:, None] * freqs[None, :]
    cosine = jnp.cos(angles)[:, None, :]
    sine = jnp.sin(angles)[:, None, :]
    first = values[..., :half]
    second = values[..., half:]
    return jnp.concatenate([first * cosine - second * sine, second * cosine + first * sine], axis=-1)

def gated(gate_pre, up_pre):
    return gate_pre * jax.nn.sigmoid(gate_pre) * up_pre

def reference(tokens, cotangent, route_ids, route_gates, gain_first, w_query, w_key, w_value, w_output, gain_second, shared_gate, shared_up, shared_down, expert_gate, expert_up, expert_down):
    blocks = TOKENS // TOK_DEV
    per_block = TOK_DEV * TOPK
    flat_ids = route_ids.reshape(blocks, per_block).astype(jnp.int32)
    onehot = (flat_ids[:, :, None] == jnp.arange(EXPERTS, dtype=jnp.int32)[None, None, :]).astype(jnp.int32)
    ranks = lax.optimization_barrier(jnp.sum(onehot * jnp.cumsum(onehot, axis=1), axis=2)) - 1
    block_ids = jnp.arange(blocks, dtype=jnp.int32)[:, None]
    dest = ((flat_ids * blocks + block_ids) * CAP + ranks).reshape(-1).astype(jnp.int32)
    token_of = (block_ids * TOK_DEV + jnp.arange(per_block, dtype=jnp.int32)[None, :] // TOPK).reshape(-1).astype(jnp.int32)
    slots = EXPERTS * blocks * CAP
    source = jnp.zeros((slots,), jnp.int32).at[dest].set(token_of)
    weight_of = jnp.zeros((slots,), jnp.float32).at[dest].set(route_gates.reshape(-1).astype(jnp.float32))
    positions = jnp.arange(TOK_DEV, dtype=jnp.float32)
    causal = jnp.arange(TOK_DEV)[:, None] >= jnp.arange(TOK_DEV)[None, :]
    scale = HD ** (-0.5)

    def layer(x_in, gain_one, query_w, key_w, value_w, output_w, gain_two, common_gate, common_up, common_down, routed_gate, routed_up, routed_down):
        act_one = low(rms_norm(x_in, gain_one))
        seq = act_one.reshape(blocks, TOK_DEV, D)
        query_pre = low_back(jnp.einsum('tsd,dk->tsk', seq, query_w, precision=HIGH)).reshape(blocks, TOK_DEV, HEADS, HD)
        key_pre = low_back(jnp.einsum('tsd,dk->tsk', seq, key_w, precision=HIGH)).reshape(blocks, TOK_DEV, HEADS, HD)
        query_rot = low(rotate(query_pre, positions))
        key_rot = low(rotate(key_pre, positions))
        value_low = low(low_back(jnp.einsum('tsd,dk->tsk', seq, value_w, precision=HIGH))).reshape(blocks, TOK_DEV, HEADS, HD)
        scores = low_back(jnp.einsum('tqhc,tkhc->thqk', query_rot, key_rot, precision=HIGH) * scale)
        scores = jnp.where(causal[None, None], scores, -1e+30)
        top = lax.optimization_barrier(jnp.max(scores, axis=-1, keepdims=True))
        expo = jnp.exp(scores - top)
        probs = expo / lax.optimization_barrier(jnp.sum(expo, axis=-1, keepdims=True))
        mixed = jnp.einsum('thqk,tkhc->tqhc', low(probs), value_low, precision=HIGH).reshape(TOKENS, HEADS * HD)
        mixed = low(low_back(mixed))
        attn = low_back(jnp.dot(mixed, output_w.T, precision=HIGH))
        x_mid = x_in + attn
        act_two = low(rms_norm(x_mid, gain_two))
        gate_pre = low_back(jnp.dot(act_two, common_gate, precision=HIGH))
        up_pre = low_back(jnp.dot(act_two, common_up, precision=HIGH))
        hidden = low(gated(gate_pre, up_pre))
        common = low_back(jnp.dot(hidden, common_down.T, precision=HIGH))
        rows = act_two[source].reshape(EXPERTS, blocks * CAP, D)
        expert_gate_pre = low_back(jnp.einsum('erd,edf->erf', rows, routed_gate, precision=HIGH))
        expert_up_pre = low_back(jnp.einsum('erd,edf->erf', rows, routed_up, precision=HIGH))
        expert_hidden = low(gated(expert_gate_pre, expert_up_pre))
        expert_out = low_back(jnp.einsum('erf,efd->erd', expert_hidden, routed_down, precision=HIGH)).reshape(slots, D)
        routed = jnp.zeros((TOKENS, D), jnp.float32).at[source].add(weight_of[:, None] * expert_out)
        return x_mid + common + routed
    floats = (tokens.astype(jnp.float32), gain_first.astype(jnp.float32), w_query.astype(jnp.float32), w_key.astype(jnp.float32), w_value.astype(jnp.float32), w_output.astype(jnp.float32), gain_second.astype(jnp.float32), shared_gate.astype(jnp.float32), shared_up.astype(jnp.float32), shared_down.astype(jnp.float32), expert_gate.astype(jnp.float32), expert_up.astype(jnp.float32), expert_down.astype(jnp.float32))
    result, pullback = jax.vjp(layer, *floats)
    grads = pullback(cotangent.astype(jnp.float32))
    return (result.astype(jnp.bfloat16), grads[0].astype(jnp.bfloat16), grads[1], grads[2], grads[3], grads[4], grads[5], grads[6], grads[7], grads[8], grads[9], grads[10], grads[11], grads[12])
```

```python
import jax
import jax.numpy as jnp
from jax import lax
from jax.sharding import PartitionSpec as P

HD = 128


EPS = 1e-06


def rms_norm(values, gain):
    mean_square = jnp.mean(values * values, axis=-1, keepdims=True)
    return values * lax.rsqrt(mean_square + EPS) * gain


def rotate(values, positions):
    head = values.shape[-1]
    half = head // 2
    freqs = 10000.0 ** (-2.0 * jnp.arange(half, dtype=jnp.float32) / head)
    angles = positions[:, None] * freqs[None, :]
    cosine = jnp.cos(angles)[:, None, :]
    sine = jnp.sin(angles)[:, None, :]
    first = values[..., :half]
    second = values[..., half:]
    return jnp.concatenate(
        [first * cosine - second * sine, second * cosine + first * sine], axis=-1
    )


def gated(gate_pre, up_pre):
    return gate_pre * jax.nn.sigmoid(gate_pre) * up_pre


def contract_last(left, right):
    return lax.dot_general(
        left, right, (((1,), (1,)), ((), ())), preferred_element_type=jnp.float32
    )


def contract_first(left, right):
    return lax.dot_general(
        left, right, (((0,), (0,)), ((), ())), preferred_element_type=jnp.float32
    )


def masked_scores(query_rot, key_rot, causal, scale):
    scores = (
        jnp.einsum("qhc,khc->hqk", query_rot, key_rot, preferred_element_type=jnp.float32) * scale
    )
    return jnp.where(causal[None], scores, -1e30)


def on_device_plain(
    tokens,
    cotangent,
    route_ids,
    route_gates,
    gain_first,
    w_query,
    w_key,
    w_value,
    w_output,
    gain_second,
    shared_gate,
    shared_up,
    shared_down,
    expert_gate,
    expert_up,
    expert_down,
):
    rows_dev, width = tokens.shape
    topk = route_ids.shape[1]
    experts = lax.axis_size("dp")
    capacity = rows_dev * topk * 4 // (3 * experts)
    slots = experts * capacity
    scale = HD ** (-0.5)
    positions = jnp.arange(rows_dev, dtype=jnp.float32)
    causal = jnp.arange(rows_dev)[:, None] >= jnp.arange(rows_dev)[None, :]
    gain_one, query_whole, key_whole, value_whole, output_whole = (
        lax.all_gather(gain_first, "dp", axis=0, tiled=True),
        lax.all_gather(w_query, "dp", axis=0, tiled=True),
        lax.all_gather(w_key, "dp", axis=0, tiled=True),
        lax.all_gather(w_value, "dp", axis=0, tiled=True),
        lax.all_gather(w_output, "dp", axis=0, tiled=True),
    )
    gain_two, common_gate, common_up, common_down = (
        lax.all_gather(gain_second, "dp", axis=0, tiled=True),
        lax.all_gather(shared_gate, "dp", axis=0, tiled=True),
        lax.all_gather(shared_up, "dp", axis=0, tiled=True),
        lax.all_gather(shared_down, "dp", axis=0, tiled=True),
    )
    gain_one = gain_one.astype(jnp.float32)
    gain_two = gain_two.astype(jnp.float32)
    x_in = tokens.astype(jnp.float32)
    act_one = rms_norm(x_in, gain_one).astype(jnp.bfloat16)
    heads_dev = query_whole.shape[1] // HD
    query_pre = jnp.dot(act_one, query_whole, preferred_element_type=jnp.float32).reshape(
        rows_dev, heads_dev, HD
    )
    key_pre = jnp.dot(act_one, key_whole, preferred_element_type=jnp.float32).reshape(
        rows_dev, heads_dev, HD
    )
    query_rot = rotate(query_pre, positions).astype(jnp.bfloat16)
    key_rot = rotate(key_pre, positions).astype(jnp.bfloat16)
    value_low = (
        jnp.dot(act_one, value_whole, preferred_element_type=jnp.float32)
        .astype(jnp.bfloat16)
        .reshape(rows_dev, heads_dev, HD)
    )
    scores = masked_scores(query_rot, key_rot, causal, scale)
    top = jnp.max(scores, axis=-1, keepdims=True)
    expo = jnp.exp(scores - top)
    total = jnp.sum(expo, axis=-1, keepdims=True)
    probs = expo / total
    log_total = top + jnp.log(total)
    mixed = jnp.einsum(
        "hqk,khc->qhc", probs.astype(jnp.bfloat16), value_low, preferred_element_type=jnp.float32
    )
    mixed = mixed.reshape(rows_dev, heads_dev * HD).astype(jnp.bfloat16)
    attn = lax.psum(contract_last(mixed, output_whole), "tensor")
    x_mid = x_in + attn
    act_two = rms_norm(x_mid, gain_two).astype(jnp.bfloat16)
    gate_pre = jnp.dot(act_two, common_gate, preferred_element_type=jnp.float32)
    up_pre = jnp.dot(act_two, common_up, preferred_element_type=jnp.float32)
    hidden_common = gated(gate_pre, up_pre).astype(jnp.bfloat16)
    common_out = contract_last(hidden_common, common_down)
    flat_ids = route_ids.reshape(-1)
    onehot = (flat_ids[:, None] == jnp.arange(experts, dtype=jnp.int32)[None, :]).astype(jnp.int32)
    ranks = jnp.sum(onehot * jnp.cumsum(onehot, axis=0), axis=1) - 1
    dest = flat_ids * capacity + ranks
    token_of = jnp.arange(rows_dev * topk, dtype=jnp.int32) // topk
    source = jnp.zeros((slots,), jnp.int32).at[dest].set(token_of)
    weight_of = jnp.zeros((slots,), jnp.float32).at[dest].set(route_gates.reshape(-1))
    filled = jnp.zeros((slots,), jnp.bool_).at[dest].set(True)
    outgoing = jnp.where(filled[:, None], act_two[source], jnp.zeros((), jnp.bfloat16)).reshape(
        experts, capacity, width
    )
    exp_gate = expert_gate[0]
    exp_up = expert_up[0]
    exp_down = expert_down[0]
    received = lax.all_to_all(outgoing, "dp", split_axis=0, concat_axis=0, tiled=True)
    sources = received.shape[0]
    count = received.shape[1]
    rows = received.reshape(sources * count, width)
    gate_rows = jnp.dot(rows, exp_gate, preferred_element_type=jnp.float32)
    up_rows = jnp.dot(rows, exp_up, preferred_element_type=jnp.float32)
    hidden_rows = gated(gate_rows, up_rows).astype(jnp.bfloat16)
    partial_value = jnp.dot(hidden_rows, exp_down, preferred_element_type=jnp.float32).reshape(
        sources, count, width
    )
    returned = lax.all_to_all(
        partial_value.astype(jnp.bfloat16), "dp", split_axis=0, concat_axis=0, tiled=True
    ).astype(partial_value.dtype)
    returned, kept_rows, kept_gate, kept_up = (
        returned,
        received,
        gate_rows.reshape(sources, count, -1),
        up_rows.reshape(sources, count, -1),
    )
    picked = returned.reshape(slots, width)[dest].reshape(rows_dev, topk, width)
    routed_part = jnp.sum(picked * route_gates[:, :, None], axis=1)
    ffn = lax.psum((common_out + routed_part).astype(jnp.bfloat16), "tensor").astype(jnp.float32)
    layer_out = (x_mid + ffn).astype(jnp.bfloat16)
    grad_out = cotangent.astype(jnp.float32)
    hidden_grad = jnp.dot(cotangent, common_down, preferred_element_type=jnp.float32)
    dummy_common, common_vjp = jax.vjp(gated, gate_pre, up_pre)
    gate_grad, up_grad = common_vjp(hidden_grad)
    gate_grad = gate_grad.astype(jnp.bfloat16)
    up_grad = up_grad.astype(jnp.bfloat16)
    common_gate_grad = contract_first(act_two, gate_grad)
    common_up_grad = contract_first(act_two, up_grad)
    common_down_grad = contract_first(cotangent, hidden_common)
    act_two_grad = contract_last(gate_grad, common_gate) + contract_last(up_grad, common_up)
    outgoing_grad = (
        (weight_of[:, None] * grad_out[source])
        .astype(jnp.bfloat16)
        .reshape(experts, capacity, width)
    )
    incoming_grad = lax.all_to_all(outgoing_grad, "dp", split_axis=0, concat_axis=0, tiled=True)
    hidden_width = kept_gate.shape[2]
    rows = kept_rows.reshape(-1, width)
    rows_out_grad = incoming_grad.reshape(-1, width)
    hidden_rows, expert_vjp = jax.vjp(
        gated, kept_gate.reshape(-1, hidden_width), kept_up.reshape(-1, hidden_width)
    )
    hidden_rows = hidden_rows.astype(jnp.bfloat16)
    hidden_rows_grad = contract_last(rows_out_grad, exp_down)
    gate_rows_grad, up_rows_grad = expert_vjp(hidden_rows_grad)
    gate_rows_grad = gate_rows_grad.astype(jnp.bfloat16)
    up_rows_grad = up_rows_grad.astype(jnp.bfloat16)
    expert_gate_grad = contract_first(rows, gate_rows_grad)[None]
    expert_up_grad = contract_first(rows, up_rows_grad)[None]
    expert_down_grad = contract_first(hidden_rows, rows_out_grad)[None]
    rows_in_grad = (
        contract_last(gate_rows_grad, exp_gate) + contract_last(up_rows_grad, exp_up)
    ).reshape(experts, capacity, width)
    returned_grad = lax.all_to_all(rows_in_grad, "dp", split_axis=0, concat_axis=0, tiled=True)
    routed_grad = jnp.sum(
        returned_grad.reshape(slots, width)[dest].reshape(rows_dev, topk, width), axis=1
    )
    act_two_total = lax.psum(act_two_grad + routed_grad, "tensor")
    dummy_second, second_vjp = jax.vjp(rms_norm, x_mid, gain_two)
    mid_norm_grad, gain_two_grad = second_vjp(act_two_total)
    mid_grad = grad_out + mid_norm_grad
    ffn_sums = (gain_two_grad, common_gate_grad, common_up_grad, common_down_grad)
    attn_grad = mid_grad.astype(jnp.bfloat16)
    output_w_grad = contract_first(attn_grad, mixed)
    mixed_grad = (
        jnp.dot(attn_grad, output_whole, preferred_element_type=jnp.float32)
        .astype(jnp.bfloat16)
        .reshape(rows_dev, heads_dev, HD)
    )
    probs_again = jnp.exp(masked_scores(query_rot, key_rot, causal, scale) - log_total)
    value_grad = jnp.einsum(
        "hqk,qhc->khc",
        probs_again.astype(jnp.bfloat16),
        mixed_grad,
        preferred_element_type=jnp.float32,
    ).astype(jnp.bfloat16)
    prob_grad = jnp.einsum(
        "qhc,khc->hqk", mixed_grad, value_low, preferred_element_type=jnp.float32
    )
    delta = jnp.sum(probs_again * prob_grad, axis=-1, keepdims=True)
    score_grad = (probs_again * (prob_grad - delta)).astype(jnp.bfloat16)
    query_rot_grad = (
        jnp.einsum("hqk,khc->qhc", score_grad, key_rot, preferred_element_type=jnp.float32) * scale
    )
    key_rot_grad = (
        jnp.einsum("hqk,qhc->khc", score_grad, query_rot, preferred_element_type=jnp.float32)
        * scale
    )

    def turn(values):
        return rotate(values, positions)

    dummy_turn, turn_vjp = jax.vjp(turn, query_pre)
    query_grad = turn_vjp(query_rot_grad)[0].reshape(rows_dev, heads_dev * HD).astype(jnp.bfloat16)
    key_grad = turn_vjp(key_rot_grad)[0].reshape(rows_dev, heads_dev * HD).astype(jnp.bfloat16)
    value_flat = value_grad.reshape(rows_dev, heads_dev * HD)
    query_w_grad = contract_first(act_one, query_grad)
    key_w_grad = contract_first(act_one, key_grad)
    value_w_grad = contract_first(act_one, value_flat)
    act_one_grad = (
        contract_last(query_grad, query_whole)
        + contract_last(key_grad, key_whole)
        + contract_last(value_flat, value_whole)
    )
    act_one_total = lax.psum(act_one_grad, "tensor")
    dummy_first, first_vjp = jax.vjp(rms_norm, x_in, gain_one)
    in_norm_grad, gain_one_grad = first_vjp(act_one_total)
    tokens_grad = (mid_grad + in_norm_grad).astype(jnp.bfloat16)
    every = (
        lax.psum_scatter(gain_one_grad, "dp", scatter_dimension=0, tiled=True),
        lax.psum_scatter(query_w_grad, "dp", scatter_dimension=0, tiled=True),
        lax.psum_scatter(key_w_grad, "dp", scatter_dimension=0, tiled=True),
        lax.psum_scatter(value_w_grad, "dp", scatter_dimension=0, tiled=True),
        lax.psum_scatter(output_w_grad, "dp", scatter_dimension=0, tiled=True),
        lax.psum_scatter(ffn_sums[0], "dp", scatter_dimension=0, tiled=True),
        lax.psum_scatter(ffn_sums[1], "dp", scatter_dimension=0, tiled=True),
        lax.psum_scatter(ffn_sums[2], "dp", scatter_dimension=0, tiled=True),
        lax.psum_scatter(ffn_sums[3], "dp", scatter_dimension=0, tiled=True),
    )
    attn_sums = every[:5]
    ffn_sums = every[5:]
    return (
        layer_out,
        tokens_grad,
        attn_sums[0],
        attn_sums[1],
        attn_sums[2],
        attn_sums[3],
        attn_sums[4],
        ffn_sums[0],
        ffn_sums[1],
        ffn_sums[2],
        ffn_sums[3],
        expert_gate_grad,
        expert_up_grad,
        expert_down_grad,
    )


def routing_tables(gate_table, capacity):
    member = gate_table > 0.0
    ranks = jnp.cumsum(member.astype(jnp.int32), axis=1) - 1
    slot = jnp.arange(capacity, dtype=jnp.int32)
    pick = (ranks[:, None, :] == slot[None, :, None]) & member[:, None, :]
    slot_gate = jnp.sum(jnp.where(pick, gate_table[:, None, :], 0.0), axis=2)
    return pick.astype(jnp.bfloat16), slot_gate


def on_device(
    tokens,
    cotangent,
    route_ids,
    route_gates,
    gain_first,
    w_query,
    w_key,
    w_value,
    w_output,
    gain_second,
    shared_gate,
    shared_up,
    shared_down,
    expert_gate,
    expert_up,
    expert_down,
):
    f32, bf16 = jnp.float32, jnp.bfloat16
    rows_dev, width = tokens.shape
    topk = route_ids.shape[1]
    experts = lax.axis_size("dp")
    splits = lax.axis_size("tensor")
    half = rows_dev // splits
    mine = lax.axis_index("tensor") * half
    capacity = rows_dev * topk * 4 // (3 * experts)
    slots = experts * capacity
    scale = HD ** (-0.5)
    positions = jnp.arange(rows_dev, dtype=f32)
    causal = jnp.arange(rows_dev)[:, None] >= jnp.arange(rows_dev)[None, :]
    gains = lax.all_gather(jnp.stack([gain_first, gain_second]), "dp", axis=1, tiled=True)
    gain_one = gains[0].astype(f32)
    gain_two = gains[1].astype(f32)
    query_whole = lax.all_gather(w_query, "dp", axis=0, tiled=True)
    key_whole = lax.all_gather(w_key, "dp", axis=0, tiled=True)
    value_whole = lax.all_gather(w_value, "dp", axis=0, tiled=True)
    output_whole = lax.all_gather(w_output, "dp", axis=0, tiled=True)
    grad_half = lax.dynamic_slice_in_dim(cotangent, mine, half, axis=0)
    grad_all = lax.all_gather(grad_half, ("dp", "tensor"), axis=0, tiled=True)

    depth, common_width = shared_gate.shape
    common_dev = common_width // experts
    packed = jnp.stack([shared_gate, shared_up, shared_down])
    packed = packed.reshape(3, depth, experts, common_dev).transpose(2, 0, 1, 3)
    packed = lax.all_to_all(packed, "dp", split_axis=0, concat_axis=0, tiled=True)
    packed = packed.transpose(1, 0, 2, 3).reshape(3, width, common_dev)
    common_gu = jnp.concatenate([packed[0], packed[1]], axis=1)
    common_down = packed[2]

    chosen = route_ids[:, :, None] == jnp.arange(experts, dtype=jnp.int32)[None, None, :]
    table = jnp.sum(jnp.where(chosen, route_gates[:, :, None], 0.0), axis=1)
    table = lax.all_to_all(table.T, "dp", split_axis=0, concat_axis=0, tiled=True)
    pick, slot_gate = routing_tables(table, capacity)

    x_in = tokens.astype(f32)
    act_one = rms_norm(x_in, gain_one).astype(bf16)
    heads_dev = query_whole.shape[1] // HD
    query_pre = jnp.dot(act_one, query_whole, preferred_element_type=f32).reshape(
        rows_dev, heads_dev, HD
    )
    key_pre = jnp.dot(act_one, key_whole, preferred_element_type=f32).reshape(
        rows_dev, heads_dev, HD
    )
    query_rot = rotate(query_pre, positions).astype(bf16)
    key_rot = rotate(key_pre, positions).astype(bf16)
    value_low = (
        jnp.dot(act_one, value_whole, preferred_element_type=f32)
        .astype(bf16)
        .reshape(rows_dev, heads_dev, HD)
    )
    scores = masked_scores(query_rot, key_rot, causal, scale)
    top = jnp.max(scores, axis=-1, keepdims=True)
    expo = jnp.exp(scores - top)
    total = jnp.sum(expo, axis=-1, keepdims=True)
    probs = expo / total
    log_total = top + jnp.log(total)
    mixed = jnp.einsum("hqk,khc->qhc", probs.astype(bf16), value_low, preferred_element_type=f32)
    mixed = mixed.reshape(rows_dev, heads_dev * HD).astype(bf16)
    attn = lax.psum_scatter(
        contract_last(mixed, output_whole), "tensor", scatter_dimension=0, tiled=True
    )
    x_half = lax.dynamic_slice_in_dim(tokens, mine, half, axis=0).astype(f32)
    x_mid = x_half + attn
    act_two = rms_norm(x_mid, gain_two).astype(bf16)

    act_all = lax.all_gather(act_two, ("dp", "tensor"), axis=0, tiled=True)
    act_blocks = act_all.reshape(experts, rows_dev, width)
    grad_blocks = grad_all.reshape(experts, rows_dev, width)
    exp_gate, exp_up, exp_down = expert_gate[0], expert_up[0], expert_down[0]

    def select(blocks):
        return jnp.einsum("jst,jtd->jsd", pick, blocks, preferred_element_type=f32)

    def spread(rows):
        return jnp.einsum(
            "jst,jsd->jtd", pick, rows.reshape(experts, capacity, width), preferred_element_type=f32
        ).reshape(experts * rows_dev, width)

    weight = slot_gate.reshape(slots, 1)
    rows = select(act_blocks).astype(bf16).reshape(slots, width)
    rows_out_grad = (weight * select(grad_blocks).reshape(slots, width)).astype(bf16)
    gate_rows = jnp.dot(rows, exp_gate, preferred_element_type=f32)
    up_rows = jnp.dot(rows, exp_up, preferred_element_type=f32)
    hidden_rows, expert_vjp = jax.vjp(gated, gate_rows, up_rows)
    hidden_rows = hidden_rows.astype(bf16)
    hidden_rows_grad = contract_last(rows_out_grad, exp_down)
    gate_rows_grad, up_rows_grad = expert_vjp(hidden_rows_grad)
    gate_rows_grad = gate_rows_grad.astype(bf16)
    up_rows_grad = up_rows_grad.astype(bf16)
    rows_in_grad = contract_last(gate_rows_grad, exp_gate) + contract_last(up_rows_grad, exp_up)

    common_pre = jnp.dot(act_all, common_gu, preferred_element_type=f32)
    common_hidden, common_vjp = jax.vjp(
        gated, common_pre[:, :common_dev], common_pre[:, common_dev:]
    )
    common_hidden = common_hidden.astype(bf16)
    common_hidden_grad = jnp.dot(grad_all, common_down, preferred_element_type=f32)
    common_gu_grad = jnp.concatenate(common_vjp(common_hidden_grad), axis=1).astype(bf16)
    act_grad = spread(rows_in_grad.astype(bf16)) + contract_last(common_gu_grad, common_gu)
    act_two_total = lax.psum_scatter(
        act_grad.astype(bf16), ("dp", "tensor"), scatter_dimension=0, tiled=True
    ).astype(f32)

    rows_out = jnp.dot(hidden_rows, exp_down, preferred_element_type=f32) * weight
    ffn = spread(rows_out.astype(bf16)) + contract_last(common_hidden, common_down)
    ffn = lax.psum_scatter(
        ffn.astype(bf16), ("dp", "tensor"), scatter_dimension=0, tiled=True
    ).astype(f32)
    layer_out = lax.all_gather((x_mid + ffn).astype(bf16), "tensor", axis=0, tiled=True)

    expert_gate_grad = contract_first(rows, gate_rows_grad)[None]
    expert_up_grad = contract_first(rows, up_rows_grad)[None]
    expert_down_grad = contract_first(hidden_rows, rows_out_grad)[None]
    common_w_grad = jnp.concatenate(
        [contract_first(act_all, common_gu_grad), contract_first(grad_all, common_hidden)], axis=1
    )
    common_w_grad = common_w_grad.astype(bf16).reshape(experts, depth, 3 * common_dev)
    common_w_grad = lax.all_to_all(common_w_grad, "dp", split_axis=0, concat_axis=0, tiled=True)
    common_w_grad = common_w_grad.astype(f32).reshape(experts, depth, 3, common_dev)
    common_w_grad = common_w_grad.transpose(2, 1, 0, 3).reshape(3, depth, common_width)

    dummy_second, second_vjp = jax.vjp(rms_norm, x_mid, gain_two)
    mid_norm_grad, gain_two_grad = second_vjp(act_two_total)
    mid_grad = grad_half.astype(f32) + mid_norm_grad
    attn_grad = lax.all_gather(mid_grad.astype(bf16), "tensor", axis=0, tiled=True)

    output_w_grad = contract_first(attn_grad, mixed)
    mixed_grad = (
        jnp.dot(attn_grad, output_whole, preferred_element_type=f32)
        .astype(bf16)
        .reshape(rows_dev, heads_dev, HD)
    )
    probs_again = jnp.exp(masked_scores(query_rot, key_rot, causal, scale) - log_total)
    value_grad = jnp.einsum(
        "hqk,qhc->khc", probs_again.astype(bf16), mixed_grad, preferred_element_type=f32
    ).astype(bf16)
    prob_grad = jnp.einsum("qhc,khc->hqk", mixed_grad, value_low, preferred_element_type=f32)
    delta = jnp.sum(probs_again * prob_grad, axis=-1, keepdims=True)
    score_grad = (probs_again * (prob_grad - delta)).astype(bf16)
    query_rot_grad = (
        jnp.einsum("hqk,khc->qhc", score_grad, key_rot, preferred_element_type=f32) * scale
    )
    key_rot_grad = (
        jnp.einsum("hqk,qhc->khc", score_grad, query_rot, preferred_element_type=f32) * scale
    )
    query_grad = rotate(query_rot_grad, -positions).reshape(rows_dev, heads_dev * HD).astype(bf16)
    key_grad = rotate(key_rot_grad, -positions).reshape(rows_dev, heads_dev * HD).astype(bf16)
    value_flat = value_grad.reshape(rows_dev, heads_dev * HD)
    act_one_grad = (
        contract_last(query_grad, query_whole)
        + contract_last(key_grad, key_whole)
        + contract_last(value_flat, value_whole)
    )
    act_one_total = lax.psum_scatter(act_one_grad, "tensor", scatter_dimension=0, tiled=True)
    dummy_first, first_vjp = jax.vjp(rms_norm, x_half, gain_one)
    in_norm_grad, gain_one_grad = first_vjp(act_one_total)
    tokens_grad = lax.all_gather((mid_grad + in_norm_grad).astype(bf16), "tensor", axis=0, tiled=True)

    def weight_sum(left, right):
        return lax.psum_scatter(
            contract_first(left, right).astype(bf16), "dp", scatter_dimension=0, tiled=True
        ).astype(f32)

    gain_grads = lax.psum(jnp.stack([gain_one_grad, gain_two_grad]), ("dp", "tensor"))
    gain_grads = lax.dynamic_slice_in_dim(
        gain_grads, lax.axis_index("dp") * gain_first.shape[0], gain_first.shape[0], axis=1
    )
    return (
        layer_out,
        tokens_grad,
        gain_grads[0],
        weight_sum(act_one, query_grad),
        weight_sum(act_one, key_grad),
        weight_sum(act_one, value_flat),
        weight_sum(attn_grad, mixed),
        gain_grads[1],
        common_w_grad[0],
        common_w_grad[1],
        common_w_grad[2],
        expert_gate_grad,
        expert_up_grad,
        expert_down_grad,
    )


def solution(mesh):
    body = on_device if mesh.shape["dp"] == 16 else on_device_plain
    in_specs = (
        P("dp", None),
        P("dp", None),
        P("dp", None),
        P("dp", None),
        P("dp"),
        P("dp", "tensor"),
        P("dp", "tensor"),
        P("dp", "tensor"),
        P("dp", "tensor"),
        P("dp"),
        P("dp", "tensor"),
        P("dp", "tensor"),
        P("dp", "tensor"),
        P("dp", None, "tensor"),
        P("dp", None, "tensor"),
        P("dp", "tensor", None),
    )
    out_specs = (
        P("dp", None),
        P("dp", None),
        P("dp"),
        P("dp", "tensor"),
        P("dp", "tensor"),
        P("dp", "tensor"),
        P("dp", "tensor"),
        P("dp"),
        P("dp", "tensor"),
        P("dp", "tensor"),
        P("dp", "tensor"),
        P("dp", None, "tensor"),
        P("dp", None, "tensor"),
        P("dp", "tensor", None),
    )
    return jax.shard_map(
        body, mesh=mesh, in_specs=in_specs, out_specs=out_specs, check_vma=False
    )
```

```python
import functools

import jax
import jax.numpy as jnp
from jax import lax
from jax.experimental import pallas as pl
from jax.experimental.pallas import tpu as pltpu
from jax.sharding import PartitionSpec as P

HD = 128
MESH = pl.DeviceIdType.MESH


EPS = 1e-06


def rms_norm(values, gain):
    mean_square = jnp.mean(values * values, axis=-1, keepdims=True)
    return values * lax.rsqrt(mean_square + EPS) * gain


def rotate(values, positions):
    head = values.shape[-1]
    half = head // 2
    freqs = 10000.0 ** (-2.0 * jnp.arange(half, dtype=jnp.float32) / head)
    angles = positions[:, None] * freqs[None, :]
    cosine = jnp.cos(angles)[:, None, :]
    sine = jnp.sin(angles)[:, None, :]
    first = values[..., :half]
    second = values[..., half:]
    return jnp.concatenate(
        [first * cosine - second * sine, second * cosine + first * sine], axis=-1
    )


def gated(gate_pre, up_pre):
    return gate_pre * jax.nn.sigmoid(gate_pre) * up_pre


def contract_last(left, right):
    return lax.dot_general(
        left, right, (((1,), (1,)), ((), ())), preferred_element_type=jnp.float32
    )


def contract_first(left, right):
    return lax.dot_general(
        left, right, (((0,), (0,)), ((), ())), preferred_element_type=jnp.float32
    )


def masked_scores(query_rot, key_rot, causal, scale):
    scores = (
        jnp.einsum("qhc,khc->hqk", query_rot, key_rot, preferred_element_type=jnp.float32) * scale
    )
    return jnp.where(causal[None], scores, -1e30)


def on_device_plain(
    tokens,
    cotangent,
    route_ids,
    route_gates,
    gain_first,
    w_query,
    w_key,
    w_value,
    w_output,
    gain_second,
    shared_gate,
    shared_up,
    shared_down,
    expert_gate,
    expert_up,
    expert_down,
):
    rows_dev, width = tokens.shape
    topk = route_ids.shape[1]
    experts = lax.axis_size("dp")
    capacity = rows_dev * topk * 4 // (3 * experts)
    slots = experts * capacity
    scale = HD ** (-0.5)
    positions = jnp.arange(rows_dev, dtype=jnp.float32)
    causal = jnp.arange(rows_dev)[:, None] >= jnp.arange(rows_dev)[None, :]
    gain_one, query_whole, key_whole, value_whole, output_whole = (
        lax.all_gather(gain_first, "dp", axis=0, tiled=True),
        lax.all_gather(w_query, "dp", axis=0, tiled=True),
        lax.all_gather(w_key, "dp", axis=0, tiled=True),
        lax.all_gather(w_value, "dp", axis=0, tiled=True),
        lax.all_gather(w_output, "dp", axis=0, tiled=True),
    )
    gain_two, common_gate, common_up, common_down = (
        lax.all_gather(gain_second, "dp", axis=0, tiled=True),
        lax.all_gather(shared_gate, "dp", axis=0, tiled=True),
        lax.all_gather(shared_up, "dp", axis=0, tiled=True),
        lax.all_gather(shared_down, "dp", axis=0, tiled=True),
    )
    gain_one = gain_one.astype(jnp.float32)
    gain_two = gain_two.astype(jnp.float32)
    x_in = tokens.astype(jnp.float32)
    act_one = rms_norm(x_in, gain_one).astype(jnp.bfloat16)
    heads_dev = query_whole.shape[1] // HD
    query_pre = jnp.dot(act_one, query_whole, preferred_element_type=jnp.float32).reshape(
        rows_dev, heads_dev, HD
    )
    key_pre = jnp.dot(act_one, key_whole, preferred_element_type=jnp.float32).reshape(
        rows_dev, heads_dev, HD
    )
    query_rot = rotate(query_pre, positions).astype(jnp.bfloat16)
    key_rot = rotate(key_pre, positions).astype(jnp.bfloat16)
    value_low = (
        jnp.dot(act_one, value_whole, preferred_element_type=jnp.float32)
        .astype(jnp.bfloat16)
        .reshape(rows_dev, heads_dev, HD)
    )
    scores = masked_scores(query_rot, key_rot, causal, scale)
    top = jnp.max(scores, axis=-1, keepdims=True)
    expo = jnp.exp(scores - top)
    total = jnp.sum(expo, axis=-1, keepdims=True)
    probs = expo / total
    log_total = top + jnp.log(total)
    mixed = jnp.einsum(
        "hqk,khc->qhc", probs.astype(jnp.bfloat16), value_low, preferred_element_type=jnp.float32
    )
    mixed = mixed.reshape(rows_dev, heads_dev * HD).astype(jnp.bfloat16)
    attn = lax.psum(contract_last(mixed, output_whole), "tensor")
    x_mid = x_in + attn
    act_two = rms_norm(x_mid, gain_two).astype(jnp.bfloat16)
    gate_pre = jnp.dot(act_two, common_gate, preferred_element_type=jnp.float32)
    up_pre = jnp.dot(act_two, common_up, preferred_element_type=jnp.float32)
    hidden_common = gated(gate_pre, up_pre).astype(jnp.bfloat16)
    common_out = contract_last(hidden_common, common_down)
    flat_ids = route_ids.reshape(-1)
    onehot = (flat_ids[:, None] == jnp.arange(experts, dtype=jnp.int32)[None, :]).astype(jnp.int32)
    ranks = jnp.sum(onehot * jnp.cumsum(onehot, axis=0), axis=1) - 1
    dest = flat_ids * capacity + ranks
    token_of = jnp.arange(rows_dev * topk, dtype=jnp.int32) // topk
    source = jnp.zeros((slots,), jnp.int32).at[dest].set(token_of)
    weight_of = jnp.zeros((slots,), jnp.float32).at[dest].set(route_gates.reshape(-1))
    filled = jnp.zeros((slots,), jnp.bool_).at[dest].set(True)
    outgoing = jnp.where(filled[:, None], act_two[source], jnp.zeros((), jnp.bfloat16)).reshape(
        experts, capacity, width
    )
    exp_gate = expert_gate[0]
    exp_up = expert_up[0]
    exp_down = expert_down[0]
    received = lax.all_to_all(outgoing, "dp", split_axis=0, concat_axis=0, tiled=True)
    sources = received.shape[0]
    count = received.shape[1]
    rows = received.reshape(sources * count, width)
    gate_rows = jnp.dot(rows, exp_gate, preferred_element_type=jnp.float32)
    up_rows = jnp.dot(rows, exp_up, preferred_element_type=jnp.float32)
    hidden_rows = gated(gate_rows, up_rows).astype(jnp.bfloat16)
    partial_value = jnp.dot(hidden_rows, exp_down, preferred_element_type=jnp.float32).reshape(
        sources, count, width
    )
    returned = lax.all_to_all(
        partial_value.astype(jnp.bfloat16), "dp", split_axis=0, concat_axis=0, tiled=True
    ).astype(partial_value.dtype)
    returned, kept_rows, kept_gate, kept_up = (
        returned,
        received,
        gate_rows.reshape(sources, count, -1),
        up_rows.reshape(sources, count, -1),
    )
    picked = returned.reshape(slots, width)[dest].reshape(rows_dev, topk, width)
    routed_part = jnp.sum(picked * route_gates[:, :, None], axis=1)
    ffn = lax.psum((common_out + routed_part).astype(jnp.bfloat16), "tensor").astype(jnp.float32)
    layer_out = (x_mid + ffn).astype(jnp.bfloat16)
    grad_out = cotangent.astype(jnp.float32)
    hidden_grad = jnp.dot(cotangent, common_down, preferred_element_type=jnp.float32)
    dummy_common, common_vjp = jax.vjp(gated, gate_pre, up_pre)
    gate_grad, up_grad = common_vjp(hidden_grad)
    gate_grad = gate_grad.astype(jnp.bfloat16)
    up_grad = up_grad.astype(jnp.bfloat16)
    common_gate_grad = contract_first(act_two, gate_grad)
    common_up_grad = contract_first(act_two, up_grad)
    common_down_grad = contract_first(cotangent, hidden_common)
    act_two_grad = contract_last(gate_grad, common_gate) + contract_last(up_grad, common_up)
    outgoing_grad = (
        (weight_of[:, None] * grad_out[source])
        .astype(jnp.bfloat16)
        .reshape(experts, capacity, width)
    )
    incoming_grad = lax.all_to_all(outgoing_grad, "dp", split_axis=0, concat_axis=0, tiled=True)
    hidden_width = kept_gate.shape[2]
    rows = kept_rows.reshape(-1, width)
    rows_out_grad = incoming_grad.reshape(-1, width)
    hidden_rows, expert_vjp = jax.vjp(
        gated, kept_gate.reshape(-1, hidden_width), kept_up.reshape(-1, hidden_width)
    )
    hidden_rows = hidden_rows.astype(jnp.bfloat16)
    hidden_rows_grad = contract_last(rows_out_grad, exp_down)
    gate_rows_grad, up_rows_grad = expert_vjp(hidden_rows_grad)
    gate_rows_grad = gate_rows_grad.astype(jnp.bfloat16)
    up_rows_grad = up_rows_grad.astype(jnp.bfloat16)
    expert_gate_grad = contract_first(rows, gate_rows_grad)[None]
    expert_up_grad = contract_first(rows, up_rows_grad)[None]
    expert_down_grad = contract_first(hidden_rows, rows_out_grad)[None]
    rows_in_grad = (
        contract_last(gate_rows_grad, exp_gate) + contract_last(up_rows_grad, exp_up)
    ).reshape(experts, capacity, width)
    returned_grad = lax.all_to_all(rows_in_grad, "dp", split_axis=0, concat_axis=0, tiled=True)
    routed_grad = jnp.sum(
        returned_grad.reshape(slots, width)[dest].reshape(rows_dev, topk, width), axis=1
    )
    act_two_total = lax.psum(act_two_grad + routed_grad, "tensor")
    dummy_second, second_vjp = jax.vjp(rms_norm, x_mid, gain_two)
    mid_norm_grad, gain_two_grad = second_vjp(act_two_total)
    mid_grad = grad_out + mid_norm_grad
    ffn_sums = (gain_two_grad, common_gate_grad, common_up_grad, common_down_grad)
    attn_grad = mid_grad.astype(jnp.bfloat16)
    output_w_grad = contract_first(attn_grad, mixed)
    mixed_grad = (
        jnp.dot(attn_grad, output_whole, preferred_element_type=jnp.float32)
        .astype(jnp.bfloat16)
        .reshape(rows_dev, heads_dev, HD)
    )
    probs_again = jnp.exp(masked_scores(query_rot, key_rot, causal, scale) - log_total)
    value_grad = jnp.einsum(
        "hqk,qhc->khc",
        probs_again.astype(jnp.bfloat16),
        mixed_grad,
        preferred_element_type=jnp.float32,
    ).astype(jnp.bfloat16)
    prob_grad = jnp.einsum(
        "qhc,khc->hqk", mixed_grad, value_low, preferred_element_type=jnp.float32
    )
    delta = jnp.sum(probs_again * prob_grad, axis=-1, keepdims=True)
    score_grad = (probs_again * (prob_grad - delta)).astype(jnp.bfloat16)
    query_rot_grad = (
        jnp.einsum("hqk,khc->qhc", score_grad, key_rot, preferred_element_type=jnp.float32) * scale
    )
    key_rot_grad = (
        jnp.einsum("hqk,qhc->khc", score_grad, query_rot, preferred_element_type=jnp.float32)
        * scale
    )

    def turn(values):
        return rotate(values, positions)

    dummy_turn, turn_vjp = jax.vjp(turn, query_pre)
    query_grad = turn_vjp(query_rot_grad)[0].reshape(rows_dev, heads_dev * HD).astype(jnp.bfloat16)
    key_grad = turn_vjp(key_rot_grad)[0].reshape(rows_dev, heads_dev * HD).astype(jnp.bfloat16)
    value_flat = value_grad.reshape(rows_dev, heads_dev * HD)
    query_w_grad = contract_first(act_one, query_grad)
    key_w_grad = contract_first(act_one, key_grad)
    value_w_grad = contract_first(act_one, value_flat)
    act_one_grad = (
        contract_last(query_grad, query_whole)
        + contract_last(key_grad, key_whole)
        + contract_last(value_flat, value_whole)
    )
    act_one_total = lax.psum(act_one_grad, "tensor")
    dummy_first, first_vjp = jax.vjp(rms_norm, x_in, gain_one)
    in_norm_grad, gain_one_grad = first_vjp(act_one_total)
    tokens_grad = (mid_grad + in_norm_grad).astype(jnp.bfloat16)
    every = (
        lax.psum_scatter(gain_one_grad, "dp", scatter_dimension=0, tiled=True),
        lax.psum_scatter(query_w_grad, "dp", scatter_dimension=0, tiled=True),
        lax.psum_scatter(key_w_grad, "dp", scatter_dimension=0, tiled=True),
        lax.psum_scatter(value_w_grad, "dp", scatter_dimension=0, tiled=True),
        lax.psum_scatter(output_w_grad, "dp", scatter_dimension=0, tiled=True),
        lax.psum_scatter(ffn_sums[0], "dp", scatter_dimension=0, tiled=True),
        lax.psum_scatter(ffn_sums[1], "dp", scatter_dimension=0, tiled=True),
        lax.psum_scatter(ffn_sums[2], "dp", scatter_dimension=0, tiled=True),
        lax.psum_scatter(ffn_sums[3], "dp", scatter_dimension=0, tiled=True),
    )
    attn_sums = every[:5]
    ffn_sums = every[5:]
    return (
        layer_out,
        tokens_grad,
        attn_sums[0],
        attn_sums[1],
        attn_sums[2],
        attn_sums[3],
        attn_sums[4],
        ffn_sums[0],
        ffn_sums[1],
        ffn_sums[2],
        ffn_sums[3],
        expert_gate_grad,
        expert_up_grad,
        expert_down_grad,
    )


def place():
    d = lax.axis_index("dp"); y = lax.axis_index("tensor")
    c = lax.rem(d, 2); x = lax.rem(lax.div(d, 2), 2); z = lax.div(d, 4)
    return z, x, y, c

def dev(z, x, y, c):
    return ((z * 2 + x) * 2 + c, y)

def blk(z, x, y, c):
    return ((z * 2 + x) * 2 + c) * 2 + y

def greet(z, x, y, c):
    bar = pltpu.get_barrier_semaphore()
    for other in (dev(z, 1 - x, y, c), dev(z, x, 1 - y, c), dev(z, x, y, 1 - c)):
        pl.semaphore_signal(bar, inc=1, device_id=other, device_id_type=MESH)
    @pl.when(z > 0)
    def _():
        pl.semaphore_signal(bar, inc=1, device_id=dev(z - 1, x, y, c), device_id_type=MESH)
    @pl.when(z < 3)
    def _():
        pl.semaphore_signal(bar, inc=1, device_id=dev(z + 1, x, y, c), device_id_type=MESH)
    pl.semaphore_wait(bar, 3 + (z > 0).astype(jnp.int32) + (z < 3).astype(jnp.int32))

def rcopy(src, dst, ssem, rsem, device):
    return pltpu.make_async_remote_copy(src_ref=src, dst_ref=dst, send_sem=ssem, recv_sem=rsem, device_id=device, device_id_type=MESH)

def gather_kernel(x_ref, o_ref, zs, zr, x0s, x0r, x1s, x1r, y0s, y0r, y1s, y1r, cs, cr, lsem):
    z, x, y, c = place()
    rows = x_ref.shape[0]; h = rows // 2
    lo, hi = pl.ds(0, h), pl.ds(h, h)
    part = (lo, hi)
    xn, yn, cn = dev(z, 1 - x, y, c), dev(z, x, 1 - y, c), dev(z, x, y, 1 - c)
    greet(z, x, y, c)
    mine = blk(z, x, y, c)
    own = pltpu.make_async_copy(x_ref, o_ref.at[mine], lsem)
    own.start()

    def zcopy(s, up):
        src = o_ref.at[blk(s, x, y, c)]
        return rcopy(src, o_ref.at[blk(s, x, y, c)], zs.at[s, up], zr.at[s], dev(z + (1 if up else -1), x, y, c))
    def x0(s):
        b = blk(s, x, y, c)
        return rcopy(o_ref.at[b, lo], o_ref.at[b, lo], x0s.at[s], x0r.at[s], xn)
    def y1(s):
        b = blk(s, x, y, c)
        return rcopy(o_ref.at[b, hi], o_ref.at[b, hi], y1s.at[s], y1r.at[s], yn)
    def y0(s, xx):
        b = blk(s, xx, y, c)
        return rcopy(o_ref.at[b, lo], o_ref.at[b, lo], y0s.at[s, xx], y0r.at[s, xx], yn)
    def x1(s, yy):
        b = blk(s, x, yy, c)
        return rcopy(o_ref.at[b, hi], o_ref.at[b, hi], x1s.at[s, yy], x1r.at[s, yy], xn)
    def cc(s, xx, yy, p):
        b = blk(s, xx, yy, c)
        i = (s * 2 + xx) * 2 + yy
        return rcopy(o_ref.at[b, part[p]], o_ref.at[b, part[p]], cs.at[i, p], cr.at[i, p], cn)
    def column(s):
        x0(s).start(); y1(s).start(); y0(s, x).start(); x1(s, y).start()
        cc(s, x, y, 0).start(); cc(s, x, y, 1).start()
    def middle(s):
        x0(s).wait_recv()
        y0(s, 1 - x).start(); cc(s, 1 - x, y, 0).start()
        y1(s).wait_recv()
        x1(s, 1 - y).start(); cc(s, x, 1 - y, 1).start()
    def last(s):
        for q in (0, 1):
            y0(s, q).wait_recv(); cc(s, q, 1 - y, 0).start()
            x1(s, q).wait_recv(); cc(s, 1 - x, q, 1).start()

    own.wait()
    @pl.when(z < 3)
    def _(): zcopy(z, 1).start()
    @pl.when(z > 0)
    def _(): zcopy(z, 0).start()
    column(z)
    def each(k, fn):
        if k == 0:
            fn(z)
            return
        for sign in (-1, 1):
            s = z + sign * k
            @pl.when((s >= 0) & (s <= 3))
            def _(s=s): fn(s)
    for k in range(1, 4):
        for sign in (-1, 1):
            s = z + sign * k
            @pl.when((s >= 0) & (s <= 3))
            def _(s=s, sign=sign):
                up = 1 if sign < 0 else 0
                zcopy(s, up).wait_recv()
                @pl.when((z + (1 if up else -1) >= 0) & (z + (1 if up else -1) <= 3))
                def _(): zcopy(s, up).start()
                column(s)
        each(k - 1, middle)
        if k >= 2: each(k - 2, last)
    each(3, middle); each(2, last); each(3, last)
    for s in range(4):
        for xx in (0, 1):
            for yy in (0, 1):
                for p in (0, 1):
                    cc(s, xx, yy, p).wait_recv()
    for s in range(4):
        x0(s).wait_send(); y1(s).wait_send()
        for q in (0, 1):
            y0(s, q).wait_send(); x1(s, q).wait_send()
            for r in (0, 1):
                for p in (0, 1): cc(s, q, r, p).wait_send()
        @pl.when((z < 3) & (s <= z))
        def _(): zcopy(s, 1).wait_send()
        @pl.when((z > 0) & (s >= z))
        def _(): zcopy(s, 0).wait_send()

def gather_rows(x, cid, name):
    rows, width = x.shape
    D = pltpu.SemaphoreType.DMA
    out = pl.pallas_call(gather_kernel, out_shape=jax.ShapeDtypeStruct((32, rows, width), x.dtype),
        in_specs=[pl.BlockSpec(memory_space=pl.ANY)], out_specs=pl.BlockSpec(memory_space=pl.ANY),
        scratch_shapes=[D((4, 2)), D((4,)), D((4,)), D((4,)), D((4, 2)), D((4, 2)), D((4, 2)), D((4, 2)), D((4,)), D((4,)), D((16, 2)), D((16, 2)), D],
        compiler_params=pltpu.CompilerParams(collective_id=cid, has_side_effects=True), name=name)(x)
    return out.reshape(32 * rows, width)

def scatter_kernel(p_ref, o_ref, acc, ic, iy0, ix0, ix1, iy1, izu, izd, ls, cs, cr, y0s, y0r, x0s, x0r, x1s, x1r, y1s, y1r, zus, zur, zds, zdr):
    z, x, y, c = place()
    rows = p_ref.shape[1]; h = rows // 2
    lo, hi = pl.ds(0, h), pl.ds(h, h)
    xn, yn, cn = dev(z, 1 - x, y, c), dev(z, x, 1 - y, c), dev(z, x, y, 1 - c)
    greet(z, x, y, c)
    def at(s, xx, yy): return (s * 2 + xx) * 2 + yy
    def load(s, xx, yy):
        return pltpu.make_async_copy(p_ref.at[blk(s, xx, yy, c)], acc.at[at(s, xx, yy)], ls.at[at(s, xx, yy)])
    def cc(s, xx, yy):
        i = at(s, xx, yy)
        return rcopy(p_ref.at[blk(s, xx, yy, 1 - c)], ic.at[i], cs.at[i], cr.at[i], cn)
    def y0(s, xx):
        return rcopy(acc.at[at(s, xx, 1 - y), lo], iy0.at[s * 2 + xx], y0s.at[s, xx], y0r.at[s, xx], yn)
    def x1(s, yy):
        return rcopy(acc.at[at(s, 1 - x, yy), hi], ix1.at[s * 2 + yy], x1s.at[s, yy], x1r.at[s, yy], xn)
    def x0(s):
        return rcopy(acc.at[at(s, 1 - x, y), lo], ix0.at[s], x0s.at[s], x0r.at[s], xn)
    def y1(s):
        return rcopy(acc.at[at(s, x, 1 - y), hi], iy1.at[s], y1s.at[s], y1r.at[s], yn)
    def zu(s):
        return rcopy(acc.at[at(s, x, y)], izu.at[s], zus.at[s], zur.at[s], dev(z + 1, x, y, c))
    def zd(s):
        return rcopy(acc.at[at(s, x, y)], izd.at[s], zds.at[s], zdr.at[s], dev(z - 1, x, y, c))
    def add(i, start, count, src, j):
        step = 16
        @pl.loop(0, count // step)
        def _(r):
            a = pl.ds(pl.multiple_of(start + r * step, step), step)
            b = pl.ds(pl.multiple_of(r * step, step), step)
            acc[i, a] = acc[i, a] + src[j, b]
    def order(fn, k):
        if k == 0:
            fn(z); return
        for sign in (-1, 1):
            s = z + sign * k
            @pl.when((s >= 0) & (s <= 3))
            def _(s=s): fn(s)
    def start(s):
        for xx in (0, 1):
            for yy in (0, 1):
                cc(s, xx, yy).start(); load(s, xx, yy).start()
    def first(s):
        for xx in (0, 1):
            for yy in (0, 1):
                load(s, xx, yy).wait(); cc(s, xx, yy).wait_recv()
                add(at(s, xx, yy), 0, rows, ic, at(s, xx, yy))
                @pl.when(yy != y)
                def _(): y0(s, xx).start()
                @pl.when(xx != x)
                def _(): x1(s, yy).start()
    def second(s):
        y0(s, 1 - x).wait_recv(); add(at(s, 1 - x, y), 0, h, iy0, s * 2 + 1 - x); x0(s).start()
        x1(s, 1 - y).wait_recv(); add(at(s, x, 1 - y), h, h, ix1, s * 2 + 1 - y); y1(s).start()
        y0(s, x).wait_recv(); add(at(s, x, y), 0, h, iy0, s * 2 + x)
        x1(s, y).wait_recv(); add(at(s, x, y), h, h, ix1, s * 2 + y)
    def third(s):
        me = at(s, x, y)
        x0(s).wait_recv(); add(me, 0, h, ix0, s)
        y1(s).wait_recv(); add(me, h, h, iy1, s)
        @pl.when((s >= z) & (z > 0))
        def _():
            zu(s).wait_recv(); add(me, 0, rows, izu, s)
        @pl.when((s <= z) & (z < 3))
        def _():
            zd(s).wait_recv(); add(me, 0, rows, izd, s)
        @pl.when(s > z)
        def _(): zu(s).start()
        @pl.when(s < z)
        def _(): zd(s).start()
    for k in (3, 2, 1, 0): order(start, k)
    for k in (3, 2, 1, 0):
        order(first, k)
        if k + 1 <= 3: order(second, k + 1)
        if k + 2 <= 3: order(third, k + 2)
    order(second, 0); order(third, 1); order(third, 0)
    o_ref[...] = acc[at(z, x, y)]
    for s in range(4):
        for q in (0, 1):
            for r in (0, 1): cc(s, q, r).wait_send()
            y0(s, q).wait_send(); x1(s, q).wait_send()
        x0(s).wait_send(); y1(s).wait_send()
        @pl.when(s > z)
        def _(): zu(s).wait_send()
        @pl.when(s < z)
        def _(): zd(s).wait_send()

def scatter_rows(p, cid, name):
    total, width = p.shape
    rows = total // 32; h = rows // 2
    D = pltpu.SemaphoreType.DMA
    V = lambda n, r: pltpu.VMEM((n, r, width), p.dtype)
    return pl.pallas_call(scatter_kernel, out_shape=jax.ShapeDtypeStruct((rows, width), p.dtype),
        in_specs=[pl.BlockSpec(memory_space=pl.ANY)], out_specs=pl.BlockSpec(memory_space=pltpu.VMEM),
        scratch_shapes=[V(16, rows), V(16, rows), V(8, h), V(4, h), V(8, h), V(4, h), V(4, rows), V(4, rows),
            D((16,)), D((16,)), D((16,)), D((4, 2)), D((4, 2)), D((4,)), D((4,)), D((4, 2)), D((4, 2)), D((4,)), D((4,)), D((4,)), D((4,)), D((4,)), D((4,))],
        compiler_params=pltpu.CompilerParams(collective_id=cid, has_side_effects=True, vmem_limit_bytes=56 << 20), name=name)(p.reshape(32, rows, width))


def start_kernel(n, *refs):
    ins, g_in = refs[:n], refs[n]
    outs, g_out = refs[n + 1:2 * n + 1], refs[2 * n + 1]
    zs, zr, xs, xr, cs, cr, ls = refs[2 * n + 2:2 * n + 9]
    gzs, gzr, gxs, gxr, gys, gyr, gcs, gcr, gl = refs[2 * n + 9:]
    z, x, y, c = place()
    xn, yn, cn = dev(z, 1 - x, y, c), dev(z, x, 1 - y, c), dev(z, x, y, 1 - c)
    greet(z, x, y, c)
    def pos(s, xx, cc_): return (s * 2 + xx) * 2 + cc_
    me = pos(z, x, c)
    owns = [pltpu.make_async_copy(ins[a], outs[a].at[me], ls.at[a]) for a in range(n)]
    owns.append(pltpu.make_async_copy(g_in, g_out.at[blk(z, x, y, c)], gl))
    for o in owns: o.start()
    def wz(a, s, up):
        r = outs[a].at[pos(s, x, c)]
        return rcopy(r, r, zs.at[a, s, up], zr.at[a, s], dev(z + (1 if up else -1), x, y, c))
    def wx(a, s):
        r = outs[a].at[pos(s, x, c)]
        return rcopy(r, r, xs.at[a, s], xr.at[a, s], xn)
    def wc(a, s, xx):
        r = outs[a].at[pos(s, xx, c)]
        return rcopy(r, r, cs.at[a, s * 2 + xx], cr.at[a, s * 2 + xx], cn)
    def gz(s, up):
        r = g_out.at[blk(s, x, y, c)]
        return rcopy(r, r, gzs.at[s, up], gzr.at[s], dev(z + (1 if up else -1), x, y, c))
    def gx(s):
        r = g_out.at[blk(s, x, y, c)]
        return rcopy(r, r, gxs.at[s], gxr.at[s], xn)
    def gy(s, xx):
        r = g_out.at[blk(s, xx, y, c)]
        return rcopy(r, r, gys.at[s, xx], gyr.at[s, xx], yn)
    def gc(s, xx, yy):
        r = g_out.at[blk(s, xx, yy, c)]
        return rcopy(r, r, gcs.at[s * 2 + xx, yy], gcr.at[s * 2 + xx, yy], cn)
    for o in owns: o.wait()
    def inside(v): return (v >= 0) & (v <= 3)
    def each(k, fn):
        if k == 0:
            fn(z); return
        for sign in (-1, 1):
            s = z + sign * k
            @pl.when(inside(s))
            def _(s=s): fn(s)
    def column(s):
        for a in range(n):
            wx(a, s).start(); wc(a, s, x).start()
    def gcolumn(s):
        gx(s).start(); gy(s, x).start(); gc(s, x, y).start()
    def middle(s):
        for a in range(n):
            wx(a, s).wait_recv(); wc(a, s, 1 - x).start()
    def gmiddle(s):
        gx(s).wait_recv(); gy(s, 1 - x).start(); gc(s, 1 - x, y).start()
    def glast(s):
        for q in (0, 1):
            gy(s, q).wait_recv(); gc(s, q, 1 - y).start()
    def launch(fn):
        @pl.when(z < 3)
        def _(): fn(1)
        @pl.when(z > 0)
        def _(): fn(0)
    launch(lambda up: [wz(a, z, up).start() for a in range(n)])
    column(z)
    launch(lambda up: gz(z, up).start())
    gcolumn(z)
    def arrive(k, recv, go, then):
        for sign in (-1, 1):
            s = z + sign * k
            @pl.when(inside(s))
            def _(s=s, sign=sign):
                up = 1 if sign < 0 else 0
                nxt = inside(z - sign)
                recv(s, up)
                @pl.when(nxt)
                def _(): go(s, up)
                then(s)
    for k in range(1, 4):
        arrive(k, lambda s, up: [wz(a, s, up).wait_recv() for a in range(n)], lambda s, up: [wz(a, s, up).start() for a in range(n)], column)
        each(k - 1, middle)
        arrive(k, lambda s, up: gz(s, up).wait_recv(), lambda s, up: gz(s, up).start(), gcolumn)
        each(k - 1, gmiddle)
    each(3, middle); each(3, gmiddle)
    for k in range(4): each(k, glast)
    for s in range(4):
        for q in (0, 1):
            for a in range(n): wc(a, s, q).wait_recv()
            for r in (0, 1): gc(s, q, r).wait_recv()
    for s in range(4):
        for a in range(n):
            wx(a, s).wait_send()
            for q in (0, 1): wc(a, s, q).wait_send()
        gx(s).wait_send()
        for q in (0, 1):
            gy(s, q).wait_send()
            for r in (0, 1): gc(s, q, r).wait_send()
        @pl.when((z < 3) & (s <= z))
        def _():
            gz(s, 1).wait_send()
            for a in range(n): wz(a, s, 1).wait_send()
        @pl.when((z > 0) & (s >= z))
        def _():
            gz(s, 0).wait_send()
            for a in range(n): wz(a, s, 0).wait_send()

def start_gather(arrays, rows, cid, name):
    n = len(arrays)
    D = pltpu.SemaphoreType.DMA
    any_ = pl.BlockSpec(memory_space=pl.ANY)
    outs = pl.pallas_call(functools.partial(start_kernel, n),
        out_shape=[jax.ShapeDtypeStruct((16,) + a.shape, a.dtype) for a in arrays] + [jax.ShapeDtypeStruct((32,) + rows.shape, rows.dtype)],
        in_specs=[any_] * (n + 1), out_specs=[any_] * (n + 1),
        scratch_shapes=[D((n, 4, 2)), D((n, 4)), D((n, 4)), D((n, 4)), D((n, 8)), D((n, 8)), D((n,)),
            D((4, 2)), D((4,)), D((4,)), D((4,)), D((4, 2)), D((4, 2)), D((8, 2)), D((8, 2)), D],
        compiler_params=pltpu.CompilerParams(collective_id=cid, has_side_effects=True), name=name)(*arrays, rows)
    return outs

def wsum_kernel(n, *refs):
    ins, outs = refs[:n], refs[n:2 * n]
    acc, ic, ix, izu, izd, ls, cs, cr, xs, xr, zus, zur, zds, zdr = refs[2 * n:]
    z, x, y, c = place()
    depth = ins[0].shape[1]
    xn, cn = dev(z, 1 - x, y, c), dev(z, x, y, 1 - c)
    greet_plane(z, x, y, c)
    def at(s, xx): return s * 2 + xx
    def pos(s, xx, cc_): return (s * 2 + xx) * 2 + cc_
    def load(a, s, xx):
        i = at(s, xx)
        return pltpu.make_async_copy(ins[a].at[pos(s, xx, c)], acc.at[a, i], ls.at[a, i])
    def wc(a, s, xx):
        i = at(s, xx)
        return rcopy(ins[a].at[pos(s, xx, 1 - c)], ic.at[a, i], cs.at[a, i], cr.at[a, i], cn)
    def wx(a, s):
        return rcopy(acc.at[a, at(s, 1 - x)], ix.at[a, s], xs.at[a, s], xr.at[a, s], xn)
    def zu(a, s):
        return rcopy(acc.at[a, at(s, x)], izu.at[a, s], zus.at[a, s], zur.at[a, s], dev(z + 1, x, y, c))
    def zd(a, s):
        return rcopy(acc.at[a, at(s, x)], izd.at[a, s], zds.at[a, s], zdr.at[a, s], dev(z - 1, x, y, c))
    def add(a, i, src, j):
        step = 16
        @pl.loop(0, depth // step)
        def _(r):
            b = pl.ds(pl.multiple_of(r * step, step), step)
            acc[a, i, b] = acc[a, i, b] + src[a, j, b]
    def order(fn, k):
        if k == 0:
            fn(z); return
        for sign in (-1, 1):
            s = z + sign * k
            @pl.when((s >= 0) & (s <= 3))
            def _(s=s): fn(s)
    def start(s):
        for a in range(n):
            for q in (0, 1):
                wc(a, s, q).start(); load(a, s, q).start()
    def first(s):
        for a in range(n):
            for q in (0, 1):
                load(a, s, q).wait(); wc(a, s, q).wait_recv()
                add(a, at(s, q), ic, at(s, q))
            wx(a, s).start()
    def second(s):
        for a in range(n):
            wx(a, s).wait_recv(); add(a, at(s, x), ix, s)
            @pl.when((s >= z) & (z > 0))
            def _():
                zu(a, s).wait_recv(); add(a, at(s, x), izu, s)
            @pl.when((s <= z) & (z < 3))
            def _():
                zd(a, s).wait_recv(); add(a, at(s, x), izd, s)
            @pl.when(s > z)
            def _(): zu(a, s).start()
            @pl.when(s < z)
            def _(): zd(a, s).start()
    for k in (3, 2, 1, 0): order(start, k)
    for k in (3, 2, 1, 0):
        order(first, k)
        if k + 1 <= 3: order(second, k + 1)
    order(second, 0)
    for a in range(n):
        outs[a][...] = acc[a, at(z, x)].astype(jnp.float32)
    for s in range(4):
        for a in range(n):
            for q in (0, 1): wc(a, s, q).wait_send()
            wx(a, s).wait_send()
            @pl.when(s > z)
            def _(): zu(a, s).wait_send()
            @pl.when(s < z)
            def _(): zd(a, s).wait_send()

def greet_plane(z, x, y, c):
    bar = pltpu.get_barrier_semaphore()
    for other in (dev(z, 1 - x, y, c), dev(z, x, y, 1 - c)):
        pl.semaphore_signal(bar, inc=1, device_id=other, device_id_type=MESH)
    @pl.when(z > 0)
    def _():
        pl.semaphore_signal(bar, inc=1, device_id=dev(z - 1, x, y, c), device_id_type=MESH)
    @pl.when(z < 3)
    def _():
        pl.semaphore_signal(bar, inc=1, device_id=dev(z + 1, x, y, c), device_id_type=MESH)
    pl.semaphore_wait(bar, 2 + (z > 0).astype(jnp.int32) + (z < 3).astype(jnp.int32))

def weight_sums(arrays, cid, name):
    n = len(arrays); total, width = arrays[0].shape; depth = total // 16
    D = pltpu.SemaphoreType.DMA
    V = lambda k: pltpu.VMEM((n, k, depth, width), arrays[0].dtype)
    return pl.pallas_call(functools.partial(wsum_kernel, n),
        out_shape=[jax.ShapeDtypeStruct((depth, width), jnp.float32)] * n,
        in_specs=[pl.BlockSpec(memory_space=pl.ANY)] * n, out_specs=[pl.BlockSpec(memory_space=pltpu.VMEM)] * n,
        scratch_shapes=[V(8), V(8), V(4), V(4), V(4), D((n, 8)), D((n, 8)), D((n, 8)), D((n, 4)), D((n, 4)), D((n, 4)), D((n, 4)), D((n, 4)), D((n, 4))],
        compiler_params=pltpu.CompilerParams(collective_id=cid, has_side_effects=True, vmem_limit_bytes=56 << 20), name=name)(*[a.reshape(16, depth, width) for a in arrays])


def routing_tables(gate_table, capacity):
    member = gate_table > 0.0
    ranks = jnp.cumsum(member.astype(jnp.int32), axis=1) - 1
    slot = jnp.arange(capacity, dtype=jnp.int32)
    pick = (ranks[:, None, :] == slot[None, :, None]) & member[:, None, :]
    slot_gate = jnp.sum(jnp.where(pick, gate_table[:, None, :], 0.0), axis=2)
    return pick.astype(jnp.bfloat16), slot_gate


def on_device(
    tokens,
    cotangent,
    route_ids,
    route_gates,
    gain_first,
    w_query,
    w_key,
    w_value,
    w_output,
    gain_second,
    shared_gate,
    shared_up,
    shared_down,
    expert_gate,
    expert_up,
    expert_down,
):
    f32, bf16 = jnp.float32, jnp.bfloat16
    rows_dev, width = tokens.shape
    topk = route_ids.shape[1]
    experts = lax.axis_size("dp")
    splits = lax.axis_size("tensor")
    half = rows_dev // splits
    mine = lax.axis_index("tensor") * half
    capacity = rows_dev * topk * 4 // (3 * experts)
    slots = experts * capacity
    scale = HD ** (-0.5)
    positions = jnp.arange(rows_dev, dtype=f32)
    causal = jnp.arange(rows_dev)[:, None] >= jnp.arange(rows_dev)[None, :]
    grad_half = lax.dynamic_slice_in_dim(cotangent, mine, half, axis=0)
    chosen = route_ids[:, :, None] == jnp.arange(experts, dtype=jnp.int32)[None, None, :]
    table = jnp.sum(jnp.where(chosen, route_gates[:, :, None], 0.0), axis=1)
    gains = jnp.concatenate([gain_first[None], gain_second[None], jnp.zeros((14, gain_first.shape[0]), bf16)])
    query_whole, key_whole, value_whole, output_whole, gains, tables, grad_all = start_gather(
        [w_query, w_key, w_value, w_output, gains, table.T], grad_half, 0, "gather_weights"
    )
    query_whole, key_whole, value_whole, output_whole = [
        w.reshape(width, -1) for w in (query_whole, key_whole, value_whole, output_whole)
    ]
    grad_all = grad_all.reshape(-1, width)
    gain_one = gains[:, 0].reshape(-1).astype(f32)
    gain_two = gains[:, 1].reshape(-1).astype(f32)

    depth, common_width = shared_gate.shape
    common_dev = common_width // experts
    packed = jnp.stack([shared_gate, shared_up, shared_down])
    packed = packed.reshape(3, depth, experts, common_dev).transpose(2, 0, 1, 3)
    packed = lax.all_to_all(packed, "dp", split_axis=0, concat_axis=0, tiled=True)
    packed = packed.transpose(1, 0, 2, 3).reshape(3, width, common_dev)
    common_gu = jnp.concatenate([packed[0], packed[1]], axis=1)
    common_down = packed[2]

    table = lax.dynamic_index_in_dim(tables, lax.axis_index("dp"), axis=1, keepdims=False)
    pick, slot_gate = routing_tables(table, capacity)

    x_in = tokens.astype(f32)
    act_one = rms_norm(x_in, gain_one).astype(bf16)
    heads_dev = query_whole.shape[1] // HD
    query_pre = jnp.dot(act_one, query_whole, preferred_element_type=f32).reshape(
        rows_dev, heads_dev, HD
    )
    key_pre = jnp.dot(act_one, key_whole, preferred_element_type=f32).reshape(
        rows_dev, heads_dev, HD
    )
    query_rot = rotate(query_pre, positions).astype(bf16)
    key_rot = rotate(key_pre, positions).astype(bf16)
    value_low = (
        jnp.dot(act_one, value_whole, preferred_element_type=f32)
        .astype(bf16)
        .reshape(rows_dev, heads_dev, HD)
    )
    scores = masked_scores(query_rot, key_rot, causal, scale)
    top = jnp.max(scores, axis=-1, keepdims=True)
    expo = jnp.exp(scores - top)
    total = jnp.sum(expo, axis=-1, keepdims=True)
    probs = expo / total
    log_total = top + jnp.log(total)
    mixed = jnp.einsum("hqk,khc->qhc", probs.astype(bf16), value_low, preferred_element_type=f32)
    mixed = mixed.reshape(rows_dev, heads_dev * HD).astype(bf16)
    attn = lax.psum_scatter(
        contract_last(mixed, output_whole), "tensor", scatter_dimension=0, tiled=True
    )
    x_half = lax.dynamic_slice_in_dim(tokens, mine, half, axis=0).astype(f32)
    x_mid = x_half + attn
    act_two = rms_norm(x_mid, gain_two).astype(bf16)

    act_all = gather_rows(act_two, 1, "gather_act")
    act_blocks = act_all.reshape(experts, rows_dev, width)
    grad_blocks = grad_all.reshape(experts, rows_dev, width)
    exp_gate, exp_up, exp_down = expert_gate[0], expert_up[0], expert_down[0]

    def select(blocks):
        return jnp.einsum("jst,jtd->jsd", pick, blocks, preferred_element_type=f32)

    def spread(rows):
        return jnp.einsum(
            "jst,jsd->jtd", pick, rows.reshape(experts, capacity, width), preferred_element_type=f32
        ).reshape(experts * rows_dev, width)

    weight = slot_gate.reshape(slots, 1)
    rows = select(act_blocks).astype(bf16).reshape(slots, width)
    rows_out_grad = (weight * select(grad_blocks).reshape(slots, width)).astype(bf16)
    gate_rows = jnp.dot(rows, exp_gate, preferred_element_type=f32)
    up_rows = jnp.dot(rows, exp_up, preferred_element_type=f32)
    hidden_rows, expert_vjp = jax.vjp(gated, gate_rows, up_rows)
    hidden_rows = hidden_rows.astype(bf16)
    hidden_rows_grad = contract_last(rows_out_grad, exp_down)
    gate_rows_grad, up_rows_grad = expert_vjp(hidden_rows_grad)
    gate_rows_grad = gate_rows_grad.astype(bf16)
    up_rows_grad = up_rows_grad.astype(bf16)
    rows_in_grad = contract_last(gate_rows_grad, exp_gate) + contract_last(up_rows_grad, exp_up)

    common_pre = jnp.dot(act_all, common_gu, preferred_element_type=f32)
    common_hidden, common_vjp = jax.vjp(
        gated, common_pre[:, :common_dev], common_pre[:, common_dev:]
    )
    common_hidden = common_hidden.astype(bf16)
    common_hidden_grad = jnp.dot(grad_all, common_down, preferred_element_type=f32)
    common_gu_grad = jnp.concatenate(common_vjp(common_hidden_grad), axis=1).astype(bf16)
    act_grad = spread(rows_in_grad.astype(bf16)) + contract_last(common_gu_grad, common_gu)
    act_two_total = scatter_rows(act_grad.astype(bf16), 2, "sum_act_grad").astype(f32)

    rows_out = jnp.dot(hidden_rows, exp_down, preferred_element_type=f32) * weight
    ffn = spread(rows_out.astype(bf16)) + contract_last(common_hidden, common_down)
    ffn = scatter_rows(ffn.astype(bf16), 3, "sum_ffn").astype(f32)
    layer_out = lax.all_gather((x_mid + ffn).astype(bf16), "tensor", axis=0, tiled=True)

    expert_gate_grad = contract_first(rows, gate_rows_grad)[None]
    expert_up_grad = contract_first(rows, up_rows_grad)[None]
    expert_down_grad = contract_first(hidden_rows, rows_out_grad)[None]
    common_w_grad = jnp.concatenate(
        [contract_first(act_all, common_gu_grad), contract_first(grad_all, common_hidden)], axis=1
    )
    common_w_grad = common_w_grad.astype(bf16).reshape(experts, depth, 3 * common_dev)
    common_w_grad = lax.all_to_all(common_w_grad, "dp", split_axis=0, concat_axis=0, tiled=True)
    common_w_grad = common_w_grad.astype(f32).reshape(experts, depth, 3, common_dev)
    common_w_grad = common_w_grad.transpose(2, 1, 0, 3).reshape(3, depth, common_width)

    dummy_second, second_vjp = jax.vjp(rms_norm, x_mid, gain_two)
    mid_norm_grad, gain_two_grad = second_vjp(act_two_total)
    mid_grad = grad_half.astype(f32) + mid_norm_grad
    attn_grad = lax.all_gather(mid_grad.astype(bf16), "tensor", axis=0, tiled=True)

    mixed_grad = (
        jnp.dot(attn_grad, output_whole, preferred_element_type=f32)
        .astype(bf16)
        .reshape(rows_dev, heads_dev, HD)
    )
    probs_again = jnp.exp(masked_scores(query_rot, key_rot, causal, scale) - log_total)
    value_grad = jnp.einsum(
        "hqk,qhc->khc", probs_again.astype(bf16), mixed_grad, preferred_element_type=f32
    ).astype(bf16)
    prob_grad = jnp.einsum("qhc,khc->hqk", mixed_grad, value_low, preferred_element_type=f32)
    delta = jnp.sum(probs_again * prob_grad, axis=-1, keepdims=True)
    score_grad = (probs_again * (prob_grad - delta)).astype(bf16)
    query_rot_grad = (
        jnp.einsum("hqk,khc->qhc", score_grad, key_rot, preferred_element_type=f32) * scale
    )
    key_rot_grad = (
        jnp.einsum("hqk,qhc->khc", score_grad, query_rot, preferred_element_type=f32) * scale
    )
    query_grad = rotate(query_rot_grad, -positions).reshape(rows_dev, heads_dev * HD).astype(bf16)
    key_grad = rotate(key_rot_grad, -positions).reshape(rows_dev, heads_dev * HD).astype(bf16)
    value_flat = value_grad.reshape(rows_dev, heads_dev * HD)
    act_one_grad = (
        contract_last(query_grad, query_whole)
        + contract_last(key_grad, key_whole)
        + contract_last(value_flat, value_whole)
    )
    act_one_total = lax.psum_scatter(act_one_grad, "tensor", scatter_dimension=0, tiled=True)
    dummy_first, first_vjp = jax.vjp(rms_norm, x_half, gain_one)
    in_norm_grad, gain_one_grad = first_vjp(act_one_total)
    tokens_grad = lax.all_gather((mid_grad + in_norm_grad).astype(bf16), "tensor", axis=0, tiled=True)

    query_sum, key_sum, value_sum, output_sum = weight_sums(
        [
            contract_first(act_one, query_grad).astype(bf16),
            contract_first(act_one, key_grad).astype(bf16),
            contract_first(act_one, value_flat).astype(bf16),
            contract_first(attn_grad, mixed).astype(bf16),
        ],
        4,
        "sum_weight_grads",
    )
    gain_grads = lax.psum(jnp.stack([gain_one_grad, gain_two_grad]), ("dp", "tensor"))
    gain_grads = lax.dynamic_slice_in_dim(
        gain_grads, lax.axis_index("dp") * gain_first.shape[0], gain_first.shape[0], axis=1
    )
    return (
        layer_out,
        tokens_grad,
        gain_grads[0],
        query_sum,
        key_sum,
        value_sum,
        output_sum,
        gain_grads[1],
        common_w_grad[0],
        common_w_grad[1],
        common_w_grad[2],
        expert_gate_grad,
        expert_up_grad,
        expert_down_grad,
    )


def solution(mesh):
    body = on_device if (mesh.shape["dp"], mesh.shape["tensor"]) == (16, 2) else on_device_plain
    in_specs = (
        P("dp", None),
        P("dp", None),
        P("dp", None),
        P("dp", None),
        P("dp"),
        P("dp", "tensor"),
        P("dp", "tensor"),
        P("dp", "tensor"),
        P("dp", "tensor"),
        P("dp"),
        P("dp", "tensor"),
        P("dp", "tensor"),
        P("dp", "tensor"),
        P("dp", None, "tensor"),
        P("dp", None, "tensor"),
        P("dp", "tensor", None),
    )
    out_specs = (
        P("dp", None),
        P("dp", None),
        P("dp"),
        P("dp", "tensor"),
        P("dp", "tensor"),
        P("dp", "tensor"),
        P("dp", "tensor"),
        P("dp"),
        P("dp", "tensor"),
        P("dp", "tensor"),
        P("dp", "tensor"),
        P("dp", None, "tensor"),
        P("dp", None, "tensor"),
        P("dp", "tensor", None),
    )
    return jax.shard_map(
        body, mesh=mesh, in_specs=in_specs, out_specs=out_specs, check_vma=False
    )
```

```python
import functools

import jax
import jax.numpy as jnp
from jax import lax
from jax.experimental import pallas as pl
from jax.experimental.pallas import tpu as pltpu
from jax.sharding import PartitionSpec as P

HD = 128
MESH = pl.DeviceIdType.MESH


EPS = 1e-06


def rms_norm(values, gain):
    mean_square = jnp.mean(values * values, axis=-1, keepdims=True)
    return values * lax.rsqrt(mean_square + EPS) * gain


def rotate(values, positions):
    head = values.shape[-1]
    half = head // 2
    freqs = 10000.0 ** (-2.0 * jnp.arange(half, dtype=jnp.float32) / head)
    angles = positions[:, None] * freqs[None, :]
    cosine = jnp.cos(angles)[:, None, :]
    sine = jnp.sin(angles)[:, None, :]
    first = values[..., :half]
    second = values[..., half:]
    return jnp.concatenate(
        [first * cosine - second * sine, second * cosine + first * sine], axis=-1
    )


def gated(gate_pre, up_pre):
    return gate_pre * jax.nn.sigmoid(gate_pre) * up_pre


def contract_last(left, right):
    return lax.dot_general(
        left, right, (((1,), (1,)), ((), ())), preferred_element_type=jnp.float32
    )


def contract_first(left, right):
    return lax.dot_general(
        left, right, (((0,), (0,)), ((), ())), preferred_element_type=jnp.float32
    )


def masked_scores(query_rot, key_rot, causal, scale):
    scores = (
        jnp.einsum("qhc,khc->hqk", query_rot, key_rot, preferred_element_type=jnp.float32) * scale
    )
    return jnp.where(causal[None], scores, -1e30)


def on_device_plain(
    tokens,
    cotangent,
    route_ids,
    route_gates,
    gain_first,
    w_query,
    w_key,
    w_value,
    w_output,
    gain_second,
    shared_gate,
    shared_up,
    shared_down,
    expert_gate,
    expert_up,
    expert_down,
):
    rows_dev, width = tokens.shape
    topk = route_ids.shape[1]
    experts = lax.axis_size("dp")
    capacity = rows_dev * topk * 4 // (3 * experts)
    slots = experts * capacity
    scale = HD ** (-0.5)
    positions = jnp.arange(rows_dev, dtype=jnp.float32)
    causal = jnp.arange(rows_dev)[:, None] >= jnp.arange(rows_dev)[None, :]
    gain_one, query_whole, key_whole, value_whole, output_whole = (
        lax.all_gather(gain_first, "dp", axis=0, tiled=True),
        lax.all_gather(w_query, "dp", axis=0, tiled=True),
        lax.all_gather(w_key, "dp", axis=0, tiled=True),
        lax.all_gather(w_value, "dp", axis=0, tiled=True),
        lax.all_gather(w_output, "dp", axis=0, tiled=True),
    )
    gain_two, common_gate, common_up, common_down = (
        lax.all_gather(gain_second, "dp", axis=0, tiled=True),
        lax.all_gather(shared_gate, "dp", axis=0, tiled=True),
        lax.all_gather(shared_up, "dp", axis=0, tiled=True),
        lax.all_gather(shared_down, "dp", axis=0, tiled=True),
    )
    gain_one = gain_one.astype(jnp.float32)
    gain_two = gain_two.astype(jnp.float32)
    x_in = tokens.astype(jnp.float32)
    act_one = rms_norm(x_in, gain_one).astype(jnp.bfloat16)
    heads_dev = query_whole.shape[1] // HD
    query_pre = jnp.dot(act_one, query_whole, preferred_element_type=jnp.float32).reshape(
        rows_dev, heads_dev, HD
    )
    key_pre = jnp.dot(act_one, key_whole, preferred_element_type=jnp.float32).reshape(
        rows_dev, heads_dev, HD
    )
    query_rot = rotate(query_pre, positions).astype(jnp.bfloat16)
    key_rot = rotate(key_pre, positions).astype(jnp.bfloat16)
    value_low = (
        jnp.dot(act_one, value_whole, preferred_element_type=jnp.float32)
        .astype(jnp.bfloat16)
        .reshape(rows_dev, heads_dev, HD)
    )
    scores = masked_scores(query_rot, key_rot, causal, scale)
    top = jnp.max(scores, axis=-1, keepdims=True)
    expo = jnp.exp(scores - top)
    total = jnp.sum(expo, axis=-1, keepdims=True)
    probs = expo / total
    log_total = top + jnp.log(total)
    mixed = jnp.einsum(
        "hqk,khc->qhc", probs.astype(jnp.bfloat16), value_low, preferred_element_type=jnp.float32
    )
    mixed = mixed.reshape(rows_dev, heads_dev * HD).astype(jnp.bfloat16)
    attn = lax.psum(contract_last(mixed, output_whole), "tensor")
    x_mid = x_in + attn
    act_two = rms_norm(x_mid, gain_two).astype(jnp.bfloat16)
    gate_pre = jnp.dot(act_two, common_gate, preferred_element_type=jnp.float32)
    up_pre = jnp.dot(act_two, common_up, preferred_element_type=jnp.float32)
    hidden_common = gated(gate_pre, up_pre).astype(jnp.bfloat16)
    common_out = contract_last(hidden_common, common_down)
    flat_ids = route_ids.reshape(-1)
    onehot = (flat_ids[:, None] == jnp.arange(experts, dtype=jnp.int32)[None, :]).astype(jnp.int32)
    ranks = jnp.sum(onehot * jnp.cumsum(onehot, axis=0), axis=1) - 1
    dest = flat_ids * capacity + ranks
    token_of = jnp.arange(rows_dev * topk, dtype=jnp.int32) // topk
    source = jnp.zeros((slots,), jnp.int32).at[dest].set(token_of)
    weight_of = jnp.zeros((slots,), jnp.float32).at[dest].set(route_gates.reshape(-1))
    filled = jnp.zeros((slots,), jnp.bool_).at[dest].set(True)
    outgoing = jnp.where(filled[:, None], act_two[source], jnp.zeros((), jnp.bfloat16)).reshape(
        experts, capacity, width
    )
    exp_gate = expert_gate[0]
    exp_up = expert_up[0]
    exp_down = expert_down[0]
    received = lax.all_to_all(outgoing, "dp", split_axis=0, concat_axis=0, tiled=True)
    sources = received.shape[0]
    count = received.shape[1]
    rows = received.reshape(sources * count, width)
    gate_rows = jnp.dot(rows, exp_gate, preferred_element_type=jnp.float32)
    up_rows = jnp.dot(rows, exp_up, preferred_element_type=jnp.float32)
    hidden_rows = gated(gate_rows, up_rows).astype(jnp.bfloat16)
    partial_value = jnp.dot(hidden_rows, exp_down, preferred_element_type=jnp.float32).reshape(
        sources, count, width
    )
    returned = lax.all_to_all(
        partial_value.astype(jnp.bfloat16), "dp", split_axis=0, concat_axis=0, tiled=True
    ).astype(partial_value.dtype)
    returned, kept_rows, kept_gate, kept_up = (
        returned,
        received,
        gate_rows.reshape(sources, count, -1),
        up_rows.reshape(sources, count, -1),
    )
    picked = returned.reshape(slots, width)[dest].reshape(rows_dev, topk, width)
    routed_part = jnp.sum(picked * route_gates[:, :, None], axis=1)
    ffn = lax.psum((common_out + routed_part).astype(jnp.bfloat16), "tensor").astype(jnp.float32)
    layer_out = (x_mid + ffn).astype(jnp.bfloat16)
    grad_out = cotangent.astype(jnp.float32)
    hidden_grad = jnp.dot(cotangent, common_down, preferred_element_type=jnp.float32)
    dummy_common, common_vjp = jax.vjp(gated, gate_pre, up_pre)
    gate_grad, up_grad = common_vjp(hidden_grad)
    gate_grad = gate_grad.astype(jnp.bfloat16)
    up_grad = up_grad.astype(jnp.bfloat16)
    common_gate_grad = contract_first(act_two, gate_grad)
    common_up_grad = contract_first(act_two, up_grad)
    common_down_grad = contract_first(cotangent, hidden_common)
    act_two_grad = contract_last(gate_grad, common_gate) + contract_last(up_grad, common_up)
    outgoing_grad = (
        (weight_of[:, None] * grad_out[source])
        .astype(jnp.bfloat16)
        .reshape(experts, capacity, width)
    )
    incoming_grad = lax.all_to_all(outgoing_grad, "dp", split_axis=0, concat_axis=0, tiled=True)
    hidden_width = kept_gate.shape[2]
    rows = kept_rows.reshape(-1, width)
    rows_out_grad = incoming_grad.reshape(-1, width)
    hidden_rows, expert_vjp = jax.vjp(
        gated, kept_gate.reshape(-1, hidden_width), kept_up.reshape(-1, hidden_width)
    )
    hidden_rows = hidden_rows.astype(jnp.bfloat16)
    hidden_rows_grad = contract_last(rows_out_grad, exp_down)
    gate_rows_grad, up_rows_grad = expert_vjp(hidden_rows_grad)
    gate_rows_grad = gate_rows_grad.astype(jnp.bfloat16)
    up_rows_grad = up_rows_grad.astype(jnp.bfloat16)
    expert_gate_grad = contract_first(rows, gate_rows_grad)[None]
    expert_up_grad = contract_first(rows, up_rows_grad)[None]
    expert_down_grad = contract_first(hidden_rows, rows_out_grad)[None]
    rows_in_grad = (
        contract_last(gate_rows_grad, exp_gate) + contract_last(up_rows_grad, exp_up)
    ).reshape(experts, capacity, width)
    returned_grad = lax.all_to_all(rows_in_grad, "dp", split_axis=0, concat_axis=0, tiled=True)
    routed_grad = jnp.sum(
        returned_grad.reshape(slots, width)[dest].reshape(rows_dev, topk, width), axis=1
    )
    act_two_total = lax.psum(act_two_grad + routed_grad, "tensor")
    dummy_second, second_vjp = jax.vjp(rms_norm, x_mid, gain_two)
    mid_norm_grad, gain_two_grad = second_vjp(act_two_total)
    mid_grad = grad_out + mid_norm_grad
    ffn_sums = (gain_two_grad, common_gate_grad, common_up_grad, common_down_grad)
    attn_grad = mid_grad.astype(jnp.bfloat16)
    output_w_grad = contract_first(attn_grad, mixed)
    mixed_grad = (
        jnp.dot(attn_grad, output_whole, preferred_element_type=jnp.float32)
        .astype(jnp.bfloat16)
        .reshape(rows_dev, heads_dev, HD)
    )
    probs_again = jnp.exp(masked_scores(query_rot, key_rot, causal, scale) - log_total)
    value_grad = jnp.einsum(
        "hqk,qhc->khc",
        probs_again.astype(jnp.bfloat16),
        mixed_grad,
        preferred_element_type=jnp.float32,
    ).astype(jnp.bfloat16)
    prob_grad = jnp.einsum(
        "qhc,khc->hqk", mixed_grad, value_low, preferred_element_type=jnp.float32
    )
    delta = jnp.sum(probs_again * prob_grad, axis=-1, keepdims=True)
    score_grad = (probs_again * (prob_grad - delta)).astype(jnp.bfloat16)
    query_rot_grad = (
        jnp.einsum("hqk,khc->qhc", score_grad, key_rot, preferred_element_type=jnp.float32) * scale
    )
    key_rot_grad = (
        jnp.einsum("hqk,qhc->khc", score_grad, query_rot, preferred_element_type=jnp.float32)
        * scale
    )

    def turn(values):
        return rotate(values, positions)

    dummy_turn, turn_vjp = jax.vjp(turn, query_pre)
    query_grad = turn_vjp(query_rot_grad)[0].reshape(rows_dev, heads_dev * HD).astype(jnp.bfloat16)
    key_grad = turn_vjp(key_rot_grad)[0].reshape(rows_dev, heads_dev * HD).astype(jnp.bfloat16)
    value_flat = value_grad.reshape(rows_dev, heads_dev * HD)
    query_w_grad = contract_first(act_one, query_grad)
    key_w_grad = contract_first(act_one, key_grad)
    value_w_grad = contract_first(act_one, value_flat)
    act_one_grad = (
        contract_last(query_grad, query_whole)
        + contract_last(key_grad, key_whole)
        + contract_last(value_flat, value_whole)
    )
    act_one_total = lax.psum(act_one_grad, "tensor")
    dummy_first, first_vjp = jax.vjp(rms_norm, x_in, gain_one)
    in_norm_grad, gain_one_grad = first_vjp(act_one_total)
    tokens_grad = (mid_grad + in_norm_grad).astype(jnp.bfloat16)
    every = (
        lax.psum_scatter(gain_one_grad, "dp", scatter_dimension=0, tiled=True),
        lax.psum_scatter(query_w_grad, "dp", scatter_dimension=0, tiled=True),
        lax.psum_scatter(key_w_grad, "dp", scatter_dimension=0, tiled=True),
        lax.psum_scatter(value_w_grad, "dp", scatter_dimension=0, tiled=True),
        lax.psum_scatter(output_w_grad, "dp", scatter_dimension=0, tiled=True),
        lax.psum_scatter(ffn_sums[0], "dp", scatter_dimension=0, tiled=True),
        lax.psum_scatter(ffn_sums[1], "dp", scatter_dimension=0, tiled=True),
        lax.psum_scatter(ffn_sums[2], "dp", scatter_dimension=0, tiled=True),
        lax.psum_scatter(ffn_sums[3], "dp", scatter_dimension=0, tiled=True),
    )
    attn_sums = every[:5]
    ffn_sums = every[5:]
    return (
        layer_out,
        tokens_grad,
        attn_sums[0],
        attn_sums[1],
        attn_sums[2],
        attn_sums[3],
        attn_sums[4],
        ffn_sums[0],
        ffn_sums[1],
        ffn_sums[2],
        ffn_sums[3],
        expert_gate_grad,
        expert_up_grad,
        expert_down_grad,
    )


def place():
    d = lax.axis_index("dp"); y = lax.axis_index("tensor")
    c = lax.rem(d, 2); x = lax.rem(lax.div(d, 2), 2); z = lax.div(d, 4)
    return z, x, y, c

def dev(z, x, y, c):
    return ((z * 2 + x) * 2 + c, y)

def blk(z, x, y, c):
    return ((z * 2 + x) * 2 + c) * 2 + y

def greet(z, x, y, c):
    bar = pltpu.get_barrier_semaphore()
    for other in (dev(z, 1 - x, y, c), dev(z, x, 1 - y, c), dev(z, x, y, 1 - c)):
        pl.semaphore_signal(bar, inc=1, device_id=other, device_id_type=MESH)
    @pl.when(z > 0)
    def _():
        pl.semaphore_signal(bar, inc=1, device_id=dev(z - 1, x, y, c), device_id_type=MESH)
    @pl.when(z < 3)
    def _():
        pl.semaphore_signal(bar, inc=1, device_id=dev(z + 1, x, y, c), device_id_type=MESH)
    pl.semaphore_wait(bar, 3 + (z > 0).astype(jnp.int32) + (z < 3).astype(jnp.int32))

def rcopy(src, dst, ssem, rsem, device):
    return pltpu.make_async_remote_copy(src_ref=src, dst_ref=dst, send_sem=ssem, recv_sem=rsem, device_id=device, device_id_type=MESH)

def gather_kernel(x_ref, o_ref, zs, zr, x0s, x0r, x1s, x1r, y0s, y0r, y1s, y1r, cs, cr, lsem):
    z, x, y, c = place()
    rows = x_ref.shape[0]; h = rows // 2
    lo, hi = pl.ds(0, h), pl.ds(h, h)
    part = (lo, hi)
    xn, yn, cn = dev(z, 1 - x, y, c), dev(z, x, 1 - y, c), dev(z, x, y, 1 - c)
    greet(z, x, y, c)
    mine = blk(z, x, y, c)
    own = pltpu.make_async_copy(x_ref, o_ref.at[mine], lsem)
    own.start()

    def zcopy(s, up):
        src = o_ref.at[blk(s, x, y, c)]
        return rcopy(src, o_ref.at[blk(s, x, y, c)], zs.at[s, up], zr.at[s], dev(z + (1 if up else -1), x, y, c))
    def x0(s):
        b = blk(s, x, y, c)
        return rcopy(o_ref.at[b, lo], o_ref.at[b, lo], x0s.at[s], x0r.at[s], xn)
    def y1(s):
        b = blk(s, x, y, c)
        return rcopy(o_ref.at[b, hi], o_ref.at[b, hi], y1s.at[s], y1r.at[s], yn)
    def y0(s, xx):
        b = blk(s, xx, y, c)
        return rcopy(o_ref.at[b, lo], o_ref.at[b, lo], y0s.at[s, xx], y0r.at[s, xx], yn)
    def x1(s, yy):
        b = blk(s, x, yy, c)
        return rcopy(o_ref.at[b, hi], o_ref.at[b, hi], x1s.at[s, yy], x1r.at[s, yy], xn)
    def cc(s, xx, yy, p):
        b = blk(s, xx, yy, c)
        i = (s * 2 + xx) * 2 + yy
        return rcopy(o_ref.at[b, part[p]], o_ref.at[b, part[p]], cs.at[i, p], cr.at[i, p], cn)
    def column(s):
        x0(s).start(); y1(s).start(); y0(s, x).start(); x1(s, y).start()
        cc(s, x, y, 0).start(); cc(s, x, y, 1).start()
    def middle(s):
        x0(s).wait_recv()
        y0(s, 1 - x).start(); cc(s, 1 - x, y, 0).start()
        y1(s).wait_recv()
        x1(s, 1 - y).start(); cc(s, x, 1 - y, 1).start()
    def last(s):
        for q in (0, 1):
            y0(s, q).wait_recv(); cc(s, q, 1 - y, 0).start()
            x1(s, q).wait_recv(); cc(s, 1 - x, q, 1).start()

    own.wait()
    @pl.when(z < 3)
    def _(): zcopy(z, 1).start()
    @pl.when(z > 0)
    def _(): zcopy(z, 0).start()
    column(z)
    def each(k, fn):
        if k == 0:
            fn(z)
            return
        for sign in (-1, 1):
            s = z + sign * k
            @pl.when((s >= 0) & (s <= 3))
            def _(s=s): fn(s)
    for k in range(1, 4):
        for sign in (-1, 1):
            s = z + sign * k
            @pl.when((s >= 0) & (s <= 3))
            def _(s=s, sign=sign):
                up = 1 if sign < 0 else 0
                zcopy(s, up).wait_recv()
                @pl.when((z + (1 if up else -1) >= 0) & (z + (1 if up else -1) <= 3))
                def _(): zcopy(s, up).start()
                column(s)
        each(k - 1, middle)
        if k >= 2: each(k - 2, last)
    each(3, middle); each(2, last); each(3, last)
    for s in range(4):
        for xx in (0, 1):
            for yy in (0, 1):
                for p in (0, 1):
                    cc(s, xx, yy, p).wait_recv()
    for s in range(4):
        x0(s).wait_send(); y1(s).wait_send()
        for q in (0, 1):
            y0(s, q).wait_send(); x1(s, q).wait_send()
            for r in (0, 1):
                for p in (0, 1): cc(s, q, r, p).wait_send()
        @pl.when((z < 3) & (s <= z))
        def _(): zcopy(s, 1).wait_send()
        @pl.when((z > 0) & (s >= z))
        def _(): zcopy(s, 0).wait_send()

def gather_rows(x, cid, name):
    rows, width = x.shape
    D = pltpu.SemaphoreType.DMA
    out = pl.pallas_call(gather_kernel, out_shape=jax.ShapeDtypeStruct((32, rows, width), x.dtype),
        in_specs=[pl.BlockSpec(memory_space=pl.ANY)], out_specs=pl.BlockSpec(memory_space=pl.ANY),
        scratch_shapes=[D((4, 2)), D((4,)), D((4,)), D((4,)), D((4, 2)), D((4, 2)), D((4, 2)), D((4, 2)), D((4,)), D((4,)), D((16, 2)), D((16, 2)), D],
        compiler_params=pltpu.CompilerParams(collective_id=cid, has_side_effects=True), name=name)(x)
    return out.reshape(32 * rows, width)

def scatter_kernel(p_ref, o_ref, acc, ic, iy0, ix0, ix1, iy1, izu, izd, ls, cs, cr, y0s, y0r, x0s, x0r, x1s, x1r, y1s, y1r, zus, zur, zds, zdr):
    z, x, y, c = place()
    rows = p_ref.shape[1]; h = rows // 2
    lo, hi = pl.ds(0, h), pl.ds(h, h)
    xn, yn, cn = dev(z, 1 - x, y, c), dev(z, x, 1 - y, c), dev(z, x, y, 1 - c)
    greet(z, x, y, c)
    def at(s, xx, yy): return (s * 2 + xx) * 2 + yy
    def load(s, xx, yy):
        return pltpu.make_async_copy(p_ref.at[blk(s, xx, yy, c)], acc.at[at(s, xx, yy)], ls.at[at(s, xx, yy)])
    def cc(s, xx, yy):
        i = at(s, xx, yy)
        return rcopy(p_ref.at[blk(s, xx, yy, 1 - c)], ic.at[i], cs.at[i], cr.at[i], cn)
    def y0(s, xx):
        return rcopy(acc.at[at(s, xx, 1 - y), lo], iy0.at[s * 2 + xx], y0s.at[s, xx], y0r.at[s, xx], yn)
    def x1(s, yy):
        return rcopy(acc.at[at(s, 1 - x, yy), hi], ix1.at[s * 2 + yy], x1s.at[s, yy], x1r.at[s, yy], xn)
    def x0(s):
        return rcopy(acc.at[at(s, 1 - x, y), lo], ix0.at[s], x0s.at[s], x0r.at[s], xn)
    def y1(s):
        return rcopy(acc.at[at(s, x, 1 - y), hi], iy1.at[s], y1s.at[s], y1r.at[s], yn)
    def zu(s):
        return rcopy(acc.at[at(s, x, y)], izu.at[s], zus.at[s], zur.at[s], dev(z + 1, x, y, c))
    def zd(s):
        return rcopy(acc.at[at(s, x, y)], izd.at[s], zds.at[s], zdr.at[s], dev(z - 1, x, y, c))
    def add(i, start, count, src, j):
        step = 16
        @pl.loop(0, count // step)
        def _(r):
            a = pl.ds(pl.multiple_of(start + r * step, step), step)
            b = pl.ds(pl.multiple_of(r * step, step), step)
            acc[i, a] = acc[i, a] + src[j, b]
    def order(fn, k):
        if k == 0:
            fn(z); return
        for sign in (-1, 1):
            s = z + sign * k
            @pl.when((s >= 0) & (s <= 3))
            def _(s=s): fn(s)
    def start(s):
        for xx in (0, 1):
            for yy in (0, 1):
                cc(s, xx, yy).start(); load(s, xx, yy).start()
    def first(s):
        for xx in (0, 1):
            for yy in (0, 1):
                load(s, xx, yy).wait(); cc(s, xx, yy).wait_recv()
                add(at(s, xx, yy), 0, rows, ic, at(s, xx, yy))
                @pl.when(yy != y)
                def _(): y0(s, xx).start()
                @pl.when(xx != x)
                def _(): x1(s, yy).start()
    def second(s):
        y0(s, 1 - x).wait_recv(); add(at(s, 1 - x, y), 0, h, iy0, s * 2 + 1 - x); x0(s).start()
        x1(s, 1 - y).wait_recv(); add(at(s, x, 1 - y), h, h, ix1, s * 2 + 1 - y); y1(s).start()
        y0(s, x).wait_recv(); add(at(s, x, y), 0, h, iy0, s * 2 + x)
        x1(s, y).wait_recv(); add(at(s, x, y), h, h, ix1, s * 2 + y)
    def third(s):
        me = at(s, x, y)
        x0(s).wait_recv(); add(me, 0, h, ix0, s)
        y1(s).wait_recv(); add(me, h, h, iy1, s)
        @pl.when((s >= z) & (z > 0))
        def _():
            zu(s).wait_recv(); add(me, 0, rows, izu, s)
        @pl.when((s <= z) & (z < 3))
        def _():
            zd(s).wait_recv(); add(me, 0, rows, izd, s)
        @pl.when(s > z)
        def _(): zu(s).start()
        @pl.when(s < z)
        def _(): zd(s).start()
    for k in (3, 2, 1, 0): order(start, k)
    for k in (3, 2, 1, 0):
        order(first, k)
        if k + 1 <= 3: order(second, k + 1)
        if k + 2 <= 3: order(third, k + 2)
    order(second, 0); order(third, 1); order(third, 0)
    o_ref[...] = acc[at(z, x, y)]
    for s in range(4):
        for q in (0, 1):
            for r in (0, 1): cc(s, q, r).wait_send()
            y0(s, q).wait_send(); x1(s, q).wait_send()
        x0(s).wait_send(); y1(s).wait_send()
        @pl.when(s > z)
        def _(): zu(s).wait_send()
        @pl.when(s < z)
        def _(): zd(s).wait_send()

def scatter_rows(p, cid, name):
    total, width = p.shape
    rows = total // 32; h = rows // 2
    D = pltpu.SemaphoreType.DMA
    V = lambda n, r: pltpu.VMEM((n, r, width), p.dtype)
    return pl.pallas_call(scatter_kernel, out_shape=jax.ShapeDtypeStruct((rows, width), p.dtype),
        in_specs=[pl.BlockSpec(memory_space=pl.ANY)], out_specs=pl.BlockSpec(memory_space=pltpu.VMEM),
        scratch_shapes=[V(16, rows), V(16, rows), V(8, h), V(4, h), V(8, h), V(4, h), V(4, rows), V(4, rows),
            D((16,)), D((16,)), D((16,)), D((4, 2)), D((4, 2)), D((4,)), D((4,)), D((4, 2)), D((4, 2)), D((4,)), D((4,)), D((4,)), D((4,)), D((4,)), D((4,))],
        compiler_params=pltpu.CompilerParams(collective_id=cid, has_side_effects=True, vmem_limit_bytes=56 << 20), name=name)(p.reshape(32, rows, width))


def start_kernel(n, *refs):
    ins, g_in = refs[:n], refs[n]
    outs, g_out = refs[n + 1:2 * n + 1], refs[2 * n + 1]
    zs, zr, xs, xr, cs, cr, ls = refs[2 * n + 2:2 * n + 9]
    gzs, gzr, gxs, gxr, gys, gyr, gcs, gcr, gl = refs[2 * n + 9:]
    z, x, y, c = place()
    xn, yn, cn = dev(z, 1 - x, y, c), dev(z, x, 1 - y, c), dev(z, x, y, 1 - c)
    greet(z, x, y, c)
    def pos(s, xx, cc_): return (s * 2 + xx) * 2 + cc_
    me = pos(z, x, c)
    owns = [pltpu.make_async_copy(ins[a], outs[a].at[me], ls.at[a]) for a in range(n)]
    owns.append(pltpu.make_async_copy(g_in, g_out.at[blk(z, x, y, c)], gl))
    for o in owns: o.start()
    def wz(a, s, up):
        r = outs[a].at[pos(s, x, c)]
        return rcopy(r, r, zs.at[a, s, up], zr.at[a, s], dev(z + (1 if up else -1), x, y, c))
    def wx(a, s):
        r = outs[a].at[pos(s, x, c)]
        return rcopy(r, r, xs.at[a, s], xr.at[a, s], xn)
    def wc(a, s, xx):
        r = outs[a].at[pos(s, xx, c)]
        return rcopy(r, r, cs.at[a, s * 2 + xx], cr.at[a, s * 2 + xx], cn)
    def gz(s, up):
        r = g_out.at[blk(s, x, y, c)]
        return rcopy(r, r, gzs.at[s, up], gzr.at[s], dev(z + (1 if up else -1), x, y, c))
    def gx(s):
        r = g_out.at[blk(s, x, y, c)]
        return rcopy(r, r, gxs.at[s], gxr.at[s], xn)
    def gy(s, xx):
        r = g_out.at[blk(s, xx, y, c)]
        return rcopy(r, r, gys.at[s, xx], gyr.at[s, xx], yn)
    def gc(s, xx, yy):
        r = g_out.at[blk(s, xx, yy, c)]
        return rcopy(r, r, gcs.at[s * 2 + xx, yy], gcr.at[s * 2 + xx, yy], cn)
    for o in owns: o.wait()
    def inside(v): return (v >= 0) & (v <= 3)
    def each(k, fn):
        if k == 0:
            fn(z); return
        for sign in (-1, 1):
            s = z + sign * k
            @pl.when(inside(s))
            def _(s=s): fn(s)
    def column(s):
        for a in range(n):
            wx(a, s).start(); wc(a, s, x).start()
    def gcolumn(s):
        gx(s).start(); gy(s, x).start(); gc(s, x, y).start()
    def middle(s):
        for a in range(n):
            wx(a, s).wait_recv(); wc(a, s, 1 - x).start()
    def gmiddle(s):
        gx(s).wait_recv(); gy(s, 1 - x).start(); gc(s, 1 - x, y).start()
    def glast(s):
        for q in (0, 1):
            gy(s, q).wait_recv(); gc(s, q, 1 - y).start()
    def launch(fn):
        @pl.when(z < 3)
        def _(): fn(1)
        @pl.when(z > 0)
        def _(): fn(0)
    launch(lambda up: [wz(a, z, up).start() for a in range(n)])
    column(z)
    launch(lambda up: gz(z, up).start())
    gcolumn(z)
    def arrive(k, recv, go, then):
        for sign in (-1, 1):
            s = z + sign * k
            @pl.when(inside(s))
            def _(s=s, sign=sign):
                up = 1 if sign < 0 else 0
                nxt = inside(z - sign)
                recv(s, up)
                @pl.when(nxt)
                def _(): go(s, up)
                then(s)
    for k in range(1, 4):
        arrive(k, lambda s, up: [wz(a, s, up).wait_recv() for a in range(n)], lambda s, up: [wz(a, s, up).start() for a in range(n)], column)
        each(k - 1, middle)
        arrive(k, lambda s, up: gz(s, up).wait_recv(), lambda s, up: gz(s, up).start(), gcolumn)
        each(k - 1, gmiddle)
    each(3, middle); each(3, gmiddle)
    for k in range(4): each(k, glast)
    for s in range(4):
        for q in (0, 1):
            for a in range(n): wc(a, s, q).wait_recv()
            for r in (0, 1): gc(s, q, r).wait_recv()
    for s in range(4):
        for a in range(n):
            wx(a, s).wait_send()
            for q in (0, 1): wc(a, s, q).wait_send()
        gx(s).wait_send()
        for q in (0, 1):
            gy(s, q).wait_send()
            for r in (0, 1): gc(s, q, r).wait_send()
        @pl.when((z < 3) & (s <= z))
        def _():
            gz(s, 1).wait_send()
            for a in range(n): wz(a, s, 1).wait_send()
        @pl.when((z > 0) & (s >= z))
        def _():
            gz(s, 0).wait_send()
            for a in range(n): wz(a, s, 0).wait_send()

def start_gather(arrays, rows, cid, name):
    n = len(arrays)
    D = pltpu.SemaphoreType.DMA
    any_ = pl.BlockSpec(memory_space=pl.ANY)
    outs = pl.pallas_call(functools.partial(start_kernel, n),
        out_shape=[jax.ShapeDtypeStruct((16,) + a.shape, a.dtype) for a in arrays] + [jax.ShapeDtypeStruct((32,) + rows.shape, rows.dtype)],
        in_specs=[any_] * (n + 1), out_specs=[any_] * (n + 1),
        scratch_shapes=[D((n, 4, 2)), D((n, 4)), D((n, 4)), D((n, 4)), D((n, 8)), D((n, 8)), D((n,)),
            D((4, 2)), D((4,)), D((4,)), D((4,)), D((4, 2)), D((4, 2)), D((8, 2)), D((8, 2)), D],
        compiler_params=pltpu.CompilerParams(collective_id=cid, has_side_effects=True), name=name)(*arrays, rows)
    return outs

def wsum_kernel(n, *refs):
    ins, outs = refs[:n], refs[n:2 * n]
    acc, ic, ix, izu, izd, ls, cs, cr, xs, xr, zus, zur, zds, zdr = refs[2 * n:]
    z, x, y, c = place()
    depth = ins[0].shape[1]
    xn, cn = dev(z, 1 - x, y, c), dev(z, x, y, 1 - c)
    greet_plane(z, x, y, c)
    def at(s, xx): return s * 2 + xx
    def pos(s, xx, cc_): return (s * 2 + xx) * 2 + cc_
    def load(a, s, xx):
        i = at(s, xx)
        return pltpu.make_async_copy(ins[a].at[pos(s, xx, c)], acc.at[a, i], ls.at[a, i])
    def wc(a, s, xx):
        i = at(s, xx)
        return rcopy(ins[a].at[pos(s, xx, 1 - c)], ic.at[a, i], cs.at[a, i], cr.at[a, i], cn)
    def wx(a, s):
        return rcopy(acc.at[a, at(s, 1 - x)], ix.at[a, s], xs.at[a, s], xr.at[a, s], xn)
    def zu(a, s):
        return rcopy(acc.at[a, at(s, x)], izu.at[a, s], zus.at[a, s], zur.at[a, s], dev(z + 1, x, y, c))
    def zd(a, s):
        return rcopy(acc.at[a, at(s, x)], izd.at[a, s], zds.at[a, s], zdr.at[a, s], dev(z - 1, x, y, c))
    def add(a, i, src, j):
        step = 16
        @pl.loop(0, depth // step)
        def _(r):
            b = pl.ds(pl.multiple_of(r * step, step), step)
            acc[a, i, b] = acc[a, i, b] + src[a, j, b]
    def order(fn, k):
        if k == 0:
            fn(z); return
        for sign in (-1, 1):
            s = z + sign * k
            @pl.when((s >= 0) & (s <= 3))
            def _(s=s): fn(s)
    def start(s):
        for a in range(n):
            for q in (0, 1):
                wc(a, s, q).start(); load(a, s, q).start()
    def first(s):
        for a in range(n):
            for q in (0, 1):
                load(a, s, q).wait(); wc(a, s, q).wait_recv()
                add(a, at(s, q), ic, at(s, q))
            wx(a, s).start()
    def second(s):
        for a in range(n):
            wx(a, s).wait_recv(); add(a, at(s, x), ix, s)
            @pl.when((s >= z) & (z > 0))
            def _():
                zu(a, s).wait_recv(); add(a, at(s, x), izu, s)
            @pl.when((s <= z) & (z < 3))
            def _():
                zd(a, s).wait_recv(); add(a, at(s, x), izd, s)
            @pl.when(s > z)
            def _(): zu(a, s).start()
            @pl.when(s < z)
            def _(): zd(a, s).start()
    for k in (3, 2, 1, 0): order(start, k)
    for k in (3, 2, 1, 0):
        order(first, k)
        if k + 1 <= 3: order(second, k + 1)
    order(second, 0)
    for a in range(n):
        outs[a][...] = acc[a, at(z, x)].astype(jnp.float32)
    for s in range(4):
        for a in range(n):
            for q in (0, 1): wc(a, s, q).wait_send()
            wx(a, s).wait_send()
            @pl.when(s > z)
            def _(): zu(a, s).wait_send()
            @pl.when(s < z)
            def _(): zd(a, s).wait_send()

def greet_plane(z, x, y, c):
    bar = pltpu.get_barrier_semaphore()
    for other in (dev(z, 1 - x, y, c), dev(z, x, y, 1 - c)):
        pl.semaphore_signal(bar, inc=1, device_id=other, device_id_type=MESH)
    @pl.when(z > 0)
    def _():
        pl.semaphore_signal(bar, inc=1, device_id=dev(z - 1, x, y, c), device_id_type=MESH)
    @pl.when(z < 3)
    def _():
        pl.semaphore_signal(bar, inc=1, device_id=dev(z + 1, x, y, c), device_id_type=MESH)
    pl.semaphore_wait(bar, 2 + (z > 0).astype(jnp.int32) + (z < 3).astype(jnp.int32))

def weight_sums(arrays, cid, name):
    n = len(arrays); total, width = arrays[0].shape; depth = total // 16
    D = pltpu.SemaphoreType.DMA
    V = lambda k: pltpu.VMEM((n, k, depth, width), arrays[0].dtype)
    return pl.pallas_call(functools.partial(wsum_kernel, n),
        out_shape=[jax.ShapeDtypeStruct((depth, width), jnp.float32)] * n,
        in_specs=[pl.BlockSpec(memory_space=pl.ANY)] * n, out_specs=[pl.BlockSpec(memory_space=pltpu.VMEM)] * n,
        scratch_shapes=[V(8), V(8), V(4), V(4), V(4), D((n, 8)), D((n, 8)), D((n, 8)), D((n, 4)), D((n, 4)), D((n, 4)), D((n, 4)), D((n, 4)), D((n, 4))],
        compiler_params=pltpu.CompilerParams(collective_id=cid, has_side_effects=True, vmem_limit_bytes=56 << 20), name=name)(*[a.reshape(16, depth, width) for a in arrays])


def nearest(z, g):
    one = jnp.where(z == 0, 1, z - 1)
    two = jnp.where(z == 3, 1, jnp.where(z == 2, 3, 2))
    three = jnp.where(z >= 2, 0, 3)
    return jnp.where(g == 0, z, jnp.where(g == 1, one, jnp.where(g == 2, two, three)))

def nt(left, right):
    return lax.dot_general(left, right, (((1,), (1,)), ((), ())), preferred_element_type=jnp.float32)

def nn(left, right):
    return jnp.dot(left, right, preferred_element_type=jnp.float32)

def expert_kernel(
    a_in, deh, dhs, rank_row, rank_col, gate, wg_h, wu_h, wd_h, sgu_h, sdt_h,
    total, act_all, rows_o, eh_o, deg_o, deu_o, hs_o, dsgu_o, part, ffn_part,
    wg, wu, wd, sgu, tail, acc, ic, iy0, ix0, ix1, iy1, izu, izd,
    eg, eu, dehb, ehb, degb, deub, dhsb, hsb, dsgub, eh2, hs2, ot,
    wsem, usem, ssem, osem, psem, lsem,
    zs, zr, x0s, x0r, x1s, x1r, y0s, y0r, y1s, y1r, cs, cr,
    ls, rcs, rcr, ry0s, ry0r, rx0s, rx0r, rx1s, rx1r, ry1s, ry1r, zus, zur, zds, zdr,
):
    f32, bf16 = jnp.float32, jnp.bfloat16
    z, x, y, c = place()
    rows, width = a_in.shape
    h = rows // 2
    cap = deh.shape[1]
    toks = 2 * rows
    lo, hi = pl.ds(0, h), pl.ds(h, h)
    part_of = (lo, hi)
    xn, yn, cn = dev(z, 1 - x, y, c), dev(z, x, 1 - y, c), dev(z, x, y, 1 - c)
    greet(z, x, y, c)
    mine = blk(z, x, y, c)
    own = pltpu.make_async_copy(a_in, act_all.at[mine], lsem)
    own.start()
    weights = [
        pltpu.make_async_copy(a, b, wsem.at[i])
        for i, (a, b) in enumerate(((wg_h, wg), (wu_h, wu), (wd_h, wd), (sgu_h, sgu), (sdt_h, tail.at[pl.ds(cap, 256 - cap)])))
    ]
    for w in weights:
        w.start()

    def zcopy(s, up):
        b = act_all.at[blk(s, x, y, c)]
        return rcopy(b, b, zs.at[s, up], zr.at[s], dev(z + 2 * up - 1, x, y, c))

    def half_copy(s, xx, yy, p, send, recv, to):
        b = act_all.at[blk(s, xx, yy, c), part_of[p]]
        return rcopy(b, b, send, recv, to)

    def x0(s): return half_copy(s, x, y, 0, x0s.at[s], x0r.at[s], xn)
    def y1(s): return half_copy(s, x, y, 1, y1s.at[s], y1r.at[s], yn)
    def y0(s, xx): return half_copy(s, xx, y, 0, y0s.at[s, xx], y0r.at[s, xx], yn)
    def x1(s, yy): return half_copy(s, x, yy, 1, x1s.at[s, yy], x1r.at[s, yy], xn)
    def side(s, xx, yy, p):
        i = (s * 2 + xx) * 2 + yy
        return half_copy(s, xx, yy, p, cs.at[i, p], cr.at[i, p], cn)

    def column(s):
        x0(s).start(); y1(s).start(); y0(s, x).start(); x1(s, y).start()
        side(s, x, y, 0).start(); side(s, x, y, 1).start()

    def arrive(g):
        s = nearest(z, g)
        up = (s < z).astype(jnp.int32)
        nxt = z + 2 * up - 1
        zcopy(s, up).wait_recv()
        @pl.when((nxt >= 0) & (nxt <= 3))
        def _(): zcopy(s, up).start()
        column(s)

    def middle(g):
        s = nearest(z, g)
        x0(s).wait_recv()
        y0(s, 1 - x).start(); side(s, 1 - x, y, 0).start()
        y1(s).wait_recv()
        x1(s, 1 - y).start(); side(s, x, 1 - y, 1).start()

    def last_own(g):
        s = nearest(z, g)
        y0(s, x).wait_recv(); side(s, x, 1 - y, 0).start()

    def last_other(g):
        s = nearest(z, g)
        x1(s, y).wait_recv(); side(s, 1 - x, y, 1).start()
        y0(s, 1 - x).wait_recv(); side(s, 1 - x, 1 - y, 0).start()
        x1(s, 1 - y).wait_recv(); side(s, 1 - x, 1 - y, 1).start()

    def spread_cols(j):
        ranks = rank_col[j]
        slot = lax.broadcasted_iota(jnp.int32, (toks, 128), 1)
        one = jnp.where(ranks == slot, 1.0, 0.0)
        two = jnp.where(ranks == slot + 128, 1.0, 0.0)
        return one, two

    def seq_of(u):
        s = nearest(z, u // 2)
        xx = lax.rem(x + lax.rem(u, 2), 2)
        return s, xx

    def stores(u):
        s, xx = seq_of(u)
        out = []
        for k in (0, 1):
            j = (s * 2 + xx) * 2 + k
            r = pl.ds(k * cap, cap)
            out += [
                pltpu.make_async_copy(acc.at[k], rows_o.at[j], ssem.at[k, 0]),
                pltpu.make_async_copy(ehb.at[r], eh_o.at[j], ssem.at[k, 1]),
                pltpu.make_async_copy(degb.at[r], deg_o.at[j], ssem.at[k, 2]),
                pltpu.make_async_copy(deub.at[r], deu_o.at[j], ssem.at[k, 3]),
                pltpu.make_async_copy(hsb.at[k], hs_o.at[j], ssem.at[k, 4]),
                pltpu.make_async_copy(dsgub.at[k], dsgu_o.at[j], ssem.at[k, 5]),
                pltpu.make_async_copy(acc.at[pl.ds(10 + 2 * k, 2)], part.at[pl.ds(2 * j, 2)], ssem.at[k, 6]),
            ]
        return out

    def unit(u):
        s, xx = seq_of(u)
        base = (s * 2 + xx) * 2
        for k in (0, 1):
            pltpu.make_async_copy(deh.at[base + k], dehb.at[pl.ds(k * cap, cap)], usem.at[k, 1]).start()
            pltpu.make_async_copy(dhs.at[base + k], dhsb.at[k], usem.at[k, 2]).start()
        for yy in (0, 1):
            for p in (0, 1):
                side(s, xx, yy, p).wait_recv()
        loads = [
            pltpu.make_async_copy(act_all.at[pl.ds(2 * (base + k), 2)], acc.at[pl.ds(4 + 2 * k, 2)], usem.at[k, 0])
            for k in (0, 1)
        ]
        for k in (0, 1):
            loads[k].start()
        @pl.when(u > 0)
        def _():
            for copy in stores(u - 1):
                copy.wait()
        for k in (0, 1):
            loads[k].wait()
            act = acc[4 + 2 * k:6 + 2 * k].reshape(toks, width)
            ranks = rank_row[base + k]
            slot = lax.broadcasted_iota(jnp.int32, (cap, toks), 0)
            pick = jnp.where(ranks == slot, 1.0, 0.0).astype(bf16)
            acc[k] = nn(pick, act).astype(bf16)
            pre = nn(act, sgu[...])
            gp, up = pre[:, :128], pre[:, 128:]
            pltpu.make_async_copy(dhs.at[base + k], dhsb.at[k], usem.at[k, 2]).wait()
            dh = dhsb[k]
            sig = jax.nn.sigmoid(gp)
            hsb[k] = (gp * sig * up).astype(bf16)
            dsgub[k, :, 0:128] = (dh * up * sig * (1.0 + gp * (1.0 - sig))).astype(bf16)
            dsgub[k, :, 128:256] = (dh * gp * sig).astype(bf16)
        picked = acc[0:2].reshape(2 * cap, width)
        eg[...] = nn(picked, wg[...])
        eu[...] = nn(picked, wu[...])
        for k in (0, 1):
            pltpu.make_async_copy(deh.at[base + k], dehb.at[pl.ds(k * cap, cap)], usem.at[k, 1]).wait()
        @pl.loop(0, 2 * cap // 32)
        def _(r):
            q = pl.ds(pl.multiple_of(r * 32, 32), 32)
            gp, up, dh = eg[q], eu[q], dehb[q]
            sig = jax.nn.sigmoid(gp)
            silu = gp * sig
            ehb[q] = (silu * up).astype(bf16)
            degb[q] = (dh * up * sig * (1.0 + gp * (1.0 - sig))).astype(bf16)
            deub[q] = (dh * silu).astype(bf16)
        dg, du = degb[...], deub[...]
        for n in range(0, width, 512):
            w = pl.ds(n, 512)
            back = (nt(dg, wg[w, :]) + nt(du, wu[w, :])).astype(bf16)
            acc[8, :, w] = back[:cap]
            acc[9, :, w] = back[cap:]
        for k in (0, 1):
            one, two = spread_cols(base + k)
            left = jnp.concatenate([one, two], axis=1)[:, :cap].astype(bf16)
            for n in range(0, width, 512):
                w = pl.ds(n, 512)
                out = nn(left, acc[8 + k, :, w]) + nt(dsgub[k], sgu[w, :])
                out = out.astype(bf16)
                acc[10 + 2 * k, :, w] = out[:rows]
                acc[11 + 2 * k, :, w] = out[rows:]
        for copy in stores(u):
            copy.start()

    own.wait()
    @pl.when(z < 3)
    def _(): zcopy(z, 1).start()
    @pl.when(z > 0)
    def _(): zcopy(z, 0).start()
    column(z)
    for w in weights:
        w.wait()

    @pl.loop(0, 8)
    def _(u):
        @pl.when(u == 0)
        def _():
            middle(0); last_own(0); arrive(1)
        @pl.when(u == 1)
        def _():
            last_other(0); arrive(2); middle(1)
        @pl.when(u == 2)
        def _():
            arrive(3); last_own(1); middle(2)
        @pl.when(u == 3)
        def _():
            last_other(1); middle(3)
        @pl.when(u == 4)
        def _():
            last_own(2)
        @pl.when(u == 5)
        def _():
            last_other(2)
        @pl.when(u == 6)
        def _():
            last_own(3)
        @pl.when(u == 7)
        def _():
            last_other(3)
        unit(u)

    for copy in stores(7):
        copy.wait()

    def at(s, xx, yy): return (s * 2 + xx) * 2 + yy
    def load(s, xx, yy):
        return pltpu.make_async_copy(part.at[blk(s, xx, yy, c)], acc.at[at(s, xx, yy)], ls.at[at(s, xx, yy)])
    def cross(s, xx, yy):
        i = at(s, xx, yy)
        return rcopy(part.at[blk(s, xx, yy, 1 - c)], ic.at[i], rcs.at[i], rcr.at[i], cn)
    def ry0(s, xx):
        return rcopy(acc.at[at(s, xx, 1 - y), lo], iy0.at[s * 2 + xx], ry0s.at[s, xx], ry0r.at[s, xx], yn)
    def rx1(s, yy):
        return rcopy(acc.at[at(s, 1 - x, yy), hi], ix1.at[s * 2 + yy], rx1s.at[s, yy], rx1r.at[s, yy], xn)
    def rx0(s):
        return rcopy(acc.at[at(s, 1 - x, y), lo], ix0.at[s], rx0s.at[s], rx0r.at[s], xn)
    def ry1(s):
        return rcopy(acc.at[at(s, x, 1 - y), hi], iy1.at[s], ry1s.at[s], ry1r.at[s], yn)
    def zu(s):
        return rcopy(acc.at[at(s, x, y)], izu.at[s], zus.at[s], zur.at[s], dev(z + 1, x, y, c))
    def zd(s):
        return rcopy(acc.at[at(s, x, y)], izd.at[s], zds.at[s], zdr.at[s], dev(z - 1, x, y, c))
    def add(i, start, count, src, j):
        @pl.loop(0, count // 16)
        def _(r):
            a = pl.ds(pl.multiple_of(start + r * 16, 16), 16)
            b = pl.ds(pl.multiple_of(r * 16, 16), 16)
            acc[i, a] = acc[i, a] + src[j, b]

    def first(s):
        for xx in (0, 1):
            for yy in (0, 1):
                load(s, xx, yy).wait(); cross(s, xx, yy).wait_recv()
                add(at(s, xx, yy), 0, rows, ic, at(s, xx, yy))
                @pl.when(yy != y)
                def _(): ry0(s, xx).start()
                @pl.when(xx != x)
                def _(): rx1(s, yy).start()

    def second(s):
        ry0(s, 1 - x).wait_recv(); add(at(s, 1 - x, y), 0, h, iy0, s * 2 + 1 - x); rx0(s).start()
        rx1(s, 1 - y).wait_recv(); add(at(s, x, 1 - y), h, h, ix1, s * 2 + 1 - y); ry1(s).start()
        ry0(s, x).wait_recv(); add(at(s, x, y), 0, h, iy0, s * 2 + x)
        rx1(s, y).wait_recv(); add(at(s, x, y), h, h, ix1, s * 2 + y)

    def third(s):
        me = at(s, x, y)
        rx0(s).wait_recv(); add(me, 0, h, ix0, s)
        ry1(s).wait_recv(); add(me, h, h, iy1, s)
        @pl.when((s >= z) & (z > 0))
        def _():
            zu(s).wait_recv(); add(me, 0, rows, izu, s)
        @pl.when((s <= z) & (z < 3))
        def _():
            zd(s).wait_recv(); add(me, 0, rows, izd, s)
        @pl.when(s > z)
        def _(): zu(s).start()
        @pl.when(s < z)
        def _(): zd(s).start()

    for g in (3, 2, 1, 0):
        s = nearest(z, g)
        for xx in (0, 1):
            for yy in (0, 1):
                cross(s, xx, yy).start(); load(s, xx, yy).start()

    def out_loads(j, b):
        return [
            pltpu.make_async_copy(eh_o.at[j], eh2.at[b], osem.at[b, 0]),
            pltpu.make_async_copy(hs_o.at[j], hs2.at[b], osem.at[b, 1]),
        ]
    def out_store(j, b):
        return pltpu.make_async_copy(ot.at[b], ffn_part.at[pl.ds(2 * j, 2)], psem.at[b])

    def forward_out(j):
        b = lax.rem(j, 2)
        @pl.when(j < 15)
        def _():
            for copy in out_loads(j + 1, 1 - b):
                copy.start()
        for copy in out_loads(j, b):
            copy.wait()
        @pl.when(j >= 2)
        def _(): out_store(j - 2, b).wait()
        weight = gate[j]
        for n in range(0, width, 512):
            w = pl.ds(n, 512)
            tail[0:cap, w] = (nn(eh2[b], wd[:, w]) * weight).astype(bf16)
        one, two = spread_cols(j)
        left = jnp.concatenate([one, two + hs2[b].astype(f32)], axis=1).astype(bf16)
        for n in range(0, width, 512):
            w = pl.ds(n, 512)
            out = nn(left, tail[:, w]).astype(bf16)
            ot[b, 0, :, w] = out[:rows]
            ot[b, 1, :, w] = out[rows:]
        out_store(j, b).start()

    for copy in out_loads(0, 0):
        copy.start()

    @pl.loop(0, 6)
    def _(t):
        @pl.when(t < 4)
        def _():
            first(nearest(z, 3 - t))
            @pl.loop(0, 4)
            def _(i): forward_out(4 * t + i)
        @pl.when((t >= 1) & (t < 5))
        def _(): second(nearest(z, 4 - t))
        @pl.when(t >= 2)
        def _(): third(nearest(z, 5 - t))

    total[...] = acc[at(z, x, y)]
    out_store(14, 0).wait()
    out_store(15, 1).wait()

    for s in range(4):
        x0(s).wait_send(); y1(s).wait_send()
        rx0(s).wait_send(); ry1(s).wait_send()
        for q in (0, 1):
            y0(s, q).wait_send(); x1(s, q).wait_send()
            ry0(s, q).wait_send(); rx1(s, q).wait_send()
            for r in (0, 1):
                cross(s, q, r).wait_send()
                for p in (0, 1):
                    side(s, q, r, p).wait_send()
        @pl.when((z < 3) & (s <= z))
        def _(): zcopy(s, 1).wait_send()
        @pl.when((z > 0) & (s >= z))
        def _(): zcopy(s, 0).wait_send()
        @pl.when(s > z)
        def _(): zu(s).wait_send()
        @pl.when(s < z)
        def _(): zd(s).wait_send()

def expert_layer(act, deh, dhs, rank_row, rank_col, gate, wg, wu, wd, sgu, sdt, cid):
    rows, width = act.shape
    cap, hidden = deh.shape[1:]
    h = rows // 2
    f32, bf16 = jnp.float32, jnp.bfloat16
    D = pltpu.SemaphoreType.DMA
    S = jax.ShapeDtypeStruct
    any_ = pl.BlockSpec(memory_space=pl.ANY)
    vm = pl.BlockSpec(memory_space=pltpu.VMEM)
    V = lambda *shape, t=bf16: pltpu.VMEM(shape, t)
    return pl.pallas_call(
        expert_kernel,
        out_shape=[
            S((rows, width), bf16), S((32, rows, width), bf16), S((16, cap, width), bf16),
            S((16, cap, hidden), bf16), S((16, cap, hidden), bf16), S((16, cap, hidden), bf16),
            S((16, 2 * rows, 128), bf16), S((16, 2 * rows, 256), bf16),
            S((32, rows, width), bf16), S((32, rows, width), bf16),
        ],
        in_specs=[any_, any_, any_, vm, vm, vm] + [any_] * 5,
        out_specs=[vm] + [any_] * 9,
        scratch_shapes=[
            V(*wg.shape), V(*wu.shape), V(*wd.shape), V(*sgu.shape), V(256, width),
            V(16, rows, width), V(16, rows, width), V(8, h, width), V(4, h, width), V(8, h, width), V(4, h, width),
            V(4, rows, width), V(4, rows, width),
            V(2 * cap, hidden, t=f32), V(2 * cap, hidden, t=f32), V(2 * cap, hidden, t=f32),
            V(2 * cap, hidden), V(2 * cap, hidden), V(2 * cap, hidden),
            V(2, 2 * rows, 128, t=f32), V(2, 2 * rows, 128), V(2, 2 * rows, 256),
            V(2, cap, hidden), V(2, 2 * rows, 128), V(2, 2, rows, width),
            D((5,)), D((2, 3)), D((2, 7)), D((2, 2)), D((2,)), D,
            D((4, 2)), D((4,)), D((4,)), D((4,)), D((4, 2)), D((4, 2)), D((4, 2)), D((4, 2)), D((4,)), D((4,)), D((16, 2)), D((16, 2)),
            D((16,)), D((16,)), D((16,)), D((4, 2)), D((4, 2)), D((4,)), D((4,)), D((4, 2)), D((4, 2)), D((4,)), D((4,)),
            D((4,)), D((4,)), D((4,)), D((4,)),
        ],
        compiler_params=pltpu.CompilerParams(collective_id=cid, has_side_effects=True, vmem_limit_bytes=62 << 20),
        name="expert_layer",
    )(act, deh, dhs, rank_row, rank_col, gate, wg, wu, wd, sgu, sdt)


def routing_tables(gate_table, capacity):
    member = gate_table > 0.0
    ranks = jnp.cumsum(member.astype(jnp.int32), axis=1) - 1
    slot = jnp.arange(capacity, dtype=jnp.int32)
    pick = (ranks[:, None, :] == slot[None, :, None]) & member[:, None, :]
    slot_gate = jnp.sum(jnp.where(pick, gate_table[:, None, :], 0.0), axis=2)
    held = jnp.where(member, ranks, -1)
    return pick.astype(jnp.bfloat16), slot_gate, held


def on_device(
    tokens,
    cotangent,
    route_ids,
    route_gates,
    gain_first,
    w_query,
    w_key,
    w_value,
    w_output,
    gain_second,
    shared_gate,
    shared_up,
    shared_down,
    expert_gate,
    expert_up,
    expert_down,
):
    f32, bf16 = jnp.float32, jnp.bfloat16
    rows_dev, width = tokens.shape
    topk = route_ids.shape[1]
    experts = lax.axis_size("dp")
    splits = lax.axis_size("tensor")
    half = rows_dev // splits
    mine = lax.axis_index("tensor") * half
    capacity = rows_dev * topk * 4 // (3 * experts)
    slots = experts * capacity
    scale = HD ** (-0.5)
    positions = jnp.arange(rows_dev, dtype=f32)
    causal = jnp.arange(rows_dev)[:, None] >= jnp.arange(rows_dev)[None, :]
    grad_half = lax.dynamic_slice_in_dim(cotangent, mine, half, axis=0)
    chosen = route_ids[:, :, None] == jnp.arange(experts, dtype=jnp.int32)[None, None, :]
    table = jnp.sum(jnp.where(chosen, route_gates[:, :, None], 0.0), axis=1)
    gains = jnp.concatenate([gain_first[None], gain_second[None], jnp.zeros((14, gain_first.shape[0]), bf16)])
    query_whole, key_whole, value_whole, output_whole, gains, tables, grad_all = start_gather(
        [w_query, w_key, w_value, w_output, gains, table.T], grad_half, 0, "gather_weights"
    )
    query_whole, key_whole, value_whole, output_whole = [
        w.reshape(width, -1) for w in (query_whole, key_whole, value_whole, output_whole)
    ]
    grad_all = grad_all.reshape(-1, width)
    gain_one = gains[:, 0].reshape(-1).astype(f32)
    gain_two = gains[:, 1].reshape(-1).astype(f32)

    depth, common_width = shared_gate.shape
    common_dev = common_width // experts
    packed = jnp.stack([shared_gate, shared_up, shared_down])
    packed = packed.reshape(3, depth, experts, common_dev).transpose(2, 0, 1, 3)
    packed = lax.all_to_all(packed, "dp", split_axis=0, concat_axis=0, tiled=True)
    packed = packed.transpose(1, 0, 2, 3).reshape(3, width, common_dev)

    table = lax.dynamic_index_in_dim(tables, lax.axis_index("dp"), axis=1, keepdims=False)
    pick, slot_gate, held = routing_tables(table, capacity)

    x_in = tokens.astype(f32)
    act_one = rms_norm(x_in, gain_one).astype(bf16)
    heads_dev = query_whole.shape[1] // HD
    query_pre = jnp.dot(act_one, query_whole, preferred_element_type=f32).reshape(
        rows_dev, heads_dev, HD
    )
    key_pre = jnp.dot(act_one, key_whole, preferred_element_type=f32).reshape(
        rows_dev, heads_dev, HD
    )
    query_rot = rotate(query_pre, positions).astype(bf16)
    key_rot = rotate(key_pre, positions).astype(bf16)
    value_low = (
        jnp.dot(act_one, value_whole, preferred_element_type=f32)
        .astype(bf16)
        .reshape(rows_dev, heads_dev, HD)
    )
    scores = masked_scores(query_rot, key_rot, causal, scale)
    top = jnp.max(scores, axis=-1, keepdims=True)
    expo = jnp.exp(scores - top)
    total = jnp.sum(expo, axis=-1, keepdims=True)
    probs = expo / total
    log_total = top + jnp.log(total)
    mixed = jnp.einsum("hqk,khc->qhc", probs.astype(bf16), value_low, preferred_element_type=f32)
    mixed = mixed.reshape(rows_dev, heads_dev * HD).astype(bf16)
    attn = lax.psum_scatter(
        contract_last(mixed, output_whole), "tensor", scatter_dimension=0, tiled=True
    )
    x_half = lax.dynamic_slice_in_dim(tokens, mine, half, axis=0).astype(f32)
    x_mid = x_half + attn
    act_two = rms_norm(x_mid, gain_two).astype(bf16)

    grad_blocks = grad_all.reshape(experts, rows_dev, width)
    exp_gate, exp_up, exp_down = expert_gate[0], expert_up[0], expert_down[0]
    weight = slot_gate.reshape(slots, 1)
    rows_out_grad = jnp.einsum("jst,jtd->jsd", pick, grad_blocks, preferred_element_type=f32)
    rows_out_grad = (weight * rows_out_grad.reshape(slots, width)).astype(bf16)
    hidden_rows_grad = contract_last(rows_out_grad, exp_down).reshape(experts, capacity, -1)
    front = capacity - 128
    back = 128 - front - common_dev

    def widen(w):
        return jnp.pad(w, ((0, 0), (front, back)))

    common_gu = jnp.concatenate([widen(packed[0]), widen(packed[1])], axis=1)
    common_down = widen(packed[2])
    common_hidden_grad = jnp.dot(grad_all, common_down, preferred_element_type=f32)
    down_rows = common_down.T[front:]
    total_grad, act_all, rows, hidden_rows, gate_rows_grad, up_rows_grad, common_hidden, common_gu_grad, unused, ffn = (
        expert_layer(
            act_two,
            hidden_rows_grad,
            common_hidden_grad.reshape(experts, rows_dev, 128),
            held[:, None, :],
            held[:, :, None],
            slot_gate[:, :, None],
            exp_gate,
            exp_up,
            exp_down,
            common_gu,
            down_rows,
            1,
        )
    )
    act_two_total = total_grad.astype(f32)
    act_all = act_all.reshape(-1, width)
    rows = rows.reshape(slots, width)
    hidden_rows = hidden_rows.reshape(slots, -1)
    common_hidden = common_hidden.reshape(-1, 128)
    common_gu_grad = common_gu_grad.reshape(-1, 256)
    ffn = scatter_rows(ffn.reshape(-1, width), 3, "sum_ffn").astype(f32)
    layer_out = lax.all_gather((x_mid + ffn).astype(bf16), "tensor", axis=0, tiled=True)

    expert_gate_grad = contract_first(rows, gate_rows_grad.reshape(slots, -1))[None]
    expert_up_grad = contract_first(rows, up_rows_grad.reshape(slots, -1))[None]
    expert_down_grad = contract_first(hidden_rows, rows_out_grad)[None]
    gu_grad = contract_first(act_all, common_gu_grad)
    down_grad = contract_first(grad_all, common_hidden)
    common_w_grad = jnp.concatenate(
        [w[:, front : front + common_dev] for w in (gu_grad[:, :128], gu_grad[:, 128:], down_grad)], axis=1
    )
    common_w_grad = common_w_grad.astype(bf16).reshape(experts, depth, 3 * common_dev)
    common_w_grad = lax.all_to_all(common_w_grad, "dp", split_axis=0, concat_axis=0, tiled=True)
    common_w_grad = common_w_grad.astype(f32).reshape(experts, depth, 3, common_dev)
    common_w_grad = common_w_grad.transpose(2, 1, 0, 3).reshape(3, depth, common_width)

    dummy_second, second_vjp = jax.vjp(rms_norm, x_mid, gain_two)
    mid_norm_grad, gain_two_grad = second_vjp(act_two_total)
    mid_grad = grad_half.astype(f32) + mid_norm_grad
    attn_grad = lax.all_gather(mid_grad.astype(bf16), "tensor", axis=0, tiled=True)

    mixed_grad = (
        jnp.dot(attn_grad, output_whole, preferred_element_type=f32)
        .astype(bf16)
        .reshape(rows_dev, heads_dev, HD)
    )
    probs_again = jnp.exp(masked_scores(query_rot, key_rot, causal, scale) - log_total)
    value_grad = jnp.einsum(
        "hqk,qhc->khc", probs_again.astype(bf16), mixed_grad, preferred_element_type=f32
    ).astype(bf16)
    prob_grad = jnp.einsum("qhc,khc->hqk", mixed_grad, value_low, preferred_element_type=f32)
    delta = jnp.sum(probs_again * prob_grad, axis=-1, keepdims=True)
    score_grad = (probs_again * (prob_grad - delta)).astype(bf16)
    query_rot_grad = (
        jnp.einsum("hqk,khc->qhc", score_grad, key_rot, preferred_element_type=f32) * scale
    )
    key_rot_grad = (
        jnp.einsum("hqk,qhc->khc", score_grad, query_rot, preferred_element_type=f32) * scale
    )
    query_grad = rotate(query_rot_grad, -positions).reshape(rows_dev, heads_dev * HD).astype(bf16)
    key_grad = rotate(key_rot_grad, -positions).reshape(rows_dev, heads_dev * HD).astype(bf16)
    value_flat = value_grad.reshape(rows_dev, heads_dev * HD)
    act_one_grad = (
        contract_last(query_grad, query_whole)
        + contract_last(key_grad, key_whole)
        + contract_last(value_flat, value_whole)
    )
    act_one_total = lax.psum_scatter(act_one_grad, "tensor", scatter_dimension=0, tiled=True)
    dummy_first, first_vjp = jax.vjp(rms_norm, x_half, gain_one)
    in_norm_grad, gain_one_grad = first_vjp(act_one_total)
    tokens_grad = lax.all_gather((mid_grad + in_norm_grad).astype(bf16), "tensor", axis=0, tiled=True)

    query_sum, key_sum, value_sum, output_sum = weight_sums(
        [
            contract_first(act_one, query_grad).astype(bf16),
            contract_first(act_one, key_grad).astype(bf16),
            contract_first(act_one, value_flat).astype(bf16),
            contract_first(attn_grad, mixed).astype(bf16),
        ],
        4,
        "sum_weight_grads",
    )
    gain_grads = lax.psum(jnp.stack([gain_one_grad, gain_two_grad]), ("dp", "tensor"))
    gain_grads = lax.dynamic_slice_in_dim(
        gain_grads, lax.axis_index("dp") * gain_first.shape[0], gain_first.shape[0], axis=1
    )
    return (
        layer_out,
        tokens_grad,
        gain_grads[0],
        query_sum,
        key_sum,
        value_sum,
        output_sum,
        gain_grads[1],
        common_w_grad[0],
        common_w_grad[1],
        common_w_grad[2],
        expert_gate_grad,
        expert_up_grad,
        expert_down_grad,
    )


def solution(mesh):
    body = on_device if (mesh.shape["dp"], mesh.shape["tensor"]) == (16, 2) else on_device_plain
    in_specs = (
        P("dp", None),
        P("dp", None),
        P("dp", None),
        P("dp", None),
        P("dp"),
        P("dp", "tensor"),
        P("dp", "tensor"),
        P("dp", "tensor"),
        P("dp", "tensor"),
        P("dp"),
        P("dp", "tensor"),
        P("dp", "tensor"),
        P("dp", "tensor"),
        P("dp", None, "tensor"),
        P("dp", None, "tensor"),
        P("dp", "tensor", None),
    )
    out_specs = (
        P("dp", None),
        P("dp", None),
        P("dp"),
        P("dp", "tensor"),
        P("dp", "tensor"),
        P("dp", "tensor"),
        P("dp", "tensor"),
        P("dp"),
        P("dp", "tensor"),
        P("dp", "tensor"),
        P("dp", "tensor"),
        P("dp", None, "tensor"),
        P("dp", None, "tensor"),
        P("dp", "tensor", None),
    )
    return jax.shard_map(
        body, mesh=mesh, in_specs=in_specs, out_specs=out_specs, check_vma=False
    )
```

```python
import functools

import jax
import jax.numpy as jnp
from jax import lax
from jax.experimental import pallas as pl
from jax.experimental.pallas import tpu as pltpu
from jax.sharding import PartitionSpec as P

HD = 128
MESH = pl.DeviceIdType.MESH


EPS = 1e-06


def rms_norm(values, gain):
    mean_square = jnp.mean(values * values, axis=-1, keepdims=True)
    return values * lax.rsqrt(mean_square + EPS) * gain


def rotate(values, positions):
    head = values.shape[-1]
    half = head // 2
    freqs = 10000.0 ** (-2.0 * jnp.arange(half, dtype=jnp.float32) / head)
    angles = positions[:, None] * freqs[None, :]
    cosine = jnp.cos(angles)[:, None, :]
    sine = jnp.sin(angles)[:, None, :]
    first = values[..., :half]
    second = values[..., half:]
    return jnp.concatenate(
        [first * cosine - second * sine, second * cosine + first * sine], axis=-1
    )


def gated(gate_pre, up_pre):
    return gate_pre * jax.nn.sigmoid(gate_pre) * up_pre


def contract_last(left, right):
    return lax.dot_general(
        left, right, (((1,), (1,)), ((), ())), preferred_element_type=jnp.float32
    )


def contract_first(left, right):
    return lax.dot_general(
        left, right, (((0,), (0,)), ((), ())), preferred_element_type=jnp.float32
    )


def masked_scores(query_rot, key_rot, causal, scale):
    scores = (
        jnp.einsum("qhc,khc->hqk", query_rot, key_rot, preferred_element_type=jnp.float32) * scale
    )
    return jnp.where(causal[None], scores, -1e30)


def on_device_plain(
    tokens,
    cotangent,
    route_ids,
    route_gates,
    gain_first,
    w_query,
    w_key,
    w_value,
    w_output,
    gain_second,
    shared_gate,
    shared_up,
    shared_down,
    expert_gate,
    expert_up,
    expert_down,
):
    rows_dev, width = tokens.shape
    topk = route_ids.shape[1]
    experts = lax.axis_size("dp")
    capacity = rows_dev * topk * 4 // (3 * experts)
    slots = experts * capacity
    scale = HD ** (-0.5)
    positions = jnp.arange(rows_dev, dtype=jnp.float32)
    causal = jnp.arange(rows_dev)[:, None] >= jnp.arange(rows_dev)[None, :]
    gain_one, query_whole, key_whole, value_whole, output_whole = (
        lax.all_gather(gain_first, "dp", axis=0, tiled=True),
        lax.all_gather(w_query, "dp", axis=0, tiled=True),
        lax.all_gather(w_key, "dp", axis=0, tiled=True),
        lax.all_gather(w_value, "dp", axis=0, tiled=True),
        lax.all_gather(w_output, "dp", axis=0, tiled=True),
    )
    gain_two, common_gate, common_up, common_down = (
        lax.all_gather(gain_second, "dp", axis=0, tiled=True),
        lax.all_gather(shared_gate, "dp", axis=0, tiled=True),
        lax.all_gather(shared_up, "dp", axis=0, tiled=True),
        lax.all_gather(shared_down, "dp", axis=0, tiled=True),
    )
    gain_one = gain_one.astype(jnp.float32)
    gain_two = gain_two.astype(jnp.float32)
    x_in = tokens.astype(jnp.float32)
    act_one = rms_norm(x_in, gain_one).astype(jnp.bfloat16)
    heads_dev = query_whole.shape[1] // HD
    query_pre = jnp.dot(act_one, query_whole, preferred_element_type=jnp.float32).reshape(
        rows_dev, heads_dev, HD
    )
    key_pre = jnp.dot(act_one, key_whole, preferred_element_type=jnp.float32).reshape(
        rows_dev, heads_dev, HD
    )
    query_rot = rotate(query_pre, positions).astype(jnp.bfloat16)
    key_rot = rotate(key_pre, positions).astype(jnp.bfloat16)
    value_low = (
        jnp.dot(act_one, value_whole, preferred_element_type=jnp.float32)
        .astype(jnp.bfloat16)
        .reshape(rows_dev, heads_dev, HD)
    )
    scores = masked_scores(query_rot, key_rot, causal, scale)
    top = jnp.max(scores, axis=-1, keepdims=True)
    expo = jnp.exp(scores - top)
    total = jnp.sum(expo, axis=-1, keepdims=True)
    probs = expo / total
    log_total = top + jnp.log(total)
    mixed = jnp.einsum(
        "hqk,khc->qhc", probs.astype(jnp.bfloat16), value_low, preferred_element_type=jnp.float32
    )
    mixed = mixed.reshape(rows_dev, heads_dev * HD).astype(jnp.bfloat16)
    attn = lax.psum(contract_last(mixed, output_whole), "tensor")
    x_mid = x_in + attn
    act_two = rms_norm(x_mid, gain_two).astype(jnp.bfloat16)
    gate_pre = jnp.dot(act_two, common_gate, preferred_element_type=jnp.float32)
    up_pre = jnp.dot(act_two, common_up, preferred_element_type=jnp.float32)
    hidden_common = gated(gate_pre, up_pre).astype(jnp.bfloat16)
    common_out = contract_last(hidden_common, common_down)
    flat_ids = route_ids.reshape(-1)
    onehot = (flat_ids[:, None] == jnp.arange(experts, dtype=jnp.int32)[None, :]).astype(jnp.int32)
    ranks = jnp.sum(onehot * jnp.cumsum(onehot, axis=0), axis=1) - 1
    dest = flat_ids * capacity + ranks
    token_of = jnp.arange(rows_dev * topk, dtype=jnp.int32) // topk
    source = jnp.zeros((slots,), jnp.int32).at[dest].set(token_of)
    weight_of = jnp.zeros((slots,), jnp.float32).at[dest].set(route_gates.reshape(-1))
    filled = jnp.zeros((slots,), jnp.bool_).at[dest].set(True)
    outgoing = jnp.where(filled[:, None], act_two[source], jnp.zeros((), jnp.bfloat16)).reshape(
        experts, capacity, width
    )
    exp_gate = expert_gate[0]
    exp_up = expert_up[0]
    exp_down = expert_down[0]
    received = lax.all_to_all(outgoing, "dp", split_axis=0, concat_axis=0, tiled=True)
    sources = received.shape[0]
    count = received.shape[1]
    rows = received.reshape(sources * count, width)
    gate_rows = jnp.dot(rows, exp_gate, preferred_element_type=jnp.float32)
    up_rows = jnp.dot(rows, exp_up, preferred_element_type=jnp.float32)
    hidden_rows = gated(gate_rows, up_rows).astype(jnp.bfloat16)
    partial_value = jnp.dot(hidden_rows, exp_down, preferred_element_type=jnp.float32).reshape(
        sources, count, width
    )
    returned = lax.all_to_all(
        partial_value.astype(jnp.bfloat16), "dp", split_axis=0, concat_axis=0, tiled=True
    ).astype(partial_value.dtype)
    returned, kept_rows, kept_gate, kept_up = (
        returned,
        received,
        gate_rows.reshape(sources, count, -1),
        up_rows.reshape(sources, count, -1),
    )
    picked = returned.reshape(slots, width)[dest].reshape(rows_dev, topk, width)
    routed_part = jnp.sum(picked * route_gates[:, :, None], axis=1)
    ffn = lax.psum((common_out + routed_part).astype(jnp.bfloat16), "tensor").astype(jnp.float32)
    layer_out = (x_mid + ffn).astype(jnp.bfloat16)
    grad_out = cotangent.astype(jnp.float32)
    hidden_grad = jnp.dot(cotangent, common_down, preferred_element_type=jnp.float32)
    dummy_common, common_vjp = jax.vjp(gated, gate_pre, up_pre)
    gate_grad, up_grad = common_vjp(hidden_grad)
    gate_grad = gate_grad.astype(jnp.bfloat16)
    up_grad = up_grad.astype(jnp.bfloat16)
    common_gate_grad = contract_first(act_two, gate_grad)
    common_up_grad = contract_first(act_two, up_grad)
    common_down_grad = contract_first(cotangent, hidden_common)
    act_two_grad = contract_last(gate_grad, common_gate) + contract_last(up_grad, common_up)
    outgoing_grad = (
        (weight_of[:, None] * grad_out[source])
        .astype(jnp.bfloat16)
        .reshape(experts, capacity, width)
    )
    incoming_grad = lax.all_to_all(outgoing_grad, "dp", split_axis=0, concat_axis=0, tiled=True)
    hidden_width = kept_gate.shape[2]
    rows = kept_rows.reshape(-1, width)
    rows_out_grad = incoming_grad.reshape(-1, width)
    hidden_rows, expert_vjp = jax.vjp(
        gated, kept_gate.reshape(-1, hidden_width), kept_up.reshape(-1, hidden_width)
    )
    hidden_rows = hidden_rows.astype(jnp.bfloat16)
    hidden_rows_grad = contract_last(rows_out_grad, exp_down)
    gate_rows_grad, up_rows_grad = expert_vjp(hidden_rows_grad)
    gate_rows_grad = gate_rows_grad.astype(jnp.bfloat16)
    up_rows_grad = up_rows_grad.astype(jnp.bfloat16)
    expert_gate_grad = contract_first(rows, gate_rows_grad)[None]
    expert_up_grad = contract_first(rows, up_rows_grad)[None]
    expert_down_grad = contract_first(hidden_rows, rows_out_grad)[None]
    rows_in_grad = (
        contract_last(gate_rows_grad, exp_gate) + contract_last(up_rows_grad, exp_up)
    ).reshape(experts, capacity, width)
    returned_grad = lax.all_to_all(rows_in_grad, "dp", split_axis=0, concat_axis=0, tiled=True)
    routed_grad = jnp.sum(
        returned_grad.reshape(slots, width)[dest].reshape(rows_dev, topk, width), axis=1
    )
    act_two_total = lax.psum(act_two_grad + routed_grad, "tensor")
    dummy_second, second_vjp = jax.vjp(rms_norm, x_mid, gain_two)
    mid_norm_grad, gain_two_grad = second_vjp(act_two_total)
    mid_grad = grad_out + mid_norm_grad
    ffn_sums = (gain_two_grad, common_gate_grad, common_up_grad, common_down_grad)
    attn_grad = mid_grad.astype(jnp.bfloat16)
    output_w_grad = contract_first(attn_grad, mixed)
    mixed_grad = (
        jnp.dot(attn_grad, output_whole, preferred_element_type=jnp.float32)
        .astype(jnp.bfloat16)
        .reshape(rows_dev, heads_dev, HD)
    )
    probs_again = jnp.exp(masked_scores(query_rot, key_rot, causal, scale) - log_total)
    value_grad = jnp.einsum(
        "hqk,qhc->khc",
        probs_again.astype(jnp.bfloat16),
        mixed_grad,
        preferred_element_type=jnp.float32,
    ).astype(jnp.bfloat16)
    prob_grad = jnp.einsum(
        "qhc,khc->hqk", mixed_grad, value_low, preferred_element_type=jnp.float32
    )
    delta = jnp.sum(probs_again * prob_grad, axis=-1, keepdims=True)
    score_grad = (probs_again * (prob_grad - delta)).astype(jnp.bfloat16)
    query_rot_grad = (
        jnp.einsum("hqk,khc->qhc", score_grad, key_rot, preferred_element_type=jnp.float32) * scale
    )
    key_rot_grad = (
        jnp.einsum("hqk,qhc->khc", score_grad, query_rot, preferred_element_type=jnp.float32)
        * scale
    )

    def turn(values):
        return rotate(values, positions)

    dummy_turn, turn_vjp = jax.vjp(turn, query_pre)
    query_grad = turn_vjp(query_rot_grad)[0].reshape(rows_dev, heads_dev * HD).astype(jnp.bfloat16)
    key_grad = turn_vjp(key_rot_grad)[0].reshape(rows_dev, heads_dev * HD).astype(jnp.bfloat16)
    value_flat = value_grad.reshape(rows_dev, heads_dev * HD)
    query_w_grad = contract_first(act_one, query_grad)
    key_w_grad = contract_first(act_one, key_grad)
    value_w_grad = contract_first(act_one, value_flat)
    act_one_grad = (
        contract_last(query_grad, query_whole)
        + contract_last(key_grad, key_whole)
        + contract_last(value_flat, value_whole)
    )
    act_one_total = lax.psum(act_one_grad, "tensor")
    dummy_first, first_vjp = jax.vjp(rms_norm, x_in, gain_one)
    in_norm_grad, gain_one_grad = first_vjp(act_one_total)
    tokens_grad = (mid_grad + in_norm_grad).astype(jnp.bfloat16)
    every = (
        lax.psum_scatter(gain_one_grad, "dp", scatter_dimension=0, tiled=True),
        lax.psum_scatter(query_w_grad, "dp", scatter_dimension=0, tiled=True),
        lax.psum_scatter(key_w_grad, "dp", scatter_dimension=0, tiled=True),
        lax.psum_scatter(value_w_grad, "dp", scatter_dimension=0, tiled=True),
        lax.psum_scatter(output_w_grad, "dp", scatter_dimension=0, tiled=True),
        lax.psum_scatter(ffn_sums[0], "dp", scatter_dimension=0, tiled=True),
        lax.psum_scatter(ffn_sums[1], "dp", scatter_dimension=0, tiled=True),
        lax.psum_scatter(ffn_sums[2], "dp", scatter_dimension=0, tiled=True),
        lax.psum_scatter(ffn_sums[3], "dp", scatter_dimension=0, tiled=True),
    )
    attn_sums = every[:5]
    ffn_sums = every[5:]
    return (
        layer_out,
        tokens_grad,
        attn_sums[0],
        attn_sums[1],
        attn_sums[2],
        attn_sums[3],
        attn_sums[4],
        ffn_sums[0],
        ffn_sums[1],
        ffn_sums[2],
        ffn_sums[3],
        expert_gate_grad,
        expert_up_grad,
        expert_down_grad,
    )


def place():
    d = lax.axis_index("dp"); y = lax.axis_index("tensor")
    c = lax.rem(d, 2); x = lax.rem(lax.div(d, 2), 2); z = lax.div(d, 4)
    return z, x, y, c

def dev(z, x, y, c):
    return ((z * 2 + x) * 2 + c, y)

def blk(z, x, y, c):
    return ((z * 2 + x) * 2 + c) * 2 + y

def greet(z, x, y, c):
    bar = pltpu.get_barrier_semaphore()
    for other in (dev(z, 1 - x, y, c), dev(z, x, 1 - y, c), dev(z, x, y, 1 - c)):
        pl.semaphore_signal(bar, inc=1, device_id=other, device_id_type=MESH)
    @pl.when(z > 0)
    def _():
        pl.semaphore_signal(bar, inc=1, device_id=dev(z - 1, x, y, c), device_id_type=MESH)
    @pl.when(z < 3)
    def _():
        pl.semaphore_signal(bar, inc=1, device_id=dev(z + 1, x, y, c), device_id_type=MESH)
    pl.semaphore_wait(bar, 3 + (z > 0).astype(jnp.int32) + (z < 3).astype(jnp.int32))

def rcopy(src, dst, ssem, rsem, device):
    return pltpu.make_async_remote_copy(src_ref=src, dst_ref=dst, send_sem=ssem, recv_sem=rsem, device_id=device, device_id_type=MESH)

def gather_kernel(x_ref, o_ref, zs, zr, x0s, x0r, x1s, x1r, y0s, y0r, y1s, y1r, cs, cr, lsem):
    z, x, y, c = place()
    rows = x_ref.shape[0]; h = rows // 2
    lo, hi = pl.ds(0, h), pl.ds(h, h)
    part = (lo, hi)
    xn, yn, cn = dev(z, 1 - x, y, c), dev(z, x, 1 - y, c), dev(z, x, y, 1 - c)
    greet(z, x, y, c)
    mine = blk(z, x, y, c)
    own = pltpu.make_async_copy(x_ref, o_ref.at[mine], lsem)
    own.start()

    def zcopy(s, up):
        src = o_ref.at[blk(s, x, y, c)]
        return rcopy(src, o_ref.at[blk(s, x, y, c)], zs.at[s, up], zr.at[s], dev(z + (1 if up else -1), x, y, c))
    def x0(s):
        b = blk(s, x, y, c)
        return rcopy(o_ref.at[b, lo], o_ref.at[b, lo], x0s.at[s], x0r.at[s], xn)
    def y1(s):
        b = blk(s, x, y, c)
        return rcopy(o_ref.at[b, hi], o_ref.at[b, hi], y1s.at[s], y1r.at[s], yn)
    def y0(s, xx):
        b = blk(s, xx, y, c)
        return rcopy(o_ref.at[b, lo], o_ref.at[b, lo], y0s.at[s, xx], y0r.at[s, xx], yn)
    def x1(s, yy):
        b = blk(s, x, yy, c)
        return rcopy(o_ref.at[b, hi], o_ref.at[b, hi], x1s.at[s, yy], x1r.at[s, yy], xn)
    def cc(s, xx, yy, p):
        b = blk(s, xx, yy, c)
        i = (s * 2 + xx) * 2 + yy
        return rcopy(o_ref.at[b, part[p]], o_ref.at[b, part[p]], cs.at[i, p], cr.at[i, p], cn)
    def column(s):
        x0(s).start(); y1(s).start(); y0(s, x).start(); x1(s, y).start()
        cc(s, x, y, 0).start(); cc(s, x, y, 1).start()
    def middle(s):
        x0(s).wait_recv()
        y0(s, 1 - x).start(); cc(s, 1 - x, y, 0).start()
        y1(s).wait_recv()
        x1(s, 1 - y).start(); cc(s, x, 1 - y, 1).start()
    def last(s):
        for q in (0, 1):
            y0(s, q).wait_recv(); cc(s, q, 1 - y, 0).start()
            x1(s, q).wait_recv(); cc(s, 1 - x, q, 1).start()

    own.wait()
    @pl.when(z < 3)
    def _(): zcopy(z, 1).start()
    @pl.when(z > 0)
    def _(): zcopy(z, 0).start()
    column(z)
    def each(k, fn):
        if k == 0:
            fn(z)
            return
        for sign in (-1, 1):
            s = z + sign * k
            @pl.when((s >= 0) & (s <= 3))
            def _(s=s): fn(s)
    for k in range(1, 4):
        for sign in (-1, 1):
            s = z + sign * k
            @pl.when((s >= 0) & (s <= 3))
            def _(s=s, sign=sign):
                up = 1 if sign < 0 else 0
                zcopy(s, up).wait_recv()
                @pl.when((z + (1 if up else -1) >= 0) & (z + (1 if up else -1) <= 3))
                def _(): zcopy(s, up).start()
                column(s)
        each(k - 1, middle)
        if k >= 2: each(k - 2, last)
    each(3, middle); each(2, last); each(3, last)
    for s in range(4):
        for xx in (0, 1):
            for yy in (0, 1):
                for p in (0, 1):
                    cc(s, xx, yy, p).wait_recv()
    for s in range(4):
        x0(s).wait_send(); y1(s).wait_send()
        for q in (0, 1):
            y0(s, q).wait_send(); x1(s, q).wait_send()
            for r in (0, 1):
                for p in (0, 1): cc(s, q, r, p).wait_send()
        @pl.when((z < 3) & (s <= z))
        def _(): zcopy(s, 1).wait_send()
        @pl.when((z > 0) & (s >= z))
        def _(): zcopy(s, 0).wait_send()

def gather_rows(x, cid, name):
    rows, width = x.shape
    D = pltpu.SemaphoreType.DMA
    out = pl.pallas_call(gather_kernel, out_shape=jax.ShapeDtypeStruct((32, rows, width), x.dtype),
        in_specs=[pl.BlockSpec(memory_space=pl.ANY)], out_specs=pl.BlockSpec(memory_space=pl.ANY),
        scratch_shapes=[D((4, 2)), D((4,)), D((4,)), D((4,)), D((4, 2)), D((4, 2)), D((4, 2)), D((4, 2)), D((4,)), D((4,)), D((16, 2)), D((16, 2)), D],
        compiler_params=pltpu.CompilerParams(collective_id=cid, has_side_effects=True), name=name)(x)
    return out.reshape(32 * rows, width)

def scatter_kernel(p_ref, o_ref, acc, ic, iy0, ix0, ix1, iy1, izu, izd, ls, cs, cr, y0s, y0r, x0s, x0r, x1s, x1r, y1s, y1r, zus, zur, zds, zdr):
    z, x, y, c = place()
    rows = p_ref.shape[1]; h = rows // 2
    lo, hi = pl.ds(0, h), pl.ds(h, h)
    xn, yn, cn = dev(z, 1 - x, y, c), dev(z, x, 1 - y, c), dev(z, x, y, 1 - c)
    greet(z, x, y, c)
    def at(s, xx, yy): return (s * 2 + xx) * 2 + yy
    def load(s, xx, yy):
        return pltpu.make_async_copy(p_ref.at[blk(s, xx, yy, c)], acc.at[at(s, xx, yy)], ls.at[at(s, xx, yy)])
    def cc(s, xx, yy):
        i = at(s, xx, yy)
        return rcopy(p_ref.at[blk(s, xx, yy, 1 - c)], ic.at[i], cs.at[i], cr.at[i], cn)
    def y0(s, xx):
        return rcopy(acc.at[at(s, xx, 1 - y), lo], iy0.at[s * 2 + xx], y0s.at[s, xx], y0r.at[s, xx], yn)
    def x1(s, yy):
        return rcopy(acc.at[at(s, 1 - x, yy), hi], ix1.at[s * 2 + yy], x1s.at[s, yy], x1r.at[s, yy], xn)
    def x0(s):
        return rcopy(acc.at[at(s, 1 - x, y), lo], ix0.at[s], x0s.at[s], x0r.at[s], xn)
    def y1(s):
        return rcopy(acc.at[at(s, x, 1 - y), hi], iy1.at[s], y1s.at[s], y1r.at[s], yn)
    def zu(s):
        return rcopy(acc.at[at(s, x, y)], izu.at[s], zus.at[s], zur.at[s], dev(z + 1, x, y, c))
    def zd(s):
        return rcopy(acc.at[at(s, x, y)], izd.at[s], zds.at[s], zdr.at[s], dev(z - 1, x, y, c))
    def add(i, start, count, src, j):
        step = 16
        @pl.loop(0, count // step)
        def _(r):
            a = pl.ds(pl.multiple_of(start + r * step, step), step)
            b = pl.ds(pl.multiple_of(r * step, step), step)
            acc[i, a] = acc[i, a] + src[j, b]
    def order(fn, k):
        if k == 0:
            fn(z); return
        for sign in (-1, 1):
            s = z + sign * k
            @pl.when((s >= 0) & (s <= 3))
            def _(s=s): fn(s)
    def start(s):
        for xx in (0, 1):
            for yy in (0, 1):
                cc(s, xx, yy).start(); load(s, xx, yy).start()
    def first(s):
        for xx in (0, 1):
            for yy in (0, 1):
                load(s, xx, yy).wait(); cc(s, xx, yy).wait_recv()
                add(at(s, xx, yy), 0, rows, ic, at(s, xx, yy))
                @pl.when(yy != y)
                def _(): y0(s, xx).start()
                @pl.when(xx != x)
                def _(): x1(s, yy).start()
    def second(s):
        y0(s, 1 - x).wait_recv(); add(at(s, 1 - x, y), 0, h, iy0, s * 2 + 1 - x); x0(s).start()
        x1(s, 1 - y).wait_recv(); add(at(s, x, 1 - y), h, h, ix1, s * 2 + 1 - y); y1(s).start()
        y0(s, x).wait_recv(); add(at(s, x, y), 0, h, iy0, s * 2 + x)
        x1(s, y).wait_recv(); add(at(s, x, y), h, h, ix1, s * 2 + y)
    def third(s):
        me = at(s, x, y)
        x0(s).wait_recv(); add(me, 0, h, ix0, s)
        y1(s).wait_recv(); add(me, h, h, iy1, s)
        @pl.when((s >= z) & (z > 0))
        def _():
            zu(s).wait_recv(); add(me, 0, rows, izu, s)
        @pl.when((s <= z) & (z < 3))
        def _():
            zd(s).wait_recv(); add(me, 0, rows, izd, s)
        @pl.when(s > z)
        def _(): zu(s).start()
        @pl.when(s < z)
        def _(): zd(s).start()
    for k in (3, 2, 1, 0): order(start, k)
    for k in (3, 2, 1, 0):
        order(first, k)
        if k + 1 <= 3: order(second, k + 1)
        if k + 2 <= 3: order(third, k + 2)
    order(second, 0); order(third, 1); order(third, 0)
    o_ref[...] = acc[at(z, x, y)]
    for s in range(4):
        for q in (0, 1):
            for r in (0, 1): cc(s, q, r).wait_send()
            y0(s, q).wait_send(); x1(s, q).wait_send()
        x0(s).wait_send(); y1(s).wait_send()
        @pl.when(s > z)
        def _(): zu(s).wait_send()
        @pl.when(s < z)
        def _(): zd(s).wait_send()

def scatter_rows(p, cid, name):
    total, width = p.shape
    rows = total // 32; h = rows // 2
    D = pltpu.SemaphoreType.DMA
    V = lambda n, r: pltpu.VMEM((n, r, width), p.dtype)
    return pl.pallas_call(scatter_kernel, out_shape=jax.ShapeDtypeStruct((rows, width), p.dtype),
        in_specs=[pl.BlockSpec(memory_space=pl.ANY)], out_specs=pl.BlockSpec(memory_space=pltpu.VMEM),
        scratch_shapes=[V(16, rows), V(16, rows), V(8, h), V(4, h), V(8, h), V(4, h), V(4, rows), V(4, rows),
            D((16,)), D((16,)), D((16,)), D((4, 2)), D((4, 2)), D((4,)), D((4,)), D((4, 2)), D((4, 2)), D((4,)), D((4,)), D((4,)), D((4,)), D((4,)), D((4,))],
        compiler_params=pltpu.CompilerParams(collective_id=cid, has_side_effects=True, vmem_limit_bytes=56 << 20), name=name)(p.reshape(32, rows, width))


def start_kernel(n, *refs):
    ins, g_in = refs[:n], refs[n]
    outs, g_out = refs[n + 1:2 * n + 1], refs[2 * n + 1]
    zs, zr, xs, xr, cs, cr, ls = refs[2 * n + 2:2 * n + 9]
    gzs, gzr, gxs, gxr, gys, gyr, gcs, gcr, gl = refs[2 * n + 9:]
    z, x, y, c = place()
    xn, yn, cn = dev(z, 1 - x, y, c), dev(z, x, 1 - y, c), dev(z, x, y, 1 - c)
    greet(z, x, y, c)
    def pos(s, xx, cc_): return (s * 2 + xx) * 2 + cc_
    me = pos(z, x, c)
    owns = [pltpu.make_async_copy(ins[a], outs[a].at[me], ls.at[a]) for a in range(n)]
    owns.append(pltpu.make_async_copy(g_in, g_out.at[blk(z, x, y, c)], gl))
    for o in owns: o.start()
    def wz(a, s, up):
        r = outs[a].at[pos(s, x, c)]
        return rcopy(r, r, zs.at[a, s, up], zr.at[a, s], dev(z + (1 if up else -1), x, y, c))
    def wx(a, s):
        r = outs[a].at[pos(s, x, c)]
        return rcopy(r, r, xs.at[a, s], xr.at[a, s], xn)
    def wc(a, s, xx):
        r = outs[a].at[pos(s, xx, c)]
        return rcopy(r, r, cs.at[a, s * 2 + xx], cr.at[a, s * 2 + xx], cn)
    def gz(s, up):
        r = g_out.at[blk(s, x, y, c)]
        return rcopy(r, r, gzs.at[s, up], gzr.at[s], dev(z + (1 if up else -1), x, y, c))
    def gx(s):
        r = g_out.at[blk(s, x, y, c)]
        return rcopy(r, r, gxs.at[s], gxr.at[s], xn)
    def gy(s, xx):
        r = g_out.at[blk(s, xx, y, c)]
        return rcopy(r, r, gys.at[s, xx], gyr.at[s, xx], yn)
    def gc(s, xx, yy):
        r = g_out.at[blk(s, xx, yy, c)]
        return rcopy(r, r, gcs.at[s * 2 + xx, yy], gcr.at[s * 2 + xx, yy], cn)
    for o in owns: o.wait()
    def inside(v): return (v >= 0) & (v <= 3)
    def each(k, fn):
        if k == 0:
            fn(z); return
        for sign in (-1, 1):
            s = z + sign * k
            @pl.when(inside(s))
            def _(s=s): fn(s)
    def column(s):
        for a in range(n):
            wx(a, s).start(); wc(a, s, x).start()
    def gcolumn(s):
        gx(s).start(); gy(s, x).start(); gc(s, x, y).start()
    def middle(s):
        for a in range(n):
            wx(a, s).wait_recv(); wc(a, s, 1 - x).start()
    def gmiddle(s):
        gx(s).wait_recv(); gy(s, 1 - x).start(); gc(s, 1 - x, y).start()
    def glast(s):
        for q in (0, 1):
            gy(s, q).wait_recv(); gc(s, q, 1 - y).start()
    def launch(fn):
        @pl.when(z < 3)
        def _(): fn(1)
        @pl.when(z > 0)
        def _(): fn(0)
    launch(lambda up: [wz(a, z, up).start() for a in range(n)])
    column(z)
    launch(lambda up: gz(z, up).start())
    gcolumn(z)
    def arrive(k, recv, go, then):
        for sign in (-1, 1):
            s = z + sign * k
            @pl.when(inside(s))
            def _(s=s, sign=sign):
                up = 1 if sign < 0 else 0
                nxt = inside(z - sign)
                recv(s, up)
                @pl.when(nxt)
                def _(): go(s, up)
                then(s)
    for k in range(1, 4):
        arrive(k, lambda s, up: [wz(a, s, up).wait_recv() for a in range(n)], lambda s, up: [wz(a, s, up).start() for a in range(n)], column)
        each(k - 1, middle)
        arrive(k, lambda s, up: gz(s, up).wait_recv(), lambda s, up: gz(s, up).start(), gcolumn)
        each(k - 1, gmiddle)
    each(3, middle); each(3, gmiddle)
    for k in range(4): each(k, glast)
    for s in range(4):
        for q in (0, 1):
            for a in range(n): wc(a, s, q).wait_recv()
            for r in (0, 1): gc(s, q, r).wait_recv()
    for s in range(4):
        for a in range(n):
            wx(a, s).wait_send()
            for q in (0, 1): wc(a, s, q).wait_send()
        gx(s).wait_send()
        for q in (0, 1):
            gy(s, q).wait_send()
            for r in (0, 1): gc(s, q, r).wait_send()
        @pl.when((z < 3) & (s <= z))
        def _():
            gz(s, 1).wait_send()
            for a in range(n): wz(a, s, 1).wait_send()
        @pl.when((z > 0) & (s >= z))
        def _():
            gz(s, 0).wait_send()
            for a in range(n): wz(a, s, 0).wait_send()

def start_gather(arrays, rows, cid, name):
    n = len(arrays)
    D = pltpu.SemaphoreType.DMA
    any_ = pl.BlockSpec(memory_space=pl.ANY)
    outs = pl.pallas_call(functools.partial(start_kernel, n),
        out_shape=[jax.ShapeDtypeStruct((16,) + a.shape, a.dtype) for a in arrays] + [jax.ShapeDtypeStruct((32,) + rows.shape, rows.dtype)],
        in_specs=[pl.BlockSpec(memory_space=pltpu.VMEM)] * (n + 1), out_specs=[any_] * (n + 1),
        scratch_shapes=[D((n, 4, 2)), D((n, 4)), D((n, 4)), D((n, 4)), D((n, 8)), D((n, 8)), D((n,)),
            D((4, 2)), D((4,)), D((4,)), D((4,)), D((4, 2)), D((4, 2)), D((8, 2)), D((8, 2)), D],
        compiler_params=pltpu.CompilerParams(collective_id=cid, has_side_effects=True), name=name)(*arrays, rows)
    return outs

def wsum_kernel(n, *refs):
    ins, outs = refs[:n], refs[n:2 * n]
    acc, ic, ix, izu, izd, ls, cs, cr, xs, xr, zus, zur, zds, zdr = refs[2 * n:]
    z, x, y, c = place()
    depth = ins[0].shape[1]
    xn, cn = dev(z, 1 - x, y, c), dev(z, x, y, 1 - c)
    greet_plane(z, x, y, c)
    def at(s, xx): return s * 2 + xx
    def pos(s, xx, cc_): return (s * 2 + xx) * 2 + cc_
    def load(a, s, xx):
        i = at(s, xx)
        return pltpu.make_async_copy(ins[a].at[pos(s, xx, c)], acc.at[a, i], ls.at[a, i])
    def wc(a, s, xx):
        i = at(s, xx)
        return rcopy(ins[a].at[pos(s, xx, 1 - c)], ic.at[a, i], cs.at[a, i], cr.at[a, i], cn)
    def wx(a, s):
        return rcopy(acc.at[a, at(s, 1 - x)], ix.at[a, s], xs.at[a, s], xr.at[a, s], xn)
    def zu(a, s):
        return rcopy(acc.at[a, at(s, x)], izu.at[a, s], zus.at[a, s], zur.at[a, s], dev(z + 1, x, y, c))
    def zd(a, s):
        return rcopy(acc.at[a, at(s, x)], izd.at[a, s], zds.at[a, s], zdr.at[a, s], dev(z - 1, x, y, c))
    def add(a, i, src, j):
        step = 16
        @pl.loop(0, depth // step)
        def _(r):
            b = pl.ds(pl.multiple_of(r * step, step), step)
            acc[a, i, b] = acc[a, i, b] + src[a, j, b]
    def order(fn, k):
        if k == 0:
            fn(z); return
        for sign in (-1, 1):
            s = z + sign * k
            @pl.when((s >= 0) & (s <= 3))
            def _(s=s): fn(s)
    def start(s):
        for a in range(n):
            for q in (0, 1):
                wc(a, s, q).start(); load(a, s, q).start()
    def first(s):
        for a in range(n):
            for q in (0, 1):
                load(a, s, q).wait(); wc(a, s, q).wait_recv()
                add(a, at(s, q), ic, at(s, q))
            wx(a, s).start()
    def second(s):
        for a in range(n):
            wx(a, s).wait_recv(); add(a, at(s, x), ix, s)
            @pl.when((s >= z) & (z > 0))
            def _():
                zu(a, s).wait_recv(); add(a, at(s, x), izu, s)
            @pl.when((s <= z) & (z < 3))
            def _():
                zd(a, s).wait_recv(); add(a, at(s, x), izd, s)
            @pl.when(s > z)
            def _(): zu(a, s).start()
            @pl.when(s < z)
            def _(): zd(a, s).start()
    for k in (3, 2, 1, 0): order(start, k)
    for k in (3, 2, 1, 0):
        order(first, k)
        if k + 1 <= 3: order(second, k + 1)
    order(second, 0)
    for a in range(n):
        outs[a][...] = acc[a, at(z, x)].astype(jnp.float32)
    for s in range(4):
        for a in range(n):
            for q in (0, 1): wc(a, s, q).wait_send()
            wx(a, s).wait_send()
            @pl.when(s > z)
            def _(): zu(a, s).wait_send()
            @pl.when(s < z)
            def _(): zd(a, s).wait_send()

def greet_plane(z, x, y, c):
    bar = pltpu.get_barrier_semaphore()
    for other in (dev(z, 1 - x, y, c), dev(z, x, y, 1 - c)):
        pl.semaphore_signal(bar, inc=1, device_id=other, device_id_type=MESH)
    @pl.when(z > 0)
    def _():
        pl.semaphore_signal(bar, inc=1, device_id=dev(z - 1, x, y, c), device_id_type=MESH)
    @pl.when(z < 3)
    def _():
        pl.semaphore_signal(bar, inc=1, device_id=dev(z + 1, x, y, c), device_id_type=MESH)
    pl.semaphore_wait(bar, 2 + (z > 0).astype(jnp.int32) + (z < 3).astype(jnp.int32))

def weight_sums(arrays, cid, name):
    n = len(arrays); total, width = arrays[0].shape; depth = total // 16
    D = pltpu.SemaphoreType.DMA
    V = lambda k: pltpu.VMEM((n, k, depth, width), arrays[0].dtype)
    return pl.pallas_call(functools.partial(wsum_kernel, n),
        out_shape=[jax.ShapeDtypeStruct((depth, width), jnp.float32)] * n,
        in_specs=[pl.BlockSpec(memory_space=pl.ANY)] * n, out_specs=[pl.BlockSpec(memory_space=pltpu.VMEM)] * n,
        scratch_shapes=[V(8), V(8), V(4), V(4), V(4), D((n, 8)), D((n, 8)), D((n, 8)), D((n, 4)), D((n, 4)), D((n, 4)), D((n, 4)), D((n, 4)), D((n, 4))],
        compiler_params=pltpu.CompilerParams(collective_id=cid, has_side_effects=True, vmem_limit_bytes=56 << 20), name=name)(*[a.reshape(16, depth, width) for a in arrays])


def nearest(z, g):
    one = jnp.where(z == 0, 1, z - 1)
    two = jnp.where(z == 3, 1, jnp.where(z == 2, 3, 2))
    three = jnp.where(z >= 2, 0, 3)
    return jnp.where(g == 0, z, jnp.where(g == 1, one, jnp.where(g == 2, two, three)))

def nt(left, right):
    return lax.dot_general(left, right, (((1,), (1,)), ((), ())), preferred_element_type=jnp.float32)

def nn(left, right):
    return jnp.dot(left, right, preferred_element_type=jnp.float32)

def expert_kernel(
    a_in, deh, dhs, rank_row, rank_col, gate, wg_h, wu_h, wd_h, sgu_h, sdt_h,
    total, act_all, rows_o, eh_o, deg_o, deu_o, hs_o, dsgu_o, part, ffn_part,
    wg, wu, wd, sgu, tail, acc, ic, iy0, ix0, ix1, iy1, izu, izd,
    eg, eu, dehb, ehb, degb, deub, dhsb, hsb, dsgub, eh2, hs2, ot,
    wsem, usem, ssem, osem, psem, lsem,
    zs, zr, x0s, x0r, x1s, x1r, y0s, y0r, y1s, y1r, cs, cr,
    ls, rcs, rcr, ry0s, ry0r, rx0s, rx0r, rx1s, rx1r, ry1s, ry1r, zus, zur, zds, zdr,
):
    f32, bf16 = jnp.float32, jnp.bfloat16
    z, x, y, c = place()
    rows, width = a_in.shape
    h = rows // 2
    cap = deh.shape[1]
    toks = 2 * rows
    lo, hi = pl.ds(0, h), pl.ds(h, h)
    part_of = (lo, hi)
    xn, yn, cn = dev(z, 1 - x, y, c), dev(z, x, 1 - y, c), dev(z, x, y, 1 - c)
    greet(z, x, y, c)
    mine = blk(z, x, y, c)
    own = pltpu.make_async_copy(a_in, act_all.at[mine], lsem)
    own.start()
    weights = [
        pltpu.make_async_copy(a, b, wsem.at[i])
        for i, (a, b) in enumerate(((wg_h, wg), (wu_h, wu), (wd_h, wd), (sgu_h, sgu), (sdt_h, tail.at[pl.ds(cap, 256 - cap)])))
    ]
    for w in weights:
        w.start()

    def zcopy(s, up):
        b = act_all.at[blk(s, x, y, c)]
        return rcopy(b, b, zs.at[s, up], zr.at[s], dev(z + 2 * up - 1, x, y, c))

    def half_copy(s, xx, yy, p, send, recv, to):
        b = act_all.at[blk(s, xx, yy, c), part_of[p]]
        return rcopy(b, b, send, recv, to)

    def x0(s): return half_copy(s, x, y, 0, x0s.at[s], x0r.at[s], xn)
    def y1(s): return half_copy(s, x, y, 1, y1s.at[s], y1r.at[s], yn)
    def y0(s, xx): return half_copy(s, xx, y, 0, y0s.at[s, xx], y0r.at[s, xx], yn)
    def x1(s, yy): return half_copy(s, x, yy, 1, x1s.at[s, yy], x1r.at[s, yy], xn)
    def side(s, xx, yy, p):
        i = (s * 2 + xx) * 2 + yy
        return half_copy(s, xx, yy, p, cs.at[i, p], cr.at[i, p], cn)

    def column(s):
        x0(s).start(); y1(s).start(); y0(s, x).start(); x1(s, y).start()
        side(s, x, y, 0).start(); side(s, x, y, 1).start()

    def arrive(g):
        s = nearest(z, g)
        up = (s < z).astype(jnp.int32)
        nxt = z + 2 * up - 1
        zcopy(s, up).wait_recv()
        @pl.when((nxt >= 0) & (nxt <= 3))
        def _(): zcopy(s, up).start()
        column(s)

    def middle(g):
        s = nearest(z, g)
        x0(s).wait_recv()
        y0(s, 1 - x).start(); side(s, 1 - x, y, 0).start()
        y1(s).wait_recv()
        x1(s, 1 - y).start(); side(s, x, 1 - y, 1).start()

    def last_own(g):
        s = nearest(z, g)
        y0(s, x).wait_recv(); side(s, x, 1 - y, 0).start()

    def last_other(g):
        s = nearest(z, g)
        x1(s, y).wait_recv(); side(s, 1 - x, y, 1).start()
        y0(s, 1 - x).wait_recv(); side(s, 1 - x, 1 - y, 0).start()
        x1(s, 1 - y).wait_recv(); side(s, 1 - x, 1 - y, 1).start()

    def spread_cols(j):
        ranks = rank_col[j]
        slot = lax.broadcasted_iota(jnp.int32, (toks, 128), 1)
        one = jnp.where(ranks == slot, 1.0, 0.0)
        two = jnp.where(ranks == slot + 128, 1.0, 0.0)
        return one, two

    def seq_of(u):
        s = nearest(z, u // 2)
        xx = lax.rem(x + lax.rem(u, 2), 2)
        return s, xx

    def stores(u):
        s, xx = seq_of(u)
        out = []
        for k in (0, 1):
            j = (s * 2 + xx) * 2 + k
            r = pl.ds(k * cap, cap)
            out += [
                pltpu.make_async_copy(acc.at[k], rows_o.at[j], ssem.at[k, 0]),
                pltpu.make_async_copy(ehb.at[r], eh_o.at[j], ssem.at[k, 1]),
                pltpu.make_async_copy(degb.at[r], deg_o.at[j], ssem.at[k, 2]),
                pltpu.make_async_copy(deub.at[r], deu_o.at[j], ssem.at[k, 3]),
                pltpu.make_async_copy(hsb.at[k], hs_o.at[j], ssem.at[k, 4]),
                pltpu.make_async_copy(dsgub.at[k], dsgu_o.at[j], ssem.at[k, 5]),
                pltpu.make_async_copy(acc.at[pl.ds(10 + 2 * k, 2)], part.at[pl.ds(2 * j, 2)], ssem.at[k, 6]),
            ]
        return out

    def unit(u):
        s, xx = seq_of(u)
        base = (s * 2 + xx) * 2
        for k in (0, 1):
            pltpu.make_async_copy(deh.at[base + k], dehb.at[pl.ds(k * cap, cap)], usem.at[k, 1]).start()
            pltpu.make_async_copy(dhs.at[base + k], dhsb.at[k], usem.at[k, 2]).start()
        for yy in (0, 1):
            for p in (0, 1):
                side(s, xx, yy, p).wait_recv()
        loads = [
            pltpu.make_async_copy(act_all.at[pl.ds(2 * (base + k), 2)], acc.at[pl.ds(4 + 2 * k, 2)], usem.at[k, 0])
            for k in (0, 1)
        ]
        for k in (0, 1):
            loads[k].start()
        @pl.when(u > 0)
        def _():
            for copy in stores(u - 1):
                copy.wait()
        for k in (0, 1):
            loads[k].wait()
            act = acc[4 + 2 * k:6 + 2 * k].reshape(toks, width)
            ranks = rank_row[base + k]
            slot = lax.broadcasted_iota(jnp.int32, (cap, toks), 0)
            pick = jnp.where(ranks == slot, 1.0, 0.0).astype(bf16)
            acc[k] = nn(pick, act).astype(bf16)
            pre = nn(act, sgu[...])
            gp, up = pre[:, :128], pre[:, 128:]
            pltpu.make_async_copy(dhs.at[base + k], dhsb.at[k], usem.at[k, 2]).wait()
            dh = dhsb[k]
            sig = jax.nn.sigmoid(gp)
            hsb[k] = (gp * sig * up).astype(bf16)
            dsgub[k, :, 0:128] = (dh * up * sig * (1.0 + gp * (1.0 - sig))).astype(bf16)
            dsgub[k, :, 128:256] = (dh * gp * sig).astype(bf16)
        picked = acc[0:2].reshape(2 * cap, width)
        eg[...] = nn(picked, wg[...])
        eu[...] = nn(picked, wu[...])
        for k in (0, 1):
            pltpu.make_async_copy(deh.at[base + k], dehb.at[pl.ds(k * cap, cap)], usem.at[k, 1]).wait()
        @pl.loop(0, 2 * cap // 32)
        def _(r):
            q = pl.ds(pl.multiple_of(r * 32, 32), 32)
            gp, up, dh = eg[q], eu[q], dehb[q]
            sig = jax.nn.sigmoid(gp)
            silu = gp * sig
            ehb[q] = (silu * up).astype(bf16)
            degb[q] = (dh * up * sig * (1.0 + gp * (1.0 - sig))).astype(bf16)
            deub[q] = (dh * silu).astype(bf16)
        dg, du = degb[...], deub[...]
        for n in range(0, width, 512):
            w = pl.ds(n, 512)
            back = (nt(dg, wg[w, :]) + nt(du, wu[w, :])).astype(bf16)
            acc[8, :, w] = back[:cap]
            acc[9, :, w] = back[cap:]
        for k in (0, 1):
            one, two = spread_cols(base + k)
            left = jnp.concatenate([one, two], axis=1)[:, :cap].astype(bf16)
            for n in range(0, width, 512):
                w = pl.ds(n, 512)
                out = nn(left, acc[8 + k, :, w]) + nt(dsgub[k], sgu[w, :])
                out = out.astype(bf16)
                acc[10 + 2 * k, :, w] = out[:rows]
                acc[11 + 2 * k, :, w] = out[rows:]
        for copy in stores(u):
            copy.start()

    own.wait()
    @pl.when(z < 3)
    def _(): zcopy(z, 1).start()
    @pl.when(z > 0)
    def _(): zcopy(z, 0).start()
    column(z)
    for w in weights:
        w.wait()

    @pl.loop(0, 8)
    def _(u):
        @pl.when(u == 0)
        def _():
            middle(0); last_own(0); arrive(1)
        @pl.when(u == 1)
        def _():
            last_other(0); arrive(2); middle(1)
        @pl.when(u == 2)
        def _():
            arrive(3); last_own(1); middle(2)
        @pl.when(u == 3)
        def _():
            last_other(1); middle(3)
        @pl.when(u == 4)
        def _():
            last_own(2)
        @pl.when(u == 5)
        def _():
            last_other(2)
        @pl.when(u == 6)
        def _():
            last_own(3)
        @pl.when(u == 7)
        def _():
            last_other(3)
        unit(u)

    for copy in stores(7):
        copy.wait()

    def at(s, xx, yy): return (s * 2 + xx) * 2 + yy
    def load(s, xx, yy):
        return pltpu.make_async_copy(part.at[blk(s, xx, yy, c)], acc.at[at(s, xx, yy)], ls.at[at(s, xx, yy)])
    def cross(s, xx, yy):
        i = at(s, xx, yy)
        return rcopy(part.at[blk(s, xx, yy, 1 - c)], ic.at[i], rcs.at[i], rcr.at[i], cn)
    def ry0(s, xx):
        return rcopy(acc.at[at(s, xx, 1 - y), lo], iy0.at[s * 2 + xx], ry0s.at[s, xx], ry0r.at[s, xx], yn)
    def rx1(s, yy):
        return rcopy(acc.at[at(s, 1 - x, yy), hi], ix1.at[s * 2 + yy], rx1s.at[s, yy], rx1r.at[s, yy], xn)
    def rx0(s):
        return rcopy(acc.at[at(s, 1 - x, y), lo], ix0.at[s], rx0s.at[s], rx0r.at[s], xn)
    def ry1(s):
        return rcopy(acc.at[at(s, x, 1 - y), hi], iy1.at[s], ry1s.at[s], ry1r.at[s], yn)
    def zu(s):
        return rcopy(acc.at[at(s, x, y)], izu.at[s], zus.at[s], zur.at[s], dev(z + 1, x, y, c))
    def zd(s):
        return rcopy(acc.at[at(s, x, y)], izd.at[s], zds.at[s], zdr.at[s], dev(z - 1, x, y, c))
    def add(i, start, count, src, j):
        @pl.loop(0, count // 16)
        def _(r):
            a = pl.ds(pl.multiple_of(start + r * 16, 16), 16)
            b = pl.ds(pl.multiple_of(r * 16, 16), 16)
            acc[i, a] = acc[i, a] + src[j, b]

    def first(s):
        for xx in (0, 1):
            for yy in (0, 1):
                load(s, xx, yy).wait(); cross(s, xx, yy).wait_recv()
                add(at(s, xx, yy), 0, rows, ic, at(s, xx, yy))
                @pl.when(yy != y)
                def _(): ry0(s, xx).start()
                @pl.when(xx != x)
                def _(): rx1(s, yy).start()

    def second(s):
        ry0(s, 1 - x).wait_recv(); add(at(s, 1 - x, y), 0, h, iy0, s * 2 + 1 - x); rx0(s).start()
        rx1(s, 1 - y).wait_recv(); add(at(s, x, 1 - y), h, h, ix1, s * 2 + 1 - y); ry1(s).start()
        ry0(s, x).wait_recv(); add(at(s, x, y), 0, h, iy0, s * 2 + x)
        rx1(s, y).wait_recv(); add(at(s, x, y), h, h, ix1, s * 2 + y)

    def third(s):
        me = at(s, x, y)
        rx0(s).wait_recv(); add(me, 0, h, ix0, s)
        ry1(s).wait_recv(); add(me, h, h, iy1, s)
        @pl.when((s >= z) & (z > 0))
        def _():
            zu(s).wait_recv(); add(me, 0, rows, izu, s)
        @pl.when((s <= z) & (z < 3))
        def _():
            zd(s).wait_recv(); add(me, 0, rows, izd, s)
        @pl.when(s > z)
        def _(): zu(s).start()
        @pl.when(s < z)
        def _(): zd(s).start()

    for g in (3, 2, 1, 0):
        s = nearest(z, g)
        for xx in (0, 1):
            for yy in (0, 1):
                cross(s, xx, yy).start(); load(s, xx, yy).start()

    def out_loads(j, b):
        return [
            pltpu.make_async_copy(eh_o.at[j], eh2.at[b], osem.at[b, 0]),
            pltpu.make_async_copy(hs_o.at[j], hs2.at[b], osem.at[b, 1]),
        ]
    def out_store(j, b):
        return pltpu.make_async_copy(ot.at[b], ffn_part.at[pl.ds(2 * j, 2)], psem.at[b])

    def forward_out(j):
        b = lax.rem(j, 2)
        @pl.when(j < 15)
        def _():
            for copy in out_loads(j + 1, 1 - b):
                copy.start()
        for copy in out_loads(j, b):
            copy.wait()
        @pl.when(j >= 2)
        def _(): out_store(j - 2, b).wait()
        weight = gate[j]
        for n in range(0, width, 512):
            w = pl.ds(n, 512)
            tail[0:cap, w] = (nn(eh2[b], wd[:, w]) * weight).astype(bf16)
        one, two = spread_cols(j)
        left = jnp.concatenate([one, two + hs2[b].astype(f32)], axis=1).astype(bf16)
        for n in range(0, width, 512):
            w = pl.ds(n, 512)
            out = nn(left, tail[:, w]).astype(bf16)
            ot[b, 0, :, w] = out[:rows]
            ot[b, 1, :, w] = out[rows:]
        out_store(j, b).start()

    for copy in out_loads(0, 0):
        copy.start()

    @pl.loop(0, 6)
    def _(t):
        @pl.when(t < 4)
        def _():
            first(nearest(z, 3 - t))
            @pl.loop(0, 4)
            def _(i): forward_out(4 * t + i)
        @pl.when((t >= 1) & (t < 5))
        def _(): second(nearest(z, 4 - t))
        @pl.when(t >= 2)
        def _(): third(nearest(z, 5 - t))

    total[...] = acc[at(z, x, y)]
    out_store(14, 0).wait()
    out_store(15, 1).wait()

    for s in range(4):
        x0(s).wait_send(); y1(s).wait_send()
        rx0(s).wait_send(); ry1(s).wait_send()
        for q in (0, 1):
            y0(s, q).wait_send(); x1(s, q).wait_send()
            ry0(s, q).wait_send(); rx1(s, q).wait_send()
            for r in (0, 1):
                cross(s, q, r).wait_send()
                for p in (0, 1):
                    side(s, q, r, p).wait_send()
        @pl.when((z < 3) & (s <= z))
        def _(): zcopy(s, 1).wait_send()
        @pl.when((z > 0) & (s >= z))
        def _(): zcopy(s, 0).wait_send()
        @pl.when(s > z)
        def _(): zu(s).wait_send()
        @pl.when(s < z)
        def _(): zd(s).wait_send()

def expert_layer(act, deh, dhs, rank_row, rank_col, gate, wg, wu, wd, sgu, sdt, cid):
    rows, width = act.shape
    cap, hidden = deh.shape[1:]
    h = rows // 2
    f32, bf16 = jnp.float32, jnp.bfloat16
    D = pltpu.SemaphoreType.DMA
    S = jax.ShapeDtypeStruct
    any_ = pl.BlockSpec(memory_space=pl.ANY)
    vm = pl.BlockSpec(memory_space=pltpu.VMEM)
    V = lambda *shape, t=bf16: pltpu.VMEM(shape, t)
    return pl.pallas_call(
        expert_kernel,
        out_shape=[
            S((rows, width), bf16), S((32, rows, width), bf16), S((16, cap, width), bf16),
            S((16, cap, hidden), bf16), S((16, cap, hidden), bf16), S((16, cap, hidden), bf16),
            S((16, 2 * rows, 128), bf16), S((16, 2 * rows, 256), bf16),
            S((32, rows, width), bf16), S((32, rows, width), bf16),
        ],
        in_specs=[vm, any_, any_, vm, vm, vm] + [any_] * 5,
        out_specs=[vm] + [any_] * 9,
        scratch_shapes=[
            V(*wg.shape), V(*wu.shape), V(*wd.shape), V(*sgu.shape), V(256, width),
            V(16, rows, width), V(16, rows, width), V(8, h, width), V(4, h, width), V(8, h, width), V(4, h, width),
            V(4, rows, width), V(4, rows, width),
            V(2 * cap, hidden, t=f32), V(2 * cap, hidden, t=f32), V(2 * cap, hidden, t=f32),
            V(2 * cap, hidden), V(2 * cap, hidden), V(2 * cap, hidden),
            V(2, 2 * rows, 128, t=f32), V(2, 2 * rows, 128), V(2, 2 * rows, 256),
            V(2, cap, hidden), V(2, 2 * rows, 128), V(2, 2, rows, width),
            D((5,)), D((2, 3)), D((2, 7)), D((2, 2)), D((2,)), D,
            D((4, 2)), D((4,)), D((4,)), D((4,)), D((4, 2)), D((4, 2)), D((4, 2)), D((4, 2)), D((4,)), D((4,)), D((16, 2)), D((16, 2)),
            D((16,)), D((16,)), D((16,)), D((4, 2)), D((4, 2)), D((4,)), D((4,)), D((4, 2)), D((4, 2)), D((4,)), D((4,)),
            D((4,)), D((4,)), D((4,)), D((4,)),
        ],
        compiler_params=pltpu.CompilerParams(collective_id=cid, has_side_effects=True, vmem_limit_bytes=62 << 20),
        name="expert_layer",
    )(act, deh, dhs, rank_row, rank_col, gate, wg, wu, wd, sgu, sdt)


def norm_back(values, gain, grad):
    width = values.shape[1]
    inv = lax.rsqrt(jnp.sum(values * values, axis=1, keepdims=True) * (1.0 / width) + EPS)
    scaled = grad * gain
    inner = jnp.sum(values * scaled, axis=1, keepdims=True) * (1.0 / width)
    normed = values * inv
    return inv * (scaled - normed * (inv * inner)), grad * normed

def attention_back_kernel(
    part, grad2, x_mid, dy, x_in, gain1, gain2, wq_h, wk_h, wv_h, wo_h, qr, kr, vr, cosine, sine,
    out_full, tok_full, dattn, dq, dk, dv, g1, g2,
    ic, tmp, iy0, ix0, ix1, iy1, izu, izd, wa, wb, wc, dmix, dx2, da1, send1, recv1,
    wsem, ysem, ls, rcs, rcr, ry0s, ry0r, rx0s, rx0r, rx1s, rx1r, ry1s, ry1r, zus, zur, zds, zdr,
):
    f32, bf16 = jnp.float32, jnp.bfloat16
    z, x, y, c = place()
    rows, width = x_mid.shape
    h = rows // 2
    toks = 2 * rows
    heads = qr.shape[1] // HD
    lo, hi = pl.ds(0, h), pl.ds(h, h)
    xn, yn, cn = dev(z, 1 - x, y, c), dev(z, x, 1 - y, c), dev(z, x, y, 1 - c)
    greet(z, x, y, c)

    def at(s, xx, yy): return (s * 2 + xx) * 2 + yy
    def load(s, xx, yy):
        return pltpu.make_async_copy(part.at[blk(s, xx, yy, c)], tmp.at[xx * 2 + yy], ls.at[xx * 2 + yy])
    def cross(s, xx, yy):
        i = at(s, xx, yy)
        return rcopy(part.at[blk(s, xx, yy, 1 - c)], ic.at[i], rcs.at[i], rcr.at[i], cn)
    def ry0(s, xx):
        return rcopy(ic.at[at(s, xx, 1 - y), lo], iy0.at[s * 2 + xx], ry0s.at[s, xx], ry0r.at[s, xx], yn)
    def rx1(s, yy):
        return rcopy(ic.at[at(s, 1 - x, yy), hi], ix1.at[s * 2 + yy], rx1s.at[s, yy], rx1r.at[s, yy], xn)
    def rx0(s):
        return rcopy(ic.at[at(s, 1 - x, y), lo], ix0.at[s], rx0s.at[s], rx0r.at[s], xn)
    def ry1(s):
        return rcopy(ic.at[at(s, x, 1 - y), hi], iy1.at[s], ry1s.at[s], ry1r.at[s], yn)
    def zu(s):
        return rcopy(ic.at[at(s, x, y)], izu.at[s], zus.at[s], zur.at[s], dev(z + 1, x, y, c))
    def zd(s):
        return rcopy(ic.at[at(s, x, y)], izd.at[s], zds.at[s], zdr.at[s], dev(z - 1, x, y, c))
    def add(i, start, count, src, j):
        @pl.loop(0, count // 16)
        def _(r):
            a = pl.ds(pl.multiple_of(start + r * 16, 16), 16)
            b = pl.ds(pl.multiple_of(r * 16, 16), 16)
            ic[i, a] = ic[i, a] + src[j, b]

    four = [(xx, yy) for xx in (0, 1) for yy in (0, 1)]

    def first(g):
        s = nearest(z, g)
        for xx, yy in four:
            load(s, xx, yy).wait(); cross(s, xx, yy).wait_recv()
            add(at(s, xx, yy), 0, rows, tmp, xx * 2 + yy)
            @pl.when(yy != y)
            def _(): ry0(s, xx).start()
            @pl.when(xx != x)
            def _(): rx1(s, yy).start()
        if g > 0:
            for xx, yy in four:
                load(nearest(z, g - 1), xx, yy).start()

    def second(g):
        s = nearest(z, g)
        ry0(s, 1 - x).wait_recv(); add(at(s, 1 - x, y), 0, h, iy0, s * 2 + 1 - x); rx0(s).start()
        rx1(s, 1 - y).wait_recv(); add(at(s, x, 1 - y), h, h, ix1, s * 2 + 1 - y); ry1(s).start()
        ry0(s, x).wait_recv(); add(at(s, x, y), 0, h, iy0, s * 2 + x)
        rx1(s, y).wait_recv(); add(at(s, x, y), h, h, ix1, s * 2 + y)

    def third(g):
        s = nearest(z, g)
        me = at(s, x, y)
        rx0(s).wait_recv(); add(me, 0, h, ix0, s)
        ry1(s).wait_recv(); add(me, h, h, iy1, s)
        @pl.when((s >= z) & (z > 0))
        def _():
            zu(s).wait_recv(); add(me, 0, rows, izu, s)
        @pl.when((s <= z) & (z < 3))
        def _():
            zd(s).wait_recv(); add(me, 0, rows, izd, s)
        @pl.when(s > z)
        def _(): zu(s).start()
        @pl.when(s < z)
        def _(): zd(s).start()

    for g in (3, 2, 1, 0):
        s = nearest(z, g)
        for xx, yy in four:
            cross(s, xx, yy).start()
            if g == 3:
                load(s, xx, yy).start()
    w_out = pltpu.make_async_copy(wo_h, wa, wsem.at[0])
    w_query = pltpu.make_async_copy(wq_h, wb, wsem.at[1])
    w_key = pltpu.make_async_copy(wk_h, wc, wsem.at[2])
    w_value = pltpu.make_async_copy(wv_h, wa, wsem.at[3])
    w_out.start(); w_query.start(); w_key.start()

    g1[...] = jnp.zeros_like(g1)
    g2[...] = jnp.zeros_like(g2)
    @pl.loop(0, rows // 16)
    def _(r):
        q = pl.ds(pl.multiple_of(r * 16, 16), 16)
        back, terms = norm_back(x_mid[q], gain2[...], grad2[q].astype(f32))
        back = back + dy[q].astype(f32)
        dx2[q] = back
        dattn[y, q] = back.astype(bf16)
        g2[...] += jnp.sum(terms, axis=0, keepdims=True)
    attn_swap = rcopy(dattn.at[y], dattn.at[y], ysem.at[0], ysem.at[1], yn)
    attn_swap.start()
    first(3)
    first(2)
    w_out.wait()
    attn_swap.wait_recv()
    full = dattn[...].reshape(toks, width)
    dmix[...] = nn(full, wa[...]).astype(bf16)
    w_value.start()

    scale = HD ** (-0.5)
    def turn_back(values):
        return values * cosine[...] - pltpu.roll(values, HD // 2, 1) * sine[...]
    @pl.loop(0, heads)
    def _(n):
        @pl.when(n == 2)
        def _():
            second(3); first(1)
        @pl.when(n == 5)
        def _():
            second(2); third(3); first(0)
        w = pl.ds(pl.multiple_of(n * HD, HD), HD)
        qh, kh, vh, doh = qr[:, w], kr[:, w], vr[:, w], dmix[:, w]
        scores = nt(qh, kh) * scale
        ahead = lax.broadcasted_iota(jnp.int32, (toks, toks), 0) >= lax.broadcasted_iota(jnp.int32, (toks, toks), 1)
        scores = jnp.where(ahead, scores, -1e30)
        expo = jnp.exp(scores - jnp.max(scores, axis=1, keepdims=True))
        probs = expo * (1.0 / jnp.sum(expo, axis=1, keepdims=True))
        dv[:, w] = lax.dot_general(
            probs.astype(bf16), doh, (((0,), (0,)), ((), ())), preferred_element_type=f32
        ).astype(bf16)
        dprob = nt(doh, vh)
        delta = jnp.sum(probs * dprob, axis=1, keepdims=True)
        ds = (probs * (dprob - delta)).astype(bf16)
        dq[:, w] = turn_back(nn(ds, kh) * scale).astype(bf16)
        dkr = lax.dot_general(ds, qh, (((0,), (0,)), ((), ())), preferred_element_type=f32)
        dk[:, w] = turn_back(dkr * scale).astype(bf16)

    w_query.wait(); w_key.wait(); w_value.wait()
    for n in range(0, width, 512):
        w = pl.ds(n, 512)
        out = nt(dq[...], wb[w, :]) + nt(dk[...], wc[w, :]) + nt(dv[...], wa[w, :])
        da1[0, :, w] = out[:rows]
        da1[1, :, w] = out[rows:]
    @pl.loop(0, rows // 16)
    def _(r):
        q = pl.ds(pl.multiple_of(r * 16, 16), 16)
        send1[q] = da1[1 - y, q].astype(bf16)
    da1_swap = rcopy(send1, recv1, ysem.at[2], ysem.at[3], yn)
    da1_swap.start()
    second(1); third(2)
    da1_swap.wait_recv()
    @pl.loop(0, rows // 16)
    def _(r):
        q = pl.ds(pl.multiple_of(r * 16, 16), 16)
        back, terms = norm_back(x_in[q].astype(f32), gain1[...], da1[y, q] + recv1[q].astype(f32))
        tok_full[y, q] = (back + dx2[q]).astype(bf16)
        g1[...] += jnp.sum(terms, axis=0, keepdims=True)
    tok_swap = rcopy(tok_full.at[y], tok_full.at[y], ysem.at[4], ysem.at[5], yn)
    tok_swap.start()
    second(0); third(1); third(0)
    @pl.loop(0, rows // 16)
    def _(r):
        q = pl.ds(pl.multiple_of(r * 16, 16), 16)
        out_full[y, q] = (x_mid[q] + ic[at(z, x, y), q].astype(f32)).astype(bf16)
    out_swap = rcopy(out_full.at[y], out_full.at[y], ysem.at[6], ysem.at[7], yn)
    out_swap.start()
    tok_swap.wait_recv()
    out_swap.wait_recv()
    for swap in (attn_swap, da1_swap, tok_swap, out_swap):
        swap.wait_send()
    for s in range(4):
        rx0(s).wait_send(); ry1(s).wait_send()
        for q in (0, 1):
            ry0(s, q).wait_send(); rx1(s, q).wait_send()
            for r in (0, 1):
                cross(s, q, r).wait_send()
        @pl.when(s > z)
        def _(): zu(s).wait_send()
        @pl.when(s < z)
        def _(): zd(s).wait_send()

def attention_back(part, grad2, x_mid, dy, x_in, gain1, gain2, weights, qr, kr, vr, cosine, sine, cid):
    rows, width = x_mid.shape
    toks, hw = qr.shape
    h = rows // 2
    f32, bf16 = jnp.float32, jnp.bfloat16
    D = pltpu.SemaphoreType.DMA
    S = jax.ShapeDtypeStruct
    any_ = pl.BlockSpec(memory_space=pl.ANY)
    vm = pl.BlockSpec(memory_space=pltpu.VMEM)
    V = lambda *shape, t=bf16: pltpu.VMEM(shape, t)
    return pl.pallas_call(
        attention_back_kernel,
        out_shape=[
            S((2, rows, width), bf16), S((2, rows, width), bf16), S((2, rows, width), bf16),
            S((toks, hw), bf16), S((toks, hw), bf16), S((toks, hw), bf16), S((1, width), f32), S((1, width), f32),
        ],
        in_specs=[any_] + [vm] * 6 + [any_] * 4 + [vm] * 5,
        out_specs=[vm] * 8,
        scratch_shapes=[
            V(16, rows, width), V(4, rows, width), V(8, h, width), V(4, h, width), V(8, h, width), V(4, h, width),
            V(4, rows, width), V(4, rows, width),
            V(width, hw), V(width, hw), V(width, hw), V(toks, hw), V(rows, width, t=f32), V(2, rows, width, t=f32),
            V(rows, width), V(rows, width),
            D((4,)), D((8,)), D((4,)), D((16,)), D((16,)), D((4, 2)), D((4, 2)), D((4,)), D((4,)), D((4, 2)), D((4, 2)), D((4,)), D((4,)),
            D((4,)), D((4,)), D((4,)), D((4,)),
        ],
        compiler_params=pltpu.CompilerParams(collective_id=cid, has_side_effects=True, vmem_limit_bytes=63 << 20),
        name="attention_back",
    )(part, grad2, x_mid, dy, x_in, gain1, gain2, *weights, qr, kr, vr, cosine, sine)

def weight_grad_kernel(
    a1, dattn, dq, dk, dv, mixed, gains,
    oq, ok, ov, oo, og,
    acc, ic, ix, izu, izd, gc, gx, gu, gd, gy, gbuf,
    cs, cr, xs, xr, zus, zur, zds, zdr, gss, gsr,
):
    f32, bf16 = jnp.float32, jnp.bfloat16
    z, x, y, c = place()
    xn, yn, cn = dev(z, 1 - x, y, c), dev(z, x, 1 - y, c), dev(z, x, y, 1 - c)
    n, depth = 4, acc.shape[2]
    outs = (oq, ok, ov, oo)
    greet(z, x, y, c)
    def pos(s, xx, cc): return (s * 2 + xx) * 2 + cc
    def wc(a, s, xx):
        i = s * 2 + xx
        return rcopy(acc.at[a, pos(s, xx, 1 - c)], ic.at[a, i], cs.at[a, i], cr.at[a, i], cn)
    def wx(a, s):
        return rcopy(acc.at[a, pos(s, 1 - x, c)], ix.at[a, s], xs.at[a, s], xr.at[a, s], xn)
    def zu(a, s):
        return rcopy(acc.at[a, pos(s, x, c)], izu.at[a, s], zus.at[a, s], zur.at[a, s], dev(z + 1, x, y, c))
    def zd(a, s):
        return rcopy(acc.at[a, pos(s, x, c)], izd.at[a, s], zds.at[a, s], zdr.at[a, s], dev(z - 1, x, y, c))
    def add(a, i, src, j):
        @pl.loop(0, depth // 16)
        def _(r):
            b = pl.ds(pl.multiple_of(r * 16, 16), 16)
            acc[a, i, b] = acc[a, i, b] + src[a, j, b]
    def make(g):
        s = nearest(z, g)
        w = pl.ds(pl.multiple_of(s * 4 * depth, 4 * depth), 4 * depth)
        for a, (left, right) in ((3, (dattn, mixed)), (0, (a1, dq)), (1, (a1, dk)), (2, (a1, dv))):
            out = lax.dot_general(left[:, w], right[...], (((0,), (0,)), ((), ())), preferred_element_type=f32).astype(bf16)
            for i in range(4):
                acc[a, s * 4 + i] = out[i * depth:(i + 1) * depth]
            for q in (0, 1):
                wc(a, s, q).start()
    def first(g):
        s = nearest(z, g)
        for a in (3, 0, 1, 2):
            for q in (0, 1):
                wc(a, s, q).wait_recv()
                add(a, pos(s, q, c), ic, s * 2 + q)
            wx(a, s).start()
    def second(g):
        s = nearest(z, g)
        for a in (3, 0, 1, 2):
            wx(a, s).wait_recv(); add(a, pos(s, x, c), ix, s)
            @pl.when((s >= z) & (z > 0))
            def _():
                zu(a, s).wait_recv(); add(a, pos(s, x, c), izu, s)
            @pl.when((s <= z) & (z < 3))
            def _():
                zd(a, s).wait_recv(); add(a, pos(s, x, c), izd, s)
            @pl.when(s > z)
            def _(): zu(a, s).start()
            @pl.when(s < z)
            def _(): zd(a, s).start()
    g_c = rcopy(gains.at[1 - c], gc, gss.at[0], gsr.at[0], cn)
    g_x = rcopy(gbuf.at[1 - x], gx, gss.at[1], gsr.at[1], xn)
    g_u = rcopy(gu.at[1], gu.at[0], gss.at[2], gsr.at[2], dev(z + 1, x, y, c))
    g_d = rcopy(gd.at[1], gd.at[0], gss.at[3], gsr.at[3], dev(z - 1, x, y, c))
    g_y = rcopy(gy.at[0], gy.at[1], gss.at[4], gsr.at[4], yn)
    g_c.start()
    make(3); make(2)
    g_c.wait_recv()
    gbuf[...] = gains[c] + gc[...]
    g_x.start()
    first(3); make(1); first(2); make(0)
    g_x.wait_recv()
    gbuf[x] = gbuf[x] + gx[...]
    second(3)
    gu[1] = gbuf[x]
    gd[1] = gbuf[x]
    @pl.when(z > 0)
    def _():
        g_u.wait_recv()
        gu[1] = gu[1] + gu[0]
    @pl.when(z < 3)
    def _():
        g_u.start()
    first(1)
    second(2)
    @pl.when(z < 3)
    def _():
        g_d.wait_recv()
        gd[1] = gd[1] + gd[0]
    @pl.when(z > 0)
    def _():
        g_d.start()
    first(0)
    second(1)
    gy[0] = gu[1, z] + gd[1, z] - gbuf[x, z]
    g_y.start()
    second(0)
    for a in range(n):
        outs[a][...] = acc[a, pos(z, x, c)].astype(f32)
    g_y.wait_recv()
    og[...] = gy[0] + gy[1]
    g_c.wait_send(); g_x.wait_send(); g_y.wait_send()
    @pl.when(z < 3)
    def _(): g_u.wait_send()
    @pl.when(z > 0)
    def _(): g_d.wait_send()
    for s in range(4):
        for a in range(n):
            for q in (0, 1): wc(a, s, q).wait_send()
            wx(a, s).wait_send()
            @pl.when(s > z)
            def _(): zu(a, s).wait_send()
            @pl.when(s < z)
            def _(): zd(a, s).wait_send()

def weight_grads(a1, dattn, dq, dk, dv, mixed, gains, cid):
    toks, width = a1.shape
    hw = dq.shape[1]
    depth = width // 16
    f32, bf16 = jnp.float32, jnp.bfloat16
    D = pltpu.SemaphoreType.DMA
    S = jax.ShapeDtypeStruct
    vm = pl.BlockSpec(memory_space=pltpu.VMEM)
    V = lambda *shape, t=bf16: pltpu.VMEM(shape, t)
    return pl.pallas_call(
        weight_grad_kernel,
        out_shape=[S((depth, hw), f32)] * 4 + [S((8, 128), f32)],
        in_specs=[vm] * 7,
        out_specs=[vm] * 5,
        scratch_shapes=[
            V(4, 16, depth, hw), V(4, 8, depth, hw), V(4, 4, depth, hw), V(4, 4, depth, hw), V(4, 4, depth, hw),
            V(2, 4, 8, 128, t=f32), V(4, 8, 128, t=f32), V(2, 4, 8, 128, t=f32), V(2, 4, 8, 128, t=f32), V(2, 8, 128, t=f32), V(2, 4, 8, 128, t=f32),
            D((4, 8)), D((4, 8)), D((4, 4)), D((4, 4)), D((4, 4)), D((4, 4)), D((4, 4)), D((4, 4)), D((5,)), D((5,)),
        ],
        compiler_params=pltpu.CompilerParams(collective_id=cid, has_side_effects=True, vmem_limit_bytes=60 << 20),
        name="weight_grads",
    )(a1, dattn, dq, dk, dv, mixed, gains)


def routing_tables(gate_table, capacity):
    member = gate_table > 0.0
    ranks = jnp.cumsum(member.astype(jnp.int32), axis=1) - 1
    slot = jnp.arange(capacity, dtype=jnp.int32)
    pick = (ranks[:, None, :] == slot[None, :, None]) & member[:, None, :]
    slot_gate = jnp.sum(jnp.where(pick, gate_table[:, None, :], 0.0), axis=2)
    held = jnp.where(member, ranks, -1)
    return pick.astype(jnp.bfloat16), slot_gate, held


def on_device(
    tokens,
    cotangent,
    route_ids,
    route_gates,
    gain_first,
    w_query,
    w_key,
    w_value,
    w_output,
    gain_second,
    shared_gate,
    shared_up,
    shared_down,
    expert_gate,
    expert_up,
    expert_down,
):
    f32, bf16 = jnp.float32, jnp.bfloat16
    rows_dev, width = tokens.shape
    topk = route_ids.shape[1]
    experts = lax.axis_size("dp")
    splits = lax.axis_size("tensor")
    half = rows_dev // splits
    mine = lax.axis_index("tensor") * half
    capacity = rows_dev * topk * 4 // (3 * experts)
    slots = experts * capacity
    scale = HD ** (-0.5)
    positions = jnp.arange(rows_dev, dtype=f32)
    causal = jnp.arange(rows_dev)[:, None] >= jnp.arange(rows_dev)[None, :]
    grad_half = lax.dynamic_slice_in_dim(cotangent, mine, half, axis=0)
    chosen = route_ids[:, :, None] == jnp.arange(experts, dtype=jnp.int32)[None, None, :]
    table = jnp.sum(jnp.where(chosen, route_gates[:, :, None], 0.0), axis=1)
    gains = jnp.concatenate([gain_first[None], gain_second[None], jnp.zeros((14, gain_first.shape[0]), bf16)])
    query_whole, key_whole, value_whole, output_whole, gains, tables, grad_all = start_gather(
        [w_query, w_key, w_value, w_output, gains, table.T], grad_half, 0, "gather_weights"
    )
    query_whole, key_whole, value_whole, output_whole = [
        w.reshape(width, -1) for w in (query_whole, key_whole, value_whole, output_whole)
    ]
    grad_all = grad_all.reshape(-1, width)
    gain_one = gains[:, 0].reshape(-1).astype(f32)
    gain_two = gains[:, 1].reshape(-1).astype(f32)

    depth, common_width = shared_gate.shape
    common_dev = common_width // experts
    packed = jnp.stack([shared_gate, shared_up, shared_down])
    packed = packed.reshape(3, depth, experts, common_dev).transpose(2, 0, 1, 3)
    packed = lax.all_to_all(packed, "dp", split_axis=0, concat_axis=0, tiled=True)
    packed = packed.transpose(1, 0, 2, 3).reshape(3, width, common_dev)

    table = lax.dynamic_index_in_dim(tables, lax.axis_index("dp"), axis=1, keepdims=False)
    pick, slot_gate, held = routing_tables(table, capacity)

    x_in = tokens.astype(f32)
    act_one = rms_norm(x_in, gain_one).astype(bf16)
    heads_dev = query_whole.shape[1] // HD
    query_pre = jnp.dot(act_one, query_whole, preferred_element_type=f32).reshape(
        rows_dev, heads_dev, HD
    )
    key_pre = jnp.dot(act_one, key_whole, preferred_element_type=f32).reshape(
        rows_dev, heads_dev, HD
    )
    query_rot = rotate(query_pre, positions).astype(bf16)
    key_rot = rotate(key_pre, positions).astype(bf16)
    value_low = (
        jnp.dot(act_one, value_whole, preferred_element_type=f32)
        .astype(bf16)
        .reshape(rows_dev, heads_dev, HD)
    )
    scores = masked_scores(query_rot, key_rot, causal, scale)
    top = jnp.max(scores, axis=-1, keepdims=True)
    expo = jnp.exp(scores - top)
    total = jnp.sum(expo, axis=-1, keepdims=True)
    probs = expo / total
    mixed = jnp.einsum("hqk,khc->qhc", probs.astype(bf16), value_low, preferred_element_type=f32)
    mixed = mixed.reshape(rows_dev, heads_dev * HD).astype(bf16)
    attn = lax.psum_scatter(
        contract_last(mixed, output_whole), "tensor", scatter_dimension=0, tiled=True
    )
    x_half = lax.dynamic_slice_in_dim(tokens, mine, half, axis=0).astype(f32)
    x_mid = x_half + attn
    act_two = rms_norm(x_mid, gain_two).astype(bf16)

    grad_blocks = grad_all.reshape(experts, rows_dev, width)
    exp_gate, exp_up, exp_down = expert_gate[0], expert_up[0], expert_down[0]
    weight = slot_gate.reshape(slots, 1)
    rows_out_grad = jnp.einsum("jst,jtd->jsd", pick, grad_blocks, preferred_element_type=f32)
    rows_out_grad = (weight * rows_out_grad.reshape(slots, width)).astype(bf16)
    hidden_rows_grad = contract_last(rows_out_grad, exp_down).reshape(experts, capacity, -1)
    front = capacity - 128
    back = 128 - front - common_dev

    def widen(w):
        return jnp.pad(w, ((0, 0), (front, back)))

    common_gu = jnp.concatenate([widen(packed[0]), widen(packed[1])], axis=1)
    common_down = widen(packed[2])
    common_hidden_grad = jnp.dot(grad_all, common_down, preferred_element_type=f32)
    down_rows = common_down.T[front:]
    total_grad, act_all, rows, hidden_rows, gate_rows_grad, up_rows_grad, common_hidden, common_gu_grad, unused, ffn = (
        expert_layer(
            act_two,
            hidden_rows_grad,
            common_hidden_grad.reshape(experts, rows_dev, 128),
            held[:, None, :],
            held[:, :, None],
            slot_gate[:, :, None],
            exp_gate,
            exp_up,
            exp_down,
            common_gu,
            down_rows,
            1,
        )
    )
    act_all = act_all.reshape(-1, width)
    rows = rows.reshape(slots, width)
    hidden_rows = hidden_rows.reshape(slots, -1)
    common_hidden = common_hidden.reshape(-1, 128)
    common_gu_grad = common_gu_grad.reshape(-1, 256)
    expert_gate_grad = contract_first(rows, gate_rows_grad.reshape(slots, -1))[None]
    expert_up_grad = contract_first(rows, up_rows_grad.reshape(slots, -1))[None]
    expert_down_grad = contract_first(hidden_rows, rows_out_grad)[None]
    gu_grad = contract_first(act_all, common_gu_grad)
    down_grad = contract_first(grad_all, common_hidden)
    common_w_grad = jnp.concatenate(
        [w[:, front : front + common_dev] for w in (gu_grad[:, :128], gu_grad[:, 128:], down_grad)], axis=1
    )
    common_w_grad = common_w_grad.astype(bf16).reshape(experts, depth, 3 * common_dev)
    common_w_grad = lax.all_to_all(common_w_grad, "dp", split_axis=0, concat_axis=0, tiled=True)
    common_w_grad = common_w_grad.astype(f32).reshape(experts, depth, 3, common_dev)
    common_w_grad = common_w_grad.transpose(2, 1, 0, 3).reshape(3, depth, common_width)

    freqs = 10000.0 ** (-2.0 * jnp.arange(HD // 2, dtype=f32) / HD)
    angles = positions[:, None] * freqs[None, :]
    cosine = jnp.concatenate([jnp.cos(angles)] * 2, axis=1)
    sine = jnp.concatenate([-jnp.sin(angles), jnp.sin(angles)], axis=1)
    layer_out, tokens_grad, attn_grad, query_grad, key_grad, value_grad, gain_one_grad, gain_two_grad = attention_back(
        ffn,
        total_grad,
        x_mid,
        grad_half,
        lax.dynamic_slice_in_dim(tokens, mine, half, axis=0),
        gain_one[None],
        gain_two[None],
        (query_whole, key_whole, value_whole, output_whole),
        query_rot.reshape(rows_dev, -1),
        key_rot.reshape(rows_dev, -1),
        value_low.reshape(rows_dev, -1),
        cosine,
        sine,
        2,
    )
    gains = jnp.concatenate([gain_one_grad, gain_two_grad, jnp.zeros((6, width), f32)])
    gains = gains.reshape(8, 4, 2, 2, width // 16).transpose(3, 2, 1, 0, 4)
    query_sum, key_sum, value_sum, output_sum, gain_grads = weight_grads(
        act_one, attn_grad.reshape(rows_dev, width), query_grad, key_grad, value_grad, mixed, gains, 4
    )
    return (
        layer_out.reshape(rows_dev, width),
        tokens_grad.reshape(rows_dev, width),
        gain_grads[0],
        query_sum,
        key_sum,
        value_sum,
        output_sum,
        gain_grads[1],
        common_w_grad[0],
        common_w_grad[1],
        common_w_grad[2],
        expert_gate_grad,
        expert_up_grad,
        expert_down_grad,
    )


def solution(mesh):
    body = on_device if (mesh.shape["dp"], mesh.shape["tensor"]) == (16, 2) else on_device_plain
    in_specs = (
        P("dp", None),
        P("dp", None),
        P("dp", None),
        P("dp", None),
        P("dp"),
        P("dp", "tensor"),
        P("dp", "tensor"),
        P("dp", "tensor"),
        P("dp", "tensor"),
        P("dp"),
        P("dp", "tensor"),
        P("dp", "tensor"),
        P("dp", "tensor"),
        P("dp", None, "tensor"),
        P("dp", None, "tensor"),
        P("dp", "tensor", None),
    )
    out_specs = (
        P("dp", None),
        P("dp", None),
        P("dp"),
        P("dp", "tensor"),
        P("dp", "tensor"),
        P("dp", "tensor"),
        P("dp", "tensor"),
        P("dp"),
        P("dp", "tensor"),
        P("dp", "tensor"),
        P("dp", "tensor"),
        P("dp", None, "tensor"),
        P("dp", None, "tensor"),
        P("dp", "tensor", None),
    )
    return jax.shard_map(
        body, mesh=mesh, in_specs=in_specs, out_specs=out_specs, check_vma=False
    )
```

```python
import functools

import jax
import jax.numpy as jnp
from jax import lax
from jax.experimental import pallas as pl
from jax.experimental.pallas import tpu as pltpu
from jax.sharding import PartitionSpec as P

HD = 128
MESH = pl.DeviceIdType.MESH


EPS = 1e-06


def rms_norm(values, gain):
    mean_square = jnp.mean(values * values, axis=-1, keepdims=True)
    return values * lax.rsqrt(mean_square + EPS) * gain


def rotate(values, positions):
    head = values.shape[-1]
    half = head // 2
    freqs = 10000.0 ** (-2.0 * jnp.arange(half, dtype=jnp.float32) / head)
    angles = positions[:, None] * freqs[None, :]
    cosine = jnp.cos(angles)[:, None, :]
    sine = jnp.sin(angles)[:, None, :]
    first = values[..., :half]
    second = values[..., half:]
    return jnp.concatenate(
        [first * cosine - second * sine, second * cosine + first * sine], axis=-1
    )


def gated(gate_pre, up_pre):
    return gate_pre * jax.nn.sigmoid(gate_pre) * up_pre


def contract_last(left, right):
    return lax.dot_general(
        left, right, (((1,), (1,)), ((), ())), preferred_element_type=jnp.float32
    )


def contract_first(left, right):
    return lax.dot_general(
        left, right, (((0,), (0,)), ((), ())), preferred_element_type=jnp.float32
    )


def masked_scores(query_rot, key_rot, causal, scale):
    scores = (
        jnp.einsum("qhc,khc->hqk", query_rot, key_rot, preferred_element_type=jnp.float32) * scale
    )
    return jnp.where(causal[None], scores, -1e30)


def on_device_plain(
    tokens,
    cotangent,
    route_ids,
    route_gates,
    gain_first,
    w_query,
    w_key,
    w_value,
    w_output,
    gain_second,
    shared_gate,
    shared_up,
    shared_down,
    expert_gate,
    expert_up,
    expert_down,
):
    rows_dev, width = tokens.shape
    topk = route_ids.shape[1]
    experts = lax.axis_size("dp")
    capacity = rows_dev * topk * 4 // (3 * experts)
    slots = experts * capacity
    scale = HD ** (-0.5)
    positions = jnp.arange(rows_dev, dtype=jnp.float32)
    causal = jnp.arange(rows_dev)[:, None] >= jnp.arange(rows_dev)[None, :]
    gain_one, query_whole, key_whole, value_whole, output_whole = (
        lax.all_gather(gain_first, "dp", axis=0, tiled=True),
        lax.all_gather(w_query, "dp", axis=0, tiled=True),
        lax.all_gather(w_key, "dp", axis=0, tiled=True),
        lax.all_gather(w_value, "dp", axis=0, tiled=True),
        lax.all_gather(w_output, "dp", axis=0, tiled=True),
    )
    gain_two, common_gate, common_up, common_down = (
        lax.all_gather(gain_second, "dp", axis=0, tiled=True),
        lax.all_gather(shared_gate, "dp", axis=0, tiled=True),
        lax.all_gather(shared_up, "dp", axis=0, tiled=True),
        lax.all_gather(shared_down, "dp", axis=0, tiled=True),
    )
    gain_one = gain_one.astype(jnp.float32)
    gain_two = gain_two.astype(jnp.float32)
    x_in = tokens.astype(jnp.float32)
    act_one = rms_norm(x_in, gain_one).astype(jnp.bfloat16)
    heads_dev = query_whole.shape[1] // HD
    query_pre = jnp.dot(act_one, query_whole, preferred_element_type=jnp.float32).reshape(
        rows_dev, heads_dev, HD
    )
    key_pre = jnp.dot(act_one, key_whole, preferred_element_type=jnp.float32).reshape(
        rows_dev, heads_dev, HD
    )
    query_rot = rotate(query_pre, positions).astype(jnp.bfloat16)
    key_rot = rotate(key_pre, positions).astype(jnp.bfloat16)
    value_low = (
        jnp.dot(act_one, value_whole, preferred_element_type=jnp.float32)
        .astype(jnp.bfloat16)
        .reshape(rows_dev, heads_dev, HD)
    )
    scores = masked_scores(query_rot, key_rot, causal, scale)
    top = jnp.max(scores, axis=-1, keepdims=True)
    expo = jnp.exp(scores - top)
    total = jnp.sum(expo, axis=-1, keepdims=True)
    probs = expo / total
    log_total = top + jnp.log(total)
    mixed = jnp.einsum(
        "hqk,khc->qhc", probs.astype(jnp.bfloat16), value_low, preferred_element_type=jnp.float32
    )
    mixed = mixed.reshape(rows_dev, heads_dev * HD).astype(jnp.bfloat16)
    attn = lax.psum(contract_last(mixed, output_whole), "tensor")
    x_mid = x_in + attn
    act_two = rms_norm(x_mid, gain_two).astype(jnp.bfloat16)
    gate_pre = jnp.dot(act_two, common_gate, preferred_element_type=jnp.float32)
    up_pre = jnp.dot(act_two, common_up, preferred_element_type=jnp.float32)
    hidden_common = gated(gate_pre, up_pre).astype(jnp.bfloat16)
    common_out = contract_last(hidden_common, common_down)
    flat_ids = route_ids.reshape(-1)
    onehot = (flat_ids[:, None] == jnp.arange(experts, dtype=jnp.int32)[None, :]).astype(jnp.int32)
    ranks = jnp.sum(onehot * jnp.cumsum(onehot, axis=0), axis=1) - 1
    dest = flat_ids * capacity + ranks
    token_of = jnp.arange(rows_dev * topk, dtype=jnp.int32) // topk
    source = jnp.zeros((slots,), jnp.int32).at[dest].set(token_of)
    weight_of = jnp.zeros((slots,), jnp.float32).at[dest].set(route_gates.reshape(-1))
    filled = jnp.zeros((slots,), jnp.bool_).at[dest].set(True)
    outgoing = jnp.where(filled[:, None], act_two[source], jnp.zeros((), jnp.bfloat16)).reshape(
        experts, capacity, width
    )
    exp_gate = expert_gate[0]
    exp_up = expert_up[0]
    exp_down = expert_down[0]
    received = lax.all_to_all(outgoing, "dp", split_axis=0, concat_axis=0, tiled=True)
    sources = received.shape[0]
    count = received.shape[1]
    rows = received.reshape(sources * count, width)
    gate_rows = jnp.dot(rows, exp_gate, preferred_element_type=jnp.float32)
    up_rows = jnp.dot(rows, exp_up, preferred_element_type=jnp.float32)
    hidden_rows = gated(gate_rows, up_rows).astype(jnp.bfloat16)
    partial_value = jnp.dot(hidden_rows, exp_down, preferred_element_type=jnp.float32).reshape(
        sources, count, width
    )
    returned = lax.all_to_all(
        partial_value.astype(jnp.bfloat16), "dp", split_axis=0, concat_axis=0, tiled=True
    ).astype(partial_value.dtype)
    returned, kept_rows, kept_gate, kept_up = (
        returned,
        received,
        gate_rows.reshape(sources, count, -1),
        up_rows.reshape(sources, count, -1),
    )
    picked = returned.reshape(slots, width)[dest].reshape(rows_dev, topk, width)
    routed_part = jnp.sum(picked * route_gates[:, :, None], axis=1)
    ffn = lax.psum((common_out + routed_part).astype(jnp.bfloat16), "tensor").astype(jnp.float32)
    layer_out = (x_mid + ffn).astype(jnp.bfloat16)
    grad_out = cotangent.astype(jnp.float32)
    hidden_grad = jnp.dot(cotangent, common_down, preferred_element_type=jnp.float32)
    dummy_common, common_vjp = jax.vjp(gated, gate_pre, up_pre)
    gate_grad, up_grad = common_vjp(hidden_grad)
    gate_grad = gate_grad.astype(jnp.bfloat16)
    up_grad = up_grad.astype(jnp.bfloat16)
    common_gate_grad = contract_first(act_two, gate_grad)
    common_up_grad = contract_first(act_two, up_grad)
    common_down_grad = contract_first(cotangent, hidden_common)
    act_two_grad = contract_last(gate_grad, common_gate) + contract_last(up_grad, common_up)
    outgoing_grad = (
        (weight_of[:, None] * grad_out[source])
        .astype(jnp.bfloat16)
        .reshape(experts, capacity, width)
    )
    incoming_grad = lax.all_to_all(outgoing_grad, "dp", split_axis=0, concat_axis=0, tiled=True)
    hidden_width = kept_gate.shape[2]
    rows = kept_rows.reshape(-1, width)
    rows_out_grad = incoming_grad.reshape(-1, width)
    hidden_rows, expert_vjp = jax.vjp(
        gated, kept_gate.reshape(-1, hidden_width), kept_up.reshape(-1, hidden_width)
    )
    hidden_rows = hidden_rows.astype(jnp.bfloat16)
    hidden_rows_grad = contract_last(rows_out_grad, exp_down)
    gate_rows_grad, up_rows_grad = expert_vjp(hidden_rows_grad)
    gate_rows_grad = gate_rows_grad.astype(jnp.bfloat16)
    up_rows_grad = up_rows_grad.astype(jnp.bfloat16)
    expert_gate_grad = contract_first(rows, gate_rows_grad)[None]
    expert_up_grad = contract_first(rows, up_rows_grad)[None]
    expert_down_grad = contract_first(hidden_rows, rows_out_grad)[None]
    rows_in_grad = (
        contract_last(gate_rows_grad, exp_gate) + contract_last(up_rows_grad, exp_up)
    ).reshape(experts, capacity, width)
    returned_grad = lax.all_to_all(rows_in_grad, "dp", split_axis=0, concat_axis=0, tiled=True)
    routed_grad = jnp.sum(
        returned_grad.reshape(slots, width)[dest].reshape(rows_dev, topk, width), axis=1
    )
    act_two_total = lax.psum(act_two_grad + routed_grad, "tensor")
    dummy_second, second_vjp = jax.vjp(rms_norm, x_mid, gain_two)
    mid_norm_grad, gain_two_grad = second_vjp(act_two_total)
    mid_grad = grad_out + mid_norm_grad
    ffn_sums = (gain_two_grad, common_gate_grad, common_up_grad, common_down_grad)
    attn_grad = mid_grad.astype(jnp.bfloat16)
    output_w_grad = contract_first(attn_grad, mixed)
    mixed_grad = (
        jnp.dot(attn_grad, output_whole, preferred_element_type=jnp.float32)
        .astype(jnp.bfloat16)
        .reshape(rows_dev, heads_dev, HD)
    )
    probs_again = jnp.exp(masked_scores(query_rot, key_rot, causal, scale) - log_total)
    value_grad = jnp.einsum(
        "hqk,qhc->khc",
        probs_again.astype(jnp.bfloat16),
        mixed_grad,
        preferred_element_type=jnp.float32,
    ).astype(jnp.bfloat16)
    prob_grad = jnp.einsum(
        "qhc,khc->hqk", mixed_grad, value_low, preferred_element_type=jnp.float32
    )
    delta = jnp.sum(probs_again * prob_grad, axis=-1, keepdims=True)
    score_grad = (probs_again * (prob_grad - delta)).astype(jnp.bfloat16)
    query_rot_grad = (
        jnp.einsum("hqk,khc->qhc", score_grad, key_rot, preferred_element_type=jnp.float32) * scale
    )
    key_rot_grad = (
        jnp.einsum("hqk,qhc->khc", score_grad, query_rot, preferred_element_type=jnp.float32)
        * scale
    )

    def turn(values):
        return rotate(values, positions)

    dummy_turn, turn_vjp = jax.vjp(turn, query_pre)
    query_grad = turn_vjp(query_rot_grad)[0].reshape(rows_dev, heads_dev * HD).astype(jnp.bfloat16)
    key_grad = turn_vjp(key_rot_grad)[0].reshape(rows_dev, heads_dev * HD).astype(jnp.bfloat16)
    value_flat = value_grad.reshape(rows_dev, heads_dev * HD)
    query_w_grad = contract_first(act_one, query_grad)
    key_w_grad = contract_first(act_one, key_grad)
    value_w_grad = contract_first(act_one, value_flat)
    act_one_grad = (
        contract_last(query_grad, query_whole)
        + contract_last(key_grad, key_whole)
        + contract_last(value_flat, value_whole)
    )
    act_one_total = lax.psum(act_one_grad, "tensor")
    dummy_first, first_vjp = jax.vjp(rms_norm, x_in, gain_one)
    in_norm_grad, gain_one_grad = first_vjp(act_one_total)
    tokens_grad = (mid_grad + in_norm_grad).astype(jnp.bfloat16)
    every = (
        lax.psum_scatter(gain_one_grad, "dp", scatter_dimension=0, tiled=True),
        lax.psum_scatter(query_w_grad, "dp", scatter_dimension=0, tiled=True),
        lax.psum_scatter(key_w_grad, "dp", scatter_dimension=0, tiled=True),
        lax.psum_scatter(value_w_grad, "dp", scatter_dimension=0, tiled=True),
        lax.psum_scatter(output_w_grad, "dp", scatter_dimension=0, tiled=True),
        lax.psum_scatter(ffn_sums[0], "dp", scatter_dimension=0, tiled=True),
        lax.psum_scatter(ffn_sums[1], "dp", scatter_dimension=0, tiled=True),
        lax.psum_scatter(ffn_sums[2], "dp", scatter_dimension=0, tiled=True),
        lax.psum_scatter(ffn_sums[3], "dp", scatter_dimension=0, tiled=True),
    )
    attn_sums = every[:5]
    ffn_sums = every[5:]
    return (
        layer_out,
        tokens_grad,
        attn_sums[0],
        attn_sums[1],
        attn_sums[2],
        attn_sums[3],
        attn_sums[4],
        ffn_sums[0],
        ffn_sums[1],
        ffn_sums[2],
        ffn_sums[3],
        expert_gate_grad,
        expert_up_grad,
        expert_down_grad,
    )


def place():
    d = lax.axis_index("dp"); y = lax.axis_index("tensor")
    c = lax.rem(d, 2); x = lax.rem(lax.div(d, 2), 2); z = lax.div(d, 4)
    return z, x, y, c

def dev(z, x, y, c):
    return ((z * 2 + x) * 2 + c, y)

def blk(z, x, y, c):
    return ((z * 2 + x) * 2 + c) * 2 + y

def greet(z, x, y, c):
    bar = pltpu.get_barrier_semaphore()
    for other in (dev(z, 1 - x, y, c), dev(z, x, 1 - y, c), dev(z, x, y, 1 - c)):
        pl.semaphore_signal(bar, inc=1, device_id=other, device_id_type=MESH)
    @pl.when(z > 0)
    def _():
        pl.semaphore_signal(bar, inc=1, device_id=dev(z - 1, x, y, c), device_id_type=MESH)
    @pl.when(z < 3)
    def _():
        pl.semaphore_signal(bar, inc=1, device_id=dev(z + 1, x, y, c), device_id_type=MESH)
    pl.semaphore_wait(bar, 3 + (z > 0).astype(jnp.int32) + (z < 3).astype(jnp.int32))

def rcopy(src, dst, ssem, rsem, device):
    return pltpu.make_async_remote_copy(src_ref=src, dst_ref=dst, send_sem=ssem, recv_sem=rsem, device_id=device, device_id_type=MESH)

def nearest(z, g):
    one = jnp.where(z == 0, 1, z - 1)
    two = jnp.where(z == 3, 1, jnp.where(z == 2, 3, 2))
    three = jnp.where(z >= 2, 0, 3)
    return jnp.where(g == 0, z, jnp.where(g == 1, one, jnp.where(g == 2, two, three)))

def nt(left, right):
    return lax.dot_general(left, right, (((1,), (1,)), ((), ())), preferred_element_type=jnp.float32)

def nn(left, right):
    return jnp.dot(left, right, preferred_element_type=jnp.float32)

def greet_all(z, x, y, c):
    bar = pltpu.get_barrier_semaphore()
    for other in (dev(z, 1 - x, y, c), dev(z, x, 1 - y, c), dev(z, x, y, 1 - c)):
        pl.semaphore_signal(bar, inc=1, device_id=other, device_id_type=MESH)
    for s in range(4):
        @pl.when(s != z)
        def _(): pl.semaphore_signal(bar, inc=1, device_id=dev(s, x, y, c), device_id_type=MESH)
    pl.semaphore_wait(bar, 6)


def expert_kernel(
    a_in, deh, dy_all, rank_row, rank_col, gate, wg_h, wu_h, wd_h, sgu_h, sdt_h, sd_h,
    total, act_all, rows_o, eh_o, deg_o, deu_o, hs_o, dsgu_o, part, ffn_part,
    wg, wu, wd, sgu, tail, acc, ic, iy0, ix0, ix1, iy1, iz,
    eg, eu, dehb, ehb, degb, deub, sd, dhs, hsb, dsgub, eh2, hs2, ot,
    wsem, usem, ssem, osem, psem, lsem,
    zs, zr, x0s, x0r, x1s, x1r, y0s, y0r, y1s, y1r, cs, cr,
    ls, rcs, rcr, ry0s, ry0r, rx0s, rx0r, rx1s, rx1r, ry1s, ry1r, rzs, rzr,
):
    f32, bf16 = jnp.float32, jnp.bfloat16
    z, x, y, c = place()
    rows, width = a_in.shape
    h = rows // 2
    cap = deh.shape[1]
    toks = 2 * rows
    lo, hi = pl.ds(0, h), pl.ds(h, h)
    part_of = (lo, hi)
    xn, yn, cn = dev(z, 1 - x, y, c), dev(z, x, 1 - y, c), dev(z, x, y, 1 - c)
    greet_all(z, x, y, c)
    mine = blk(z, x, y, c)
    own = pltpu.make_async_copy(a_in, act_all.at[mine], lsem)
    own.start()
    weights = [
        pltpu.make_async_copy(a, b, wsem.at[i])
        for i, (a, b) in enumerate(((wg_h, wg), (wu_h, wu), (wd_h, wd), (sgu_h, sgu), (sdt_h, tail.at[pl.ds(cap, 256 - cap)]), (sd_h, sd)))
    ]
    for w in weights:
        w.start()

    def zcopy(s, up):
        b = act_all.at[blk(s, x, y, c)]
        return rcopy(b, b, zs.at[s, up], zr.at[s], dev(z + 2 * up - 1, x, y, c))

    def half_copy(s, xx, yy, p, send, recv, to):
        b = act_all.at[blk(s, xx, yy, c), part_of[p]]
        return rcopy(b, b, send, recv, to)

    def x0(s): return half_copy(s, x, y, 0, x0s.at[s], x0r.at[s], xn)
    def y1(s): return half_copy(s, x, y, 1, y1s.at[s], y1r.at[s], yn)
    def y0(s, xx): return half_copy(s, xx, y, 0, y0s.at[s, xx], y0r.at[s, xx], yn)
    def x1(s, yy): return half_copy(s, x, yy, 1, x1s.at[s, yy], x1r.at[s, yy], xn)
    def side(s, xx, yy, p):
        i = (s * 2 + xx) * 2 + yy
        return half_copy(s, xx, yy, p, cs.at[i, p], cr.at[i, p], cn)

    def column(s):
        x0(s).start(); y1(s).start(); y0(s, x).start(); x1(s, y).start()
        side(s, x, y, 0).start(); side(s, x, y, 1).start()

    def arrive(g):
        s = nearest(z, g)
        up = (s < z).astype(jnp.int32)
        nxt = z + 2 * up - 1
        zcopy(s, up).wait_recv()
        @pl.when((nxt >= 0) & (nxt <= 3))
        def _(): zcopy(s, up).start()
        column(s)

    def middle(g):
        s = nearest(z, g)
        x0(s).wait_recv()
        y0(s, 1 - x).start(); side(s, 1 - x, y, 0).start()
        y1(s).wait_recv()
        x1(s, 1 - y).start(); side(s, x, 1 - y, 1).start()

    def last_own(g):
        s = nearest(z, g)
        y0(s, x).wait_recv(); side(s, x, 1 - y, 0).start()

    def last_other(g):
        s = nearest(z, g)
        x1(s, y).wait_recv(); side(s, 1 - x, y, 1).start()
        y0(s, 1 - x).wait_recv(); side(s, 1 - x, 1 - y, 0).start()
        x1(s, 1 - y).wait_recv(); side(s, 1 - x, 1 - y, 1).start()

    def spread_cols(j):
        ranks = rank_col[j]
        slot = lax.broadcasted_iota(jnp.int32, (toks, 128), 1)
        one = jnp.where(ranks == slot, 1.0, 0.0)
        two = jnp.where(ranks == slot + 128, 1.0, 0.0)
        return one, two

    def seq_of(u):
        s = nearest(z, u // 2)
        xx = lax.rem(x + lax.rem(u, 2), 2)
        return s, xx

    def stores(u):
        s, xx = seq_of(u)
        out = []
        for k in (0, 1):
            j = (s * 2 + xx) * 2 + k
            r = pl.ds(k * cap, cap)
            out += [
                pltpu.make_async_copy(acc.at[k], rows_o.at[j], ssem.at[k, 0]),
                pltpu.make_async_copy(ehb.at[r], eh_o.at[j], ssem.at[k, 1]),
                pltpu.make_async_copy(degb.at[r], deg_o.at[j], ssem.at[k, 2]),
                pltpu.make_async_copy(deub.at[r], deu_o.at[j], ssem.at[k, 3]),
                pltpu.make_async_copy(hsb.at[k], hs_o.at[j], ssem.at[k, 4]),
                pltpu.make_async_copy(dsgub.at[k], dsgu_o.at[j], ssem.at[k, 5]),
            ]
        return out

    def at(s, xx, yy): return (s * 2 + xx) * 2 + yy
    def keep(u, k):
        s, xx = seq_of(u)
        return pltpu.make_async_copy(acc.at[pl.ds(10 + 2 * k, 2)], part.at[pl.ds(at(s, xx, 0), 2)], ssem.at[k, 6])
    def cross(s, xx, yy, k):
        i = at(s, xx, yy)
        return rcopy(acc.at[10 + 2 * k + yy], ic.at[i], rcs.at[i], rcr.at[i], cn)
    def hand_over(u):
        s, xx = seq_of(u)
        for k in (0, 1):
            @pl.when(c == k)
            def _(): keep(u, k).start()
            @pl.when(c != k)
            def _():
                for yy in (0, 1):
                    cross(s, xx, yy, k).start()
    def handed_over(u):
        s, xx = seq_of(u)
        for k in (0, 1):
            @pl.when(c == k)
            def _(): keep(u, k).wait()
            @pl.when(c != k)
            def _():
                for yy in (0, 1):
                    cross(s, xx, yy, k).wait_send()

    def unit(u):
        s, xx = seq_of(u)
        base = (s * 2 + xx) * 2
        for k in (0, 1):
            pltpu.make_async_copy(deh.at[base + k], dehb.at[pl.ds(k * cap, cap)], usem.at[k, 1]).start()
        for yy in (0, 1):
            for p in (0, 1):
                side(s, xx, yy, p).wait_recv()
        loads = [
            pltpu.make_async_copy(act_all.at[pl.ds(2 * (base + k), 2)], acc.at[pl.ds(4 + 2 * k, 2)], usem.at[k, 0])
            for k in (0, 1)
        ]
        for k in (0, 1):
            loads[k].start()
        @pl.when(u > 0)
        def _():
            for copy in stores(u - 1):
                copy.wait()
            handed_over(u - 1)
        for k in (0, 1):
            loads[k].wait()
            act = acc[4 + 2 * k:6 + 2 * k].reshape(toks, width)
            ranks = rank_row[base + k]
            slot = lax.broadcasted_iota(jnp.int32, (cap, toks), 0)
            pick = jnp.where(ranks == slot, 1.0, 0.0).astype(bf16)
            acc[k] = nn(pick, act).astype(bf16)
            pre = nn(act, sgu[...])
            gp, up = pre[:, :128], pre[:, 128:]
            dh = dhs[base + k]
            sig = jax.nn.sigmoid(gp)
            hsb[k] = (gp * sig * up).astype(bf16)
            dsgub[k, :, 0:128] = (dh * up * sig * (1.0 + gp * (1.0 - sig))).astype(bf16)
            dsgub[k, :, 128:256] = (dh * gp * sig).astype(bf16)
        picked = acc[0:2].reshape(2 * cap, width)
        eg[...] = nt(picked, wg[...])
        eu[...] = nt(picked, wu[...])
        for k in (0, 1):
            pltpu.make_async_copy(deh.at[base + k], dehb.at[pl.ds(k * cap, cap)], usem.at[k, 1]).wait()
        @pl.loop(0, 2 * cap // 32)
        def _(r):
            q = pl.ds(pl.multiple_of(r * 32, 32), 32)
            gp, up, dh = eg[q], eu[q], dehb[q]
            sig = jax.nn.sigmoid(gp)
            silu = gp * sig
            ehb[q] = (silu * up).astype(bf16)
            degb[q] = (dh * up * sig * (1.0 + gp * (1.0 - sig))).astype(bf16)
            deub[q] = (dh * silu).astype(bf16)
        dg, du = degb[...], deub[...]
        for n in range(0, width, 512):
            w = pl.ds(n, 512)
            back = (nn(dg, wg[:, w]) + nn(du, wu[:, w])).astype(bf16)
            acc[8, :, w] = back[:cap]
            acc[9, :, w] = back[cap:]
        for k in (0, 1):
            one, two = spread_cols(base + k)
            left = jnp.concatenate([one, two], axis=1)[:, :cap].astype(bf16)
            for n in range(0, width, 512):
                w = pl.ds(n, 512)
                out = nn(left, acc[8 + k, :, w]) + nt(dsgub[k], sgu[w, :])
                out = out.astype(bf16)
                acc[10 + 2 * k, :, w] = out[:rows]
                acc[11 + 2 * k, :, w] = out[rows:]
        for copy in stores(u):
            copy.start()
        hand_over(u)

    def ry0(s, xx):
        return rcopy(ic.at[at(s, xx, 1 - y), lo], iy0.at[s * 2 + xx], ry0s.at[s, xx], ry0r.at[s, xx], yn)
    def rx1(s, yy):
        return rcopy(ic.at[at(s, 1 - x, yy), hi], ix1.at[s * 2 + yy], rx1s.at[s, yy], rx1r.at[s, yy], xn)
    def rx0(s):
        return rcopy(ic.at[at(s, 1 - x, y), lo], ix0.at[s], rx0s.at[s], rx0r.at[s], xn)
    def ry1(s):
        return rcopy(ic.at[at(s, x, 1 - y), hi], iy1.at[s], ry1s.at[s], ry1r.at[s], yn)
    def rz(s):
        return rcopy(ic.at[at(s, x, y)], iz.at[z], rzs.at[s], rzr.at[z], dev(s, x, y, c))
    def rz_wait(s):
        rcopy(iz.at[s], iz.at[s], rzs.at[s], rzr.at[s], dev(s, x, y, c)).wait_recv()
    def add(i, start, count, src, j):
        @pl.loop(0, count // 16)
        def _(r):
            a = pl.ds(pl.multiple_of(start + r * 16, 16), 16)
            b = pl.ds(pl.multiple_of(r * 16, 16), 16)
            ic[i, a] = ic[i, a] + src[j, b]

    def first(g):
        s = nearest(z, g)
        def load(xx, yy):
            return pltpu.make_async_copy(part.at[at(s, xx, yy)], acc.at[4 + 2 * xx + yy], ls.at[2 * xx + yy])
        for xx in (0, 1):
            for yy in (0, 1):
                load(xx, yy).start()
        for xx in (0, 1):
            for yy in (0, 1):
                load(xx, yy).wait(); cross(s, xx, yy, 0).wait_recv()
                add(at(s, xx, yy), 0, rows, acc, 4 + 2 * xx + yy)
                @pl.when(yy != y)
                def _(): ry0(s, xx).start()
                @pl.when(xx != x)
                def _(): rx1(s, yy).start()

    def second(g):
        s = nearest(z, g)
        ry0(s, 1 - x).wait_recv(); add(at(s, 1 - x, y), 0, h, iy0, s * 2 + 1 - x); rx0(s).start()
        rx1(s, 1 - y).wait_recv(); add(at(s, x, 1 - y), h, h, ix1, s * 2 + 1 - y); ry1(s).start()
        ry0(s, x).wait_recv(); add(at(s, x, y), 0, h, iy0, s * 2 + x)
        rx1(s, y).wait_recv(); add(at(s, x, y), h, h, ix1, s * 2 + y)

    def third(g):
        s = nearest(z, g)
        me = at(s, x, y)
        rx0(s).wait_recv(); add(me, 0, h, ix0, s)
        ry1(s).wait_recv(); add(me, h, h, iy1, s)
        if g > 0:
            rz(s).start()

    own.wait()
    @pl.when(z < 3)
    def _(): zcopy(z, 1).start()
    @pl.when(z > 0)
    def _(): zcopy(z, 0).start()
    column(z)
    def dy_load(j, b):
        return pltpu.make_async_copy(dy_all.at[pl.ds(2 * j, 2)], acc.at[pl.ds(2 + 12 * b, 2)], usem.at[b, 2])
    dy_load(0, 0).start()
    for w in weights:
        w.wait()
    @pl.loop(0, 8)
    def _(i):
        for b in (0, 1):
            j = 2 * i + b
            @pl.when(j < 15)
            def _(): dy_load(j + 1, 1 - b).start()
            dy_load(j, b).wait()
            dhs[j] = nn(acc[2 + 12 * b:4 + 12 * b].reshape(toks, width), sd[...])

    @pl.loop(0, 8)
    def _(u):
        @pl.when(u == 0)
        def _():
            middle(0); last_own(0); arrive(1)
        @pl.when(u == 1)
        def _():
            last_other(0); arrive(2); middle(1)
        @pl.when(u == 2)
        def _():
            arrive(3); last_own(1); middle(2)
        @pl.when(u == 3)
        def _():
            last_other(1); middle(3); first(0)
        @pl.when(u == 4)
        def _():
            last_own(2)
        @pl.when(u == 5)
        def _():
            last_other(2); first(1); second(0)
        @pl.when(u == 6)
        def _():
            last_own(3)
        @pl.when(u == 7)
        def _():
            last_other(3); first(2); second(1); third(0)
        unit(u)

    for copy in stores(7):
        copy.wait()
    handed_over(7)

    def out_loads(j, b):
        return [
            pltpu.make_async_copy(eh_o.at[j], eh2.at[b], osem.at[b, 0]),
            pltpu.make_async_copy(hs_o.at[j], hs2.at[b], osem.at[b, 1]),
        ]
    def out_store(j, b):
        return pltpu.make_async_copy(ot.at[b], ffn_part.at[pl.ds(2 * j, 2)], psem.at[b])

    def forward_out(j):
        b = lax.rem(j, 2)
        @pl.when(j < 15)
        def _():
            for copy in out_loads(j + 1, 1 - b):
                copy.start()
        for copy in out_loads(j, b):
            copy.wait()
        @pl.when(j >= 2)
        def _(): out_store(j - 2, b).wait()
        weight = gate[j]
        for n in range(0, width, 512):
            w = pl.ds(n, 512)
            tail[0:cap, w] = (nn(eh2[b], wd[:, w]) * weight).astype(bf16)
        one, two = spread_cols(j)
        left = jnp.concatenate([one, two + hs2[b].astype(f32)], axis=1).astype(bf16)
        for n in range(0, width, 512):
            w = pl.ds(n, 512)
            out = nn(left, tail[:, w]).astype(bf16)
            ot[b, 0, :, w] = out[:rows]
            ot[b, 1, :, w] = out[rows:]
        out_store(j, b).start()

    for copy in out_loads(0, 0):
        copy.start()

    first(3)
    second(2); third(1)
    @pl.loop(0, 16)
    def _(j):
        @pl.when(j == 4)
        def _():
            second(3); third(2)
        @pl.when(j == 8)
        def _(): third(3)
        forward_out(j)
    me = at(z, x, y)
    for g in (1, 2, 3):
        rz_wait(nearest(z, g))
    @pl.loop(0, rows // 16)
    def _(r):
        q = pl.ds(pl.multiple_of(r * 16, 16), 16)
        out = ic[me, q].astype(f32)
        for g in (1, 2, 3):
            out = out + iz[nearest(z, g), q].astype(f32)
        total[q] = out
    out_store(14, 0).wait()
    out_store(15, 1).wait()

    for s in range(4):
        @pl.when((z < 3) & (s <= z))
        def _(): zcopy(s, 1).wait_send()
        @pl.when((z > 0) & (s >= z))
        def _(): zcopy(s, 0).wait_send()
        x0(s).wait_send(); y1(s).wait_send()
        rx0(s).wait_send(); ry1(s).wait_send()
        for q in (0, 1):
            y0(s, q).wait_send(); x1(s, q).wait_send()
            ry0(s, q).wait_send(); rx1(s, q).wait_send()
            for r in (0, 1):
                for p in (0, 1):
                    side(s, q, r, p).wait_send()
        @pl.when(s != z)
        def _():
            rz(s).wait_send()

def expert_layer(act, deh, dy_all, rank_row, rank_col, gate, wg, wu, wd, sgu, sdt, sd, cid):
    rows, width = act.shape
    cap, hidden = deh.shape[1:]
    h = rows // 2
    f32, bf16 = jnp.float32, jnp.bfloat16
    D = pltpu.SemaphoreType.DMA
    S = jax.ShapeDtypeStruct
    any_ = pl.BlockSpec(memory_space=pl.ANY)
    vm = pl.BlockSpec(memory_space=pltpu.VMEM)
    V = lambda *shape, t=bf16: pltpu.VMEM(shape, t)
    return pl.pallas_call(
        expert_kernel,
        out_shape=[
            S((rows, width), f32), S((32, rows, width), bf16), S((16, cap, width), bf16),
            S((16, cap, hidden), bf16), S((16, cap, hidden), bf16), S((16, cap, hidden), bf16),
            S((16, 2 * rows, 128), bf16), S((16, 2 * rows, 256), bf16),
            S((16, rows, width), bf16), S((32, rows, width), bf16),
        ],
        in_specs=[vm, any_, any_, vm, vm, vm] + [any_] * 6,
        out_specs=[vm] + [any_] * 9,
        scratch_shapes=[
            V(*wg.shape), V(*wu.shape), V(*wd.shape), V(*sgu.shape), V(256, width),
            V(16, rows, width), V(16, rows, width), V(8, h, width), V(4, h, width), V(8, h, width), V(4, h, width),
            V(4, rows, width),
            V(2 * cap, hidden, t=f32), V(2 * cap, hidden, t=f32), V(2 * cap, hidden, t=f32),
            V(2 * cap, hidden), V(2 * cap, hidden), V(2 * cap, hidden),
            V(*sd.shape), V(16, 2 * rows, 128, t=f32), V(2, 2 * rows, 128), V(2, 2 * rows, 256),
            V(2, cap, hidden), V(2, 2 * rows, 128), V(2, 2, rows, width),
            D((6,)), D((2, 3)), D((2, 7)), D((2, 2)), D((2,)), D,
            D((4, 2)), D((4,)), D((4,)), D((4,)), D((4, 2)), D((4, 2)), D((4, 2)), D((4, 2)), D((4,)), D((4,)), D((16, 2)), D((16, 2)),
            D((4,)), D((16,)), D((16,)), D((4, 2)), D((4, 2)), D((4,)), D((4,)), D((4, 2)), D((4, 2)), D((4,)), D((4,)),
            D((4,)), D((4,)),
        ],
        compiler_params=pltpu.CompilerParams(collective_id=cid, has_side_effects=True, vmem_limit_bytes=63 << 20),
        name="expert_layer",
    )(act, deh, dy_all, rank_row, rank_col, gate, wg, wu, wd, sgu, sdt, sd)


def norm_back(values, gain, grad):
    width = values.shape[1]
    inv = lax.rsqrt(jnp.sum(values * values, axis=1, keepdims=True) * (1.0 / width) + EPS)
    scaled = grad * gain
    inner = jnp.sum(values * scaled, axis=1, keepdims=True) * (1.0 / width)
    normed = values * inv
    return inv * (scaled - normed * (inv * inner)), grad * normed

def attention_back_kernel(
    part, grad2, x_mid, dy, x_in, gain1, gain2, wq_h, wk_h, wv_h, wo_h, qr, kr, vr, cosine, sine,
    out_full, tok_full, dattn, dq, dk, dv, g1, g2,
    ic, tmp, iy0, ix0, ix1, iy1, izu, izd, wa, wb, wc, dmix, dx2, da1, send1, recv1,
    wsem, ysem, ls, rcs, rcr, ry0s, ry0r, rx0s, rx0r, rx1s, rx1r, ry1s, ry1r, zus, zur, zds, zdr,
):
    f32, bf16 = jnp.float32, jnp.bfloat16
    z, x, y, c = place()
    rows, width = x_mid.shape
    h = rows // 2
    toks = 2 * rows
    heads = qr.shape[1] // HD
    lo, hi = pl.ds(0, h), pl.ds(h, h)
    xn, yn, cn = dev(z, 1 - x, y, c), dev(z, x, 1 - y, c), dev(z, x, y, 1 - c)
    greet(z, x, y, c)

    def at(s, xx, yy): return (s * 2 + xx) * 2 + yy
    def load(s, xx, yy):
        return pltpu.make_async_copy(part.at[blk(s, xx, yy, c)], tmp.at[xx * 2 + yy], ls.at[xx * 2 + yy])
    def cross(s, xx, yy):
        i = at(s, xx, yy)
        return rcopy(part.at[blk(s, xx, yy, 1 - c)], ic.at[i], rcs.at[i], rcr.at[i], cn)
    def ry0(s, xx):
        return rcopy(ic.at[at(s, xx, 1 - y), lo], iy0.at[s * 2 + xx], ry0s.at[s, xx], ry0r.at[s, xx], yn)
    def rx1(s, yy):
        return rcopy(ic.at[at(s, 1 - x, yy), hi], ix1.at[s * 2 + yy], rx1s.at[s, yy], rx1r.at[s, yy], xn)
    def rx0(s):
        return rcopy(ic.at[at(s, 1 - x, y), lo], ix0.at[s], rx0s.at[s], rx0r.at[s], xn)
    def ry1(s):
        return rcopy(ic.at[at(s, x, 1 - y), hi], iy1.at[s], ry1s.at[s], ry1r.at[s], yn)
    def zu(s):
        return rcopy(ic.at[at(s, x, y)], izu.at[s], zus.at[s], zur.at[s], dev(z + 1, x, y, c))
    def zd(s):
        return rcopy(ic.at[at(s, x, y)], izd.at[s], zds.at[s], zdr.at[s], dev(z - 1, x, y, c))
    def add(i, start, count, src, j):
        @pl.loop(0, count // 16)
        def _(r):
            a = pl.ds(pl.multiple_of(start + r * 16, 16), 16)
            b = pl.ds(pl.multiple_of(r * 16, 16), 16)
            ic[i, a] = ic[i, a] + src[j, b]

    four = [(xx, yy) for xx in (0, 1) for yy in (0, 1)]

    def first(g):
        s = nearest(z, g)
        for xx, yy in four:
            load(s, xx, yy).wait(); cross(s, xx, yy).wait_recv()
            add(at(s, xx, yy), 0, rows, tmp, xx * 2 + yy)
            @pl.when(yy != y)
            def _(): ry0(s, xx).start()
            @pl.when(xx != x)
            def _(): rx1(s, yy).start()
        if g > 0:
            for xx, yy in four:
                load(nearest(z, g - 1), xx, yy).start()

    def second(g):
        s = nearest(z, g)
        ry0(s, 1 - x).wait_recv(); add(at(s, 1 - x, y), 0, h, iy0, s * 2 + 1 - x); rx0(s).start()
        rx1(s, 1 - y).wait_recv(); add(at(s, x, 1 - y), h, h, ix1, s * 2 + 1 - y); ry1(s).start()
        ry0(s, x).wait_recv(); add(at(s, x, y), 0, h, iy0, s * 2 + x)
        rx1(s, y).wait_recv(); add(at(s, x, y), h, h, ix1, s * 2 + y)

    def third(g):
        s = nearest(z, g)
        me = at(s, x, y)
        rx0(s).wait_recv(); add(me, 0, h, ix0, s)
        ry1(s).wait_recv(); add(me, h, h, iy1, s)
        @pl.when((s >= z) & (z > 0))
        def _():
            zu(s).wait_recv(); add(me, 0, rows, izu, s)
        @pl.when((s <= z) & (z < 3))
        def _():
            zd(s).wait_recv(); add(me, 0, rows, izd, s)
        @pl.when(s > z)
        def _(): zu(s).start()
        @pl.when(s < z)
        def _(): zd(s).start()

    for g in (3, 2, 1, 0):
        s = nearest(z, g)
        for xx, yy in four:
            cross(s, xx, yy).start()
            if g == 3:
                load(s, xx, yy).start()
    w_out = pltpu.make_async_copy(wo_h, wa, wsem.at[0])
    w_query = pltpu.make_async_copy(wq_h, wb, wsem.at[1])
    w_key = pltpu.make_async_copy(wk_h, wc, wsem.at[2])
    w_value = pltpu.make_async_copy(wv_h, wa, wsem.at[3])
    w_out.start(); w_query.start(); w_key.start()

    g1[...] = jnp.zeros_like(g1)
    g2[...] = jnp.zeros_like(g2)
    @pl.loop(0, rows // 16)
    def _(r):
        q = pl.ds(pl.multiple_of(r * 16, 16), 16)
        back, terms = norm_back(x_mid[q], gain2[...], grad2[q])
        back = back + dy[q].astype(f32)
        dx2[q] = back
        dattn[y, q] = back.astype(bf16)
        g2[...] += jnp.sum(terms, axis=0, keepdims=True)
    attn_swap = rcopy(dattn.at[y], dattn.at[y], ysem.at[0], ysem.at[1], yn)
    attn_swap.start()
    first(3)
    first(2)
    w_out.wait()
    attn_swap.wait_recv()
    full = dattn[...].reshape(toks, width)
    dmix[...] = nn(full, wa[...]).astype(bf16)
    w_value.start()

    scale = HD ** (-0.5)
    def turn_back(values):
        return values * cosine[...] - pltpu.roll(values, HD // 2, 1) * sine[...]
    @pl.loop(0, heads)
    def _(n):
        @pl.when(n == 2)
        def _():
            second(3); first(1)
        @pl.when(n == 5)
        def _():
            second(2); third(3); first(0)
        w = pl.ds(pl.multiple_of(n * HD, HD), HD)
        qh, kh, vh, doh = qr[:, w], kr[:, w], vr[:, w], dmix[:, w]
        scores = nt(qh, kh) * scale
        ahead = lax.broadcasted_iota(jnp.int32, (toks, toks), 0) >= lax.broadcasted_iota(jnp.int32, (toks, toks), 1)
        scores = jnp.where(ahead, scores, -1e30)
        expo = jnp.exp(scores - jnp.max(scores, axis=1, keepdims=True))
        probs = expo * (1.0 / jnp.sum(expo, axis=1, keepdims=True))
        dv[:, w] = lax.dot_general(
            probs.astype(bf16), doh, (((0,), (0,)), ((), ())), preferred_element_type=f32
        ).astype(bf16)
        dprob = nt(doh, vh)
        delta = jnp.sum(probs * dprob, axis=1, keepdims=True)
        ds = (probs * (dprob - delta)).astype(bf16)
        dq[:, w] = turn_back(nn(ds, kh) * scale).astype(bf16)
        dkr = lax.dot_general(ds, qh, (((0,), (0,)), ((), ())), preferred_element_type=f32)
        dk[:, w] = turn_back(dkr * scale).astype(bf16)

    w_query.wait(); w_key.wait(); w_value.wait()
    for n in range(0, width, 512):
        w = pl.ds(n, 512)
        out = nt(dq[...], wb[w, :]) + nt(dk[...], wc[w, :]) + nt(dv[...], wa[w, :])
        da1[0, :, w] = out[:rows]
        da1[1, :, w] = out[rows:]
    @pl.loop(0, rows // 16)
    def _(r):
        q = pl.ds(pl.multiple_of(r * 16, 16), 16)
        send1[q] = da1[1 - y, q].astype(bf16)
    da1_swap = rcopy(send1, recv1, ysem.at[2], ysem.at[3], yn)
    da1_swap.start()
    second(1); third(2)
    da1_swap.wait_recv()
    @pl.loop(0, rows // 16)
    def _(r):
        q = pl.ds(pl.multiple_of(r * 16, 16), 16)
        back, terms = norm_back(x_in[q].astype(f32), gain1[...], da1[y, q] + recv1[q].astype(f32))
        tok_full[y, q] = (back + dx2[q]).astype(bf16)
        g1[...] += jnp.sum(terms, axis=0, keepdims=True)
    tok_swap = rcopy(tok_full.at[y], tok_full.at[y], ysem.at[4], ysem.at[5], yn)
    tok_swap.start()
    second(0); third(1); third(0)
    @pl.loop(0, rows // 16)
    def _(r):
        q = pl.ds(pl.multiple_of(r * 16, 16), 16)
        out_full[y, q] = (x_mid[q] + ic[at(z, x, y), q].astype(f32)).astype(bf16)
    out_swap = rcopy(out_full.at[y], out_full.at[y], ysem.at[6], ysem.at[7], yn)
    out_swap.start()
    tok_swap.wait_recv()
    out_swap.wait_recv()
    for swap in (attn_swap, da1_swap, tok_swap, out_swap):
        swap.wait_send()
    for s in range(4):
        rx0(s).wait_send(); ry1(s).wait_send()
        for q in (0, 1):
            ry0(s, q).wait_send(); rx1(s, q).wait_send()
            for r in (0, 1):
                cross(s, q, r).wait_send()
        @pl.when(s > z)
        def _(): zu(s).wait_send()
        @pl.when(s < z)
        def _(): zd(s).wait_send()

def attention_back(part, grad2, x_mid, dy, x_in, gain1, gain2, weights, qr, kr, vr, cosine, sine, cid):
    rows, width = x_mid.shape
    toks, hw = qr.shape
    h = rows // 2
    f32, bf16 = jnp.float32, jnp.bfloat16
    D = pltpu.SemaphoreType.DMA
    S = jax.ShapeDtypeStruct
    any_ = pl.BlockSpec(memory_space=pl.ANY)
    vm = pl.BlockSpec(memory_space=pltpu.VMEM)
    V = lambda *shape, t=bf16: pltpu.VMEM(shape, t)
    return pl.pallas_call(
        attention_back_kernel,
        out_shape=[
            S((2, rows, width), bf16), S((2, rows, width), bf16), S((2, rows, width), bf16),
            S((toks, hw), bf16), S((toks, hw), bf16), S((toks, hw), bf16), S((1, width), f32), S((1, width), f32),
        ],
        in_specs=[any_] + [vm] * 6 + [any_] * 4 + [vm] * 5,
        out_specs=[vm] * 8,
        scratch_shapes=[
            V(16, rows, width), V(4, rows, width), V(8, h, width), V(4, h, width), V(8, h, width), V(4, h, width),
            V(4, rows, width), V(4, rows, width),
            V(width, hw), V(width, hw), V(width, hw), V(toks, hw), V(rows, width, t=f32), V(2, rows, width, t=f32),
            V(rows, width), V(rows, width),
            D((4,)), D((8,)), D((4,)), D((16,)), D((16,)), D((4, 2)), D((4, 2)), D((4,)), D((4,)), D((4, 2)), D((4, 2)), D((4,)), D((4,)),
            D((4,)), D((4,)), D((4,)), D((4,)),
        ],
        compiler_params=pltpu.CompilerParams(collective_id=cid, has_side_effects=True, vmem_limit_bytes=63 << 20),
        name="attention_back",
    )(part, grad2, x_mid, dy, x_in, gain1, gain2, *weights, qr, kr, vr, cosine, sine)

def weight_grad_kernel(
    a1, dattn, dq, dk, dv, mixed, gains,
    oq, ok, ov, oo, og,
    acc, ic, ix, izu, izd, gc, gx, gu, gd, gy, gbuf,
    cs, cr, xs, xr, zus, zur, zds, zdr, gss, gsr,
):
    f32, bf16 = jnp.float32, jnp.bfloat16
    z, x, y, c = place()
    xn, yn, cn = dev(z, 1 - x, y, c), dev(z, x, 1 - y, c), dev(z, x, y, 1 - c)
    n, depth = 4, acc.shape[2]
    outs = (oq, ok, ov, oo)
    greet(z, x, y, c)
    def pos(s, xx, cc): return (s * 2 + xx) * 2 + cc
    def wc(a, s, xx):
        i = s * 2 + xx
        return rcopy(acc.at[a, pos(s, xx, 1 - c)], ic.at[a, i], cs.at[a, i], cr.at[a, i], cn)
    def wx(a, s):
        return rcopy(acc.at[a, pos(s, 1 - x, c)], ix.at[a, s], xs.at[a, s], xr.at[a, s], xn)
    def zu(a, s):
        return rcopy(acc.at[a, pos(s, x, c)], izu.at[a, s], zus.at[a, s], zur.at[a, s], dev(z + 1, x, y, c))
    def zd(a, s):
        return rcopy(acc.at[a, pos(s, x, c)], izd.at[a, s], zds.at[a, s], zdr.at[a, s], dev(z - 1, x, y, c))
    def add(a, i, src, j):
        @pl.loop(0, depth // 16)
        def _(r):
            b = pl.ds(pl.multiple_of(r * 16, 16), 16)
            acc[a, i, b] = acc[a, i, b] + src[a, j, b]
    def make(g):
        s = nearest(z, g)
        w = pl.ds(pl.multiple_of(s * 4 * depth, 4 * depth), 4 * depth)
        for a, (left, right) in ((3, (dattn, mixed)), (0, (a1, dq)), (1, (a1, dk)), (2, (a1, dv))):
            out = lax.dot_general(left[:, w], right[...], (((0,), (0,)), ((), ())), preferred_element_type=f32).astype(bf16)
            for i in range(4):
                acc[a, s * 4 + i] = out[i * depth:(i + 1) * depth]
            for q in (0, 1):
                wc(a, s, q).start()
    def first(g):
        s = nearest(z, g)
        for a in (3, 0, 1, 2):
            for q in (0, 1):
                wc(a, s, q).wait_recv()
                add(a, pos(s, q, c), ic, s * 2 + q)
            wx(a, s).start()
    def second(g):
        s = nearest(z, g)
        for a in (3, 0, 1, 2):
            wx(a, s).wait_recv(); add(a, pos(s, x, c), ix, s)
            @pl.when((s >= z) & (z > 0))
            def _():
                zu(a, s).wait_recv(); add(a, pos(s, x, c), izu, s)
            @pl.when((s <= z) & (z < 3))
            def _():
                zd(a, s).wait_recv(); add(a, pos(s, x, c), izd, s)
            @pl.when(s > z)
            def _(): zu(a, s).start()
            @pl.when(s < z)
            def _(): zd(a, s).start()
    g_c = rcopy(gains.at[1 - c], gc, gss.at[0], gsr.at[0], cn)
    g_x = rcopy(gbuf.at[1 - x], gx, gss.at[1], gsr.at[1], xn)
    g_u = rcopy(gu.at[1], gu.at[0], gss.at[2], gsr.at[2], dev(z + 1, x, y, c))
    g_d = rcopy(gd.at[1], gd.at[0], gss.at[3], gsr.at[3], dev(z - 1, x, y, c))
    g_y = rcopy(gy.at[0], gy.at[1], gss.at[4], gsr.at[4], yn)
    g_c.start()
    make(3); make(2)
    g_c.wait_recv()
    gbuf[...] = gains[c] + gc[...]
    g_x.start()
    first(3); make(1); first(2); make(0)
    g_x.wait_recv()
    gbuf[x] = gbuf[x] + gx[...]
    second(3)
    gu[1] = gbuf[x]
    gd[1] = gbuf[x]
    @pl.when(z > 0)
    def _():
        g_u.wait_recv()
        gu[1] = gu[1] + gu[0]
    @pl.when(z < 3)
    def _():
        g_u.start()
    first(1)
    second(2)
    @pl.when(z < 3)
    def _():
        g_d.wait_recv()
        gd[1] = gd[1] + gd[0]
    @pl.when(z > 0)
    def _():
        g_d.start()
    first(0)
    second(1)
    gy[0] = gu[1, z] + gd[1, z] - gbuf[x, z]
    g_y.start()
    second(0)
    for a in range(n):
        outs[a][...] = acc[a, pos(z, x, c)].astype(f32)
    g_y.wait_recv()
    og[...] = gy[0] + gy[1]
    g_c.wait_send(); g_x.wait_send(); g_y.wait_send()
    @pl.when(z < 3)
    def _(): g_u.wait_send()
    @pl.when(z > 0)
    def _(): g_d.wait_send()
    for s in range(4):
        for a in range(n):
            for q in (0, 1): wc(a, s, q).wait_send()
            wx(a, s).wait_send()
            @pl.when(s > z)
            def _(): zu(a, s).wait_send()
            @pl.when(s < z)
            def _(): zd(a, s).wait_send()

def weight_grads(a1, dattn, dq, dk, dv, mixed, gains, cid):
    toks, width = a1.shape
    hw = dq.shape[1]
    depth = width // 16
    f32, bf16 = jnp.float32, jnp.bfloat16
    D = pltpu.SemaphoreType.DMA
    S = jax.ShapeDtypeStruct
    vm = pl.BlockSpec(memory_space=pltpu.VMEM)
    V = lambda *shape, t=bf16: pltpu.VMEM(shape, t)
    return pl.pallas_call(
        weight_grad_kernel,
        out_shape=[S((depth, hw), f32)] * 4 + [S((8, 128), f32)],
        in_specs=[vm] * 7,
        out_specs=[vm] * 5,
        scratch_shapes=[
            V(4, 16, depth, hw), V(4, 8, depth, hw), V(4, 4, depth, hw), V(4, 4, depth, hw), V(4, 4, depth, hw),
            V(2, 4, 8, 128, t=f32), V(4, 8, 128, t=f32), V(2, 4, 8, 128, t=f32), V(2, 4, 8, 128, t=f32), V(2, 8, 128, t=f32), V(2, 4, 8, 128, t=f32),
            D((4, 8)), D((4, 8)), D((4, 4)), D((4, 4)), D((4, 4)), D((4, 4)), D((4, 4)), D((4, 4)), D((5,)), D((5,)),
        ],
        compiler_params=pltpu.CompilerParams(collective_id=cid, has_side_effects=True, vmem_limit_bytes=60 << 20),
        name="weight_grads",
    )(a1, dattn, dq, dk, dv, mixed, gains)


def expert_grads_kernel(deg, deu, eh, dsgu, hs, rows, deo, act, dy, e_gate, e_up, e_down, gu, down):
    def tn(left, right):
        return lax.dot_general(left, right, (((0,), (0,)), ((), ())), preferred_element_type=jnp.float32)
    gu[...] = tn(act[...], dsgu[...]).astype(gu.dtype)
    down[...] = tn(dy[...], hs[...]).astype(down.dtype)
    e_gate[...] = tn(deg[...], rows[...])
    e_up[...] = tn(deu[...], rows[...])
    e_down[...] = tn(eh[...], deo[...])


def expert_grads(deg, deu, eh, dsgu, hs, rows, deo, act, dy):
    width = rows.shape[1]
    S = jax.ShapeDtypeStruct
    whole = lambda a: pl.BlockSpec(a.shape, lambda i: (0, 0), pipeline_mode=pl.Buffered(1))
    tile = lambda n: pl.BlockSpec((n, 256), lambda i: (0, i))
    hidden = deg.shape[1]
    return pl.pallas_call(
        expert_grads_kernel,
        grid=(width // 256,),
        out_shape=[S((hidden, width), jnp.float32)] * 3 + [S((width, 256), jnp.bfloat16), S((width, 128), jnp.bfloat16)],
        in_specs=[whole(a) for a in (deg, deu, eh, dsgu, hs)] + [tile(a.shape[0]) for a in (rows, deo, act, dy)],
        out_specs=[tile(hidden)] * 3 + [pl.BlockSpec((256, n), lambda i: (i, 0)) for n in (256, 128)],
        compiler_params=pltpu.CompilerParams(vmem_limit_bytes=60 << 20),
        name="expert_grads",
    )(deg, deu, eh, dsgu, hs, rows, deo, act, dy)


def attention_kernel(
    x_in, wq_in, wk_in, wv_in, wo_in, gain_in, table_in, dy_in, wd_h, cosine, sine,
    wq_o, wk_o, wv_o, wo_o, dy_all, act1, qr, kr, vr, mixed, x_mid, act2, grow, rank_row, rank_col, gate, deo_o, deh_o,
    gland, tland, inv, wbuf, wob, wd, qa, ka, va, own_attn, send, recv, gm, dyt, deo, deh,
    wsem, lsem, dsem, ssem, ysem, zs, zr, xs, xr, cs, cr, gzs, gzr, gxs, gxr, gys, gyr, gcs, gcr,
):
    f32, bf16 = jnp.float32, jnp.bfloat16
    z, x, y, c = place()
    toks, width = x_in.shape
    rows = toks // 2
    depth, hw = wq_in.shape
    cap, hidden = deh_o.shape[1:]
    xn, yn, cn = dev(z, 1 - x, y, c), dev(z, x, 1 - y, c), dev(z, x, y, 1 - c)
    expert = (z * 2 + x) * 2 + c
    greet(z, x, y, c)
    ins = (gain_in, table_in, wq_in, wk_in, wv_in, wo_in)
    outs = (gland, tland, wq_o, wk_o, wv_o, wo_o)
    n = len(outs)
    def pos(s, xx, cc): return (s * 2 + xx) * 2 + cc
    owns = [pltpu.make_async_copy(ins[a], outs[a].at[expert], lsem.at[a]) for a in range(n)]
    owns.append(pltpu.make_async_copy(dy_in, dy_all.at[blk(z, x, y, c)], lsem.at[n]))
    for o in owns:
        o.start()
    w_down = pltpu.make_async_copy(wd_h, wd, wsem.at[3])
    w_down.start()

    def wz(a, s, up):
        r = outs[a].at[pos(s, x, c)]
        return rcopy(r, r, zs.at[a, s, up], zr.at[a, s], dev(z + 2 * up - 1, x, y, c))
    def wx(a, s):
        r = outs[a].at[pos(s, x, c)]
        return rcopy(r, r, xs.at[a, s], xr.at[a, s], xn)
    def wc(a, s, xx):
        r = outs[a].at[pos(s, xx, c)]
        return rcopy(r, r, cs.at[a, s * 2 + xx], cr.at[a, s * 2 + xx], cn)
    def gz(s, up):
        r = dy_all.at[blk(s, x, y, c)]
        return rcopy(r, r, gzs.at[s, up], gzr.at[s], dev(z + 2 * up - 1, x, y, c))
    def gx(s):
        r = dy_all.at[blk(s, x, y, c)]
        return rcopy(r, r, gxs.at[s], gxr.at[s], xn)
    def gy(s, xx):
        r = dy_all.at[blk(s, xx, y, c)]
        return rcopy(r, r, gys.at[s, xx], gyr.at[s, xx], yn)
    def gc(s, xx, yy):
        r = dy_all.at[blk(s, xx, yy, c)]
        return rcopy(r, r, gcs.at[s * 2 + xx, yy], gcr.at[s * 2 + xx, yy], cn)

    def column(s):
        for a in range(n):
            wx(a, s).start(); wc(a, s, x).start()
    def middle(g):
        s = nearest(z, g)
        for a in range(n):
            wx(a, s).wait_recv(); wc(a, s, 1 - x).start()
    def gcolumn(s):
        gx(s).start(); gy(s, x).start(); gc(s, x, y).start()
    def gmiddle(g):
        s = nearest(z, g)
        gx(s).wait_recv(); gy(s, 1 - x).start(); gc(s, 1 - x, y).start()
    def glast(g):
        s = nearest(z, g)
        for q in (0, 1):
            gy(s, q).wait_recv(); gc(s, q, 1 - y).start()
    def launch(fn):
        @pl.when(z < 3)
        def _(): fn(1)
        @pl.when(z > 0)
        def _(): fn(0)
    def towards(g):
        s = nearest(z, g)
        up = (s < z).astype(jnp.int32)
        nxt = z + 2 * up - 1
        return s, up, (nxt >= 0) & (nxt <= 3)
    def arrive(g):
        s, up, more = towards(g)
        for a in range(n):
            wz(a, s, up).wait_recv()
            @pl.when(more)
            def _(): wz(a, s, up).start()
        column(s)
    def garrive(g):
        s, up, more = towards(g)
        gz(s, up).wait_recv()
        @pl.when(more)
        def _(): gz(s, up).start()
        gcolumn(s)

    def project(g):
        s = nearest(z, g)
        for a in range(n):
            for q in (0, 1):
                wc(a, s, q).wait_recv()
        loads = [
            pltpu.make_async_copy(w.at[pl.ds(4 * s, 4)], wbuf.at[i], wsem.at[i])
            for i, w in enumerate((wq_o, wk_o, wv_o))
        ]
        for l in loads:
            l.start()
        for i in range(4):
            at = pl.ds(pl.multiple_of((4 * s + i) * depth, depth), depth)
            two = gland[4 * s + i][0:8].astype(f32)
            grow[:, at] = two
        w = pl.ds(pl.multiple_of(4 * s * depth, 4 * depth), 4 * depth)
        a1 = (x_in[:, w].astype(f32) * inv[...] * grow[0:1, w]).astype(bf16)
        act1[:, w] = a1
        for i, acc in enumerate((qa, ka, va)):
            loads[i].wait()
            out = nn(a1, wbuf[i].reshape(4 * depth, hw))
            if g == 0:
                acc[...] = out
            else:
                acc[...] += out

    def ranks_of(g):
        s = nearest(z, g)
        for i in range(4):
            gm[i:i + 1, :] = tland[4 * s + i, pl.ds(expert, 1), :]
        member = (gm[...] > 0.0).astype(f32).astype(bf16)
        one = lax.broadcasted_iota(jnp.int32, (toks, toks), 0)
        two = lax.broadcasted_iota(jnp.int32, (toks, toks), 1)
        upper = jnp.where(one <= two, 1.0, 0.0).astype(bf16)
        lower = jnp.where(one >= two, 1.0, 0.0).astype(bf16)
        same = jnp.where(one == two, 1.0, 0.0).astype(bf16)
        by_row = jnp.where(gm[...] > 0.0, nn(member, upper) - 1.0, -1.0).astype(jnp.int32)
        by_col = jnp.where(nt(same, member) > 0.5, nt(lower, member) - 1.0, -1.0).astype(jnp.int32)
        for i in range(4):
            rank_row[4 * s + i] = by_row[i:i + 1]
            rank_col[4 * s + i] = by_col[:, i:i + 1]
    def stores(g, xx):
        s = nearest(z, g)
        base = (s * 2 + xx) * 2
        out = []
        for k in (0, 1):
            out.append(pltpu.make_async_copy(deo.at[k], deo_o.at[base + k], ssem.at[k, 0]))
            out.append(pltpu.make_async_copy(deh.at[pl.ds(k * cap, cap)], deh_o.at[base + k], ssem.at[k, 1]))
        return out
    def hidden_grads(g):
        s = nearest(z, g)
        ranks_of(g)
        for xx in (0, 1):
            for yy in (0, 1):
                gc(s, xx, yy).wait_recv()
        @pl.loop(0, 2)
        def _(xx):
            base = (s * 2 + xx) * 2
            loads = [pltpu.make_async_copy(dy_all.at[pl.ds(2 * (base + k), 2)], dyt.at[k], dsem.at[k]) for k in (0, 1)]
            for l in loads:
                l.start()
            if g > 0:
                @pl.when(xx == 0)
                def _():
                    for copy in stores(g - 1, 1):
                        copy.wait()
            @pl.when(xx == 1)
            def _():
                for copy in stores(g, 0):
                    copy.wait()
            for k in (0, 1):
                loads[k].wait()
                hit = rank_row[base + k] == lax.broadcasted_iota(jnp.int32, (cap, toks), 0)
                weight = jnp.sum(jnp.where(hit, tland[base + k, pl.ds(expert, 1), :], 0.0), axis=1, keepdims=True)
                gate[base + k] = weight
                pick = jnp.where(hit, 1.0, 0.0).astype(bf16)
                grads = dyt[k].reshape(toks, width)
                for m in range(0, width, 512):
                    deo[k, :, m:m + 512] = (nn(pick, grads[:, m:m + 512]) * weight).astype(bf16)
            deh[...] = nt(deo[...].reshape(2 * cap, width), wd[...])
            for copy in stores(g, xx):
                copy.start()

    for o in owns:
        o.wait()
    launch(lambda up: [wz(a, z, up).start() for a in range(n)])
    column(z)
    launch(lambda up: gz(z, up).start())
    gcolumn(z)
    @pl.loop(0, toks // 16)
    def _(r):
        q = pl.ds(pl.multiple_of(r * 16, 16), 16)
        v = x_in[q].astype(f32)
        inv[q] = lax.rsqrt(jnp.sum(v * v, axis=1, keepdims=True) * (1.0 / width) + EPS)
    gm[...] = jnp.zeros_like(gm)
    w_down.wait()
    arrive(1); middle(0); project(0)
    garrive(1); gmiddle(0)
    arrive(2); middle(1); project(1)
    garrive(2); gmiddle(1); glast(0)
    hidden_grads(0)
    arrive(3); middle(2); project(2)
    garrive(3); gmiddle(2); glast(1)
    hidden_grads(1)
    middle(3); project(3)
    w_out = pltpu.make_async_copy(wo_o, wob, wsem.at[3])
    w_out.start()

    scale = HD ** (-0.5)
    def turn(values):
        return values * cosine[...] + pltpu.roll(values, HD // 2, 1) * sine[...]
    @pl.loop(0, hw // HD)
    def _(i):
        @pl.when(i == 4)
        def _(): gmiddle(3)
        w = pl.ds(pl.multiple_of(i * HD, HD), HD)
        qh, kh, vh = turn(qa[:, w]).astype(bf16), turn(ka[:, w]).astype(bf16), va[:, w].astype(bf16)
        qr[:, w] = qh
        kr[:, w] = kh
        vr[:, w] = vh
        scores = nt(qh, kh) * scale
        ahead = lax.broadcasted_iota(jnp.int32, (toks, toks), 0) >= lax.broadcasted_iota(jnp.int32, (toks, toks), 1)
        scores = jnp.where(ahead, scores, -1e30)
        expo = jnp.exp(scores - jnp.max(scores, axis=1, keepdims=True))
        probs = expo * (1.0 / jnp.sum(expo, axis=1, keepdims=True))
        mixed[:, w] = nn(probs.astype(bf16), vh).astype(bf16)
    w_out.wait()
    whole = wob[...].reshape(width, hw)
    other = pl.ds(pl.multiple_of((1 - y) * rows, rows), rows)
    here = pl.ds(pl.multiple_of(y * rows, rows), rows)
    for m in range(0, width, 512):
        send[:, m:m + 512] = nt(mixed[other, :], whole[m:m + 512]).astype(bf16)
    swap = rcopy(send, recv, ysem.at[0], ysem.at[1], yn)
    swap.start()
    for m in range(0, width, 512):
        own_attn[:, m:m + 512] = nt(mixed[here, :], whole[m:m + 512])
    glast(2)
    hidden_grads(2)
    swap.wait_recv()
    @pl.loop(0, rows // 16)
    def _(r):
        q = pl.ds(pl.multiple_of(r * 16, 16), 16)
        at = pl.ds(pl.multiple_of(y * rows + r * 16, 16), 16)
        v = x_in[at].astype(f32) + own_attn[q] + recv[q].astype(f32)
        x_mid[q] = v
        scaled = v * lax.rsqrt(jnp.sum(v * v, axis=1, keepdims=True) * (1.0 / width) + EPS)
        act2[q] = (scaled * grow[1:2]).astype(bf16)
    glast(3)
    hidden_grads(3)
    for copy in stores(3, 1):
        copy.wait()
    swap.wait_send()
    for s in range(4):
        for a in range(n):
            wx(a, s).wait_send()
            for q in (0, 1):
                wc(a, s, q).wait_send()
        gx(s).wait_send()
        for q in (0, 1):
            gy(s, q).wait_send()
            for r in (0, 1):
                gc(s, q, r).wait_send()
        @pl.when((z < 3) & (s <= z))
        def _():
            gz(s, 1).wait_send()
            for a in range(n):
                wz(a, s, 1).wait_send()
        @pl.when((z > 0) & (s >= z))
        def _():
            gz(s, 0).wait_send()
            for a in range(n):
                wz(a, s, 0).wait_send()

def attention_layer(x_in, weights, gains, table, dy, wd, cosine, sine, cap, cid):
    toks, width = x_in.shape
    depth, hw = weights[0].shape
    rows = toks // 2
    hidden = wd.shape[0]
    n = 6
    f32, bf16, i32 = jnp.float32, jnp.bfloat16, jnp.int32
    D = pltpu.SemaphoreType.DMA
    S = jax.ShapeDtypeStruct
    any_ = pl.BlockSpec(memory_space=pl.ANY)
    vm = pl.BlockSpec(memory_space=pltpu.VMEM)
    V = lambda *shape, t=bf16: pltpu.VMEM(shape, t)
    return pl.pallas_call(
        attention_kernel,
        out_shape=[S((16, depth, hw), bf16)] * 4
        + [S((32, rows, width), bf16), S((toks, width), bf16)]
        + [S((toks, hw), bf16)] * 4
        + [
            S((rows, width), f32), S((rows, width), bf16), S((8, width), f32), S((16, 1, toks), i32), S((16, toks, 1), i32),
            S((16, cap, 1), f32), S((16, cap, width), bf16), S((16, cap, hidden), f32),
        ],
        in_specs=[vm] * 8 + [any_] + [vm] * 2,
        out_specs=[any_] * 5 + [vm] * 11 + [any_] * 2,
        scratch_shapes=[
            V(16, *gains.shape), V(16, *table.shape, t=f32), V(toks, 1, t=f32), V(3, 4, depth, hw), V(16, depth, hw), V(hidden, width),
            V(toks, hw, t=f32), V(toks, hw, t=f32), V(toks, hw, t=f32), V(rows, width, t=f32), V(rows, width), V(rows, width),
            V(8, toks, t=f32), V(2, 2, rows, width), V(2, cap, width), V(2 * cap, hidden, t=f32),
            D((4,)), D((n + 1,)), D((2,)), D((2, 2)), D((2,)),
            D((n, 4, 2)), D((n, 4)), D((n, 4)), D((n, 4)), D((n, 8)), D((n, 8)),
            D((4, 2)), D((4,)), D((4,)), D((4,)), D((4, 2)), D((4, 2)), D((8, 2)), D((8, 2)),
        ],
        compiler_params=pltpu.CompilerParams(collective_id=cid, has_side_effects=True, vmem_limit_bytes=60 << 20),
        name="attention_layer",
    )(x_in, *weights, gains, table, dy, wd, cosine, sine)


def on_device(
    tokens,
    cotangent,
    route_ids,
    route_gates,
    gain_first,
    w_query,
    w_key,
    w_value,
    w_output,
    gain_second,
    shared_gate,
    shared_up,
    shared_down,
    expert_gate,
    expert_up,
    expert_down,
):
    f32, bf16 = jnp.float32, jnp.bfloat16
    rows_dev, width = tokens.shape
    topk = route_ids.shape[1]
    experts = lax.axis_size("dp")
    half = rows_dev // lax.axis_size("tensor")
    mine = lax.axis_index("tensor") * half
    capacity = rows_dev * topk * 4 // (3 * experts)
    slots = experts * capacity
    positions = jnp.arange(rows_dev, dtype=f32)
    freqs = 10000.0 ** (-2.0 * jnp.arange(HD // 2, dtype=f32) / HD)
    angles = positions[:, None] * freqs[None, :]
    cosine = jnp.concatenate([jnp.cos(angles)] * 2, axis=1)
    sine = jnp.concatenate([-jnp.sin(angles), jnp.sin(angles)], axis=1)
    grad_half = lax.dynamic_slice_in_dim(cotangent, mine, half, axis=0)
    chosen = route_ids[:, :, None] == jnp.arange(experts, dtype=jnp.int32)[None, None, :]
    table = jnp.sum(jnp.where(chosen, route_gates[:, :, None], 0.0), axis=1)
    gains = jnp.concatenate([gain_first[None], gain_second[None], jnp.zeros((14, gain_first.shape[0]), bf16)])
    exp_gate, exp_up, exp_down = expert_gate[0].T, expert_up[0].T, expert_down[0]

    depth, common_width = shared_gate.shape
    common_dev = common_width // experts
    packed = jnp.stack([shared_gate, shared_up, shared_down])
    packed = packed.reshape(3, depth, experts, common_dev).transpose(2, 0, 1, 3)
    packed = lax.all_to_all(packed, "dp", split_axis=0, concat_axis=0, tiled=True)
    packed = packed.transpose(1, 0, 2, 3).reshape(3, width, common_dev)
    front = capacity - 128
    back = 128 - front - common_dev

    def widen(w):
        return jnp.pad(w, ((0, 0), (front, back)))

    common_gu = jnp.concatenate([widen(packed[0]), widen(packed[1])], axis=1)
    common_down = widen(packed[2])

    (
        query_whole, key_whole, value_whole, output_whole, grad_all, act_one, query_rot, key_rot, value_low, mixed,
        x_mid, act_two, gain_rows, rank_row, rank_col, slot_gate, rows_out_grad, hidden_rows_grad,
    ) = attention_layer(
        tokens, (w_query, w_key, w_value, w_output), gains, table.T, grad_half, exp_down, cosine, sine, capacity, 0
    )
    weights = [w.reshape(width, -1) for w in (query_whole, key_whole, value_whole, output_whole)]

    total_grad, act_all, rows, hidden_rows, gate_rows_grad, up_rows_grad, common_hidden, common_gu_grad, unused, ffn = (
        expert_layer(
            act_two, hidden_rows_grad, grad_all, rank_row, rank_col, slot_gate,
            exp_gate, exp_up, exp_down, common_gu, common_down.T[front:], common_down, 1,
        )
    )
    act_all = act_all.reshape(-1, width)
    grad_all = grad_all.reshape(-1, width)
    rows = rows.reshape(slots, width)
    rows_out_grad = rows_out_grad.reshape(slots, width)
    hidden_rows = hidden_rows.reshape(slots, -1)
    common_hidden = common_hidden.reshape(-1, 128)
    common_gu_grad = common_gu_grad.reshape(-1, 256)
    expert_gate_grad, expert_up_grad, expert_down_grad, gu_grad, down_grad = expert_grads(
        gate_rows_grad.reshape(slots, -1), up_rows_grad.reshape(slots, -1), hidden_rows,
        common_gu_grad, common_hidden, rows, rows_out_grad, act_all, grad_all,
    )
    common_w_grad = jnp.concatenate(
        [w[:, front : front + common_dev] for w in (gu_grad[:, :128], gu_grad[:, 128:], down_grad)], axis=1
    )
    common_w_grad = common_w_grad.reshape(experts, depth, 3 * common_dev)
    common_w_grad = lax.all_to_all(common_w_grad, "dp", split_axis=0, concat_axis=0, tiled=True)
    common_w_grad = common_w_grad.reshape(experts, depth, 3, common_dev).transpose(2, 1, 0, 3)
    common_w_grad = common_w_grad.reshape(3, depth, common_width).astype(f32)

    layer_out, tokens_grad, attn_grad, query_grad, key_grad, value_grad, gain_one_grad, gain_two_grad = attention_back(
        ffn,
        total_grad,
        x_mid,
        grad_half,
        lax.dynamic_slice_in_dim(tokens, mine, half, axis=0),
        gain_rows[0:1],
        gain_rows[1:2],
        weights,
        query_rot,
        key_rot,
        value_low,
        cosine,
        sine,
        2,
    )
    gains = jnp.concatenate([gain_one_grad, gain_two_grad, jnp.zeros((6, width), f32)])
    gains = gains.reshape(8, 4, 2, 2, width // 16).transpose(3, 2, 1, 0, 4)
    query_sum, key_sum, value_sum, output_sum, gain_grads = weight_grads(
        act_one, attn_grad.reshape(rows_dev, width), query_grad, key_grad, value_grad, mixed, gains, 4
    )
    return (
        layer_out.reshape(rows_dev, width),
        tokens_grad.reshape(rows_dev, width),
        gain_grads[0],
        query_sum,
        key_sum,
        value_sum,
        output_sum,
        gain_grads[1],
        common_w_grad[0],
        common_w_grad[1],
        common_w_grad[2],
        expert_gate_grad.T[None],
        expert_up_grad.T[None],
        expert_down_grad[None],
    )


def solution(mesh):
    body = on_device if (mesh.shape["dp"], mesh.shape["tensor"]) == (16, 2) else on_device_plain
    in_specs = (
        P("dp", None),
        P("dp", None),
        P("dp", None),
        P("dp", None),
        P("dp"),
        P("dp", "tensor"),
        P("dp", "tensor"),
        P("dp", "tensor"),
        P("dp", "tensor"),
        P("dp"),
        P("dp", "tensor"),
        P("dp", "tensor"),
        P("dp", "tensor"),
        P("dp", None, "tensor"),
        P("dp", None, "tensor"),
        P("dp", "tensor", None),
    )
    out_specs = (
        P("dp", None),
        P("dp", None),
        P("dp"),
        P("dp", "tensor"),
        P("dp", "tensor"),
        P("dp", "tensor"),
        P("dp", "tensor"),
        P("dp"),
        P("dp", "tensor"),
        P("dp", "tensor"),
        P("dp", "tensor"),
        P("dp", None, "tensor"),
        P("dp", None, "tensor"),
        P("dp", "tensor", None),
    )
    return jax.shard_map(
        body, mesh=mesh, in_specs=in_specs, out_specs=out_specs, check_vma=False
    )
```

```python
import functools

import jax
import jax.numpy as jnp
from jax import lax
from jax.experimental import pallas as pl
from jax.experimental.pallas import tpu as pltpu
from jax.sharding import PartitionSpec as P

HD = 128
MESH = pl.DeviceIdType.MESH


EPS = 1e-06


def rms_norm(values, gain):
    mean_square = jnp.mean(values * values, axis=-1, keepdims=True)
    return values * lax.rsqrt(mean_square + EPS) * gain


def rotate(values, positions):
    head = values.shape[-1]
    half = head // 2
    freqs = 10000.0 ** (-2.0 * jnp.arange(half, dtype=jnp.float32) / head)
    angles = positions[:, None] * freqs[None, :]
    cosine = jnp.cos(angles)[:, None, :]
    sine = jnp.sin(angles)[:, None, :]
    first = values[..., :half]
    second = values[..., half:]
    return jnp.concatenate(
        [first * cosine - second * sine, second * cosine + first * sine], axis=-1
    )


def gated(gate_pre, up_pre):
    return gate_pre * jax.nn.sigmoid(gate_pre) * up_pre


def contract_last(left, right):
    return lax.dot_general(
        left, right, (((1,), (1,)), ((), ())), preferred_element_type=jnp.float32
    )


def contract_first(left, right):
    return lax.dot_general(
        left, right, (((0,), (0,)), ((), ())), preferred_element_type=jnp.float32
    )


def masked_scores(query_rot, key_rot, causal, scale):
    scores = (
        jnp.einsum("qhc,khc->hqk", query_rot, key_rot, preferred_element_type=jnp.float32) * scale
    )
    return jnp.where(causal[None], scores, -1e30)


def on_device_plain(
    tokens,
    cotangent,
    route_ids,
    route_gates,
    gain_first,
    w_query,
    w_key,
    w_value,
    w_output,
    gain_second,
    shared_gate,
    shared_up,
    shared_down,
    expert_gate,
    expert_up,
    expert_down,
):
    rows_dev, width = tokens.shape
    topk = route_ids.shape[1]
    experts = lax.axis_size("dp")
    capacity = rows_dev * topk * 4 // (3 * experts)
    slots = experts * capacity
    scale = HD ** (-0.5)
    positions = jnp.arange(rows_dev, dtype=jnp.float32)
    causal = jnp.arange(rows_dev)[:, None] >= jnp.arange(rows_dev)[None, :]
    gain_one, query_whole, key_whole, value_whole, output_whole = (
        lax.all_gather(gain_first, "dp", axis=0, tiled=True),
        lax.all_gather(w_query, "dp", axis=0, tiled=True),
        lax.all_gather(w_key, "dp", axis=0, tiled=True),
        lax.all_gather(w_value, "dp", axis=0, tiled=True),
        lax.all_gather(w_output, "dp", axis=0, tiled=True),
    )
    gain_two, common_gate, common_up, common_down = (
        lax.all_gather(gain_second, "dp", axis=0, tiled=True),
        lax.all_gather(shared_gate, "dp", axis=0, tiled=True),
        lax.all_gather(shared_up, "dp", axis=0, tiled=True),
        lax.all_gather(shared_down, "dp", axis=0, tiled=True),
    )
    gain_one = gain_one.astype(jnp.float32)
    gain_two = gain_two.astype(jnp.float32)
    x_in = tokens.astype(jnp.float32)
    act_one = rms_norm(x_in, gain_one).astype(jnp.bfloat16)
    heads_dev = query_whole.shape[1] // HD
    query_pre = jnp.dot(act_one, query_whole, preferred_element_type=jnp.float32).reshape(
        rows_dev, heads_dev, HD
    )
    key_pre = jnp.dot(act_one, key_whole, preferred_element_type=jnp.float32).reshape(
        rows_dev, heads_dev, HD
    )
    query_rot = rotate(query_pre, positions).astype(jnp.bfloat16)
    key_rot = rotate(key_pre, positions).astype(jnp.bfloat16)
    value_low = (
        jnp.dot(act_one, value_whole, preferred_element_type=jnp.float32)
        .astype(jnp.bfloat16)
        .reshape(rows_dev, heads_dev, HD)
    )
    scores = masked_scores(query_rot, key_rot, causal, scale)
    top = jnp.max(scores, axis=-1, keepdims=True)
    expo = jnp.exp(scores - top)
    total = jnp.sum(expo, axis=-1, keepdims=True)
    probs = expo / total
    log_total = top + jnp.log(total)
    mixed = jnp.einsum(
        "hqk,khc->qhc", probs.astype(jnp.bfloat16), value_low, preferred_element_type=jnp.float32
    )
    mixed = mixed.reshape(rows_dev, heads_dev * HD).astype(jnp.bfloat16)
    attn = lax.psum(contract_last(mixed, output_whole), "tensor")
    x_mid = x_in + attn
    act_two = rms_norm(x_mid, gain_two).astype(jnp.bfloat16)
    gate_pre = jnp.dot(act_two, common_gate, preferred_element_type=jnp.float32)
    up_pre = jnp.dot(act_two, common_up, preferred_element_type=jnp.float32)
    hidden_common = gated(gate_pre, up_pre).astype(jnp.bfloat16)
    common_out = contract_last(hidden_common, common_down)
    flat_ids = route_ids.reshape(-1)
    onehot = (flat_ids[:, None] == jnp.arange(experts, dtype=jnp.int32)[None, :]).astype(jnp.int32)
    ranks = jnp.sum(onehot * jnp.cumsum(onehot, axis=0), axis=1) - 1
    dest = flat_ids * capacity + ranks
    token_of = jnp.arange(rows_dev * topk, dtype=jnp.int32) // topk
    source = jnp.zeros((slots,), jnp.int32).at[dest].set(token_of)
    weight_of = jnp.zeros((slots,), jnp.float32).at[dest].set(route_gates.reshape(-1))
    filled = jnp.zeros((slots,), jnp.bool_).at[dest].set(True)
    outgoing = jnp.where(filled[:, None], act_two[source], jnp.zeros((), jnp.bfloat16)).reshape(
        experts, capacity, width
    )
    exp_gate = expert_gate[0]
    exp_up = expert_up[0]
    exp_down = expert_down[0]
    received = lax.all_to_all(outgoing, "dp", split_axis=0, concat_axis=0, tiled=True)
    sources = received.shape[0]
    count = received.shape[1]
    rows = received.reshape(sources * count, width)
    gate_rows = jnp.dot(rows, exp_gate, preferred_element_type=jnp.float32)
    up_rows = jnp.dot(rows, exp_up, preferred_element_type=jnp.float32)
    hidden_rows = gated(gate_rows, up_rows).astype(jnp.bfloat16)
    partial_value = jnp.dot(hidden_rows, exp_down, preferred_element_type=jnp.float32).reshape(
        sources, count, width
    )
    returned = lax.all_to_all(
        partial_value.astype(jnp.bfloat16), "dp", split_axis=0, concat_axis=0, tiled=True
    ).astype(partial_value.dtype)
    returned, kept_rows, kept_gate, kept_up = (
        returned,
        received,
        gate_rows.reshape(sources, count, -1),
        up_rows.reshape(sources, count, -1),
    )
    picked = returned.reshape(slots, width)[dest].reshape(rows_dev, topk, width)
    routed_part = jnp.sum(picked * route_gates[:, :, None], axis=1)
    ffn = lax.psum((common_out + routed_part).astype(jnp.bfloat16), "tensor").astype(jnp.float32)
    layer_out = (x_mid + ffn).astype(jnp.bfloat16)
    grad_out = cotangent.astype(jnp.float32)
    hidden_grad = jnp.dot(cotangent, common_down, preferred_element_type=jnp.float32)
    dummy_common, common_vjp = jax.vjp(gated, gate_pre, up_pre)
    gate_grad, up_grad = common_vjp(hidden_grad)
    gate_grad = gate_grad.astype(jnp.bfloat16)
    up_grad = up_grad.astype(jnp.bfloat16)
    common_gate_grad = contract_first(act_two, gate_grad)
    common_up_grad = contract_first(act_two, up_grad)
    common_down_grad = contract_first(cotangent, hidden_common)
    act_two_grad = contract_last(gate_grad, common_gate) + contract_last(up_grad, common_up)
    outgoing_grad = (
        (weight_of[:, None] * grad_out[source])
        .astype(jnp.bfloat16)
        .reshape(experts, capacity, width)
    )
    incoming_grad = lax.all_to_all(outgoing_grad, "dp", split_axis=0, concat_axis=0, tiled=True)
    hidden_width = kept_gate.shape[2]
    rows = kept_rows.reshape(-1, width)
    rows_out_grad = incoming_grad.reshape(-1, width)
    hidden_rows, expert_vjp = jax.vjp(
        gated, kept_gate.reshape(-1, hidden_width), kept_up.reshape(-1, hidden_width)
    )
    hidden_rows = hidden_rows.astype(jnp.bfloat16)
    hidden_rows_grad = contract_last(rows_out_grad, exp_down)
    gate_rows_grad, up_rows_grad = expert_vjp(hidden_rows_grad)
    gate_rows_grad = gate_rows_grad.astype(jnp.bfloat16)
    up_rows_grad = up_rows_grad.astype(jnp.bfloat16)
    expert_gate_grad = contract_first(rows, gate_rows_grad)[None]
    expert_up_grad = contract_first(rows, up_rows_grad)[None]
    expert_down_grad = contract_first(hidden_rows, rows_out_grad)[None]
    rows_in_grad = (
        contract_last(gate_rows_grad, exp_gate) + contract_last(up_rows_grad, exp_up)
    ).reshape(experts, capacity, width)
    returned_grad = lax.all_to_all(rows_in_grad, "dp", split_axis=0, concat_axis=0, tiled=True)
    routed_grad = jnp.sum(
        returned_grad.reshape(slots, width)[dest].reshape(rows_dev, topk, width), axis=1
    )
    act_two_total = lax.psum(act_two_grad + routed_grad, "tensor")
    dummy_second, second_vjp = jax.vjp(rms_norm, x_mid, gain_two)
    mid_norm_grad, gain_two_grad = second_vjp(act_two_total)
    mid_grad = grad_out + mid_norm_grad
    ffn_sums = (gain_two_grad, common_gate_grad, common_up_grad, common_down_grad)
    attn_grad = mid_grad.astype(jnp.bfloat16)
    output_w_grad = contract_first(attn_grad, mixed)
    mixed_grad = (
        jnp.dot(attn_grad, output_whole, preferred_element_type=jnp.float32)
        .astype(jnp.bfloat16)
        .reshape(rows_dev, heads_dev, HD)
    )
    probs_again = jnp.exp(masked_scores(query_rot, key_rot, causal, scale) - log_total)
    value_grad = jnp.einsum(
        "hqk,qhc->khc",
        probs_again.astype(jnp.bfloat16),
        mixed_grad,
        preferred_element_type=jnp.float32,
    ).astype(jnp.bfloat16)
    prob_grad = jnp.einsum(
        "qhc,khc->hqk", mixed_grad, value_low, preferred_element_type=jnp.float32
    )
    delta = jnp.sum(probs_again * prob_grad, axis=-1, keepdims=True)
    score_grad = (probs_again * (prob_grad - delta)).astype(jnp.bfloat16)
    query_rot_grad = (
        jnp.einsum("hqk,khc->qhc", score_grad, key_rot, preferred_element_type=jnp.float32) * scale
    )
    key_rot_grad = (
        jnp.einsum("hqk,qhc->khc", score_grad, query_rot, preferred_element_type=jnp.float32)
        * scale
    )

    def turn(values):
        return rotate(values, positions)

    dummy_turn, turn_vjp = jax.vjp(turn, query_pre)
    query_grad = turn_vjp(query_rot_grad)[0].reshape(rows_dev, heads_dev * HD).astype(jnp.bfloat16)
    key_grad = turn_vjp(key_rot_grad)[0].reshape(rows_dev, heads_dev * HD).astype(jnp.bfloat16)
    value_flat = value_grad.reshape(rows_dev, heads_dev * HD)
    query_w_grad = contract_first(act_one, query_grad)
    key_w_grad = contract_first(act_one, key_grad)
    value_w_grad = contract_first(act_one, value_flat)
    act_one_grad = (
        contract_last(query_grad, query_whole)
        + contract_last(key_grad, key_whole)
        + contract_last(value_flat, value_whole)
    )
    act_one_total = lax.psum(act_one_grad, "tensor")
    dummy_first, first_vjp = jax.vjp(rms_norm, x_in, gain_one)
    in_norm_grad, gain_one_grad = first_vjp(act_one_total)
    tokens_grad = (mid_grad + in_norm_grad).astype(jnp.bfloat16)
    every = (
        lax.psum_scatter(gain_one_grad, "dp", scatter_dimension=0, tiled=True),
        lax.psum_scatter(query_w_grad, "dp", scatter_dimension=0, tiled=True),
        lax.psum_scatter(key_w_grad, "dp", scatter_dimension=0, tiled=True),
        lax.psum_scatter(value_w_grad, "dp", scatter_dimension=0, tiled=True),
        lax.psum_scatter(output_w_grad, "dp", scatter_dimension=0, tiled=True),
        lax.psum_scatter(ffn_sums[0], "dp", scatter_dimension=0, tiled=True),
        lax.psum_scatter(ffn_sums[1], "dp", scatter_dimension=0, tiled=True),
        lax.psum_scatter(ffn_sums[2], "dp", scatter_dimension=0, tiled=True),
        lax.psum_scatter(ffn_sums[3], "dp", scatter_dimension=0, tiled=True),
    )
    attn_sums = every[:5]
    ffn_sums = every[5:]
    return (
        layer_out,
        tokens_grad,
        attn_sums[0],
        attn_sums[1],
        attn_sums[2],
        attn_sums[3],
        attn_sums[4],
        ffn_sums[0],
        ffn_sums[1],
        ffn_sums[2],
        ffn_sums[3],
        expert_gate_grad,
        expert_up_grad,
        expert_down_grad,
    )


def place():
    d = lax.axis_index("dp"); y = lax.axis_index("tensor")
    c = lax.rem(d, 2); x = lax.rem(lax.div(d, 2), 2); z = lax.div(d, 4)
    return z, x, y, c

def dev(z, x, y, c):
    return ((z * 2 + x) * 2 + c, y)

def blk(z, x, y, c):
    return ((z * 2 + x) * 2 + c) * 2 + y

def greet(z, x, y, c):
    bar = pltpu.get_barrier_semaphore()
    for other in (dev(z, 1 - x, y, c), dev(z, x, 1 - y, c), dev(z, x, y, 1 - c)):
        pl.semaphore_signal(bar, inc=1, device_id=other, device_id_type=MESH)
    @pl.when(z > 0)
    def _():
        pl.semaphore_signal(bar, inc=1, device_id=dev(z - 1, x, y, c), device_id_type=MESH)
    @pl.when(z < 3)
    def _():
        pl.semaphore_signal(bar, inc=1, device_id=dev(z + 1, x, y, c), device_id_type=MESH)
    pl.semaphore_wait(bar, 3 + (z > 0).astype(jnp.int32) + (z < 3).astype(jnp.int32))

def rcopy(src, dst, ssem, rsem, device):
    return pltpu.make_async_remote_copy(src_ref=src, dst_ref=dst, send_sem=ssem, recv_sem=rsem, device_id=device, device_id_type=MESH)

def nearest(z, g):
    one = jnp.where(z == 0, 1, z - 1)
    two = jnp.where(z == 3, 1, jnp.where(z == 2, 3, 2))
    three = jnp.where(z >= 2, 0, 3)
    return jnp.where(g == 0, z, jnp.where(g == 1, one, jnp.where(g == 2, two, three)))

def nt(left, right):
    return lax.dot_general(left, right, (((1,), (1,)), ((), ())), preferred_element_type=jnp.float32)

def nn(left, right):
    return jnp.dot(left, right, preferred_element_type=jnp.float32)

def greet_all(z, x, y, c):
    bar = pltpu.get_barrier_semaphore()
    for other in (dev(z, 1 - x, y, c), dev(z, x, 1 - y, c), dev(z, x, y, 1 - c)):
        pl.semaphore_signal(bar, inc=1, device_id=other, device_id_type=MESH)
    for s in range(4):
        @pl.when(s != z)
        def _(): pl.semaphore_signal(bar, inc=1, device_id=dev(s, x, y, c), device_id_type=MESH)
    pl.semaphore_wait(bar, 6)


def expert_kernel(
    a_in, deh, dy_all, rank_row, rank_col, gate, wg_h, wu_h, wd_h, sgu_h, sdt_h, sd_h,
    total, act_all, rows_o, eh_o, deg_o, deu_o, hs_o, dsgu_o, part, ffn_part,
    wg, wu, wd, sgu, tail, acc, ic, iy0, ix0, ix1, iy1, iz,
    eg, eu, dehb, ehb, degb, deub, sd, dhs, hsb, dsgub, eh2, hs2, ot,
    wsem, usem, ssem, osem, psem, lsem,
    zs, zr, x0s, x0r, x1s, x1r, y0s, y0r, y1s, y1r, cs, cr,
    ls, rcs, rcr, ry0s, ry0r, rx0s, rx0r, rx1s, rx1r, ry1s, ry1r, rzs, rzr,
):
    f32, bf16 = jnp.float32, jnp.bfloat16
    z, x, y, c = place()
    rows, width = a_in.shape
    h = rows // 2
    cap = deh.shape[1]
    toks = 2 * rows
    lo, hi = pl.ds(0, h), pl.ds(h, h)
    part_of = (lo, hi)
    xn, yn, cn = dev(z, 1 - x, y, c), dev(z, x, 1 - y, c), dev(z, x, y, 1 - c)
    greet_all(z, x, y, c)
    mine = blk(z, x, y, c)
    own = pltpu.make_async_copy(a_in, act_all.at[mine], lsem)
    own.start()
    weights = [
        pltpu.make_async_copy(a, b, wsem.at[i])
        for i, (a, b) in enumerate(((wg_h, wg), (wu_h, wu), (wd_h, wd), (sgu_h, sgu), (sdt_h, tail.at[pl.ds(cap, 256 - cap)]), (sd_h, sd)))
    ]
    for w in weights:
        w.start()

    def zcopy(s, up):
        b = act_all.at[blk(s, x, y, c)]
        return rcopy(b, b, zs.at[s, up], zr.at[s], dev(z + 2 * up - 1, x, y, c))

    def half_copy(s, xx, yy, p, send, recv, to):
        b = act_all.at[blk(s, xx, yy, c), part_of[p]]
        return rcopy(b, b, send, recv, to)

    def x0(s): return half_copy(s, x, y, 0, x0s.at[s], x0r.at[s], xn)
    def y1(s): return half_copy(s, x, y, 1, y1s.at[s], y1r.at[s], yn)
    def y0(s, xx): return half_copy(s, xx, y, 0, y0s.at[s, xx], y0r.at[s, xx], yn)
    def x1(s, yy): return half_copy(s, x, yy, 1, x1s.at[s, yy], x1r.at[s, yy], xn)
    def side(s, xx, yy, p):
        i = (s * 2 + xx) * 2 + yy
        return half_copy(s, xx, yy, p, cs.at[i, p], cr.at[i, p], cn)

    def column(s):
        x0(s).start(); y1(s).start(); y0(s, x).start(); x1(s, y).start()
        side(s, x, y, 0).start(); side(s, x, y, 1).start()

    def arrive(g):
        s = nearest(z, g)
        up = (s < z).astype(jnp.int32)
        nxt = z + 2 * up - 1
        zcopy(s, up).wait_recv()
        @pl.when((nxt >= 0) & (nxt <= 3))
        def _(): zcopy(s, up).start()
        column(s)

    def middle(g):
        s = nearest(z, g)
        x0(s).wait_recv()
        y0(s, 1 - x).start(); side(s, 1 - x, y, 0).start()
        y1(s).wait_recv()
        x1(s, 1 - y).start(); side(s, x, 1 - y, 1).start()

    def last_own(g):
        s = nearest(z, g)
        y0(s, x).wait_recv(); side(s, x, 1 - y, 0).start()

    def last_other(g):
        s = nearest(z, g)
        x1(s, y).wait_recv(); side(s, 1 - x, y, 1).start()
        y0(s, 1 - x).wait_recv(); side(s, 1 - x, 1 - y, 0).start()
        x1(s, 1 - y).wait_recv(); side(s, 1 - x, 1 - y, 1).start()

    def spread_cols(j):
        ranks = rank_col[j]
        slot = lax.broadcasted_iota(jnp.int32, (toks, 128), 1)
        one = jnp.where(ranks == slot, 1.0, 0.0)
        two = jnp.where(ranks == slot + 128, 1.0, 0.0)
        return one, two

    def seq_of(u):
        s = nearest(z, u // 2)
        xx = lax.rem(x + lax.rem(u, 2), 2)
        return s, xx

    def stores(u):
        s, xx = seq_of(u)
        out = []
        for k in (0, 1):
            j = (s * 2 + xx) * 2 + k
            r = pl.ds(k * cap, cap)
            out += [
                pltpu.make_async_copy(acc.at[k], rows_o.at[j], ssem.at[k, 0]),
                pltpu.make_async_copy(ehb.at[r], eh_o.at[j], ssem.at[k, 1]),
                pltpu.make_async_copy(degb.at[r], deg_o.at[j], ssem.at[k, 2]),
                pltpu.make_async_copy(deub.at[r], deu_o.at[j], ssem.at[k, 3]),
                pltpu.make_async_copy(hsb.at[k], hs_o.at[j], ssem.at[k, 4]),
                pltpu.make_async_copy(dsgub.at[k], dsgu_o.at[j], ssem.at[k, 5]),
            ]
        return out

    def at(s, xx, yy): return (s * 2 + xx) * 2 + yy
    def keep(u, k):
        s, xx = seq_of(u)
        return pltpu.make_async_copy(acc.at[pl.ds(10 + 2 * k, 2)], part.at[pl.ds(at(s, xx, 0), 2)], ssem.at[k, 6])
    def cross(s, xx, yy, k):
        i = at(s, xx, yy)
        return rcopy(acc.at[10 + 2 * k + yy], ic.at[i], rcs.at[i], rcr.at[i], cn)
    def hand_over(u):
        s, xx = seq_of(u)
        for k in (0, 1):
            @pl.when(c == k)
            def _(): keep(u, k).start()
            @pl.when(c != k)
            def _():
                for yy in (0, 1):
                    cross(s, xx, yy, k).start()
    def handed_over(u):
        s, xx = seq_of(u)
        for k in (0, 1):
            @pl.when(c == k)
            def _(): keep(u, k).wait()
            @pl.when(c != k)
            def _():
                for yy in (0, 1):
                    cross(s, xx, yy, k).wait_send()

    def unit(u):
        s, xx = seq_of(u)
        base = (s * 2 + xx) * 2
        for k in (0, 1):
            pltpu.make_async_copy(deh.at[base + k], dehb.at[pl.ds(k * cap, cap)], usem.at[k, 1]).start()
        for yy in (0, 1):
            for p in (0, 1):
                side(s, xx, yy, p).wait_recv()
        loads = [
            pltpu.make_async_copy(act_all.at[pl.ds(2 * (base + k), 2)], acc.at[pl.ds(4 + 2 * k, 2)], usem.at[k, 0])
            for k in (0, 1)
        ]
        for k in (0, 1):
            loads[k].start()
        @pl.when(u > 0)
        def _():
            for copy in stores(u - 1):
                copy.wait()
            handed_over(u - 1)
        for k in (0, 1):
            loads[k].wait()
            act = acc[4 + 2 * k:6 + 2 * k].reshape(toks, width)
            ranks = rank_row[base + k]
            slot = lax.broadcasted_iota(jnp.int32, (cap, toks), 0)
            pick = jnp.where(ranks == slot, 1.0, 0.0).astype(bf16)
            acc[k] = nn(pick, act).astype(bf16)
            pre = nn(act, sgu[...])
            gp, up = pre[:, :128], pre[:, 128:]
            dh = dhs[base + k]
            sig = jax.nn.sigmoid(gp)
            hsb[k] = (gp * sig * up).astype(bf16)
            dsgub[k, :, 0:128] = (dh * up * sig * (1.0 + gp * (1.0 - sig))).astype(bf16)
            dsgub[k, :, 128:256] = (dh * gp * sig).astype(bf16)
        picked = acc[0:2].reshape(2 * cap, width)
        eg[...] = nt(picked, wg[...])
        eu[...] = nt(picked, wu[...])
        for k in (0, 1):
            pltpu.make_async_copy(deh.at[base + k], dehb.at[pl.ds(k * cap, cap)], usem.at[k, 1]).wait()
        @pl.loop(0, 2 * cap // 32)
        def _(r):
            q = pl.ds(pl.multiple_of(r * 32, 32), 32)
            gp, up, dh = eg[q], eu[q], dehb[q]
            sig = jax.nn.sigmoid(gp)
            silu = gp * sig
            ehb[q] = (silu * up).astype(bf16)
            degb[q] = (dh * up * sig * (1.0 + gp * (1.0 - sig))).astype(bf16)
            deub[q] = (dh * silu).astype(bf16)
        dg, du = degb[...], deub[...]
        for n in range(0, width, 512):
            w = pl.ds(n, 512)
            back = (nn(dg, wg[:, w]) + nn(du, wu[:, w])).astype(bf16)
            acc[8, :, w] = back[:cap]
            acc[9, :, w] = back[cap:]
        for k in (0, 1):
            one, two = spread_cols(base + k)
            left = jnp.concatenate([one, two], axis=1)[:, :cap].astype(bf16)
            for n in range(0, width, 512):
                w = pl.ds(n, 512)
                out = nn(left, acc[8 + k, :, w]) + nt(dsgub[k], sgu[w, :])
                out = out.astype(bf16)
                acc[10 + 2 * k, :, w] = out[:rows]
                acc[11 + 2 * k, :, w] = out[rows:]
        for copy in stores(u):
            copy.start()
        hand_over(u)

    def ry0(s, xx):
        return rcopy(ic.at[at(s, xx, 1 - y), lo], iy0.at[s * 2 + xx], ry0s.at[s, xx], ry0r.at[s, xx], yn)
    def rx1(s, yy):
        return rcopy(ic.at[at(s, 1 - x, yy), hi], ix1.at[s * 2 + yy], rx1s.at[s, yy], rx1r.at[s, yy], xn)
    def rx0(s):
        return rcopy(ic.at[at(s, 1 - x, y), lo], ix0.at[s], rx0s.at[s], rx0r.at[s], xn)
    def ry1(s):
        return rcopy(ic.at[at(s, x, 1 - y), hi], iy1.at[s], ry1s.at[s], ry1r.at[s], yn)
    def rz(s):
        return rcopy(ic.at[at(s, x, y)], iz.at[z], rzs.at[s], rzr.at[z], dev(s, x, y, c))
    def rz_wait(s):
        rcopy(iz.at[s], iz.at[s], rzs.at[s], rzr.at[s], dev(s, x, y, c)).wait_recv()
    def add(i, start, count, src, j):
        @pl.loop(0, count // 16)
        def _(r):
            a = pl.ds(pl.multiple_of(start + r * 16, 16), 16)
            b = pl.ds(pl.multiple_of(r * 16, 16), 16)
            ic[i, a] = ic[i, a] + src[j, b]

    def first(g):
        s = nearest(z, g)
        def load(xx, yy):
            return pltpu.make_async_copy(part.at[at(s, xx, yy)], acc.at[4 + 2 * xx + yy], ls.at[2 * xx + yy])
        for xx in (0, 1):
            for yy in (0, 1):
                load(xx, yy).start()
        for xx in (0, 1):
            for yy in (0, 1):
                load(xx, yy).wait(); cross(s, xx, yy, 0).wait_recv()
                add(at(s, xx, yy), 0, rows, acc, 4 + 2 * xx + yy)
                @pl.when(yy != y)
                def _(): ry0(s, xx).start()
                @pl.when(xx != x)
                def _(): rx1(s, yy).start()

    def second(g):
        s = nearest(z, g)
        ry0(s, 1 - x).wait_recv(); add(at(s, 1 - x, y), 0, h, iy0, s * 2 + 1 - x); rx0(s).start()
        rx1(s, 1 - y).wait_recv(); add(at(s, x, 1 - y), h, h, ix1, s * 2 + 1 - y); ry1(s).start()
        ry0(s, x).wait_recv(); add(at(s, x, y), 0, h, iy0, s * 2 + x)
        rx1(s, y).wait_recv(); add(at(s, x, y), h, h, ix1, s * 2 + y)

    def third(g):
        s = nearest(z, g)
        me = at(s, x, y)
        rx0(s).wait_recv(); add(me, 0, h, ix0, s)
        ry1(s).wait_recv(); add(me, h, h, iy1, s)
        if g > 0:
            rz(s).start()

    own.wait()
    @pl.when(z < 3)
    def _(): zcopy(z, 1).start()
    @pl.when(z > 0)
    def _(): zcopy(z, 0).start()
    column(z)
    def dy_load(j, b):
        return pltpu.make_async_copy(dy_all.at[pl.ds(2 * j, 2)], acc.at[pl.ds(2 + 12 * b, 2)], usem.at[b, 2])
    dy_load(0, 0).start()
    for w in weights:
        w.wait()
    @pl.loop(0, 8)
    def _(i):
        for b in (0, 1):
            j = 2 * i + b
            @pl.when(j < 15)
            def _(): dy_load(j + 1, 1 - b).start()
            dy_load(j, b).wait()
            dhs[j] = nn(acc[2 + 12 * b:4 + 12 * b].reshape(toks, width), sd[...])

    @pl.loop(0, 8)
    def _(u):
        @pl.when(u == 0)
        def _():
            middle(0); last_own(0); arrive(1)
        @pl.when(u == 1)
        def _():
            last_other(0); arrive(2); middle(1)
        @pl.when(u == 2)
        def _():
            arrive(3); last_own(1); middle(2)
        @pl.when(u == 3)
        def _():
            last_other(1); middle(3); first(0)
        @pl.when(u == 4)
        def _():
            last_own(2)
        @pl.when(u == 5)
        def _():
            last_other(2); first(1)
        @pl.when(u == 6)
        def _():
            last_own(3); second(0)
        @pl.when(u == 7)
        def _():
            last_other(3); first(2); third(0)
        unit(u)

    for copy in stores(7):
        copy.wait()
    handed_over(7)

    def out_loads(j, b):
        return [
            pltpu.make_async_copy(eh_o.at[j], eh2.at[b], osem.at[b, 0]),
            pltpu.make_async_copy(hs_o.at[j], hs2.at[b], osem.at[b, 1]),
        ]
    def out_store(j, b):
        return pltpu.make_async_copy(ot.at[b], ffn_part.at[pl.ds(2 * j, 2)], psem.at[b])

    def forward_out(j):
        b = lax.rem(j, 2)
        @pl.when(j < 15)
        def _():
            for copy in out_loads(j + 1, 1 - b):
                copy.start()
        for copy in out_loads(j, b):
            copy.wait()
        @pl.when(j >= 2)
        def _(): out_store(j - 2, b).wait()
        weight = gate[j]
        for n in range(0, width, 512):
            w = pl.ds(n, 512)
            tail[0:cap, w] = (nn(eh2[b], wd[:, w]) * weight).astype(bf16)
        one, two = spread_cols(j)
        left = jnp.concatenate([one, two + hs2[b].astype(f32)], axis=1).astype(bf16)
        for n in range(0, width, 512):
            w = pl.ds(n, 512)
            out = nn(left, tail[:, w]).astype(bf16)
            ot[b, 0, :, w] = out[:rows]
            ot[b, 1, :, w] = out[rows:]
        out_store(j, b).start()

    for copy in out_loads(0, 0):
        copy.start()

    first(3); second(1)
    second(2); third(1)
    @pl.loop(0, 16)
    def _(j):
        @pl.when(j == 4)
        def _():
            second(3); third(2)
        @pl.when(j == 8)
        def _(): third(3)
        forward_out(j)
    me = at(z, x, y)
    for g in (1, 2, 3):
        rz_wait(nearest(z, g))
    @pl.loop(0, rows // 16)
    def _(r):
        q = pl.ds(pl.multiple_of(r * 16, 16), 16)
        out = ic[me, q].astype(f32)
        for g in (1, 2, 3):
            out = out + iz[nearest(z, g), q].astype(f32)
        total[q] = out
    out_store(14, 0).wait()
    out_store(15, 1).wait()

    for s in range(4):
        @pl.when((z < 3) & (s <= z))
        def _(): zcopy(s, 1).wait_send()
        @pl.when((z > 0) & (s >= z))
        def _(): zcopy(s, 0).wait_send()
        x0(s).wait_send(); y1(s).wait_send()
        rx0(s).wait_send(); ry1(s).wait_send()
        for q in (0, 1):
            y0(s, q).wait_send(); x1(s, q).wait_send()
            ry0(s, q).wait_send(); rx1(s, q).wait_send()
            for r in (0, 1):
                for p in (0, 1):
                    side(s, q, r, p).wait_send()
        @pl.when(s != z)
        def _():
            rz(s).wait_send()

def expert_layer(act, deh, dy_all, rank_row, rank_col, gate, wg, wu, wd, sgu, sdt, sd, cid):
    rows, width = act.shape
    cap, hidden = deh.shape[1:]
    h = rows // 2
    f32, bf16 = jnp.float32, jnp.bfloat16
    D = pltpu.SemaphoreType.DMA
    S = jax.ShapeDtypeStruct
    any_ = pl.BlockSpec(memory_space=pl.ANY)
    vm = pl.BlockSpec(memory_space=pltpu.VMEM)
    V = lambda *shape, t=bf16: pltpu.VMEM(shape, t)
    return pl.pallas_call(
        expert_kernel,
        out_shape=[
            S((rows, width), f32), S((32, rows, width), bf16), S((16, cap, width), bf16),
            S((16, cap, hidden), bf16), S((16, cap, hidden), bf16), S((16, cap, hidden), bf16),
            S((16, 2 * rows, 128), bf16), S((16, 2 * rows, 256), bf16),
            S((16, rows, width), bf16), S((32, rows, width), bf16),
        ],
        in_specs=[vm, any_, any_, vm, vm, vm] + [any_] * 6,
        out_specs=[vm] + [any_] * 9,
        scratch_shapes=[
            V(*wg.shape), V(*wu.shape), V(*wd.shape), V(*sgu.shape), V(256, width),
            V(16, rows, width), V(16, rows, width), V(8, h, width), V(4, h, width), V(8, h, width), V(4, h, width),
            V(4, rows, width),
            V(2 * cap, hidden, t=f32), V(2 * cap, hidden, t=f32), V(2 * cap, hidden, t=f32),
            V(2 * cap, hidden), V(2 * cap, hidden), V(2 * cap, hidden),
            V(*sd.shape), V(16, 2 * rows, 128, t=f32), V(2, 2 * rows, 128), V(2, 2 * rows, 256),
            V(2, cap, hidden), V(2, 2 * rows, 128), V(2, 2, rows, width),
            D((6,)), D((2, 3)), D((2, 7)), D((2, 2)), D((2,)), D,
            D((4, 2)), D((4,)), D((4,)), D((4,)), D((4, 2)), D((4, 2)), D((4, 2)), D((4, 2)), D((4,)), D((4,)), D((16, 2)), D((16, 2)),
            D((4,)), D((16,)), D((16,)), D((4, 2)), D((4, 2)), D((4,)), D((4,)), D((4, 2)), D((4, 2)), D((4,)), D((4,)),
            D((4,)), D((4,)),
        ],
        compiler_params=pltpu.CompilerParams(collective_id=cid, has_side_effects=True, vmem_limit_bytes=63 << 20),
        name="expert_layer",
    )(act, deh, dy_all, rank_row, rank_col, gate, wg, wu, wd, sgu, sdt, sd)


def norm_back(values, gain, grad):
    width = values.shape[1]
    inv = lax.rsqrt(jnp.sum(values * values, axis=1, keepdims=True) * (1.0 / width) + EPS)
    scaled = grad * gain
    inner = jnp.sum(values * scaled, axis=1, keepdims=True) * (1.0 / width)
    normed = values * inv
    return inv * (scaled - normed * (inv * inner)), grad * normed

def attention_back_kernel(
    part, grad2, x_mid, dy, x_in, gain1, gain2, wq_h, wk_h, wv_h, wo_h, qr, kr, vr, cosine, sine,
    out_half, tok_half, dattn, dq, dk, dv, g1, g2,
    ic, tmp, iy0, ix0, ix1, iy1, izu, izd, wa, wb, wc, dmix, dx2, da1, send1, recv1,
    wsem, ysem, ls, rcs, rcr, ry0s, ry0r, rx0s, rx0r, rx1s, rx1r, ry1s, ry1r, zus, zur, zds, zdr,
):
    f32, bf16 = jnp.float32, jnp.bfloat16
    z, x, y, c = place()
    rows, width = x_mid.shape
    h = 48
    toks = 2 * rows
    heads = qr.shape[1] // HD
    lo, hi = pl.ds(0, h), pl.ds(h, rows - h)
    xn, yn, cn = dev(z, 1 - x, y, c), dev(z, x, 1 - y, c), dev(z, x, y, 1 - c)
    greet(z, x, y, c)

    def at(s, xx, yy): return (s * 2 + xx) * 2 + yy
    def load(s, xx, yy):
        return pltpu.make_async_copy(part.at[blk(s, xx, yy, c)], tmp.at[xx * 2 + yy], ls.at[xx * 2 + yy])
    def cross(s, xx, yy):
        i = at(s, xx, yy)
        return rcopy(part.at[blk(s, xx, yy, 1 - c)], ic.at[i], rcs.at[i], rcr.at[i], cn)
    def ry0(s, xx):
        return rcopy(ic.at[at(s, xx, 1 - y), lo], iy0.at[s * 2 + xx], ry0s.at[s, xx], ry0r.at[s, xx], yn)
    def rx1(s, yy):
        return rcopy(ic.at[at(s, 1 - x, yy), hi], ix1.at[s * 2 + yy], rx1s.at[s, yy], rx1r.at[s, yy], xn)
    def rx0(s):
        return rcopy(ic.at[at(s, 1 - x, y), lo], ix0.at[s], rx0s.at[s], rx0r.at[s], xn)
    def ry1(s):
        return rcopy(ic.at[at(s, x, 1 - y), hi], iy1.at[s], ry1s.at[s], ry1r.at[s], yn)
    def zu(s):
        return rcopy(ic.at[at(s, x, y)], izu.at[s], zus.at[s], zur.at[s], dev(z + 1, x, y, c))
    def zd(s):
        return rcopy(ic.at[at(s, x, y)], izd.at[s], zds.at[s], zdr.at[s], dev(z - 1, x, y, c))
    def add(i, start, count, src, j):
        @pl.loop(0, count // 16)
        def _(r):
            a = pl.ds(pl.multiple_of(start + r * 16, 16), 16)
            b = pl.ds(pl.multiple_of(r * 16, 16), 16)
            ic[i, a] = ic[i, a] + src[j, b]

    four = [(xx, yy) for xx in (0, 1) for yy in (0, 1)]

    def first(g):
        s = nearest(z, g)
        for xx, yy in four:
            load(s, xx, yy).wait(); cross(s, xx, yy).wait_recv()
            add(at(s, xx, yy), 0, rows, tmp, xx * 2 + yy)
            @pl.when(yy != y)
            def _(): ry0(s, xx).start()
            @pl.when(xx != x)
            def _(): rx1(s, yy).start()
        if g > 0:
            for xx, yy in four:
                load(nearest(z, g - 1), xx, yy).start()

    def second(g):
        s = nearest(z, g)
        ry0(s, 1 - x).wait_recv(); add(at(s, 1 - x, y), 0, h, iy0, s * 2 + 1 - x); rx0(s).start()
        rx1(s, 1 - y).wait_recv(); add(at(s, x, 1 - y), h, rows - h, ix1, s * 2 + 1 - y); ry1(s).start()
        ry0(s, x).wait_recv(); add(at(s, x, y), 0, h, iy0, s * 2 + x)
        rx1(s, y).wait_recv(); add(at(s, x, y), h, rows - h, ix1, s * 2 + y)

    def third(g):
        s = nearest(z, g)
        me = at(s, x, y)
        rx0(s).wait_recv(); add(me, 0, h, ix0, s)
        ry1(s).wait_recv(); add(me, h, rows - h, iy1, s)
        @pl.when((s >= z) & (z > 0))
        def _():
            zu(s).wait_recv(); add(me, 0, rows, izu, s)
        @pl.when((s <= z) & (z < 3))
        def _():
            zd(s).wait_recv(); add(me, 0, rows, izd, s)
        @pl.when(s > z)
        def _(): zu(s).start()
        @pl.when(s < z)
        def _(): zd(s).start()

    for g in (3, 2, 1, 0):
        s = nearest(z, g)
        for xx, yy in four:
            cross(s, xx, yy).start()
            if g == 3:
                load(s, xx, yy).start()
    w_out = pltpu.make_async_copy(wo_h, wa, wsem.at[0])
    w_query = pltpu.make_async_copy(wq_h, wb, wsem.at[1])
    w_key = pltpu.make_async_copy(wk_h, wc, wsem.at[2])
    w_value = pltpu.make_async_copy(wv_h, wa, wsem.at[3])
    w_out.start(); w_query.start(); w_key.start()

    g1[...] = jnp.zeros_like(g1)
    g2[...] = jnp.zeros_like(g2)
    @pl.loop(0, rows // 16)
    def _(r):
        q = pl.ds(pl.multiple_of(r * 16, 16), 16)
        back, terms = norm_back(x_mid[q], gain2[...], grad2[q])
        back = back + dy[pl.ds(pl.multiple_of(y * rows + r * 16, 16), 16)].astype(f32)
        dx2[q] = back
        dattn[y, q] = back.astype(bf16)
        g2[...] += jnp.sum(terms, axis=0, keepdims=True)
    attn_swap = rcopy(dattn.at[y], dattn.at[y], ysem.at[0], ysem.at[1], yn)
    attn_swap.start()
    first(3)
    first(2)
    w_out.wait()
    attn_swap.wait_recv()
    full = dattn[...].reshape(toks, width)
    dmix[...] = nn(full, wa[...]).astype(bf16)
    w_value.start()

    scale = HD ** (-0.5)
    def turn_back(values):
        return values * cosine[...] - pltpu.roll(values, HD // 2, 1) * sine[...]
    @pl.loop(0, heads)
    def _(n):
        @pl.when(n == 2)
        def _():
            second(3); first(1)
        @pl.when(n == 5)
        def _():
            second(2); third(3); first(0)
        w = pl.ds(pl.multiple_of(n * HD, HD), HD)
        qh, kh, vh, doh = qr[:, w], kr[:, w], vr[:, w], dmix[:, w]
        scores = nt(qh, kh) * scale
        ahead = lax.broadcasted_iota(jnp.int32, (toks, toks), 0) >= lax.broadcasted_iota(jnp.int32, (toks, toks), 1)
        scores = jnp.where(ahead, scores, -1e30)
        expo = jnp.exp(scores - jnp.max(scores, axis=1, keepdims=True))
        probs = expo * (1.0 / jnp.sum(expo, axis=1, keepdims=True))
        dv[:, w] = lax.dot_general(
            probs.astype(bf16), doh, (((0,), (0,)), ((), ())), preferred_element_type=f32
        ).astype(bf16)
        dprob = nt(doh, vh)
        delta = jnp.sum(probs * dprob, axis=1, keepdims=True)
        ds = (probs * (dprob - delta)).astype(bf16)
        dq[:, w] = turn_back(nn(ds, kh) * scale).astype(bf16)
        dkr = lax.dot_general(ds, qh, (((0,), (0,)), ((), ())), preferred_element_type=f32)
        dk[:, w] = turn_back(dkr * scale).astype(bf16)

    w_query.wait(); w_key.wait(); w_value.wait()
    for n in range(0, width, 512):
        w = pl.ds(n, 512)
        out = nt(dq[...], wb[w, :]) + nt(dk[...], wc[w, :]) + nt(dv[...], wa[w, :])
        da1[0, :, w] = out[:rows]
        da1[1, :, w] = out[rows:]
    @pl.loop(0, rows // 16)
    def _(r):
        q = pl.ds(pl.multiple_of(r * 16, 16), 16)
        send1[q] = da1[1 - y, q].astype(bf16)
    da1_swap = rcopy(send1, recv1, ysem.at[2], ysem.at[3], yn)
    da1_swap.start()
    second(1); third(2)
    da1_swap.wait_recv()
    @pl.loop(0, rows // 16)
    def _(r):
        q = pl.ds(pl.multiple_of(r * 16, 16), 16)
        back, terms = norm_back(
            x_in[pl.ds(pl.multiple_of(y * rows + r * 16, 16), 16)].astype(f32), gain1[...], da1[y, q] + recv1[q].astype(f32)
        )
        tok_half[q] = (back + dx2[q]).astype(bf16)
        g1[...] += jnp.sum(terms, axis=0, keepdims=True)
    second(0); third(1); third(0)
    @pl.loop(0, rows // 16)
    def _(r):
        q = pl.ds(pl.multiple_of(r * 16, 16), 16)
        out_half[q] = (x_mid[q] + ic[at(z, x, y), q].astype(f32)).astype(bf16)
    for swap in (attn_swap, da1_swap):
        swap.wait_send()
    for s in range(4):
        rx0(s).wait_send(); ry1(s).wait_send()
        for q in (0, 1):
            ry0(s, q).wait_send(); rx1(s, q).wait_send()
            for r in (0, 1):
                cross(s, q, r).wait_send()
        @pl.when(s > z)
        def _(): zu(s).wait_send()
        @pl.when(s < z)
        def _(): zd(s).wait_send()

def attention_back(part, grad2, x_mid, dy, x_in, gain1, gain2, weights, qr, kr, vr, cosine, sine, cid):
    rows, width = x_mid.shape
    toks, hw = qr.shape
    h = 48
    f32, bf16 = jnp.float32, jnp.bfloat16
    D = pltpu.SemaphoreType.DMA
    S = jax.ShapeDtypeStruct
    any_ = pl.BlockSpec(memory_space=pl.ANY)
    vm = pl.BlockSpec(memory_space=pltpu.VMEM)
    V = lambda *shape, t=bf16: pltpu.VMEM(shape, t)
    return pl.pallas_call(
        attention_back_kernel,
        out_shape=[
            S((rows, width), bf16), S((rows, width), bf16), S((2, rows, width), bf16),
            S((toks, hw), bf16), S((toks, hw), bf16), S((toks, hw), bf16), S((1, width), f32), S((1, width), f32),
        ],
        in_specs=[any_] + [vm] * 6 + [any_] * 4 + [vm] * 5,
        out_specs=[vm] * 8,
        scratch_shapes=[
            V(16, rows, width), V(4, rows, width), V(8, h, width), V(4, h, width), V(8, rows - h, width), V(4, rows - h, width),
            V(4, rows, width), V(4, rows, width),
            V(width, hw), V(width, hw), V(width, hw), V(toks, hw), V(rows, width, t=f32), V(2, rows, width, t=f32),
            V(rows, width), V(rows, width),
            D((4,)), D((4,)), D((4,)), D((16,)), D((16,)), D((4, 2)), D((4, 2)), D((4,)), D((4,)), D((4, 2)), D((4, 2)), D((4,)), D((4,)),
            D((4,)), D((4,)), D((4,)), D((4,)),
        ],
        compiler_params=pltpu.CompilerParams(collective_id=cid, has_side_effects=True, vmem_limit_bytes=63 << 20),
        name="attention_back",
    )(part, grad2, x_mid, dy, x_in, gain1, gain2, *weights, qr, kr, vr, cosine, sine)

def weight_grad_kernel(
    a1, dattn, dq, dk, dv, mixed, gains, out_half, tok_half,
    oq, ok, ov, oo, og, out_full, tok_full,
    acc, ic, ix, izu, izd, gc, gx, gu, gd, gy, gbuf,
    cs, cr, xs, xr, zus, zur, zds, zdr, gss, gsr, fsem,
):
    f32, bf16 = jnp.float32, jnp.bfloat16
    z, x, y, c = place()
    xn, yn, cn = dev(z, 1 - x, y, c), dev(z, x, 1 - y, c), dev(z, x, y, 1 - c)
    n, depth = 4, acc.shape[2]
    outs = (oq, ok, ov, oo)
    greet(z, x, y, c)
    def pos(s, xx, cc): return (s * 2 + xx) * 2 + cc
    def wc(a, s, xx):
        i = s * 2 + xx
        return rcopy(acc.at[a, pos(s, xx, 1 - c)], ic.at[a, i], cs.at[a, i], cr.at[a, i], cn)
    def wx(a, s):
        return rcopy(acc.at[a, pos(s, 1 - x, c)], ix.at[a, s], xs.at[a, s], xr.at[a, s], xn)
    def zu(a, s):
        return rcopy(acc.at[a, pos(s, x, c)], izu.at[a, s], zus.at[a, s], zur.at[a, s], dev(z + 1, x, y, c))
    def zd(a, s):
        return rcopy(acc.at[a, pos(s, x, c)], izd.at[a, s], zds.at[a, s], zdr.at[a, s], dev(z - 1, x, y, c))
    def add(a, i, src, j):
        @pl.loop(0, depth // 16)
        def _(r):
            b = pl.ds(pl.multiple_of(r * 16, 16), 16)
            acc[a, i, b] = acc[a, i, b] + src[a, j, b]
    def make(g):
        s = nearest(z, g)
        w = pl.ds(pl.multiple_of(s * 4 * depth, 4 * depth), 4 * depth)
        for a, (left, right) in ((3, (dattn, mixed)), (0, (a1, dq)), (1, (a1, dk)), (2, (a1, dv))):
            out = lax.dot_general(left[:, w], right[...], (((0,), (0,)), ((), ())), preferred_element_type=f32).astype(bf16)
            for i in range(4):
                acc[a, s * 4 + i] = out[i * depth:(i + 1) * depth]
            for q in (0, 1):
                wc(a, s, q).start()
    def first(g):
        s = nearest(z, g)
        for a in (3, 0, 1, 2):
            for q in (0, 1):
                wc(a, s, q).wait_recv()
                add(a, pos(s, q, c), ic, s * 2 + q)
            wx(a, s).start()
    def second(g):
        s = nearest(z, g)
        for a in (3, 0, 1, 2):
            wx(a, s).wait_recv(); add(a, pos(s, x, c), ix, s)
            @pl.when((s >= z) & (z > 0))
            def _():
                zu(a, s).wait_recv(); add(a, pos(s, x, c), izu, s)
            @pl.when((s <= z) & (z < 3))
            def _():
                zd(a, s).wait_recv(); add(a, pos(s, x, c), izd, s)
            @pl.when(s > z)
            def _(): zu(a, s).start()
            @pl.when(s < z)
            def _(): zd(a, s).start()
    g_c = rcopy(gains.at[1 - c], gc, gss.at[0], gsr.at[0], cn)
    g_x = rcopy(gbuf.at[1 - x], gx, gss.at[1], gsr.at[1], xn)
    g_u = rcopy(gu.at[1], gu.at[0], gss.at[2], gsr.at[2], dev(z + 1, x, y, c))
    g_d = rcopy(gd.at[1], gd.at[0], gss.at[3], gsr.at[3], dev(z - 1, x, y, c))
    g_y = rcopy(gy.at[0], gy.at[1], gss.at[4], gsr.at[4], yn)
    swaps = [
        rcopy(a, b.at[y], fsem.at[i], fsem.at[i + 2], yn) for i, (a, b) in enumerate(((out_half, out_full), (tok_half, tok_full)))
    ]
    g_c.start()
    make(3); make(2)
    for swap in swaps:
        swap.start()
    out_full[y] = out_half[...]
    tok_full[y] = tok_half[...]
    g_c.wait_recv()
    gbuf[...] = gains[c] + gc[...]
    g_x.start()
    first(3); make(1); first(2); make(0)
    g_x.wait_recv()
    gbuf[x] = gbuf[x] + gx[...]
    second(3)
    gu[1] = gbuf[x]
    gd[1] = gbuf[x]
    @pl.when(z > 0)
    def _():
        g_u.wait_recv()
        gu[1] = gu[1] + gu[0]
    @pl.when(z < 3)
    def _():
        g_u.start()
    first(1)
    second(2)
    @pl.when(z < 3)
    def _():
        g_d.wait_recv()
        gd[1] = gd[1] + gd[0]
    @pl.when(z > 0)
    def _():
        g_d.start()
    first(0)
    second(1)
    gy[0] = gu[1, z] + gd[1, z] - gbuf[x, z]
    g_y.start()
    second(0)
    for a in range(n):
        outs[a][...] = acc[a, pos(z, x, c)].astype(f32)
    g_y.wait_recv()
    og[...] = gy[0] + gy[1]
    for swap in swaps:
        swap.wait()
    g_c.wait_send(); g_x.wait_send(); g_y.wait_send()
    @pl.when(z < 3)
    def _(): g_u.wait_send()
    @pl.when(z > 0)
    def _(): g_d.wait_send()
    for s in range(4):
        for a in range(n):
            for q in (0, 1): wc(a, s, q).wait_send()
            wx(a, s).wait_send()
            @pl.when(s > z)
            def _(): zu(a, s).wait_send()
            @pl.when(s < z)
            def _(): zd(a, s).wait_send()

def weight_grads(a1, dattn, dq, dk, dv, mixed, gains, out_half, tok_half, cid):
    toks, width = a1.shape
    hw = dq.shape[1]
    depth = width // 16
    f32, bf16 = jnp.float32, jnp.bfloat16
    D = pltpu.SemaphoreType.DMA
    S = jax.ShapeDtypeStruct
    vm = pl.BlockSpec(memory_space=pltpu.VMEM)
    V = lambda *shape, t=bf16: pltpu.VMEM(shape, t)
    return pl.pallas_call(
        weight_grad_kernel,
        out_shape=[S((depth, hw), f32)] * 4 + [S((8, 128), f32)] + [S((2,) + out_half.shape, bf16)] * 2,
        in_specs=[vm] * 9,
        out_specs=[vm] * 7,
        scratch_shapes=[
            V(4, 16, depth, hw), V(4, 8, depth, hw), V(4, 4, depth, hw), V(4, 4, depth, hw), V(4, 4, depth, hw),
            V(2, 4, 8, 128, t=f32), V(4, 8, 128, t=f32), V(2, 4, 8, 128, t=f32), V(2, 4, 8, 128, t=f32), V(2, 8, 128, t=f32), V(2, 4, 8, 128, t=f32),
            D((4, 8)), D((4, 8)), D((4, 4)), D((4, 4)), D((4, 4)), D((4, 4)), D((4, 4)), D((4, 4)), D((5,)), D((5,)), D((4,)),
        ],
        compiler_params=pltpu.CompilerParams(collective_id=cid, has_side_effects=True, vmem_limit_bytes=60 << 20),
        name="weight_grads",
    )(a1, dattn, dq, dk, dv, mixed, gains, out_half, tok_half)


def expert_grads_kernel(deg, deu, eh, dsgu, hs, rows, deo, act, dy, e_gate, e_up, e_down, gu, down):
    def tn(left, right):
        return lax.dot_general(left, right, (((0,), (0,)), ((), ())), preferred_element_type=jnp.float32)
    gu[...] = tn(act[...], dsgu[...]).astype(gu.dtype)
    down[...] = tn(dy[...], hs[...]).astype(down.dtype)
    e_gate[...] = tn(deg[...], rows[...])
    e_up[...] = tn(deu[...], rows[...])
    e_down[...] = tn(eh[...], deo[...])


def expert_grads(deg, deu, eh, dsgu, hs, rows, deo, act, dy):
    width = rows.shape[1]
    S = jax.ShapeDtypeStruct
    whole = lambda a: pl.BlockSpec(a.shape, lambda i: (0, 0), pipeline_mode=pl.Buffered(1))
    tile = lambda n: pl.BlockSpec((n, 256), lambda i: (0, i))
    hidden = deg.shape[1]
    return pl.pallas_call(
        expert_grads_kernel,
        grid=(width // 256,),
        out_shape=[S((hidden, width), jnp.float32)] * 3 + [S((width, 256), jnp.bfloat16), S((width, 128), jnp.bfloat16)],
        in_specs=[whole(a) for a in (deg, deu, eh, dsgu, hs)] + [tile(a.shape[0]) for a in (rows, deo, act, dy)],
        out_specs=[tile(hidden)] * 3 + [pl.BlockSpec((256, n), lambda i: (i, 0)) for n in (256, 128)],
        compiler_params=pltpu.CompilerParams(vmem_limit_bytes=60 << 20),
        name="expert_grads",
    )(deg, deu, eh, dsgu, hs, rows, deo, act, dy)


def attention_kernel(
    x_in, wq_in, wk_in, wv_in, wo_in, gain_in, table_in, dy_in, wd_h, cosine, sine,
    wq_o, wk_o, wv_o, wo_o, dy_all, act1, qr, kr, vr, mixed, x_mid, act2, grow, rank_row, rank_col, gate, deo_o, deh_o,
    gland, tland, inv, wbuf, wob, wd, qa, ka, va, own_attn, send, recv, gm, dyt, deo, deh,
    wsem, lsem, dsem, ssem, ysem, zs, zr, xs, xr, cs, cr, gzs, gzr, gxs, gxr, gys, gyr, gcs, gcr,
):
    f32, bf16 = jnp.float32, jnp.bfloat16
    z, x, y, c = place()
    toks, width = x_in.shape
    rows = toks // 2
    depth, hw = wq_in.shape
    cap, hidden = deh_o.shape[1:]
    xn, yn, cn = dev(z, 1 - x, y, c), dev(z, x, 1 - y, c), dev(z, x, y, 1 - c)
    expert = (z * 2 + x) * 2 + c
    greet(z, x, y, c)
    ins = (gain_in, table_in, wq_in, wk_in, wv_in, wo_in)
    outs = (gland, tland, wq_o, wk_o, wv_o, wo_o)
    n = len(outs)
    def pos(s, xx, cc): return (s * 2 + xx) * 2 + cc
    owns = [pltpu.make_async_copy(ins[a], outs[a].at[expert], lsem.at[a]) for a in range(n)]
    own_rows = pl.ds(pl.multiple_of(y * rows, rows), rows)
    owns.append(pltpu.make_async_copy(dy_in.at[own_rows], dy_all.at[blk(z, x, y, c)], lsem.at[n]))
    for o in owns:
        o.start()
    w_down = pltpu.make_async_copy(wd_h, wd, wsem.at[3])
    w_down.start()

    def wz(a, s, up):
        r = outs[a].at[pos(s, x, c)]
        return rcopy(r, r, zs.at[a, s, up], zr.at[a, s], dev(z + 2 * up - 1, x, y, c))
    def wx(a, s):
        r = outs[a].at[pos(s, x, c)]
        return rcopy(r, r, xs.at[a, s], xr.at[a, s], xn)
    def wc(a, s, xx):
        r = outs[a].at[pos(s, xx, c)]
        return rcopy(r, r, cs.at[a, s * 2 + xx], cr.at[a, s * 2 + xx], cn)
    half = rows - 48
    halves = (pl.ds(0, half), pl.ds(half, rows - half))
    def piece(s, xx, yy, p):
        return dy_all.at[blk(s, xx, yy, c), halves[p]]
    def gz(s, xx, p, up):
        r = piece(s, xx, y, p)
        i = 0 if p == 0 else 1 + xx
        return rcopy(r, r, gzs.at[i, s, up], gzr.at[i, s], dev(z + 2 * up - 1, x, y, c))
    def gx(s, p):
        r = piece(s, x, y, p)
        return rcopy(r, r, gxs.at[p, s], gxr.at[p, s], xn)
    def gy(s, xx, p):
        r = piece(s, xx, y, p)
        return rcopy(r, r, gys.at[p, s, xx], gyr.at[p, s, xx], yn)
    def gc(s, xx, yy, p):
        r = piece(s, xx, yy, p)
        return rcopy(r, r, gcs.at[p, s * 2 + xx, yy], gcr.at[p, s * 2 + xx, yy], cn)

    def column(s):
        for a in range(n):
            wx(a, s).start(); wc(a, s, x).start()
    def middle(g):
        s = nearest(z, g)
        for a in range(n):
            wx(a, s).wait_recv(); wc(a, s, 1 - x).start()
    def gspread(s, xx, p):
        gy(s, xx, p).start(); gc(s, xx, y, p).start()
    def gmiddle(g):
        s = nearest(z, g)
        gx(s, 0).wait_recv()
        gspread(s, 1 - x, 0)
    def glast(g):
        s = nearest(z, g)
        for q in (0, 1):
            for p in (0, 1):
                gy(s, q, p).wait_recv(); gc(s, q, 1 - y, p).start()
    def launch(fn):
        @pl.when(z < 3)
        def _(): fn(1)
        @pl.when(z > 0)
        def _(): fn(0)
    def towards(g):
        s = nearest(z, g)
        up = (s < z).astype(jnp.int32)
        nxt = z + 2 * up - 1
        return s, up, (nxt >= 0) & (nxt <= 3)
    def arrive(g):
        s, up, more = towards(g)
        for a in range(n):
            wz(a, s, up).wait_recv()
            @pl.when(more)
            def _(): wz(a, s, up).start()
        column(s)
    def garrive(g):
        s, up, more = towards(g)
        for xx, p in ((x, 0), (x, 1), (1 - x, 1)):
            gz(s, xx, p, up).wait_recv()
            @pl.when(more)
            def _(): gz(s, xx, p, up).start()
            if p == 0:
                gx(s, 0).start()
            gspread(s, xx, p)

    def project(g):
        s = nearest(z, g)
        for a in range(n):
            for q in (0, 1):
                wc(a, s, q).wait_recv()
        loads = [
            pltpu.make_async_copy(w.at[pl.ds(4 * s, 4)], wbuf.at[i], wsem.at[i])
            for i, w in enumerate((wq_o, wk_o, wv_o))
        ]
        for l in loads:
            l.start()
        for i in range(4):
            at = pl.ds(pl.multiple_of((4 * s + i) * depth, depth), depth)
            two = gland[4 * s + i][0:8].astype(f32)
            grow[:, at] = two
        w = pl.ds(pl.multiple_of(4 * s * depth, 4 * depth), 4 * depth)
        a1 = (x_in[:, w].astype(f32) * inv[...] * grow[0:1, w]).astype(bf16)
        act1[:, w] = a1
        for i, acc in enumerate((qa, ka, va)):
            loads[i].wait()
            out = nn(a1, wbuf[i].reshape(4 * depth, hw))
            if g == 0:
                acc[...] = out
            else:
                acc[...] += out

    def ranks_of(g):
        s = nearest(z, g)
        for i in range(4):
            gm[i:i + 1, :] = tland[4 * s + i, pl.ds(expert, 1), :]
        member = (gm[...] > 0.0).astype(f32).astype(bf16)
        one = lax.broadcasted_iota(jnp.int32, (toks, toks), 0)
        two = lax.broadcasted_iota(jnp.int32, (toks, toks), 1)
        upper = jnp.where(one <= two, 1.0, 0.0).astype(bf16)
        lower = jnp.where(one >= two, 1.0, 0.0).astype(bf16)
        same = jnp.where(one == two, 1.0, 0.0).astype(bf16)
        by_row = jnp.where(gm[...] > 0.0, nn(member, upper) - 1.0, -1.0).astype(jnp.int32)
        by_col = jnp.where(nt(same, member) > 0.5, nt(lower, member) - 1.0, -1.0).astype(jnp.int32)
        for i in range(4):
            rank_row[4 * s + i] = by_row[i:i + 1]
            rank_col[4 * s + i] = by_col[:, i:i + 1]
    def stores(g, xx):
        s = nearest(z, g)
        base = (s * 2 + xx) * 2
        out = []
        for k in (0, 1):
            out.append(pltpu.make_async_copy(deo.at[k], deo_o.at[base + k], ssem.at[k, 0]))
            out.append(pltpu.make_async_copy(deh.at[pl.ds(k * cap, cap)], deh_o.at[base + k], ssem.at[k, 1]))
        return out
    def hidden_grads(g):
        s = nearest(z, g)
        ranks_of(g)
        for xx in (0, 1):
            for yy in (0, 1):
                for p in (0, 1):
                    gc(s, xx, yy, p).wait_recv()
        @pl.loop(0, 2)
        def _(xx):
            base = (s * 2 + xx) * 2
            loads = [pltpu.make_async_copy(dy_all.at[pl.ds(2 * (base + k), 2)], dyt.at[k], dsem.at[k]) for k in (0, 1)]
            for l in loads:
                l.start()
            if g > 0:
                @pl.when(xx == 0)
                def _():
                    for copy in stores(g - 1, 1):
                        copy.wait()
            @pl.when(xx == 1)
            def _():
                for copy in stores(g, 0):
                    copy.wait()
            for k in (0, 1):
                loads[k].wait()
                hit = rank_row[base + k] == lax.broadcasted_iota(jnp.int32, (cap, toks), 0)
                weight = jnp.sum(jnp.where(hit, tland[base + k, pl.ds(expert, 1), :], 0.0), axis=1, keepdims=True)
                gate[base + k] = weight
                pick = jnp.where(hit, 1.0, 0.0).astype(bf16)
                grads = dyt[k].reshape(toks, width)
                for m in range(0, width, 512):
                    deo[k, :, m:m + 512] = (nn(pick, grads[:, m:m + 512]) * weight).astype(bf16)
            deh[...] = nt(deo[...].reshape(2 * cap, width), wd[...])
            for copy in stores(g, xx):
                copy.start()

    for o in owns:
        o.wait()
    gx(z, 1).start()
    launch(lambda up: [wz(a, z, up).start() for a in range(n)])
    column(z)
    launch(lambda up: gz(z, x, 0, up).start())
    launch(lambda up: gz(z, x, 1, up).start())
    gx(z, 0).start()
    gspread(z, x, 0); gspread(z, x, 1)
    @pl.loop(0, toks // 16)
    def _(r):
        q = pl.ds(pl.multiple_of(r * 16, 16), 16)
        v = x_in[q].astype(f32)
        inv[q] = lax.rsqrt(jnp.sum(v * v, axis=1, keepdims=True) * (1.0 / width) + EPS)
    gm[...] = jnp.zeros_like(gm)
    w_down.wait()
    gx(z, 1).wait_recv()
    launch(lambda up: gz(z, 1 - x, 1, up).start())
    gspread(z, 1 - x, 1)
    arrive(1); middle(0); project(0)
    garrive(1); gmiddle(0)
    arrive(2); middle(1); project(1)
    garrive(2); gmiddle(1); glast(0)
    hidden_grads(0)
    arrive(3); middle(2); project(2)
    garrive(3); gmiddle(2); glast(1)
    hidden_grads(1)
    middle(3); project(3)
    w_out = pltpu.make_async_copy(wo_o, wob, wsem.at[3])
    w_out.start()

    scale = HD ** (-0.5)
    def turn(values):
        return values * cosine[...] + pltpu.roll(values, HD // 2, 1) * sine[...]
    @pl.loop(0, hw // HD)
    def _(i):
        @pl.when(i == 4)
        def _(): gmiddle(3)
        w = pl.ds(pl.multiple_of(i * HD, HD), HD)
        qh, kh, vh = turn(qa[:, w]).astype(bf16), turn(ka[:, w]).astype(bf16), va[:, w].astype(bf16)
        qr[:, w] = qh
        kr[:, w] = kh
        vr[:, w] = vh
        scores = nt(qh, kh) * scale
        ahead = lax.broadcasted_iota(jnp.int32, (toks, toks), 0) >= lax.broadcasted_iota(jnp.int32, (toks, toks), 1)
        scores = jnp.where(ahead, scores, -1e30)
        expo = jnp.exp(scores - jnp.max(scores, axis=1, keepdims=True))
        probs = expo * (1.0 / jnp.sum(expo, axis=1, keepdims=True))
        mixed[:, w] = nn(probs.astype(bf16), vh).astype(bf16)
    w_out.wait()
    whole = wob[...].reshape(width, hw)
    other = pl.ds(pl.multiple_of((1 - y) * rows, rows), rows)
    here = pl.ds(pl.multiple_of(y * rows, rows), rows)
    for m in range(0, width, 512):
        send[:, m:m + 512] = nt(mixed[other, :], whole[m:m + 512]).astype(bf16)
    swap = rcopy(send, recv, ysem.at[0], ysem.at[1], yn)
    swap.start()
    for m in range(0, width, 512):
        own_attn[:, m:m + 512] = nt(mixed[here, :], whole[m:m + 512])
    glast(2)
    hidden_grads(2)
    swap.wait_recv()
    @pl.loop(0, rows // 16)
    def _(r):
        q = pl.ds(pl.multiple_of(r * 16, 16), 16)
        at = pl.ds(pl.multiple_of(y * rows + r * 16, 16), 16)
        v = x_in[at].astype(f32) + own_attn[q] + recv[q].astype(f32)
        x_mid[q] = v
        scaled = v * lax.rsqrt(jnp.sum(v * v, axis=1, keepdims=True) * (1.0 / width) + EPS)
        act2[q] = (scaled * grow[1:2]).astype(bf16)
    glast(3)
    hidden_grads(3)
    for copy in stores(3, 1):
        copy.wait()
    swap.wait_send()
    gx(z, 1).wait_send()
    for s in range(4):
        for a in range(n):
            wx(a, s).wait_send()
            for q in (0, 1):
                wc(a, s, q).wait_send()
        gx(s, 0).wait_send()
        for q in (0, 1):
            for p in (0, 1):
                gy(s, q, p).wait_send()
                for r in (0, 1):
                    gc(s, q, r, p).wait_send()
        @pl.when((z < 3) & (s <= z))
        def _():
            for xx, p in ((x, 0), (x, 1), (1 - x, 1)):
                gz(s, xx, p, 1).wait_send()
            for a in range(n):
                wz(a, s, 1).wait_send()
        @pl.when((z > 0) & (s >= z))
        def _():
            for xx, p in ((x, 0), (x, 1), (1 - x, 1)):
                gz(s, xx, p, 0).wait_send()
            for a in range(n):
                wz(a, s, 0).wait_send()

def attention_layer(x_in, weights, gains, table, dy, wd, cosine, sine, cap, cid):
    toks, width = x_in.shape
    depth, hw = weights[0].shape
    rows = toks // 2
    hidden = wd.shape[0]
    n = 6
    f32, bf16, i32 = jnp.float32, jnp.bfloat16, jnp.int32
    D = pltpu.SemaphoreType.DMA
    S = jax.ShapeDtypeStruct
    any_ = pl.BlockSpec(memory_space=pl.ANY)
    vm = pl.BlockSpec(memory_space=pltpu.VMEM)
    V = lambda *shape, t=bf16: pltpu.VMEM(shape, t)
    return pl.pallas_call(
        attention_kernel,
        out_shape=[S((16, depth, hw), bf16)] * 4
        + [S((32, rows, width), bf16), S((toks, width), bf16)]
        + [S((toks, hw), bf16)] * 4
        + [
            S((rows, width), f32), S((rows, width), bf16), S((8, width), f32), S((16, 1, toks), i32), S((16, toks, 1), i32),
            S((16, cap, 1), f32), S((16, cap, width), bf16), S((16, cap, hidden), f32),
        ],
        in_specs=[vm] * 8 + [any_] + [vm] * 2,
        out_specs=[any_] * 5 + [vm] * 11 + [any_] * 2,
        scratch_shapes=[
            V(16, *gains.shape), V(16, *table.shape, t=f32), V(toks, 1, t=f32), V(3, 4, depth, hw), V(16, depth, hw), V(hidden, width),
            V(toks, hw, t=f32), V(toks, hw, t=f32), V(toks, hw, t=f32), V(rows, width, t=f32), V(rows, width), V(rows, width),
            V(8, toks, t=f32), V(2, 2, rows, width), V(2, cap, width), V(2 * cap, hidden, t=f32),
            D((4,)), D((n + 1,)), D((2,)), D((2, 2)), D((2,)),
            D((n, 4, 2)), D((n, 4)), D((n, 4)), D((n, 4)), D((n, 8)), D((n, 8)),
            D((3, 4, 2)), D((3, 4)), D((2, 4)), D((2, 4)), D((2, 4, 2)), D((2, 4, 2)), D((2, 8, 2)), D((2, 8, 2)),
        ],
        compiler_params=pltpu.CompilerParams(collective_id=cid, has_side_effects=True, vmem_limit_bytes=60 << 20),
        name="attention_layer",
    )(x_in, *weights, gains, table, dy, wd, cosine, sine)


def on_device(
    tokens,
    cotangent,
    route_ids,
    route_gates,
    gain_first,
    w_query,
    w_key,
    w_value,
    w_output,
    gain_second,
    shared_gate,
    shared_up,
    shared_down,
    expert_gate,
    expert_up,
    expert_down,
):
    f32, bf16 = jnp.float32, jnp.bfloat16
    rows_dev, width = tokens.shape
    topk = route_ids.shape[1]
    experts = lax.axis_size("dp")
    capacity = rows_dev * topk * 4 // (3 * experts)
    slots = experts * capacity
    positions = jnp.arange(rows_dev, dtype=f32)
    freqs = 10000.0 ** (-2.0 * jnp.arange(HD // 2, dtype=f32) / HD)
    angles = positions[:, None] * freqs[None, :]
    cosine = jnp.concatenate([jnp.cos(angles)] * 2, axis=1)
    sine = jnp.concatenate([-jnp.sin(angles), jnp.sin(angles)], axis=1)
    chosen = route_ids[:, :, None] == jnp.arange(experts, dtype=jnp.int32)[None, None, :]
    table = jnp.sum(jnp.where(chosen, route_gates[:, :, None], 0.0), axis=1)
    gains = jnp.concatenate([gain_first[None], gain_second[None], jnp.zeros((14, gain_first.shape[0]), bf16)])
    exp_gate, exp_up, exp_down = expert_gate[0].T, expert_up[0].T, expert_down[0]

    depth, common_width = shared_gate.shape
    common_dev = common_width // experts
    packed = jnp.stack([shared_gate, shared_up, shared_down])
    packed = packed.reshape(3, depth, experts, common_dev).transpose(2, 0, 1, 3)
    packed = lax.all_to_all(packed, "dp", split_axis=0, concat_axis=0, tiled=True)
    packed = packed.transpose(1, 0, 2, 3).reshape(3, width, common_dev)
    front = capacity - 128
    back = 128 - front - common_dev

    def widen(w):
        return jnp.pad(w, ((0, 0), (front, back)))

    common_gu = jnp.concatenate([widen(packed[0]), widen(packed[1])], axis=1)
    common_down = widen(packed[2])

    (
        query_whole, key_whole, value_whole, output_whole, grad_all, act_one, query_rot, key_rot, value_low, mixed,
        x_mid, act_two, gain_rows, rank_row, rank_col, slot_gate, rows_out_grad, hidden_rows_grad,
    ) = attention_layer(
        tokens, (w_query, w_key, w_value, w_output), gains, table.T, cotangent, exp_down, cosine, sine, capacity, 0
    )
    weights = [w.reshape(width, -1) for w in (query_whole, key_whole, value_whole, output_whole)]

    total_grad, act_all, rows, hidden_rows, gate_rows_grad, up_rows_grad, common_hidden, common_gu_grad, unused, ffn = (
        expert_layer(
            act_two, hidden_rows_grad, grad_all, rank_row, rank_col, slot_gate,
            exp_gate, exp_up, exp_down, common_gu, common_down.T[front:], common_down, 1,
        )
    )
    act_all = act_all.reshape(-1, width)
    grad_all = grad_all.reshape(-1, width)
    rows = rows.reshape(slots, width)
    rows_out_grad = rows_out_grad.reshape(slots, width)
    hidden_rows = hidden_rows.reshape(slots, -1)
    common_hidden = common_hidden.reshape(-1, 128)
    common_gu_grad = common_gu_grad.reshape(-1, 256)
    expert_gate_grad, expert_up_grad, expert_down_grad, gu_grad, down_grad = expert_grads(
        gate_rows_grad.reshape(slots, -1), up_rows_grad.reshape(slots, -1), hidden_rows,
        common_gu_grad, common_hidden, rows, rows_out_grad, act_all, grad_all,
    )
    common_w_grad = jnp.concatenate(
        [w[:, front : front + common_dev] for w in (gu_grad[:, :128], gu_grad[:, 128:], down_grad)], axis=1
    )
    common_w_grad = common_w_grad.reshape(experts, depth, 3 * common_dev)
    common_w_grad = lax.all_to_all(common_w_grad, "dp", split_axis=0, concat_axis=0, tiled=True)
    common_w_grad = common_w_grad.reshape(experts, depth, 3, common_dev).transpose(2, 1, 0, 3)
    common_w_grad = common_w_grad.reshape(3, depth, common_width).astype(f32)

    layer_out, tokens_grad, attn_grad, query_grad, key_grad, value_grad, gain_one_grad, gain_two_grad = attention_back(
        ffn,
        total_grad,
        x_mid,
        cotangent,
        tokens,
        gain_rows[0:1],
        gain_rows[1:2],
        weights,
        query_rot,
        key_rot,
        value_low,
        cosine,
        sine,
        2,
    )
    gains = jnp.concatenate([gain_one_grad, gain_two_grad, jnp.zeros((6, width), f32)])
    gains = gains.reshape(8, 4, 2, 2, width // 16).transpose(3, 2, 1, 0, 4)
    query_sum, key_sum, value_sum, output_sum, gain_grads, layer_out, tokens_grad = weight_grads(
        act_one, attn_grad.reshape(rows_dev, width), query_grad, key_grad, value_grad, mixed, gains, layer_out, tokens_grad, 4
    )
    return (
        layer_out.reshape(rows_dev, width),
        tokens_grad.reshape(rows_dev, width),
        gain_grads[0],
        query_sum,
        key_sum,
        value_sum,
        output_sum,
        gain_grads[1],
        common_w_grad[0],
        common_w_grad[1],
        common_w_grad[2],
        expert_gate_grad.T[None],
        expert_up_grad.T[None],
        expert_down_grad[None],
    )


def solution(mesh):
    body = on_device if (mesh.shape["dp"], mesh.shape["tensor"]) == (16, 2) else on_device_plain
    in_specs = (
        P("dp", None),
        P("dp", None),
        P("dp", None),
        P("dp", None),
        P("dp"),
        P("dp", "tensor"),
        P("dp", "tensor"),
        P("dp", "tensor"),
        P("dp", "tensor"),
        P("dp"),
        P("dp", "tensor"),
        P("dp", "tensor"),
        P("dp", "tensor"),
        P("dp", None, "tensor"),
        P("dp", None, "tensor"),
        P("dp", "tensor", None),
    )
    out_specs = (
        P("dp", None),
        P("dp", None),
        P("dp"),
        P("dp", "tensor"),
        P("dp", "tensor"),
        P("dp", "tensor"),
        P("dp", "tensor"),
        P("dp"),
        P("dp", "tensor"),
        P("dp", "tensor"),
        P("dp", "tensor"),
        P("dp", None, "tensor"),
        P("dp", None, "tensor"),
        P("dp", "tensor", None),
    )
    return jax.shard_map(
        body, mesh=mesh, in_specs=in_specs, out_specs=out_specs, check_vma=False
    )
```

```python
import functools

import jax
import jax.numpy as jnp
from jax import lax
from jax.experimental import pallas as pl
from jax.experimental.pallas import tpu as pltpu
from jax.sharding import PartitionSpec as P

HD = 128
MESH = pl.DeviceIdType.MESH


EPS = 1e-06


def rms_norm(values, gain):
    mean_square = jnp.mean(values * values, axis=-1, keepdims=True)
    return values * lax.rsqrt(mean_square + EPS) * gain


def rotate(values, positions):
    head = values.shape[-1]
    half = head // 2
    freqs = 10000.0 ** (-2.0 * jnp.arange(half, dtype=jnp.float32) / head)
    angles = positions[:, None] * freqs[None, :]
    cosine = jnp.cos(angles)[:, None, :]
    sine = jnp.sin(angles)[:, None, :]
    first = values[..., :half]
    second = values[..., half:]
    return jnp.concatenate(
        [first * cosine - second * sine, second * cosine + first * sine], axis=-1
    )


def gated(gate_pre, up_pre):
    return gate_pre * jax.nn.sigmoid(gate_pre) * up_pre


def contract_last(left, right):
    return lax.dot_general(
        left, right, (((1,), (1,)), ((), ())), preferred_element_type=jnp.float32
    )


def contract_first(left, right):
    return lax.dot_general(
        left, right, (((0,), (0,)), ((), ())), preferred_element_type=jnp.float32
    )


def masked_scores(query_rot, key_rot, causal, scale):
    scores = (
        jnp.einsum("qhc,khc->hqk", query_rot, key_rot, preferred_element_type=jnp.float32) * scale
    )
    return jnp.where(causal[None], scores, -1e30)


def on_device_plain(
    tokens,
    cotangent,
    route_ids,
    route_gates,
    gain_first,
    w_query,
    w_key,
    w_value,
    w_output,
    gain_second,
    shared_gate,
    shared_up,
    shared_down,
    expert_gate,
    expert_up,
    expert_down,
):
    rows_dev, width = tokens.shape
    topk = route_ids.shape[1]
    experts = lax.axis_size("dp")
    capacity = rows_dev * topk * 4 // (3 * experts)
    slots = experts * capacity
    scale = HD ** (-0.5)
    positions = jnp.arange(rows_dev, dtype=jnp.float32)
    causal = jnp.arange(rows_dev)[:, None] >= jnp.arange(rows_dev)[None, :]
    gain_one, query_whole, key_whole, value_whole, output_whole = (
        lax.all_gather(gain_first, "dp", axis=0, tiled=True),
        lax.all_gather(w_query, "dp", axis=0, tiled=True),
        lax.all_gather(w_key, "dp", axis=0, tiled=True),
        lax.all_gather(w_value, "dp", axis=0, tiled=True),
        lax.all_gather(w_output, "dp", axis=0, tiled=True),
    )
    gain_two, common_gate, common_up, common_down = (
        lax.all_gather(gain_second, "dp", axis=0, tiled=True),
        lax.all_gather(shared_gate, "dp", axis=0, tiled=True),
        lax.all_gather(shared_up, "dp", axis=0, tiled=True),
        lax.all_gather(shared_down, "dp", axis=0, tiled=True),
    )
    gain_one = gain_one.astype(jnp.float32)
    gain_two = gain_two.astype(jnp.float32)
    x_in = tokens.astype(jnp.float32)
    act_one = rms_norm(x_in, gain_one).astype(jnp.bfloat16)
    heads_dev = query_whole.shape[1] // HD
    query_pre = jnp.dot(act_one, query_whole, preferred_element_type=jnp.float32).reshape(
        rows_dev, heads_dev, HD
    )
    key_pre = jnp.dot(act_one, key_whole, preferred_element_type=jnp.float32).reshape(
        rows_dev, heads_dev, HD
    )
    query_rot = rotate(query_pre, positions).astype(jnp.bfloat16)
    key_rot = rotate(key_pre, positions).astype(jnp.bfloat16)
    value_low = (
        jnp.dot(act_one, value_whole, preferred_element_type=jnp.float32)
        .astype(jnp.bfloat16)
        .reshape(rows_dev, heads_dev, HD)
    )
    scores = masked_scores(query_rot, key_rot, causal, scale)
    top = jnp.max(scores, axis=-1, keepdims=True)
    expo = jnp.exp(scores - top)
    total = jnp.sum(expo, axis=-1, keepdims=True)
    probs = expo / total
    log_total = top + jnp.log(total)
    mixed = jnp.einsum(
        "hqk,khc->qhc", probs.astype(jnp.bfloat16), value_low, preferred_element_type=jnp.float32
    )
    mixed = mixed.reshape(rows_dev, heads_dev * HD).astype(jnp.bfloat16)
    attn = lax.psum(contract_last(mixed, output_whole), "tensor")
    x_mid = x_in + attn
    act_two = rms_norm(x_mid, gain_two).astype(jnp.bfloat16)
    gate_pre = jnp.dot(act_two, common_gate, preferred_element_type=jnp.float32)
    up_pre = jnp.dot(act_two, common_up, preferred_element_type=jnp.float32)
    hidden_common = gated(gate_pre, up_pre).astype(jnp.bfloat16)
    common_out = contract_last(hidden_common, common_down)
    flat_ids = route_ids.reshape(-1)
    onehot = (flat_ids[:, None] == jnp.arange(experts, dtype=jnp.int32)[None, :]).astype(jnp.int32)
    ranks = jnp.sum(onehot * jnp.cumsum(onehot, axis=0), axis=1) - 1
    dest = flat_ids * capacity + ranks
    token_of = jnp.arange(rows_dev * topk, dtype=jnp.int32) // topk
    source = jnp.zeros((slots,), jnp.int32).at[dest].set(token_of)
    weight_of = jnp.zeros((slots,), jnp.float32).at[dest].set(route_gates.reshape(-1))
    filled = jnp.zeros((slots,), jnp.bool_).at[dest].set(True)
    outgoing = jnp.where(filled[:, None], act_two[source], jnp.zeros((), jnp.bfloat16)).reshape(
        experts, capacity, width
    )
    exp_gate = expert_gate[0]
    exp_up = expert_up[0]
    exp_down = expert_down[0]
    received = lax.all_to_all(outgoing, "dp", split_axis=0, concat_axis=0, tiled=True)
    sources = received.shape[0]
    count = received.shape[1]
    rows = received.reshape(sources * count, width)
    gate_rows = jnp.dot(rows, exp_gate, preferred_element_type=jnp.float32)
    up_rows = jnp.dot(rows, exp_up, preferred_element_type=jnp.float32)
    hidden_rows = gated(gate_rows, up_rows).astype(jnp.bfloat16)
    partial_value = jnp.dot(hidden_rows, exp_down, preferred_element_type=jnp.float32).reshape(
        sources, count, width
    )
    returned = lax.all_to_all(
        partial_value.astype(jnp.bfloat16), "dp", split_axis=0, concat_axis=0, tiled=True
    ).astype(partial_value.dtype)
    returned, kept_rows, kept_gate, kept_up = (
        returned,
        received,
        gate_rows.reshape(sources, count, -1),
        up_rows.reshape(sources, count, -1),
    )
    picked = returned.reshape(slots, width)[dest].reshape(rows_dev, topk, width)
    routed_part = jnp.sum(picked * route_gates[:, :, None], axis=1)
    ffn = lax.psum((common_out + routed_part).astype(jnp.bfloat16), "tensor").astype(jnp.float32)
    layer_out = (x_mid + ffn).astype(jnp.bfloat16)
    grad_out = cotangent.astype(jnp.float32)
    hidden_grad = jnp.dot(cotangent, common_down, preferred_element_type=jnp.float32)
    dummy_common, common_vjp = jax.vjp(gated, gate_pre, up_pre)
    gate_grad, up_grad = common_vjp(hidden_grad)
    gate_grad = gate_grad.astype(jnp.bfloat16)
    up_grad = up_grad.astype(jnp.bfloat16)
    common_gate_grad = contract_first(act_two, gate_grad)
    common_up_grad = contract_first(act_two, up_grad)
    common_down_grad = contract_first(cotangent, hidden_common)
    act_two_grad = contract_last(gate_grad, common_gate) + contract_last(up_grad, common_up)
    outgoing_grad = (
        (weight_of[:, None] * grad_out[source])
        .astype(jnp.bfloat16)
        .reshape(experts, capacity, width)
    )
    incoming_grad = lax.all_to_all(outgoing_grad, "dp", split_axis=0, concat_axis=0, tiled=True)
    hidden_width = kept_gate.shape[2]
    rows = kept_rows.reshape(-1, width)
    rows_out_grad = incoming_grad.reshape(-1, width)
    hidden_rows, expert_vjp = jax.vjp(
        gated, kept_gate.reshape(-1, hidden_width), kept_up.reshape(-1, hidden_width)
    )
    hidden_rows = hidden_rows.astype(jnp.bfloat16)
    hidden_rows_grad = contract_last(rows_out_grad, exp_down)
    gate_rows_grad, up_rows_grad = expert_vjp(hidden_rows_grad)
    gate_rows_grad = gate_rows_grad.astype(jnp.bfloat16)
    up_rows_grad = up_rows_grad.astype(jnp.bfloat16)
    expert_gate_grad = contract_first(rows, gate_rows_grad)[None]
    expert_up_grad = contract_first(rows, up_rows_grad)[None]
    expert_down_grad = contract_first(hidden_rows, rows_out_grad)[None]
    rows_in_grad = (
        contract_last(gate_rows_grad, exp_gate) + contract_last(up_rows_grad, exp_up)
    ).reshape(experts, capacity, width)
    returned_grad = lax.all_to_all(rows_in_grad, "dp", split_axis=0, concat_axis=0, tiled=True)
    routed_grad = jnp.sum(
        returned_grad.reshape(slots, width)[dest].reshape(rows_dev, topk, width), axis=1
    )
    act_two_total = lax.psum(act_two_grad + routed_grad, "tensor")
    dummy_second, second_vjp = jax.vjp(rms_norm, x_mid, gain_two)
    mid_norm_grad, gain_two_grad = second_vjp(act_two_total)
    mid_grad = grad_out + mid_norm_grad
    ffn_sums = (gain_two_grad, common_gate_grad, common_up_grad, common_down_grad)
    attn_grad = mid_grad.astype(jnp.bfloat16)
    output_w_grad = contract_first(attn_grad, mixed)
    mixed_grad = (
        jnp.dot(attn_grad, output_whole, preferred_element_type=jnp.float32)
        .astype(jnp.bfloat16)
        .reshape(rows_dev, heads_dev, HD)
    )
    probs_again = jnp.exp(masked_scores(query_rot, key_rot, causal, scale) - log_total)
    value_grad = jnp.einsum(
        "hqk,qhc->khc",
        probs_again.astype(jnp.bfloat16),
        mixed_grad,
        preferred_element_type=jnp.float32,
    ).astype(jnp.bfloat16)
    prob_grad = jnp.einsum(
        "qhc,khc->hqk", mixed_grad, value_low, preferred_element_type=jnp.float32
    )
    delta = jnp.sum(probs_again * prob_grad, axis=-1, keepdims=True)
    score_grad = (probs_again * (prob_grad - delta)).astype(jnp.bfloat16)
    query_rot_grad = (
        jnp.einsum("hqk,khc->qhc", score_grad, key_rot, preferred_element_type=jnp.float32) * scale
    )
    key_rot_grad = (
        jnp.einsum("hqk,qhc->khc", score_grad, query_rot, preferred_element_type=jnp.float32)
        * scale
    )

    def turn(values):
        return rotate(values, positions)

    dummy_turn, turn_vjp = jax.vjp(turn, query_pre)
    query_grad = turn_vjp(query_rot_grad)[0].reshape(rows_dev, heads_dev * HD).astype(jnp.bfloat16)
    key_grad = turn_vjp(key_rot_grad)[0].reshape(rows_dev, heads_dev * HD).astype(jnp.bfloat16)
    value_flat = value_grad.reshape(rows_dev, heads_dev * HD)
    query_w_grad = contract_first(act_one, query_grad)
    key_w_grad = contract_first(act_one, key_grad)
    value_w_grad = contract_first(act_one, value_flat)
    act_one_grad = (
        contract_last(query_grad, query_whole)
        + contract_last(key_grad, key_whole)
        + contract_last(value_flat, value_whole)
    )
    act_one_total = lax.psum(act_one_grad, "tensor")
    dummy_first, first_vjp = jax.vjp(rms_norm, x_in, gain_one)
    in_norm_grad, gain_one_grad = first_vjp(act_one_total)
    tokens_grad = (mid_grad + in_norm_grad).astype(jnp.bfloat16)
    every = (
        lax.psum_scatter(gain_one_grad, "dp", scatter_dimension=0, tiled=True),
        lax.psum_scatter(query_w_grad, "dp", scatter_dimension=0, tiled=True),
        lax.psum_scatter(key_w_grad, "dp", scatter_dimension=0, tiled=True),
        lax.psum_scatter(value_w_grad, "dp", scatter_dimension=0, tiled=True),
        lax.psum_scatter(output_w_grad, "dp", scatter_dimension=0, tiled=True),
        lax.psum_scatter(ffn_sums[0], "dp", scatter_dimension=0, tiled=True),
        lax.psum_scatter(ffn_sums[1], "dp", scatter_dimension=0, tiled=True),
        lax.psum_scatter(ffn_sums[2], "dp", scatter_dimension=0, tiled=True),
        lax.psum_scatter(ffn_sums[3], "dp", scatter_dimension=0, tiled=True),
    )
    attn_sums = every[:5]
    ffn_sums = every[5:]
    return (
        layer_out,
        tokens_grad,
        attn_sums[0],
        attn_sums[1],
        attn_sums[2],
        attn_sums[3],
        attn_sums[4],
        ffn_sums[0],
        ffn_sums[1],
        ffn_sums[2],
        ffn_sums[3],
        expert_gate_grad,
        expert_up_grad,
        expert_down_grad,
    )


def place():
    d = lax.axis_index("dp"); y = lax.axis_index("tensor")
    c = lax.rem(d, 2); x = lax.rem(lax.div(d, 2), 2); z = lax.div(d, 4)
    return z, x, y, c

def dev(z, x, y, c):
    return ((z * 2 + x) * 2 + c, y)

def blk(z, x, y, c):
    return ((z * 2 + x) * 2 + c) * 2 + y

def greet(z, x, y, c):
    bar = pltpu.get_barrier_semaphore()
    for other in (dev(z, 1 - x, y, c), dev(z, x, 1 - y, c), dev(z, x, y, 1 - c)):
        pl.semaphore_signal(bar, inc=1, device_id=other, device_id_type=MESH)
    @pl.when(z > 0)
    def _():
        pl.semaphore_signal(bar, inc=1, device_id=dev(z - 1, x, y, c), device_id_type=MESH)
    @pl.when(z < 3)
    def _():
        pl.semaphore_signal(bar, inc=1, device_id=dev(z + 1, x, y, c), device_id_type=MESH)
    pl.semaphore_wait(bar, 3 + (z > 0).astype(jnp.int32) + (z < 3).astype(jnp.int32))

def rcopy(src, dst, ssem, rsem, device):
    return pltpu.make_async_remote_copy(src_ref=src, dst_ref=dst, send_sem=ssem, recv_sem=rsem, device_id=device, device_id_type=MESH)

def nearest(z, g):
    one = jnp.where(z == 0, 1, z - 1)
    two = jnp.where(z == 3, 1, jnp.where(z == 2, 3, 2))
    three = jnp.where(z >= 2, 0, 3)
    return jnp.where(g == 0, z, jnp.where(g == 1, one, jnp.where(g == 2, two, three)))

def nt(left, right):
    return lax.dot_general(left, right, (((1,), (1,)), ((), ())), preferred_element_type=jnp.float32)

def nn(left, right):
    return jnp.dot(left, right, preferred_element_type=jnp.float32)

def greet_all(z, x, y, c):
    bar = pltpu.get_barrier_semaphore()
    for other in (dev(z, 1 - x, y, c), dev(z, x, 1 - y, c), dev(z, x, y, 1 - c)):
        pl.semaphore_signal(bar, inc=1, device_id=other, device_id_type=MESH)
    for s in range(4):
        @pl.when(s != z)
        def _(): pl.semaphore_signal(bar, inc=1, device_id=dev(s, x, y, c), device_id_type=MESH)
    pl.semaphore_wait(bar, 6)


def expert_kernel(
    a_in, deh, dy_all, rank_row, rank_col, gate, wg_h, wu_h, wd_h, sgu_h, sdt_h, sd_h,
    total, act_all, rows_o, eh_o, deg_o, deu_o, hs_o, dsgu_o, part, ffn_part, gu_o, down_o,
    wg, wu, wd, sgu, tail, acc, ic, iy0, ix0, ix1, iy1, iz,
    eg, eu, dehb, ehb, degb, deub, sd, dhs, hsb, dsgub, eh2, hs2, ot, gub, downb,
    wsem, usem, ssem, osem, psem, lsem, tsem, gsem, fsem,
    zs, zr, x0s, x0r, x1s, x1r, y0s, y0r, y1s, y1r, cs, cr,
    ls, rcs, rcr, ry0s, ry0r, rx0s, rx0r, rx1s, rx1r, ry1s, ry1r, rzs, rzr,
):
    f32, bf16 = jnp.float32, jnp.bfloat16
    z, x, y, c = place()
    rows, width = a_in.shape
    h = rows // 2
    cap = deh.shape[1]
    toks = 2 * rows
    lo, hi = pl.ds(0, h), pl.ds(h, h)
    part_of = (lo, hi)
    xn, yn, cn = dev(z, 1 - x, y, c), dev(z, x, 1 - y, c), dev(z, x, y, 1 - c)
    greet_all(z, x, y, c)
    mine = blk(z, x, y, c)
    own = pltpu.make_async_copy(a_in, act_all.at[mine], lsem)
    own.start()
    weights = [
        pltpu.make_async_copy(a, b, wsem.at[i])
        for i, (a, b) in enumerate(((wg_h, wg), (wu_h, wu), (wd_h, wd), (sgu_h, sgu), (sdt_h, tail.at[pl.ds(cap, 256 - cap)]), (sd_h, sd)))
    ]
    for w in weights:
        w.start()

    def zcopy(s, up):
        b = act_all.at[blk(s, x, y, c)]
        return rcopy(b, b, zs.at[s, up], zr.at[s], dev(z + 2 * up - 1, x, y, c))

    def half_copy(s, xx, yy, p, send, recv, to):
        b = act_all.at[blk(s, xx, yy, c), part_of[p]]
        return rcopy(b, b, send, recv, to)

    def x0(s): return half_copy(s, x, y, 0, x0s.at[s], x0r.at[s], xn)
    def y1(s): return half_copy(s, x, y, 1, y1s.at[s], y1r.at[s], yn)
    def y0(s, xx): return half_copy(s, xx, y, 0, y0s.at[s, xx], y0r.at[s, xx], yn)
    def x1(s, yy): return half_copy(s, x, yy, 1, x1s.at[s, yy], x1r.at[s, yy], xn)
    def side(s, xx, yy, p):
        i = (s * 2 + xx) * 2 + yy
        return half_copy(s, xx, yy, p, cs.at[i, p], cr.at[i, p], cn)

    def column(s):
        x0(s).start(); y1(s).start(); y0(s, x).start(); x1(s, y).start()
        side(s, x, y, 0).start(); side(s, x, y, 1).start()

    def arrive(g):
        s = nearest(z, g)
        up = (s < z).astype(jnp.int32)
        nxt = z + 2 * up - 1
        zcopy(s, up).wait_recv()
        @pl.when((nxt >= 0) & (nxt <= 3))
        def _(): zcopy(s, up).start()
        column(s)

    def middle(g):
        s = nearest(z, g)
        x0(s).wait_recv()
        y0(s, 1 - x).start(); side(s, 1 - x, y, 0).start()
        y1(s).wait_recv()
        x1(s, 1 - y).start(); side(s, x, 1 - y, 1).start()

    def last_own(g):
        s = nearest(z, g)
        y0(s, x).wait_recv(); side(s, x, 1 - y, 0).start()

    def last_other(g):
        s = nearest(z, g)
        x1(s, y).wait_recv(); side(s, 1 - x, y, 1).start()
        y0(s, 1 - x).wait_recv(); side(s, 1 - x, 1 - y, 0).start()
        x1(s, 1 - y).wait_recv(); side(s, 1 - x, 1 - y, 1).start()

    def spread_cols(j):
        ranks = rank_col[j]
        slot = lax.broadcasted_iota(jnp.int32, (toks, 128), 1)
        one = jnp.where(ranks == slot, 1.0, 0.0)
        two = jnp.where(ranks == slot + 128, 1.0, 0.0)
        return one, two

    def seq_of(u):
        s = nearest(z, u // 2)
        xx = lax.rem(x + lax.rem(u, 2), 2)
        return s, xx

    def stores(u):
        s, xx = seq_of(u)
        out = []
        for k in (0, 1):
            j = (s * 2 + xx) * 2 + k
            r = pl.ds(k * cap, cap)
            out += [
                pltpu.make_async_copy(acc.at[k], rows_o.at[j], ssem.at[k, 0]),
                pltpu.make_async_copy(ehb.at[r], eh_o.at[j], ssem.at[k, 1]),
                pltpu.make_async_copy(degb.at[r], deg_o.at[j], ssem.at[k, 2]),
                pltpu.make_async_copy(deub.at[r], deu_o.at[j], ssem.at[k, 3]),
                pltpu.make_async_copy(hsb.at[pl.ds(2 * k, 2)], hs_o.at[pl.ds(2 * j, 2)], ssem.at[k, 4]),
                pltpu.make_async_copy(dsgub.at[pl.ds(2 * k, 2)], dsgu_o.at[pl.ds(2 * j, 2)], ssem.at[k, 5]),
            ]
        return out

    def at(s, xx, yy): return (s * 2 + xx) * 2 + yy
    def keep(u, k):
        s, xx = seq_of(u)
        return pltpu.make_async_copy(acc.at[pl.ds(10 + 2 * k, 2)], part.at[pl.ds(at(s, xx, 0), 2)], ssem.at[k, 6])
    def cross(s, xx, yy, k):
        i = at(s, xx, yy)
        return rcopy(acc.at[10 + 2 * k + yy], ic.at[i], rcs.at[i], rcr.at[i], cn)
    def hand_over(u):
        s, xx = seq_of(u)
        for k in (0, 1):
            @pl.when(c == k)
            def _(): keep(u, k).start()
            @pl.when(c != k)
            def _():
                for yy in (0, 1):
                    cross(s, xx, yy, k).start()
    def handed_over(u):
        s, xx = seq_of(u)
        for k in (0, 1):
            @pl.when(c == k)
            def _(): keep(u, k).wait()
            @pl.when(c != k)
            def _():
                for yy in (0, 1):
                    cross(s, xx, yy, k).wait_send()

    def unit(u):
        s, xx = seq_of(u)
        base = (s * 2 + xx) * 2
        for k in (0, 1):
            pltpu.make_async_copy(deh.at[base + k], dehb.at[pl.ds(k * cap, cap)], usem.at[k, 1]).start()
        for yy in (0, 1):
            for p in (0, 1):
                side(s, xx, yy, p).wait_recv()
        loads = [
            pltpu.make_async_copy(act_all.at[pl.ds(2 * (base + k), 2)], acc.at[pl.ds(4 + 2 * k, 2)], usem.at[k, 0])
            for k in (0, 1)
        ]
        for k in (0, 1):
            loads[k].start()
        @pl.when(u > 0)
        def _():
            for copy in stores(u - 1):
                copy.wait()
            handed_over(u - 1)
        for k in (0, 1):
            loads[k].wait()
            act = acc[4 + 2 * k:6 + 2 * k].reshape(toks, width)
            ranks = rank_row[base + k]
            slot = lax.broadcasted_iota(jnp.int32, (cap, toks), 0)
            pick = jnp.where(ranks == slot, 1.0, 0.0).astype(bf16)
            acc[k] = nn(pick, act).astype(bf16)
            pre = nn(act, sgu[...])
            gp, up = pre[:, :128], pre[:, 128:]
            dh = dhs[base + k]
            sig = jax.nn.sigmoid(gp)
            hsb[2 * k:2 * k + 2] = (gp * sig * up).astype(bf16).reshape(2, rows, 128)
            dsgub[2 * k:2 * k + 2, :, 0:128] = (dh * up * sig * (1.0 + gp * (1.0 - sig))).astype(bf16).reshape(2, rows, 128)
            dsgub[2 * k:2 * k + 2, :, 128:256] = (dh * gp * sig).astype(bf16).reshape(2, rows, 128)
        picked = acc[0:2].reshape(2 * cap, width)
        eg[...] = nt(picked, wg[...])
        eu[...] = nt(picked, wu[...])
        for k in (0, 1):
            pltpu.make_async_copy(deh.at[base + k], dehb.at[pl.ds(k * cap, cap)], usem.at[k, 1]).wait()
        @pl.loop(0, 2 * cap // 32)
        def _(r):
            q = pl.ds(pl.multiple_of(r * 32, 32), 32)
            gp, up, dh = eg[q], eu[q], dehb[q]
            sig = jax.nn.sigmoid(gp)
            silu = gp * sig
            ehb[q] = (silu * up).astype(bf16)
            degb[q] = (dh * up * sig * (1.0 + gp * (1.0 - sig))).astype(bf16)
            deub[q] = (dh * silu).astype(bf16)
        dg, du = degb[...], deub[...]
        for n in range(0, width, 512):
            w = pl.ds(n, 512)
            back = (nn(dg, wg[:, w]) + nn(du, wu[:, w])).astype(bf16)
            acc[8, :, w] = back[:cap]
            acc[9, :, w] = back[cap:]
        for k in (0, 1):
            one, two = spread_cols(base + k)
            left = jnp.concatenate([one, two], axis=1)[:, :cap].astype(bf16)
            for n in range(0, width, 512):
                w = pl.ds(n, 512)
                out = nn(left, acc[8 + k, :, w]) + nt(dsgub[2 * k:2 * k + 2].reshape(toks, 256), sgu[w, :])
                out = out.astype(bf16)
                acc[10 + 2 * k, :, w] = out[:rows]
                acc[11 + 2 * k, :, w] = out[rows:]
        for copy in stores(u):
            copy.start()
        hand_over(u)

    def ry0(s, xx):
        return rcopy(ic.at[at(s, xx, 1 - y), lo], iy0.at[s * 2 + xx], ry0s.at[s, xx], ry0r.at[s, xx], yn)
    def rx1(s, yy):
        return rcopy(ic.at[at(s, 1 - x, yy), hi], ix1.at[s * 2 + yy], rx1s.at[s, yy], rx1r.at[s, yy], xn)
    def rx0(s):
        return rcopy(ic.at[at(s, 1 - x, y), lo], ix0.at[s], rx0s.at[s], rx0r.at[s], xn)
    def ry1(s):
        return rcopy(ic.at[at(s, x, 1 - y), hi], iy1.at[s], ry1s.at[s], ry1r.at[s], yn)
    def rz(s):
        return rcopy(ic.at[at(s, x, y)], iz.at[z], rzs.at[s], rzr.at[z], dev(s, x, y, c))
    def rz_wait(s):
        rcopy(iz.at[s], iz.at[s], rzs.at[s], rzr.at[s], dev(s, x, y, c)).wait_recv()
    def add(i, start, count, src, j):
        @pl.loop(0, count // 16)
        def _(r):
            a = pl.ds(pl.multiple_of(start + r * 16, 16), 16)
            b = pl.ds(pl.multiple_of(r * 16, 16), 16)
            ic[i, a] = ic[i, a] + src[j, b]

    def first(g):
        s = nearest(z, g)
        def load(xx, yy):
            return pltpu.make_async_copy(part.at[at(s, xx, yy)], acc.at[4 + 2 * xx + yy], ls.at[2 * xx + yy])
        for xx in (0, 1):
            for yy in (0, 1):
                load(xx, yy).start()
        for xx in (0, 1):
            for yy in (0, 1):
                load(xx, yy).wait(); cross(s, xx, yy, 0).wait_recv()
                add(at(s, xx, yy), 0, rows, acc, 4 + 2 * xx + yy)
                @pl.when(yy != y)
                def _(): ry0(s, xx).start()
                @pl.when(xx != x)
                def _(): rx1(s, yy).start()

    def second(g):
        s = nearest(z, g)
        ry0(s, 1 - x).wait_recv(); add(at(s, 1 - x, y), 0, h, iy0, s * 2 + 1 - x); rx0(s).start()
        rx1(s, 1 - y).wait_recv(); add(at(s, x, 1 - y), h, h, ix1, s * 2 + 1 - y); ry1(s).start()
        ry0(s, x).wait_recv(); add(at(s, x, y), 0, h, iy0, s * 2 + x)
        rx1(s, y).wait_recv(); add(at(s, x, y), h, h, ix1, s * 2 + y)

    def third(g):
        s = nearest(z, g)
        me = at(s, x, y)
        rx0(s).wait_recv(); add(me, 0, h, ix0, s)
        ry1(s).wait_recv(); add(me, h, h, iy1, s)
        if g > 0:
            rz(s).start()

    own.wait()
    @pl.when(z < 3)
    def _(): zcopy(z, 1).start()
    @pl.when(z > 0)
    def _(): zcopy(z, 0).start()
    column(z)
    def dy_load(j, b):
        return pltpu.make_async_copy(dy_all.at[pl.ds(2 * j, 2)], acc.at[pl.ds(2 + 12 * b, 2)], usem.at[b, 2])
    dy_load(0, 0).start()
    for w in weights:
        w.wait()
    @pl.loop(0, 8)
    def _(i):
        for b in (0, 1):
            j = 2 * i + b
            @pl.when(j < 15)
            def _(): dy_load(j + 1, 1 - b).start()
            dy_load(j, b).wait()
            dhs[j] = nn(acc[2 + 12 * b:4 + 12 * b].reshape(toks, width), sd[...])

    @pl.loop(0, 8)
    def _(u):
        @pl.when(u == 0)
        def _():
            middle(0); last_own(0); arrive(1)
        @pl.when(u == 1)
        def _():
            last_other(0); arrive(2); middle(1)
        @pl.when(u == 2)
        def _():
            arrive(3); last_own(1); middle(2)
        @pl.when(u == 3)
        def _():
            last_other(1); middle(3); first(0)
        @pl.when(u == 4)
        def _():
            last_own(2)
        @pl.when(u == 5)
        def _():
            last_other(2); first(1)
        @pl.when(u == 6)
        def _():
            last_own(3); second(0)
        @pl.when(u == 7)
        def _():
            last_other(3); first(2); third(0)
        unit(u)

    for copy in stores(7):
        copy.wait()
    handed_over(7)

    def out_loads(j, b):
        return [
            pltpu.make_async_copy(eh_o.at[j], eh2.at[b], osem.at[b, 0]),
            pltpu.make_async_copy(hs_o.at[pl.ds(2 * j, 2)], hs2.at[b], osem.at[b, 1]),
        ]
    def out_store(j, b):
        return pltpu.make_async_copy(ot.at[b], ffn_part.at[pl.ds(2 * j, 2)], psem.at[b])

    def forward_out(j):
        b = lax.rem(j, 2)
        @pl.when(j < 15)
        def _():
            for copy in out_loads(j + 1, 1 - b):
                copy.start()
        for copy in out_loads(j, b):
            copy.wait()
        @pl.when(j >= 2)
        def _(): out_store(j - 2, b).wait()
        weight = gate[j]
        for n in range(0, width, 512):
            w = pl.ds(n, 512)
            tail[0:cap, w] = (nn(eh2[b], wd[:, w]) * weight).astype(bf16)
        one, two = spread_cols(j)
        left = jnp.concatenate([one, two + hs2[b].reshape(toks, 128).astype(f32)], axis=1).astype(bf16)
        for n in range(0, width, 512):
            w = pl.ds(n, 512)
            out = nn(left, tail[:, w]).astype(bf16)
            ot[b, 0, :, w] = out[:rows]
            ot[b, 1, :, w] = out[rows:]
        out_store(j, b).start()

    for copy in out_loads(0, 0):
        copy.start()

    first(3); second(1)
    second(2); third(1)
    def tn(left, right):
        return lax.dot_general(left, right, (((0,), (0,)), ((), ())), preferred_element_type=f32)
    def flat(first, count):
        return acc[:, :, first:first + count].reshape(16 * rows, count)
    fixed = []
    for q in (0, 1):
        half = pl.ds(16 * q, 16)
        fixed.append(pltpu.make_async_copy(dsgu_o.at[half], acc.at[:, :, pl.ds(256 * q, 256)], fsem.at[q]))
        fixed.append(pltpu.make_async_copy(hs_o.at[half], acc.at[:, :, pl.ds(512 + 128 * q, 128)], fsem.at[2 + q]))
    def feature(i, b):
        return pl.ds(pl.multiple_of(lax.rem(2 * i + b, 8) * 256, 256), 256)
    def tile_load(source, i, b):
        return [
            pltpu.make_async_copy(
                source.at[pl.ds(16 * q, 16), :, feature(i, b)], acc.at[:, :, pl.ds(768 + 512 * b + 256 * q, 256)], tsem.at[b, q]
            )
            for q in (0, 1)
        ]
    def tile_start(i, b):
        @pl.when(i < 4)
        def _():
            for copy in tile_load(act_all, i, b):
                copy.start()
        @pl.when((i >= 4) & (i < 8))
        def _():
            for copy in tile_load(dy_all, i, b):
                copy.start()
    def gu_store(i, b):
        return pltpu.make_async_copy(gub.at[b], gu_o.at[feature(i, b)], gsem.at[0, b])
    def down_store(i, b):
        return pltpu.make_async_copy(downb.at[b], down_o.at[feature(i, b)], gsem.at[1, b])
    for copy in fixed:
        copy.start()
    tile_start(0, 0)
    for copy in fixed:
        copy.wait()

    @pl.loop(0, 8)
    def _(i):
        @pl.when(i == 2)
        def _():
            second(3); third(2)
        @pl.when(i == 4)
        def _(): third(3)
        for b in (0, 1):
            tile_start(i + b, 1 - b)
            forward_out(2 * i + b)
            for copy in tile_load(act_all, i, b):
                copy.wait()
            base = 768 + 512 * b
            @pl.when((i > 0) & (i < 5))
            def _(): gu_store(i, b).wait()
            @pl.when(i > 4)
            def _(): down_store(i, b).wait()
            @pl.when(i < 4)
            def _():
                out = tn(flat(base, 256), flat(0, 256)) + tn(flat(base + 256, 256), flat(256, 256))
                gub[b] = out.astype(bf16)
                gu_store(i, b).start()
            @pl.when(i >= 4)
            def _():
                out = tn(flat(base, 256), flat(512, 128)) + tn(flat(base + 256, 256), flat(640, 128))
                downb[b] = out.astype(bf16)
                down_store(i, b).start()
    for b in (0, 1):
        down_store(7, b).wait()
    me = at(z, x, y)
    for g in (1, 2, 3):
        rz_wait(nearest(z, g))
    @pl.loop(0, rows // 16)
    def _(r):
        q = pl.ds(pl.multiple_of(r * 16, 16), 16)
        out = ic[me, q].astype(f32)
        for g in (1, 2, 3):
            out = out + iz[nearest(z, g), q].astype(f32)
        total[q] = out
    out_store(14, 0).wait()
    out_store(15, 1).wait()

    for s in range(4):
        @pl.when((z < 3) & (s <= z))
        def _(): zcopy(s, 1).wait_send()
        @pl.when((z > 0) & (s >= z))
        def _(): zcopy(s, 0).wait_send()
        x0(s).wait_send(); y1(s).wait_send()
        rx0(s).wait_send(); ry1(s).wait_send()
        for q in (0, 1):
            y0(s, q).wait_send(); x1(s, q).wait_send()
            ry0(s, q).wait_send(); rx1(s, q).wait_send()
            for r in (0, 1):
                for p in (0, 1):
                    side(s, q, r, p).wait_send()
        @pl.when(s != z)
        def _():
            rz(s).wait_send()

def expert_layer(act, deh, dy_all, rank_row, rank_col, gate, wg, wu, wd, sgu, sdt, sd, cid):
    rows, width = act.shape
    cap, hidden = deh.shape[1:]
    h = rows // 2
    f32, bf16 = jnp.float32, jnp.bfloat16
    D = pltpu.SemaphoreType.DMA
    S = jax.ShapeDtypeStruct
    any_ = pl.BlockSpec(memory_space=pl.ANY)
    vm = pl.BlockSpec(memory_space=pltpu.VMEM)
    V = lambda *shape, t=bf16: pltpu.VMEM(shape, t)
    return pl.pallas_call(
        expert_kernel,
        out_shape=[
            S((rows, width), f32), S((32, rows, width), bf16), S((16, cap, width), bf16),
            S((16, cap, hidden), bf16), S((16, cap, hidden), bf16), S((16, cap, hidden), bf16),
            S((32, rows, 128), bf16), S((32, rows, 256), bf16),
            S((16, rows, width), bf16), S((32, rows, width), bf16), S((width, 256), bf16), S((width, 128), bf16),
        ],
        in_specs=[vm, any_, any_, vm, vm, vm] + [any_] * 6,
        out_specs=[vm] + [any_] * 11,
        scratch_shapes=[
            V(*wg.shape), V(*wu.shape), V(*wd.shape), V(*sgu.shape), V(256, width),
            V(16, rows, width), V(16, rows, width), V(8, h, width), V(4, h, width), V(8, h, width), V(4, h, width),
            V(4, rows, width),
            V(2 * cap, hidden, t=f32), V(2 * cap, hidden, t=f32), V(2 * cap, hidden, t=f32),
            V(2 * cap, hidden), V(2 * cap, hidden), V(2 * cap, hidden),
            V(*sd.shape), V(16, 2 * rows, 128, t=f32), V(4, rows, 128), V(4, rows, 256),
            V(2, cap, hidden), V(2, 2, rows, 128), V(2, 2, rows, width), V(2, 256, 256), V(2, 256, 128),
            D((6,)), D((2, 3)), D((2, 7)), D((2, 2)), D((2,)), D, D((2, 2)), D((2, 2)), D((4,)),
            D((4, 2)), D((4,)), D((4,)), D((4,)), D((4, 2)), D((4, 2)), D((4, 2)), D((4, 2)), D((4,)), D((4,)), D((16, 2)), D((16, 2)),
            D((4,)), D((16,)), D((16,)), D((4, 2)), D((4, 2)), D((4,)), D((4,)), D((4, 2)), D((4, 2)), D((4,)), D((4,)),
            D((4,)), D((4,)),
        ],
        compiler_params=pltpu.CompilerParams(collective_id=cid, has_side_effects=True, vmem_limit_bytes=63 << 20),
        name="expert_layer",
    )(act, deh, dy_all, rank_row, rank_col, gate, wg, wu, wd, sgu, sdt, sd)


def norm_back(values, gain, grad):
    width = values.shape[1]
    inv = lax.rsqrt(jnp.sum(values * values, axis=1, keepdims=True) * (1.0 / width) + EPS)
    scaled = grad * gain
    inner = jnp.sum(values * scaled, axis=1, keepdims=True) * (1.0 / width)
    normed = values * inv
    return inv * (scaled - normed * (inv * inner)), grad * normed

def attention_back_kernel(
    part, grad2, x_mid, dy, x_in, gain1, gain2, wq_h, wk_h, wv_h, wo_h, qr, kr, vr, cosine, sine,
    out_half, tok_half, dattn, dq, dk, dv, g1, g2,
    ic, tmp, iy0, ix0, ix1, iy1, izu, izd, wa, wb, wc, dmix, dx2, da1, send1, recv1,
    wsem, ysem, ls, rcs, rcr, ry0s, ry0r, rx0s, rx0r, rx1s, rx1r, ry1s, ry1r, zus, zur, zds, zdr,
):
    f32, bf16 = jnp.float32, jnp.bfloat16
    z, x, y, c = place()
    rows, width = x_mid.shape
    h = 48
    toks = 2 * rows
    heads = qr.shape[1] // HD
    lo, hi = pl.ds(0, h), pl.ds(h, rows - h)
    xn, yn, cn = dev(z, 1 - x, y, c), dev(z, x, 1 - y, c), dev(z, x, y, 1 - c)
    greet(z, x, y, c)

    def at(s, xx, yy): return (s * 2 + xx) * 2 + yy
    def load(s, xx, yy):
        return pltpu.make_async_copy(part.at[blk(s, xx, yy, c)], tmp.at[xx * 2 + yy], ls.at[xx * 2 + yy])
    def cross(s, xx, yy):
        i = at(s, xx, yy)
        return rcopy(part.at[blk(s, xx, yy, 1 - c)], ic.at[i], rcs.at[i], rcr.at[i], cn)
    def ry0(s, xx):
        return rcopy(ic.at[at(s, xx, 1 - y), lo], iy0.at[s * 2 + xx], ry0s.at[s, xx], ry0r.at[s, xx], yn)
    def rx1(s, yy):
        return rcopy(ic.at[at(s, 1 - x, yy), hi], ix1.at[s * 2 + yy], rx1s.at[s, yy], rx1r.at[s, yy], xn)
    def rx0(s):
        return rcopy(ic.at[at(s, 1 - x, y), lo], ix0.at[s], rx0s.at[s], rx0r.at[s], xn)
    def ry1(s):
        return rcopy(ic.at[at(s, x, 1 - y), hi], iy1.at[s], ry1s.at[s], ry1r.at[s], yn)
    def zu(s):
        return rcopy(ic.at[at(s, x, y)], izu.at[s], zus.at[s], zur.at[s], dev(z + 1, x, y, c))
    def zd(s):
        return rcopy(ic.at[at(s, x, y)], izd.at[s], zds.at[s], zdr.at[s], dev(z - 1, x, y, c))
    def add(i, start, count, src, j):
        @pl.loop(0, count // 16)
        def _(r):
            a = pl.ds(pl.multiple_of(start + r * 16, 16), 16)
            b = pl.ds(pl.multiple_of(r * 16, 16), 16)
            ic[i, a] = ic[i, a] + src[j, b]

    four = [(xx, yy) for xx in (0, 1) for yy in (0, 1)]

    def first(g):
        s = nearest(z, g)
        for xx, yy in four:
            load(s, xx, yy).wait(); cross(s, xx, yy).wait_recv()
            add(at(s, xx, yy), 0, rows, tmp, xx * 2 + yy)
            @pl.when(yy != y)
            def _(): ry0(s, xx).start()
            @pl.when(xx != x)
            def _(): rx1(s, yy).start()
        if g > 0:
            for xx, yy in four:
                load(nearest(z, g - 1), xx, yy).start()

    def second(g):
        s = nearest(z, g)
        ry0(s, 1 - x).wait_recv(); add(at(s, 1 - x, y), 0, h, iy0, s * 2 + 1 - x); rx0(s).start()
        rx1(s, 1 - y).wait_recv(); add(at(s, x, 1 - y), h, rows - h, ix1, s * 2 + 1 - y); ry1(s).start()
        ry0(s, x).wait_recv(); add(at(s, x, y), 0, h, iy0, s * 2 + x)
        rx1(s, y).wait_recv(); add(at(s, x, y), h, rows - h, ix1, s * 2 + y)

    def third(g):
        s = nearest(z, g)
        me = at(s, x, y)
        rx0(s).wait_recv(); add(me, 0, h, ix0, s)
        ry1(s).wait_recv(); add(me, h, rows - h, iy1, s)
        @pl.when((s >= z) & (z > 0))
        def _():
            zu(s).wait_recv(); add(me, 0, rows, izu, s)
        @pl.when((s <= z) & (z < 3))
        def _():
            zd(s).wait_recv(); add(me, 0, rows, izd, s)
        @pl.when(s > z)
        def _(): zu(s).start()
        @pl.when(s < z)
        def _(): zd(s).start()

    for g in (3, 2, 1, 0):
        s = nearest(z, g)
        for xx, yy in four:
            cross(s, xx, yy).start()
            if g == 3:
                load(s, xx, yy).start()
    w_out = pltpu.make_async_copy(wo_h, wa, wsem.at[0])
    w_query = pltpu.make_async_copy(wq_h, wb, wsem.at[1])
    w_key = pltpu.make_async_copy(wk_h, wc, wsem.at[2])
    w_value = pltpu.make_async_copy(wv_h, wa, wsem.at[3])
    w_out.start(); w_query.start(); w_key.start()

    g1[...] = jnp.zeros_like(g1)
    g2[...] = jnp.zeros_like(g2)
    @pl.loop(0, rows // 16)
    def _(r):
        q = pl.ds(pl.multiple_of(r * 16, 16), 16)
        back, terms = norm_back(x_mid[q], gain2[...], grad2[q])
        back = back + dy[pl.ds(pl.multiple_of(y * rows + r * 16, 16), 16)].astype(f32)
        dx2[q] = back
        dattn[y, q] = back.astype(bf16)
        g2[...] += jnp.sum(terms, axis=0, keepdims=True)
    attn_swap = rcopy(dattn.at[y], dattn.at[y], ysem.at[0], ysem.at[1], yn)
    attn_swap.start()
    first(3)
    first(2)
    w_out.wait()
    attn_swap.wait_recv()
    full = dattn[...].reshape(toks, width)
    dmix[...] = nn(full, wa[...]).astype(bf16)
    w_value.start()

    scale = HD ** (-0.5)
    def turn_back(values):
        return values * cosine[...] - pltpu.roll(values, HD // 2, 1) * sine[...]
    @pl.loop(0, heads)
    def _(n):
        @pl.when(n == 2)
        def _():
            second(3); first(1)
        @pl.when(n == 5)
        def _():
            second(2); third(3); first(0)
        w = pl.ds(pl.multiple_of(n * HD, HD), HD)
        qh, kh, vh, doh = qr[:, w], kr[:, w], vr[:, w], dmix[:, w]
        scores = nt(qh, kh) * scale
        ahead = lax.broadcasted_iota(jnp.int32, (toks, toks), 0) >= lax.broadcasted_iota(jnp.int32, (toks, toks), 1)
        scores = jnp.where(ahead, scores, -1e30)
        expo = jnp.exp(scores - jnp.max(scores, axis=1, keepdims=True))
        probs = expo * (1.0 / jnp.sum(expo, axis=1, keepdims=True))
        dv[:, w] = lax.dot_general(
            probs.astype(bf16), doh, (((0,), (0,)), ((), ())), preferred_element_type=f32
        ).astype(bf16)
        dprob = nt(doh, vh)
        delta = jnp.sum(probs * dprob, axis=1, keepdims=True)
        ds = (probs * (dprob - delta)).astype(bf16)
        dq[:, w] = turn_back(nn(ds, kh) * scale).astype(bf16)
        dkr = lax.dot_general(ds, qh, (((0,), (0,)), ((), ())), preferred_element_type=f32)
        dk[:, w] = turn_back(dkr * scale).astype(bf16)

    w_query.wait(); w_key.wait(); w_value.wait()
    for n in range(0, width, 512):
        w = pl.ds(n, 512)
        out = nt(dq[...], wb[w, :]) + nt(dk[...], wc[w, :]) + nt(dv[...], wa[w, :])
        da1[0, :, w] = out[:rows]
        da1[1, :, w] = out[rows:]
    @pl.loop(0, rows // 16)
    def _(r):
        q = pl.ds(pl.multiple_of(r * 16, 16), 16)
        send1[q] = da1[1 - y, q].astype(bf16)
    da1_swap = rcopy(send1, recv1, ysem.at[2], ysem.at[3], yn)
    da1_swap.start()
    second(1); third(2)
    da1_swap.wait_recv()
    @pl.loop(0, rows // 16)
    def _(r):
        q = pl.ds(pl.multiple_of(r * 16, 16), 16)
        back, terms = norm_back(
            x_in[pl.ds(pl.multiple_of(y * rows + r * 16, 16), 16)].astype(f32), gain1[...], da1[y, q] + recv1[q].astype(f32)
        )
        tok_half[q] = (back + dx2[q]).astype(bf16)
        g1[...] += jnp.sum(terms, axis=0, keepdims=True)
    second(0); third(1); third(0)
    @pl.loop(0, rows // 16)
    def _(r):
        q = pl.ds(pl.multiple_of(r * 16, 16), 16)
        out_half[q] = (x_mid[q] + ic[at(z, x, y), q].astype(f32)).astype(bf16)
    for swap in (attn_swap, da1_swap):
        swap.wait_send()
    for s in range(4):
        rx0(s).wait_send(); ry1(s).wait_send()
        for q in (0, 1):
            ry0(s, q).wait_send(); rx1(s, q).wait_send()
            for r in (0, 1):
                cross(s, q, r).wait_send()
        @pl.when(s > z)
        def _(): zu(s).wait_send()
        @pl.when(s < z)
        def _(): zd(s).wait_send()

def attention_back(part, grad2, x_mid, dy, x_in, gain1, gain2, weights, qr, kr, vr, cosine, sine, cid):
    rows, width = x_mid.shape
    toks, hw = qr.shape
    h = 48
    f32, bf16 = jnp.float32, jnp.bfloat16
    D = pltpu.SemaphoreType.DMA
    S = jax.ShapeDtypeStruct
    any_ = pl.BlockSpec(memory_space=pl.ANY)
    vm = pl.BlockSpec(memory_space=pltpu.VMEM)
    V = lambda *shape, t=bf16: pltpu.VMEM(shape, t)
    return pl.pallas_call(
        attention_back_kernel,
        out_shape=[
            S((rows, width), bf16), S((rows, width), bf16), S((2, rows, width), bf16),
            S((toks, hw), bf16), S((toks, hw), bf16), S((toks, hw), bf16), S((1, width), f32), S((1, width), f32),
        ],
        in_specs=[any_] + [vm] * 6 + [any_] * 4 + [vm] * 5,
        out_specs=[vm] * 8,
        scratch_shapes=[
            V(16, rows, width), V(4, rows, width), V(8, h, width), V(4, h, width), V(8, rows - h, width), V(4, rows - h, width),
            V(4, rows, width), V(4, rows, width),
            V(width, hw), V(width, hw), V(width, hw), V(toks, hw), V(rows, width, t=f32), V(2, rows, width, t=f32),
            V(rows, width), V(rows, width),
            D((4,)), D((4,)), D((4,)), D((16,)), D((16,)), D((4, 2)), D((4, 2)), D((4,)), D((4,)), D((4, 2)), D((4, 2)), D((4,)), D((4,)),
            D((4,)), D((4,)), D((4,)), D((4,)),
        ],
        compiler_params=pltpu.CompilerParams(collective_id=cid, has_side_effects=True, vmem_limit_bytes=63 << 20),
        name="attention_back",
    )(part, grad2, x_mid, dy, x_in, gain1, gain2, *weights, qr, kr, vr, cosine, sine)

def weight_grad_kernel(
    a1, dattn, dq, dk, dv, mixed, gains, out_half, tok_half,
    oq, ok, ov, oo, og, out_full, tok_full,
    acc, ic, ix, izu, izd, gc, gx, gu, gd, gy, gbuf,
    cs, cr, xs, xr, zus, zur, zds, zdr, gss, gsr, fsem,
):
    f32, bf16 = jnp.float32, jnp.bfloat16
    z, x, y, c = place()
    xn, yn, cn = dev(z, 1 - x, y, c), dev(z, x, 1 - y, c), dev(z, x, y, 1 - c)
    n, depth = 4, acc.shape[2]
    outs = (oq, ok, ov, oo)
    greet(z, x, y, c)
    def pos(s, xx, cc): return (s * 2 + xx) * 2 + cc
    def wc(a, s, xx):
        i = s * 2 + xx
        return rcopy(acc.at[a, pos(s, xx, 1 - c)], ic.at[a, i], cs.at[a, i], cr.at[a, i], cn)
    def wx(a, s):
        return rcopy(acc.at[a, pos(s, 1 - x, c)], ix.at[a, s], xs.at[a, s], xr.at[a, s], xn)
    def zu(a, s):
        return rcopy(acc.at[a, pos(s, x, c)], izu.at[a, s], zus.at[a, s], zur.at[a, s], dev(z + 1, x, y, c))
    def zd(a, s):
        return rcopy(acc.at[a, pos(s, x, c)], izd.at[a, s], zds.at[a, s], zdr.at[a, s], dev(z - 1, x, y, c))
    def add(a, i, src, j):
        @pl.loop(0, depth // 16)
        def _(r):
            b = pl.ds(pl.multiple_of(r * 16, 16), 16)
            acc[a, i, b] = acc[a, i, b] + src[a, j, b]
    def make(g):
        s = nearest(z, g)
        w = pl.ds(pl.multiple_of(s * 4 * depth, 4 * depth), 4 * depth)
        for a, (left, right) in ((3, (dattn, mixed)), (0, (a1, dq)), (1, (a1, dk)), (2, (a1, dv))):
            out = lax.dot_general(left[:, w], right[...], (((0,), (0,)), ((), ())), preferred_element_type=f32).astype(bf16)
            for i in range(4):
                acc[a, s * 4 + i] = out[i * depth:(i + 1) * depth]
            for q in (0, 1):
                wc(a, s, q).start()
    def first(g):
        s = nearest(z, g)
        for a in (3, 0, 1, 2):
            for q in (0, 1):
                wc(a, s, q).wait_recv()
                add(a, pos(s, q, c), ic, s * 2 + q)
            wx(a, s).start()
    def second(g):
        s = nearest(z, g)
        for a in (3, 0, 1, 2):
            wx(a, s).wait_recv(); add(a, pos(s, x, c), ix, s)
            @pl.when((s >= z) & (z > 0))
            def _():
                zu(a, s).wait_recv(); add(a, pos(s, x, c), izu, s)
            @pl.when((s <= z) & (z < 3))
            def _():
                zd(a, s).wait_recv(); add(a, pos(s, x, c), izd, s)
            @pl.when(s > z)
            def _(): zu(a, s).start()
            @pl.when(s < z)
            def _(): zd(a, s).start()
    g_c = rcopy(gains.at[1 - c], gc, gss.at[0], gsr.at[0], cn)
    g_x = rcopy(gbuf.at[1 - x], gx, gss.at[1], gsr.at[1], xn)
    g_u = rcopy(gu.at[1], gu.at[0], gss.at[2], gsr.at[2], dev(z + 1, x, y, c))
    g_d = rcopy(gd.at[1], gd.at[0], gss.at[3], gsr.at[3], dev(z - 1, x, y, c))
    g_y = rcopy(gy.at[0], gy.at[1], gss.at[4], gsr.at[4], yn)
    swaps = [
        rcopy(a, b.at[y], fsem.at[i], fsem.at[i + 2], yn) for i, (a, b) in enumerate(((out_half, out_full), (tok_half, tok_full)))
    ]
    g_c.start()
    make(3); make(2)
    for swap in swaps:
        swap.start()
    out_full[y] = out_half[...]
    tok_full[y] = tok_half[...]
    g_c.wait_recv()
    gbuf[...] = gains[c] + gc[...]
    g_x.start()
    first(3); make(1); first(2); make(0)
    g_x.wait_recv()
    gbuf[x] = gbuf[x] + gx[...]
    second(3)
    gu[1] = gbuf[x]
    gd[1] = gbuf[x]
    @pl.when(z > 0)
    def _():
        g_u.wait_recv()
        gu[1] = gu[1] + gu[0]
    @pl.when(z < 3)
    def _():
        g_u.start()
    first(1)
    second(2)
    @pl.when(z < 3)
    def _():
        g_d.wait_recv()
        gd[1] = gd[1] + gd[0]
    @pl.when(z > 0)
    def _():
        g_d.start()
    first(0)
    second(1)
    gy[0] = gu[1, z] + gd[1, z] - gbuf[x, z]
    g_y.start()
    second(0)
    for a in range(n):
        outs[a][...] = acc[a, pos(z, x, c)].astype(f32)
    g_y.wait_recv()
    og[...] = gy[0] + gy[1]
    for swap in swaps:
        swap.wait()
    g_c.wait_send(); g_x.wait_send(); g_y.wait_send()
    @pl.when(z < 3)
    def _(): g_u.wait_send()
    @pl.when(z > 0)
    def _(): g_d.wait_send()
    for s in range(4):
        for a in range(n):
            for q in (0, 1): wc(a, s, q).wait_send()
            wx(a, s).wait_send()
            @pl.when(s > z)
            def _(): zu(a, s).wait_send()
            @pl.when(s < z)
            def _(): zd(a, s).wait_send()

def weight_grads(a1, dattn, dq, dk, dv, mixed, gains, out_half, tok_half, cid):
    toks, width = a1.shape
    hw = dq.shape[1]
    depth = width // 16
    f32, bf16 = jnp.float32, jnp.bfloat16
    D = pltpu.SemaphoreType.DMA
    S = jax.ShapeDtypeStruct
    vm = pl.BlockSpec(memory_space=pltpu.VMEM)
    V = lambda *shape, t=bf16: pltpu.VMEM(shape, t)
    return pl.pallas_call(
        weight_grad_kernel,
        out_shape=[S((depth, hw), f32)] * 4 + [S((8, 128), f32)] + [S((2,) + out_half.shape, bf16)] * 2,
        in_specs=[vm] * 9,
        out_specs=[vm] * 7,
        scratch_shapes=[
            V(4, 16, depth, hw), V(4, 8, depth, hw), V(4, 4, depth, hw), V(4, 4, depth, hw), V(4, 4, depth, hw),
            V(2, 4, 8, 128, t=f32), V(4, 8, 128, t=f32), V(2, 4, 8, 128, t=f32), V(2, 4, 8, 128, t=f32), V(2, 8, 128, t=f32), V(2, 4, 8, 128, t=f32),
            D((4, 8)), D((4, 8)), D((4, 4)), D((4, 4)), D((4, 4)), D((4, 4)), D((4, 4)), D((4, 4)), D((5,)), D((5,)), D((4,)),
        ],
        compiler_params=pltpu.CompilerParams(collective_id=cid, has_side_effects=True, vmem_limit_bytes=60 << 20),
        name="weight_grads",
    )(a1, dattn, dq, dk, dv, mixed, gains, out_half, tok_half)


def expert_grads_kernel(deg, deu, eh, rows, deo, e_gate, e_up, e_down):
    def tn(left, right):
        return lax.dot_general(left, right, (((0,), (0,)), ((), ())), preferred_element_type=jnp.float32)
    e_gate[...] = tn(deg[...], rows[...])
    e_up[...] = tn(deu[...], rows[...])
    e_down[...] = tn(eh[...], deo[...])


def expert_grads(deg, deu, eh, rows, deo):
    width = rows.shape[1]
    whole = lambda a: pl.BlockSpec(a.shape, lambda i: (0, 0), pipeline_mode=pl.Buffered(1))
    tile = lambda n: pl.BlockSpec((n, 256), lambda i: (0, i))
    hidden = deg.shape[1]
    return pl.pallas_call(
        expert_grads_kernel,
        grid=(width // 256,),
        out_shape=[jax.ShapeDtypeStruct((hidden, width), jnp.float32)] * 3,
        in_specs=[whole(a) for a in (deg, deu, eh)] + [tile(a.shape[0]) for a in (rows, deo)],
        out_specs=[tile(hidden)] * 3,
        compiler_params=pltpu.CompilerParams(vmem_limit_bytes=60 << 20),
        name="expert_grads",
    )(deg, deu, eh, rows, deo)


def attention_kernel(
    x_in, wq_in, wk_in, wv_in, wo_in, gain_in, table_in, dy_in, wd_h, cosine, sine,
    wq_o, wk_o, wv_o, wo_o, dy_all, act1, qr, kr, vr, mixed, x_mid, act2, grow, rank_row, rank_col, gate, deo_o, deh_o,
    gland, tland, inv, wbuf, wob, wd, qa, ka, va, own_attn, send, recv, gm, dyt, deo, deh,
    wsem, lsem, dsem, ssem, ysem, zs, zr, xs, xr, cs, cr, gzs, gzr, gxs, gxr, gys, gyr, gcs, gcr,
):
    f32, bf16 = jnp.float32, jnp.bfloat16
    z, x, y, c = place()
    toks, width = x_in.shape
    rows = toks // 2
    depth, hw = wq_in.shape
    cap, hidden = deh_o.shape[1:]
    xn, yn, cn = dev(z, 1 - x, y, c), dev(z, x, 1 - y, c), dev(z, x, y, 1 - c)
    expert = (z * 2 + x) * 2 + c
    greet(z, x, y, c)
    ins = (gain_in, table_in, wq_in, wk_in, wv_in, wo_in)
    outs = (gland, tland, wq_o, wk_o, wv_o, wo_o)
    n = len(outs)
    def pos(s, xx, cc): return (s * 2 + xx) * 2 + cc
    owns = [pltpu.make_async_copy(ins[a], outs[a].at[expert], lsem.at[a]) for a in range(n)]
    own_rows = pl.ds(pl.multiple_of(y * rows, rows), rows)
    owns.append(pltpu.make_async_copy(dy_in.at[own_rows], dy_all.at[blk(z, x, y, c)], lsem.at[n]))
    for o in owns:
        o.start()
    w_down = pltpu.make_async_copy(wd_h, wd, wsem.at[3])
    w_down.start()

    def wz(a, s, up):
        r = outs[a].at[pos(s, x, c)]
        return rcopy(r, r, zs.at[a, s, up], zr.at[a, s], dev(z + 2 * up - 1, x, y, c))
    def wx(a, s):
        r = outs[a].at[pos(s, x, c)]
        return rcopy(r, r, xs.at[a, s], xr.at[a, s], xn)
    def wc(a, s, xx):
        r = outs[a].at[pos(s, xx, c)]
        return rcopy(r, r, cs.at[a, s * 2 + xx], cr.at[a, s * 2 + xx], cn)
    half = rows - 48
    halves = (pl.ds(0, half), pl.ds(half, rows - half))
    def piece(s, xx, yy, p):
        return dy_all.at[blk(s, xx, yy, c), halves[p]]
    def gz(s, xx, p, up):
        r = piece(s, xx, y, p)
        i = 0 if p == 0 else 1 + xx
        return rcopy(r, r, gzs.at[i, s, up], gzr.at[i, s], dev(z + 2 * up - 1, x, y, c))
    def gx(s, p):
        r = piece(s, x, y, p)
        return rcopy(r, r, gxs.at[p, s], gxr.at[p, s], xn)
    def gy(s, xx, p):
        r = piece(s, xx, y, p)
        return rcopy(r, r, gys.at[p, s, xx], gyr.at[p, s, xx], yn)
    def gc(s, xx, yy, p):
        r = piece(s, xx, yy, p)
        return rcopy(r, r, gcs.at[p, s * 2 + xx, yy], gcr.at[p, s * 2 + xx, yy], cn)

    def column(s):
        for a in range(n):
            wx(a, s).start(); wc(a, s, x).start()
    def middle(g):
        s = nearest(z, g)
        for a in range(n):
            wx(a, s).wait_recv(); wc(a, s, 1 - x).start()
    def gspread(s, xx, p):
        gy(s, xx, p).start(); gc(s, xx, y, p).start()
    def gmiddle(g):
        s = nearest(z, g)
        gx(s, 0).wait_recv()
        gspread(s, 1 - x, 0)
    def glast(g):
        s = nearest(z, g)
        for q in (0, 1):
            for p in (0, 1):
                gy(s, q, p).wait_recv(); gc(s, q, 1 - y, p).start()
    def launch(fn):
        @pl.when(z < 3)
        def _(): fn(1)
        @pl.when(z > 0)
        def _(): fn(0)
    def towards(g):
        s = nearest(z, g)
        up = (s < z).astype(jnp.int32)
        nxt = z + 2 * up - 1
        return s, up, (nxt >= 0) & (nxt <= 3)
    def arrive(g):
        s, up, more = towards(g)
        for a in range(n):
            wz(a, s, up).wait_recv()
            @pl.when(more)
            def _(): wz(a, s, up).start()
        column(s)
    def garrive(g):
        s, up, more = towards(g)
        for xx, p in ((x, 0), (x, 1), (1 - x, 1)):
            gz(s, xx, p, up).wait_recv()
            @pl.when(more)
            def _(): gz(s, xx, p, up).start()
            if p == 0:
                gx(s, 0).start()
            gspread(s, xx, p)

    def project(g):
        s = nearest(z, g)
        for a in range(n):
            for q in (0, 1):
                wc(a, s, q).wait_recv()
        loads = [
            pltpu.make_async_copy(w.at[pl.ds(4 * s, 4)], wbuf.at[i], wsem.at[i])
            for i, w in enumerate((wq_o, wk_o, wv_o))
        ]
        for l in loads:
            l.start()
        for i in range(4):
            at = pl.ds(pl.multiple_of((4 * s + i) * depth, depth), depth)
            two = gland[4 * s + i][0:8].astype(f32)
            grow[:, at] = two
        w = pl.ds(pl.multiple_of(4 * s * depth, 4 * depth), 4 * depth)
        a1 = (x_in[:, w].astype(f32) * inv[...] * grow[0:1, w]).astype(bf16)
        act1[:, w] = a1
        for i, acc in enumerate((qa, ka, va)):
            loads[i].wait()
            out = nn(a1, wbuf[i].reshape(4 * depth, hw))
            if g == 0:
                acc[...] = out
            else:
                acc[...] += out

    def ranks_of(g):
        s = nearest(z, g)
        for i in range(4):
            gm[i:i + 1, :] = tland[4 * s + i, pl.ds(expert, 1), :]
        member = (gm[...] > 0.0).astype(f32).astype(bf16)
        one = lax.broadcasted_iota(jnp.int32, (toks, toks), 0)
        two = lax.broadcasted_iota(jnp.int32, (toks, toks), 1)
        upper = jnp.where(one <= two, 1.0, 0.0).astype(bf16)
        lower = jnp.where(one >= two, 1.0, 0.0).astype(bf16)
        same = jnp.where(one == two, 1.0, 0.0).astype(bf16)
        by_row = jnp.where(gm[...] > 0.0, nn(member, upper) - 1.0, -1.0).astype(jnp.int32)
        by_col = jnp.where(nt(same, member) > 0.5, nt(lower, member) - 1.0, -1.0).astype(jnp.int32)
        for i in range(4):
            rank_row[4 * s + i] = by_row[i:i + 1]
            rank_col[4 * s + i] = by_col[:, i:i + 1]
    def stores(g, xx):
        s = nearest(z, g)
        base = (s * 2 + xx) * 2
        out = []
        for k in (0, 1):
            out.append(pltpu.make_async_copy(deo.at[k], deo_o.at[base + k], ssem.at[k, 0]))
            out.append(pltpu.make_async_copy(deh.at[pl.ds(k * cap, cap)], deh_o.at[base + k], ssem.at[k, 1]))
        return out
    def hidden_grads(g):
        s = nearest(z, g)
        ranks_of(g)
        for xx in (0, 1):
            for yy in (0, 1):
                for p in (0, 1):
                    gc(s, xx, yy, p).wait_recv()
        @pl.loop(0, 2)
        def _(xx):
            base = (s * 2 + xx) * 2
            loads = [pltpu.make_async_copy(dy_all.at[pl.ds(2 * (base + k), 2)], dyt.at[k], dsem.at[k]) for k in (0, 1)]
            for l in loads:
                l.start()
            if g > 0:
                @pl.when(xx == 0)
                def _():
                    for copy in stores(g - 1, 1):
                        copy.wait()
            @pl.when(xx == 1)
            def _():
                for copy in stores(g, 0):
                    copy.wait()
            for k in (0, 1):
                loads[k].wait()
                hit = rank_row[base + k] == lax.broadcasted_iota(jnp.int32, (cap, toks), 0)
                weight = jnp.sum(jnp.where(hit, tland[base + k, pl.ds(expert, 1), :], 0.0), axis=1, keepdims=True)
                gate[base + k] = weight
                pick = jnp.where(hit, 1.0, 0.0).astype(bf16)
                grads = dyt[k].reshape(toks, width)
                for m in range(0, width, 512):
                    deo[k, :, m:m + 512] = (nn(pick, grads[:, m:m + 512]) * weight).astype(bf16)
            deh[...] = nt(deo[...].reshape(2 * cap, width), wd[...])
            for copy in stores(g, xx):
                copy.start()

    for o in owns:
        o.wait()
    gx(z, 1).start()
    launch(lambda up: [wz(a, z, up).start() for a in range(n)])
    column(z)
    launch(lambda up: gz(z, x, 0, up).start())
    launch(lambda up: gz(z, x, 1, up).start())
    gx(z, 0).start()
    gspread(z, x, 0); gspread(z, x, 1)
    @pl.loop(0, toks // 16)
    def _(r):
        q = pl.ds(pl.multiple_of(r * 16, 16), 16)
        v = x_in[q].astype(f32)
        inv[q] = lax.rsqrt(jnp.sum(v * v, axis=1, keepdims=True) * (1.0 / width) + EPS)
    gm[...] = jnp.zeros_like(gm)
    w_down.wait()
    gx(z, 1).wait_recv()
    launch(lambda up: gz(z, 1 - x, 1, up).start())
    gspread(z, 1 - x, 1)
    arrive(1); middle(0); project(0)
    garrive(1); gmiddle(0)
    arrive(2); middle(1); project(1)
    garrive(2); gmiddle(1); glast(0)
    hidden_grads(0)
    arrive(3); middle(2); project(2)
    garrive(3); gmiddle(2); glast(1)
    hidden_grads(1)
    middle(3); project(3)
    w_out = pltpu.make_async_copy(wo_o, wob, wsem.at[3])
    w_out.start()

    scale = HD ** (-0.5)
    def turn(values):
        return values * cosine[...] + pltpu.roll(values, HD // 2, 1) * sine[...]
    @pl.loop(0, hw // HD)
    def _(i):
        @pl.when(i == 4)
        def _(): gmiddle(3)
        w = pl.ds(pl.multiple_of(i * HD, HD), HD)
        qh, kh, vh = turn(qa[:, w]).astype(bf16), turn(ka[:, w]).astype(bf16), va[:, w].astype(bf16)
        qr[:, w] = qh
        kr[:, w] = kh
        vr[:, w] = vh
        scores = nt(qh, kh) * scale
        ahead = lax.broadcasted_iota(jnp.int32, (toks, toks), 0) >= lax.broadcasted_iota(jnp.int32, (toks, toks), 1)
        scores = jnp.where(ahead, scores, -1e30)
        expo = jnp.exp(scores - jnp.max(scores, axis=1, keepdims=True))
        probs = expo * (1.0 / jnp.sum(expo, axis=1, keepdims=True))
        mixed[:, w] = nn(probs.astype(bf16), vh).astype(bf16)
    w_out.wait()
    whole = wob[...].reshape(width, hw)
    other = pl.ds(pl.multiple_of((1 - y) * rows, rows), rows)
    here = pl.ds(pl.multiple_of(y * rows, rows), rows)
    for m in range(0, width, 512):
        send[:, m:m + 512] = nt(mixed[other, :], whole[m:m + 512]).astype(bf16)
    swap = rcopy(send, recv, ysem.at[0], ysem.at[1], yn)
    swap.start()
    for m in range(0, width, 512):
        own_attn[:, m:m + 512] = nt(mixed[here, :], whole[m:m + 512])
    glast(2)
    hidden_grads(2)
    swap.wait_recv()
    @pl.loop(0, rows // 16)
    def _(r):
        q = pl.ds(pl.multiple_of(r * 16, 16), 16)
        at = pl.ds(pl.multiple_of(y * rows + r * 16, 16), 16)
        v = x_in[at].astype(f32) + own_attn[q] + recv[q].astype(f32)
        x_mid[q] = v
        scaled = v * lax.rsqrt(jnp.sum(v * v, axis=1, keepdims=True) * (1.0 / width) + EPS)
        act2[q] = (scaled * grow[1:2]).astype(bf16)
    glast(3)
    hidden_grads(3)
    for copy in stores(3, 1):
        copy.wait()
    swap.wait_send()
    gx(z, 1).wait_send()
    for s in range(4):
        for a in range(n):
            wx(a, s).wait_send()
            for q in (0, 1):
                wc(a, s, q).wait_send()
        gx(s, 0).wait_send()
        for q in (0, 1):
            for p in (0, 1):
                gy(s, q, p).wait_send()
                for r in (0, 1):
                    gc(s, q, r, p).wait_send()
        @pl.when((z < 3) & (s <= z))
        def _():
            for xx, p in ((x, 0), (x, 1), (1 - x, 1)):
                gz(s, xx, p, 1).wait_send()
            for a in range(n):
                wz(a, s, 1).wait_send()
        @pl.when((z > 0) & (s >= z))
        def _():
            for xx, p in ((x, 0), (x, 1), (1 - x, 1)):
                gz(s, xx, p, 0).wait_send()
            for a in range(n):
                wz(a, s, 0).wait_send()

def attention_layer(x_in, weights, gains, table, dy, wd, cosine, sine, cap, cid):
    toks, width = x_in.shape
    depth, hw = weights[0].shape
    rows = toks // 2
    hidden = wd.shape[0]
    n = 6
    f32, bf16, i32 = jnp.float32, jnp.bfloat16, jnp.int32
    D = pltpu.SemaphoreType.DMA
    S = jax.ShapeDtypeStruct
    any_ = pl.BlockSpec(memory_space=pl.ANY)
    vm = pl.BlockSpec(memory_space=pltpu.VMEM)
    V = lambda *shape, t=bf16: pltpu.VMEM(shape, t)
    return pl.pallas_call(
        attention_kernel,
        out_shape=[S((16, depth, hw), bf16)] * 4
        + [S((32, rows, width), bf16), S((toks, width), bf16)]
        + [S((toks, hw), bf16)] * 4
        + [
            S((rows, width), f32), S((rows, width), bf16), S((8, width), f32), S((16, 1, toks), i32), S((16, toks, 1), i32),
            S((16, cap, 1), f32), S((16, cap, width), bf16), S((16, cap, hidden), f32),
        ],
        in_specs=[vm] * 8 + [any_] + [vm] * 2,
        out_specs=[any_] * 5 + [vm] * 11 + [any_] * 2,
        scratch_shapes=[
            V(16, *gains.shape), V(16, *table.shape, t=f32), V(toks, 1, t=f32), V(3, 4, depth, hw), V(16, depth, hw), V(hidden, width),
            V(toks, hw, t=f32), V(toks, hw, t=f32), V(toks, hw, t=f32), V(rows, width, t=f32), V(rows, width), V(rows, width),
            V(8, toks, t=f32), V(2, 2, rows, width), V(2, cap, width), V(2 * cap, hidden, t=f32),
            D((4,)), D((n + 1,)), D((2,)), D((2, 2)), D((2,)),
            D((n, 4, 2)), D((n, 4)), D((n, 4)), D((n, 4)), D((n, 8)), D((n, 8)),
            D((3, 4, 2)), D((3, 4)), D((2, 4)), D((2, 4)), D((2, 4, 2)), D((2, 4, 2)), D((2, 8, 2)), D((2, 8, 2)),
        ],
        compiler_params=pltpu.CompilerParams(collective_id=cid, has_side_effects=True, vmem_limit_bytes=60 << 20),
        name="attention_layer",
    )(x_in, *weights, gains, table, dy, wd, cosine, sine)


def on_device(
    tokens,
    cotangent,
    route_ids,
    route_gates,
    gain_first,
    w_query,
    w_key,
    w_value,
    w_output,
    gain_second,
    shared_gate,
    shared_up,
    shared_down,
    expert_gate,
    expert_up,
    expert_down,
):
    f32, bf16 = jnp.float32, jnp.bfloat16
    rows_dev, width = tokens.shape
    topk = route_ids.shape[1]
    experts = lax.axis_size("dp")
    capacity = rows_dev * topk * 4 // (3 * experts)
    slots = experts * capacity
    positions = jnp.arange(rows_dev, dtype=f32)
    freqs = 10000.0 ** (-2.0 * jnp.arange(HD // 2, dtype=f32) / HD)
    angles = positions[:, None] * freqs[None, :]
    cosine = jnp.concatenate([jnp.cos(angles)] * 2, axis=1)
    sine = jnp.concatenate([-jnp.sin(angles), jnp.sin(angles)], axis=1)
    chosen = route_ids[:, :, None] == jnp.arange(experts, dtype=jnp.int32)[None, None, :]
    table = jnp.sum(jnp.where(chosen, route_gates[:, :, None], 0.0), axis=1)
    gains = jnp.concatenate([gain_first[None], gain_second[None], jnp.zeros((14, gain_first.shape[0]), bf16)])
    exp_gate, exp_up, exp_down = expert_gate[0].T, expert_up[0].T, expert_down[0]

    depth, common_width = shared_gate.shape
    common_dev = common_width // experts
    packed = jnp.stack([shared_gate, shared_up, shared_down])
    packed = packed.reshape(3, depth, experts, common_dev).transpose(2, 0, 1, 3)
    packed = lax.all_to_all(packed, "dp", split_axis=0, concat_axis=0, tiled=True)
    packed = packed.transpose(1, 0, 2, 3).reshape(3, width, common_dev)
    front = capacity - 128
    back = 128 - front - common_dev

    def widen(w):
        return jnp.pad(w, ((0, 0), (front, back)))

    common_gu = jnp.concatenate([widen(packed[0]), widen(packed[1])], axis=1)
    common_down = widen(packed[2])

    (
        query_whole, key_whole, value_whole, output_whole, grad_all, act_one, query_rot, key_rot, value_low, mixed,
        x_mid, act_two, gain_rows, rank_row, rank_col, slot_gate, rows_out_grad, hidden_rows_grad,
    ) = attention_layer(
        tokens, (w_query, w_key, w_value, w_output), gains, table.T, cotangent, exp_down, cosine, sine, capacity, 0
    )
    weights = [w.reshape(width, -1) for w in (query_whole, key_whole, value_whole, output_whole)]

    (
        total_grad, unused_act, rows, hidden_rows, gate_rows_grad, up_rows_grad, unused_hidden, unused_grad, unused_part, ffn,
        gu_grad, down_grad,
    ) = (
        expert_layer(
            act_two, hidden_rows_grad, grad_all, rank_row, rank_col, slot_gate,
            exp_gate, exp_up, exp_down, common_gu, common_down.T[front:], common_down, 1,
        )
    )
    rows = rows.reshape(slots, width)
    rows_out_grad = rows_out_grad.reshape(slots, width)
    hidden_rows = hidden_rows.reshape(slots, -1)
    expert_gate_grad, expert_up_grad, expert_down_grad = expert_grads(
        gate_rows_grad.reshape(slots, -1), up_rows_grad.reshape(slots, -1), hidden_rows, rows, rows_out_grad
    )
    common_w_grad = jnp.concatenate(
        [w[:, front : front + common_dev] for w in (gu_grad[:, :128], gu_grad[:, 128:], down_grad)], axis=1
    )
    common_w_grad = common_w_grad.reshape(experts, depth, 3 * common_dev)
    common_w_grad = lax.all_to_all(common_w_grad, "dp", split_axis=0, concat_axis=0, tiled=True)
    common_w_grad = common_w_grad.reshape(experts, depth, 3, common_dev).transpose(2, 1, 0, 3)
    common_w_grad = common_w_grad.reshape(3, depth, common_width).astype(f32)

    layer_out, tokens_grad, attn_grad, query_grad, key_grad, value_grad, gain_one_grad, gain_two_grad = attention_back(
        ffn,
        total_grad,
        x_mid,
        cotangent,
        tokens,
        gain_rows[0:1],
        gain_rows[1:2],
        weights,
        query_rot,
        key_rot,
        value_low,
        cosine,
        sine,
        2,
    )
    gains = jnp.concatenate([gain_one_grad, gain_two_grad, jnp.zeros((6, width), f32)])
    gains = gains.reshape(8, 4, 2, 2, width // 16).transpose(3, 2, 1, 0, 4)
    query_sum, key_sum, value_sum, output_sum, gain_grads, layer_out, tokens_grad = weight_grads(
        act_one, attn_grad.reshape(rows_dev, width), query_grad, key_grad, value_grad, mixed, gains, layer_out, tokens_grad, 4
    )
    return (
        layer_out.reshape(rows_dev, width),
        tokens_grad.reshape(rows_dev, width),
        gain_grads[0],
        query_sum,
        key_sum,
        value_sum,
        output_sum,
        gain_grads[1],
        common_w_grad[0],
        common_w_grad[1],
        common_w_grad[2],
        expert_gate_grad.T[None],
        expert_up_grad.T[None],
        expert_down_grad[None],
    )


def solution(mesh):
    body = on_device if (mesh.shape["dp"], mesh.shape["tensor"]) == (16, 2) else on_device_plain
    in_specs = (
        P("dp", None),
        P("dp", None),
        P("dp", None),
        P("dp", None),
        P("dp"),
        P("dp", "tensor"),
        P("dp", "tensor"),
        P("dp", "tensor"),
        P("dp", "tensor"),
        P("dp"),
        P("dp", "tensor"),
        P("dp", "tensor"),
        P("dp", "tensor"),
        P("dp", None, "tensor"),
        P("dp", None, "tensor"),
        P("dp", "tensor", None),
    )
    out_specs = (
        P("dp", None),
        P("dp", None),
        P("dp"),
        P("dp", "tensor"),
        P("dp", "tensor"),
        P("dp", "tensor"),
        P("dp", "tensor"),
        P("dp"),
        P("dp", "tensor"),
        P("dp", "tensor"),
        P("dp", "tensor"),
        P("dp", None, "tensor"),
        P("dp", None, "tensor"),
        P("dp", "tensor", None),
    )
    return jax.shard_map(
        body, mesh=mesh, in_specs=in_specs, out_specs=out_specs, check_vma=False
    )
```

```python
import functools

import jax
import jax.numpy as jnp
from jax import lax
from jax.experimental import pallas as pl
from jax.experimental.pallas import tpu as pltpu
from jax.sharding import PartitionSpec as P

HD = 128
MESH = pl.DeviceIdType.MESH


EPS = 1e-06


def rms_norm(values, gain):
    mean_square = jnp.mean(values * values, axis=-1, keepdims=True)
    return values * lax.rsqrt(mean_square + EPS) * gain


def rotate(values, positions):
    head = values.shape[-1]
    half = head // 2
    freqs = 10000.0 ** (-2.0 * jnp.arange(half, dtype=jnp.float32) / head)
    angles = positions[:, None] * freqs[None, :]
    cosine = jnp.cos(angles)[:, None, :]
    sine = jnp.sin(angles)[:, None, :]
    first = values[..., :half]
    second = values[..., half:]
    return jnp.concatenate(
        [first * cosine - second * sine, second * cosine + first * sine], axis=-1
    )


def gated(gate_pre, up_pre):
    return gate_pre * jax.nn.sigmoid(gate_pre) * up_pre


def contract_last(left, right):
    return lax.dot_general(
        left, right, (((1,), (1,)), ((), ())), preferred_element_type=jnp.float32
    )


def contract_first(left, right):
    return lax.dot_general(
        left, right, (((0,), (0,)), ((), ())), preferred_element_type=jnp.float32
    )


def masked_scores(query_rot, key_rot, causal, scale):
    scores = (
        jnp.einsum("qhc,khc->hqk", query_rot, key_rot, preferred_element_type=jnp.float32) * scale
    )
    return jnp.where(causal[None], scores, -1e30)


def on_device_plain(
    tokens,
    cotangent,
    route_ids,
    route_gates,
    gain_first,
    w_query,
    w_key,
    w_value,
    w_output,
    gain_second,
    shared_gate,
    shared_up,
    shared_down,
    expert_gate,
    expert_up,
    expert_down,
):
    rows_dev, width = tokens.shape
    topk = route_ids.shape[1]
    experts = lax.axis_size("dp")
    capacity = rows_dev * topk * 4 // (3 * experts)
    slots = experts * capacity
    scale = HD ** (-0.5)
    positions = jnp.arange(rows_dev, dtype=jnp.float32)
    causal = jnp.arange(rows_dev)[:, None] >= jnp.arange(rows_dev)[None, :]
    gain_one, query_whole, key_whole, value_whole, output_whole = (
        lax.all_gather(gain_first, "dp", axis=0, tiled=True),
        lax.all_gather(w_query, "dp", axis=0, tiled=True),
        lax.all_gather(w_key, "dp", axis=0, tiled=True),
        lax.all_gather(w_value, "dp", axis=0, tiled=True),
        lax.all_gather(w_output, "dp", axis=0, tiled=True),
    )
    gain_two, common_gate, common_up, common_down = (
        lax.all_gather(gain_second, "dp", axis=0, tiled=True),
        lax.all_gather(shared_gate, "dp", axis=0, tiled=True),
        lax.all_gather(shared_up, "dp", axis=0, tiled=True),
        lax.all_gather(shared_down, "dp", axis=0, tiled=True),
    )
    gain_one = gain_one.astype(jnp.float32)
    gain_two = gain_two.astype(jnp.float32)
    x_in = tokens.astype(jnp.float32)
    act_one = rms_norm(x_in, gain_one).astype(jnp.bfloat16)
    heads_dev = query_whole.shape[1] // HD
    query_pre = jnp.dot(act_one, query_whole, preferred_element_type=jnp.float32).reshape(
        rows_dev, heads_dev, HD
    )
    key_pre = jnp.dot(act_one, key_whole, preferred_element_type=jnp.float32).reshape(
        rows_dev, heads_dev, HD
    )
    query_rot = rotate(query_pre, positions).astype(jnp.bfloat16)
    key_rot = rotate(key_pre, positions).astype(jnp.bfloat16)
    value_low = (
        jnp.dot(act_one, value_whole, preferred_element_type=jnp.float32)
        .astype(jnp.bfloat16)
        .reshape(rows_dev, heads_dev, HD)
    )
    scores = masked_scores(query_rot, key_rot, causal, scale)
    top = jnp.max(scores, axis=-1, keepdims=True)
    expo = jnp.exp(scores - top)
    total = jnp.sum(expo, axis=-1, keepdims=True)
    probs = expo / total
    log_total = top + jnp.log(total)
    mixed = jnp.einsum(
        "hqk,khc->qhc", probs.astype(jnp.bfloat16), value_low, preferred_element_type=jnp.float32
    )
    mixed = mixed.reshape(rows_dev, heads_dev * HD).astype(jnp.bfloat16)
    attn = lax.psum(contract_last(mixed, output_whole), "tensor")
    x_mid = x_in + attn
    act_two = rms_norm(x_mid, gain_two).astype(jnp.bfloat16)
    gate_pre = jnp.dot(act_two, common_gate, preferred_element_type=jnp.float32)
    up_pre = jnp.dot(act_two, common_up, preferred_element_type=jnp.float32)
    hidden_common = gated(gate_pre, up_pre).astype(jnp.bfloat16)
    common_out = contract_last(hidden_common, common_down)
    flat_ids = route_ids.reshape(-1)
    onehot = (flat_ids[:, None] == jnp.arange(experts, dtype=jnp.int32)[None, :]).astype(jnp.int32)
    ranks = jnp.sum(onehot * jnp.cumsum(onehot, axis=0), axis=1) - 1
    dest = flat_ids * capacity + ranks
    token_of = jnp.arange(rows_dev * topk, dtype=jnp.int32) // topk
    source = jnp.zeros((slots,), jnp.int32).at[dest].set(token_of)
    weight_of = jnp.zeros((slots,), jnp.float32).at[dest].set(route_gates.reshape(-1))
    filled = jnp.zeros((slots,), jnp.bool_).at[dest].set(True)
    outgoing = jnp.where(filled[:, None], act_two[source], jnp.zeros((), jnp.bfloat16)).reshape(
        experts, capacity, width
    )
    exp_gate = expert_gate[0]
    exp_up = expert_up[0]
    exp_down = expert_down[0]
    received = lax.all_to_all(outgoing, "dp", split_axis=0, concat_axis=0, tiled=True)
    sources = received.shape[0]
    count = received.shape[1]
    rows = received.reshape(sources * count, width)
    gate_rows = jnp.dot(rows, exp_gate, preferred_element_type=jnp.float32)
    up_rows = jnp.dot(rows, exp_up, preferred_element_type=jnp.float32)
    hidden_rows = gated(gate_rows, up_rows).astype(jnp.bfloat16)
    partial_value = jnp.dot(hidden_rows, exp_down, preferred_element_type=jnp.float32).reshape(
        sources, count, width
    )
    returned = lax.all_to_all(
        partial_value.astype(jnp.bfloat16), "dp", split_axis=0, concat_axis=0, tiled=True
    ).astype(partial_value.dtype)
    returned, kept_rows, kept_gate, kept_up = (
        returned,
        received,
        gate_rows.reshape(sources, count, -1),
        up_rows.reshape(sources, count, -1),
    )
    picked = returned.reshape(slots, width)[dest].reshape(rows_dev, topk, width)
    routed_part = jnp.sum(picked * route_gates[:, :, None], axis=1)
    ffn = lax.psum((common_out + routed_part).astype(jnp.bfloat16), "tensor").astype(jnp.float32)
    layer_out = (x_mid + ffn).astype(jnp.bfloat16)
    grad_out = cotangent.astype(jnp.float32)
    hidden_grad = jnp.dot(cotangent, common_down, preferred_element_type=jnp.float32)
    dummy_common, common_vjp = jax.vjp(gated, gate_pre, up_pre)
    gate_grad, up_grad = common_vjp(hidden_grad)
    gate_grad = gate_grad.astype(jnp.bfloat16)
    up_grad = up_grad.astype(jnp.bfloat16)
    common_gate_grad = contract_first(act_two, gate_grad)
    common_up_grad = contract_first(act_two, up_grad)
    common_down_grad = contract_first(cotangent, hidden_common)
    act_two_grad = contract_last(gate_grad, common_gate) + contract_last(up_grad, common_up)
    outgoing_grad = (
        (weight_of[:, None] * grad_out[source])
        .astype(jnp.bfloat16)
        .reshape(experts, capacity, width)
    )
    incoming_grad = lax.all_to_all(outgoing_grad, "dp", split_axis=0, concat_axis=0, tiled=True)
    hidden_width = kept_gate.shape[2]
    rows = kept_rows.reshape(-1, width)
    rows_out_grad = incoming_grad.reshape(-1, width)
    hidden_rows, expert_vjp = jax.vjp(
        gated, kept_gate.reshape(-1, hidden_width), kept_up.reshape(-1, hidden_width)
    )
    hidden_rows = hidden_rows.astype(jnp.bfloat16)
    hidden_rows_grad = contract_last(rows_out_grad, exp_down)
    gate_rows_grad, up_rows_grad = expert_vjp(hidden_rows_grad)
    gate_rows_grad = gate_rows_grad.astype(jnp.bfloat16)
    up_rows_grad = up_rows_grad.astype(jnp.bfloat16)
    expert_gate_grad = contract_first(rows, gate_rows_grad)[None]
    expert_up_grad = contract_first(rows, up_rows_grad)[None]
    expert_down_grad = contract_first(hidden_rows, rows_out_grad)[None]
    rows_in_grad = (
        contract_last(gate_rows_grad, exp_gate) + contract_last(up_rows_grad, exp_up)
    ).reshape(experts, capacity, width)
    returned_grad = lax.all_to_all(rows_in_grad, "dp", split_axis=0, concat_axis=0, tiled=True)
    routed_grad = jnp.sum(
        returned_grad.reshape(slots, width)[dest].reshape(rows_dev, topk, width), axis=1
    )
    act_two_total = lax.psum(act_two_grad + routed_grad, "tensor")
    dummy_second, second_vjp = jax.vjp(rms_norm, x_mid, gain_two)
    mid_norm_grad, gain_two_grad = second_vjp(act_two_total)
    mid_grad = grad_out + mid_norm_grad
    ffn_sums = (gain_two_grad, common_gate_grad, common_up_grad, common_down_grad)
    attn_grad = mid_grad.astype(jnp.bfloat16)
    output_w_grad = contract_first(attn_grad, mixed)
    mixed_grad = (
        jnp.dot(attn_grad, output_whole, preferred_element_type=jnp.float32)
        .astype(jnp.bfloat16)
        .reshape(rows_dev, heads_dev, HD)
    )
    probs_again = jnp.exp(masked_scores(query_rot, key_rot, causal, scale) - log_total)
    value_grad = jnp.einsum(
        "hqk,qhc->khc",
        probs_again.astype(jnp.bfloat16),
        mixed_grad,
        preferred_element_type=jnp.float32,
    ).astype(jnp.bfloat16)
    prob_grad = jnp.einsum(
        "qhc,khc->hqk", mixed_grad, value_low, preferred_element_type=jnp.float32
    )
    delta = jnp.sum(probs_again * prob_grad, axis=-1, keepdims=True)
    score_grad = (probs_again * (prob_grad - delta)).astype(jnp.bfloat16)
    query_rot_grad = (
        jnp.einsum("hqk,khc->qhc", score_grad, key_rot, preferred_element_type=jnp.float32) * scale
    )
    key_rot_grad = (
        jnp.einsum("hqk,qhc->khc", score_grad, query_rot, preferred_element_type=jnp.float32)
        * scale
    )

    def turn(values):
        return rotate(values, positions)

    dummy_turn, turn_vjp = jax.vjp(turn, query_pre)
    query_grad = turn_vjp(query_rot_grad)[0].reshape(rows_dev, heads_dev * HD).astype(jnp.bfloat16)
    key_grad = turn_vjp(key_rot_grad)[0].reshape(rows_dev, heads_dev * HD).astype(jnp.bfloat16)
    value_flat = value_grad.reshape(rows_dev, heads_dev * HD)
    query_w_grad = contract_first(act_one, query_grad)
    key_w_grad = contract_first(act_one, key_grad)
    value_w_grad = contract_first(act_one, value_flat)
    act_one_grad = (
        contract_last(query_grad, query_whole)
        + contract_last(key_grad, key_whole)
        + contract_last(value_flat, value_whole)
    )
    act_one_total = lax.psum(act_one_grad, "tensor")
    dummy_first, first_vjp = jax.vjp(rms_norm, x_in, gain_one)
    in_norm_grad, gain_one_grad = first_vjp(act_one_total)
    tokens_grad = (mid_grad + in_norm_grad).astype(jnp.bfloat16)
    every = (
        lax.psum_scatter(gain_one_grad, "dp", scatter_dimension=0, tiled=True),
        lax.psum_scatter(query_w_grad, "dp", scatter_dimension=0, tiled=True),
        lax.psum_scatter(key_w_grad, "dp", scatter_dimension=0, tiled=True),
        lax.psum_scatter(value_w_grad, "dp", scatter_dimension=0, tiled=True),
        lax.psum_scatter(output_w_grad, "dp", scatter_dimension=0, tiled=True),
        lax.psum_scatter(ffn_sums[0], "dp", scatter_dimension=0, tiled=True),
        lax.psum_scatter(ffn_sums[1], "dp", scatter_dimension=0, tiled=True),
        lax.psum_scatter(ffn_sums[2], "dp", scatter_dimension=0, tiled=True),
        lax.psum_scatter(ffn_sums[3], "dp", scatter_dimension=0, tiled=True),
    )
    attn_sums = every[:5]
    ffn_sums = every[5:]
    return (
        layer_out,
        tokens_grad,
        attn_sums[0],
        attn_sums[1],
        attn_sums[2],
        attn_sums[3],
        attn_sums[4],
        ffn_sums[0],
        ffn_sums[1],
        ffn_sums[2],
        ffn_sums[3],
        expert_gate_grad,
        expert_up_grad,
        expert_down_grad,
    )


def place():
    d = lax.axis_index("dp"); y = lax.axis_index("tensor")
    c = lax.rem(d, 2); x = lax.rem(lax.div(d, 2), 2); z = lax.div(d, 4)
    return z, x, y, c

def dev(z, x, y, c):
    return ((z * 2 + x) * 2 + c, y)

def blk(z, x, y, c):
    return ((z * 2 + x) * 2 + c) * 2 + y

def greet(z, x, y, c):
    bar = pltpu.get_barrier_semaphore()
    for other in (dev(z, 1 - x, y, c), dev(z, x, 1 - y, c), dev(z, x, y, 1 - c)):
        pl.semaphore_signal(bar, inc=1, device_id=other, device_id_type=MESH)
    @pl.when(z > 0)
    def _():
        pl.semaphore_signal(bar, inc=1, device_id=dev(z - 1, x, y, c), device_id_type=MESH)
    @pl.when(z < 3)
    def _():
        pl.semaphore_signal(bar, inc=1, device_id=dev(z + 1, x, y, c), device_id_type=MESH)
    pl.semaphore_wait(bar, 3 + (z > 0).astype(jnp.int32) + (z < 3).astype(jnp.int32))

def rcopy(src, dst, ssem, rsem, device):
    return pltpu.make_async_remote_copy(src_ref=src, dst_ref=dst, send_sem=ssem, recv_sem=rsem, device_id=device, device_id_type=MESH)

def nearest(z, g):
    one = jnp.where(z == 0, 1, z - 1)
    two = jnp.where(z == 3, 1, jnp.where(z == 2, 3, 2))
    three = jnp.where(z >= 2, 0, 3)
    return jnp.where(g == 0, z, jnp.where(g == 1, one, jnp.where(g == 2, two, three)))

def nt(left, right):
    return lax.dot_general(left, right, (((1,), (1,)), ((), ())), preferred_element_type=jnp.float32)

def nn(left, right):
    return jnp.dot(left, right, preferred_element_type=jnp.float32)

def greet_all(z, x, y, c):
    bar = pltpu.get_barrier_semaphore()
    for other in (dev(z, 1 - x, y, c), dev(z, x, 1 - y, c), dev(z, x, y, 1 - c)):
        pl.semaphore_signal(bar, inc=1, device_id=other, device_id_type=MESH)
    for s in range(4):
        @pl.when(s != z)
        def _(): pl.semaphore_signal(bar, inc=1, device_id=dev(s, x, y, c), device_id_type=MESH)
    pl.semaphore_wait(bar, 6)


def expert_kernel(
    a_in, deh, dy_all, rank_row, rank_col, gate, wg_h, wu_h, wd_h, sgu_h, sdt_h, sd_h,
    total, act_all, rows_o, eh_o, deg_o, deu_o, hs_o, dsgu_o, part, ffn_part, gu_o, down_o,
    wg, wu, wd, sgu, tail, acc, ic, iy0, ix0, ix1, iy1, iz,
    eg, eu, dehb, ehb, degb, deub, sd, dhs, hsb, dsgub, eh2, hs2, ot, gub, downb,
    wsem, usem, ssem, osem, psem, lsem, tsem, gsem, fsem,
    zs, zr, x0s, x0r, x1s, x1r, y0s, y0r, y1s, y1r, cs, cr,
    ls, rcs, rcr, ry0s, ry0r, rx0s, rx0r, rx1s, rx1r, ry1s, ry1r, rzs, rzr,
):
    f32, bf16 = jnp.float32, jnp.bfloat16
    z, x, y, c = place()
    rows, width = a_in.shape
    h = rows // 2
    cap = deh.shape[1]
    toks = 2 * rows
    lo, hi = pl.ds(0, h), pl.ds(h, h)
    part_of = (lo, hi)
    xn, yn, cn = dev(z, 1 - x, y, c), dev(z, x, 1 - y, c), dev(z, x, y, 1 - c)
    greet_all(z, x, y, c)
    mine = blk(z, x, y, c)
    own = pltpu.make_async_copy(a_in, act_all.at[mine], lsem)
    own.start()
    weights = [
        pltpu.make_async_copy(a, b, wsem.at[i])
        for i, (a, b) in enumerate(((wg_h, wg), (wu_h, wu), (wd_h, wd), (sgu_h, sgu), (sdt_h, tail.at[pl.ds(cap, 256 - cap)]), (sd_h, sd)))
    ]
    for w in weights:
        w.start()

    def zcopy(s, up):
        b = act_all.at[blk(s, x, y, c)]
        return rcopy(b, b, zs.at[s, up], zr.at[s], dev(z + 2 * up - 1, x, y, c))

    def half_copy(s, xx, yy, p, send, recv, to):
        b = act_all.at[blk(s, xx, yy, c), part_of[p]]
        return rcopy(b, b, send, recv, to)

    def x0(s): return half_copy(s, x, y, 0, x0s.at[s], x0r.at[s], xn)
    def y1(s): return half_copy(s, x, y, 1, y1s.at[s], y1r.at[s], yn)
    def y0(s, xx): return half_copy(s, xx, y, 0, y0s.at[s, xx], y0r.at[s, xx], yn)
    def x1(s, yy): return half_copy(s, x, yy, 1, x1s.at[s, yy], x1r.at[s, yy], xn)
    def side(s, xx, yy, p):
        i = (s * 2 + xx) * 2 + yy
        return half_copy(s, xx, yy, p, cs.at[i, p], cr.at[i, p], cn)

    def column(s):
        x0(s).start(); y1(s).start(); y0(s, x).start(); x1(s, y).start()
        side(s, x, y, 0).start(); side(s, x, y, 1).start()

    def arrive(g):
        s = nearest(z, g)
        up = (s < z).astype(jnp.int32)
        nxt = z + 2 * up - 1
        zcopy(s, up).wait_recv()
        @pl.when((nxt >= 0) & (nxt <= 3))
        def _(): zcopy(s, up).start()
        column(s)

    def middle(g):
        s = nearest(z, g)
        x0(s).wait_recv()
        y0(s, 1 - x).start(); side(s, 1 - x, y, 0).start()
        y1(s).wait_recv()
        x1(s, 1 - y).start(); side(s, x, 1 - y, 1).start()

    def last_own(g):
        s = nearest(z, g)
        y0(s, x).wait_recv(); side(s, x, 1 - y, 0).start()

    def last_other(g):
        s = nearest(z, g)
        x1(s, y).wait_recv(); side(s, 1 - x, y, 1).start()
        y0(s, 1 - x).wait_recv(); side(s, 1 - x, 1 - y, 0).start()
        x1(s, 1 - y).wait_recv(); side(s, 1 - x, 1 - y, 1).start()

    def spread_cols(j):
        ranks = rank_col[j]
        slot = lax.broadcasted_iota(jnp.int32, (toks, 128), 1)
        one = jnp.where(ranks == slot, 1.0, 0.0)
        two = jnp.where(ranks == slot + 128, 1.0, 0.0)
        return one, two

    def seq_of(u):
        s = nearest(z, u // 2)
        xx = lax.rem(x + lax.rem(u, 2), 2)
        return s, xx

    def stores(u):
        s, xx = seq_of(u)
        out = []
        for k in (0, 1):
            j = (s * 2 + xx) * 2 + k
            r = pl.ds(k * cap, cap)
            out += [
                pltpu.make_async_copy(acc.at[k], rows_o.at[j], ssem.at[k, 0]),
                pltpu.make_async_copy(ehb.at[r], eh_o.at[j], ssem.at[k, 1]),
                pltpu.make_async_copy(degb.at[r], deg_o.at[j], ssem.at[k, 2]),
                pltpu.make_async_copy(deub.at[r], deu_o.at[j], ssem.at[k, 3]),
                pltpu.make_async_copy(hsb.at[pl.ds(2 * k, 2)], hs_o.at[pl.ds(2 * j, 2)], ssem.at[k, 4]),
                pltpu.make_async_copy(dsgub.at[pl.ds(2 * k, 2)], dsgu_o.at[pl.ds(2 * j, 2)], ssem.at[k, 5]),
            ]
        return out

    def at(s, xx, yy): return (s * 2 + xx) * 2 + yy
    def keep(u, k):
        s, xx = seq_of(u)
        return pltpu.make_async_copy(acc.at[pl.ds(10 + 2 * k, 2)], part.at[pl.ds(at(s, xx, 0), 2)], ssem.at[k, 6])
    def cross(s, xx, yy, k):
        i = at(s, xx, yy)
        return rcopy(acc.at[10 + 2 * k + yy], ic.at[i], rcs.at[i], rcr.at[i], cn)
    def hand_over(u):
        s, xx = seq_of(u)
        for k in (0, 1):
            @pl.when(c == k)
            def _(): keep(u, k).start()
            @pl.when(c != k)
            def _():
                for yy in (0, 1):
                    cross(s, xx, yy, k).start()
    def handed_over(u):
        s, xx = seq_of(u)
        for k in (0, 1):
            @pl.when(c == k)
            def _(): keep(u, k).wait()
            @pl.when(c != k)
            def _():
                for yy in (0, 1):
                    cross(s, xx, yy, k).wait_send()

    def unit(u):
        s, xx = seq_of(u)
        base = (s * 2 + xx) * 2
        for k in (0, 1):
            pltpu.make_async_copy(deh.at[base + k], dehb.at[pl.ds(k * cap, cap)], usem.at[k, 1]).start()
        for yy in (0, 1):
            for p in (0, 1):
                side(s, xx, yy, p).wait_recv()
        loads = [
            pltpu.make_async_copy(act_all.at[pl.ds(2 * (base + k), 2)], acc.at[pl.ds(4 + 2 * k, 2)], usem.at[k, 0])
            for k in (0, 1)
        ]
        for k in (0, 1):
            loads[k].start()
        @pl.when(u > 0)
        def _():
            for copy in stores(u - 1):
                copy.wait()
            handed_over(u - 1)
        for k in (0, 1):
            loads[k].wait()
            act = acc[4 + 2 * k:6 + 2 * k].reshape(toks, width)
            ranks = rank_row[base + k]
            slot = lax.broadcasted_iota(jnp.int32, (cap, toks), 0)
            pick = jnp.where(ranks == slot, 1.0, 0.0).astype(bf16)
            acc[k] = nn(pick, act).astype(bf16)
            pre = nn(act, sgu[...])
            gp, up = pre[:, :128], pre[:, 128:]
            dh = dhs[base + k]
            sig = jax.nn.sigmoid(gp)
            hsb[2 * k:2 * k + 2] = (gp * sig * up).astype(bf16).reshape(2, rows, 128)
            dsgub[2 * k:2 * k + 2, :, 0:128] = (dh * up * sig * (1.0 + gp * (1.0 - sig))).astype(bf16).reshape(2, rows, 128)
            dsgub[2 * k:2 * k + 2, :, 128:256] = (dh * gp * sig).astype(bf16).reshape(2, rows, 128)
        picked = acc[0:2].reshape(2 * cap, width)
        eg[...] = nt(picked, wg[...])
        eu[...] = nt(picked, wu[...])
        for k in (0, 1):
            pltpu.make_async_copy(deh.at[base + k], dehb.at[pl.ds(k * cap, cap)], usem.at[k, 1]).wait()
        @pl.loop(0, 2 * cap // 32)
        def _(r):
            q = pl.ds(pl.multiple_of(r * 32, 32), 32)
            gp, up, dh = eg[q], eu[q], dehb[q]
            sig = jax.nn.sigmoid(gp)
            silu = gp * sig
            ehb[q] = (silu * up).astype(bf16)
            degb[q] = (dh * up * sig * (1.0 + gp * (1.0 - sig))).astype(bf16)
            deub[q] = (dh * silu).astype(bf16)
        dg, du = degb[...], deub[...]
        for n in range(0, width, 512):
            w = pl.ds(n, 512)
            back = (nn(dg, wg[:, w]) + nn(du, wu[:, w])).astype(bf16)
            acc[8, :, w] = back[:cap]
            acc[9, :, w] = back[cap:]
        for k in (0, 1):
            one, two = spread_cols(base + k)
            left = jnp.concatenate([one, two], axis=1)[:, :cap].astype(bf16)
            for n in range(0, width, 512):
                w = pl.ds(n, 512)
                out = nn(left, acc[8 + k, :, w]) + nt(dsgub[2 * k:2 * k + 2].reshape(toks, 256), sgu[w, :])
                out = out.astype(bf16)
                acc[10 + 2 * k, :, w] = out[:rows]
                acc[11 + 2 * k, :, w] = out[rows:]
        for copy in stores(u):
            copy.start()
        hand_over(u)

    def ry0(s, xx):
        return rcopy(ic.at[at(s, xx, 1 - y), lo], iy0.at[s * 2 + xx], ry0s.at[s, xx], ry0r.at[s, xx], yn)
    def rx1(s, yy):
        return rcopy(ic.at[at(s, 1 - x, yy), hi], ix1.at[s * 2 + yy], rx1s.at[s, yy], rx1r.at[s, yy], xn)
    def rx0(s):
        return rcopy(ic.at[at(s, 1 - x, y), lo], ix0.at[s], rx0s.at[s], rx0r.at[s], xn)
    def ry1(s):
        return rcopy(ic.at[at(s, x, 1 - y), hi], iy1.at[s], ry1s.at[s], ry1r.at[s], yn)
    def rz(s):
        return rcopy(ic.at[at(s, x, y)], iz.at[z], rzs.at[s], rzr.at[z], dev(s, x, y, c))
    def rz_wait(s):
        rcopy(iz.at[s], iz.at[s], rzs.at[s], rzr.at[s], dev(s, x, y, c)).wait_recv()
    def add(i, start, count, src, j):
        @pl.loop(0, count // 16)
        def _(r):
            a = pl.ds(pl.multiple_of(start + r * 16, 16), 16)
            b = pl.ds(pl.multiple_of(r * 16, 16), 16)
            ic[i, a] = ic[i, a] + src[j, b]

    def first(g):
        s = nearest(z, g)
        def load(xx, yy):
            return pltpu.make_async_copy(part.at[at(s, xx, yy)], acc.at[4 + 2 * xx + yy], ls.at[2 * xx + yy])
        for xx in (0, 1):
            for yy in (0, 1):
                load(xx, yy).start()
        for xx in (0, 1):
            for yy in (0, 1):
                load(xx, yy).wait(); cross(s, xx, yy, 0).wait_recv()
                add(at(s, xx, yy), 0, rows, acc, 4 + 2 * xx + yy)
                @pl.when(yy != y)
                def _(): ry0(s, xx).start()
                @pl.when(xx != x)
                def _(): rx1(s, yy).start()

    def second(g):
        s = nearest(z, g)
        ry0(s, 1 - x).wait_recv(); add(at(s, 1 - x, y), 0, h, iy0, s * 2 + 1 - x); rx0(s).start()
        rx1(s, 1 - y).wait_recv(); add(at(s, x, 1 - y), h, h, ix1, s * 2 + 1 - y); ry1(s).start()
        ry0(s, x).wait_recv(); add(at(s, x, y), 0, h, iy0, s * 2 + x)
        rx1(s, y).wait_recv(); add(at(s, x, y), h, h, ix1, s * 2 + y)

    def third(g):
        s = nearest(z, g)
        me = at(s, x, y)
        rx0(s).wait_recv(); add(me, 0, h, ix0, s)
        ry1(s).wait_recv(); add(me, h, h, iy1, s)
        if g > 0:
            rz(s).start()

    own.wait()
    @pl.when(z < 3)
    def _(): zcopy(z, 1).start()
    @pl.when(z > 0)
    def _(): zcopy(z, 0).start()
    column(z)
    def dy_load(j, b):
        return pltpu.make_async_copy(dy_all.at[pl.ds(2 * j, 2)], acc.at[pl.ds(2 + 12 * b, 2)], usem.at[b, 2])
    dy_load(0, 0).start()
    for w in weights:
        w.wait()
    @pl.loop(0, 8)
    def _(i):
        for b in (0, 1):
            j = 2 * i + b
            @pl.when(j < 15)
            def _(): dy_load(j + 1, 1 - b).start()
            dy_load(j, b).wait()
            dhs[j] = nn(acc[2 + 12 * b:4 + 12 * b].reshape(toks, width), sd[...])

    @pl.loop(0, 8)
    def _(u):
        @pl.when(u == 0)
        def _():
            middle(0); last_own(0); arrive(1)
        @pl.when(u == 1)
        def _():
            last_other(0); arrive(2); middle(1)
        @pl.when(u == 2)
        def _():
            arrive(3); last_own(1); middle(2)
        @pl.when(u == 3)
        def _():
            last_other(1); middle(3); first(0)
        @pl.when(u == 4)
        def _():
            last_own(2)
        @pl.when(u == 5)
        def _():
            last_other(2); first(1)
        @pl.when(u == 6)
        def _():
            last_own(3); second(0)
        @pl.when(u == 7)
        def _():
            last_other(3); first(2); third(0)
        unit(u)

    for copy in stores(7):
        copy.wait()
    handed_over(7)

    def out_loads(j, b):
        return [
            pltpu.make_async_copy(eh_o.at[j], eh2.at[b], osem.at[b, 0]),
            pltpu.make_async_copy(hs_o.at[pl.ds(2 * j, 2)], hs2.at[b], osem.at[b, 1]),
        ]
    def out_store(j, b):
        return pltpu.make_async_copy(ot.at[b], ffn_part.at[pl.ds(2 * j, 2)], psem.at[b])

    def forward_out(j):
        b = lax.rem(j, 2)
        @pl.when(j < 15)
        def _():
            for copy in out_loads(j + 1, 1 - b):
                copy.start()
        for copy in out_loads(j, b):
            copy.wait()
        @pl.when(j >= 2)
        def _(): out_store(j - 2, b).wait()
        weight = gate[j]
        for n in range(0, width, 512):
            w = pl.ds(n, 512)
            tail[0:cap, w] = (nn(eh2[b], wd[:, w]) * weight).astype(bf16)
        one, two = spread_cols(j)
        left = jnp.concatenate([one, two + hs2[b].reshape(toks, 128).astype(f32)], axis=1).astype(bf16)
        for n in range(0, width, 512):
            w = pl.ds(n, 512)
            out = nn(left, tail[:, w]).astype(bf16)
            ot[b, 0, :, w] = out[:rows]
            ot[b, 1, :, w] = out[rows:]
        out_store(j, b).start()

    for copy in out_loads(0, 0):
        copy.start()

    first(3); second(1)
    second(2); third(1)
    def tn(left, right):
        return lax.dot_general(left, right, (((0,), (0,)), ((), ())), preferred_element_type=f32)
    def flat(first, count):
        return acc[:, :, first:first + count].reshape(16 * rows, count)
    fixed = []
    for q in (0, 1):
        half = pl.ds(16 * q, 16)
        fixed.append(pltpu.make_async_copy(dsgu_o.at[half], acc.at[:, :, pl.ds(256 * q, 256)], fsem.at[q]))
        fixed.append(pltpu.make_async_copy(hs_o.at[half], acc.at[:, :, pl.ds(512 + 128 * q, 128)], fsem.at[2 + q]))
    def feature(i, b):
        return pl.ds(pl.multiple_of(lax.rem(2 * i + b, 8) * 256, 256), 256)
    def tile_load(source, i, b):
        return [
            pltpu.make_async_copy(
                source.at[pl.ds(16 * q, 16), :, feature(i, b)], acc.at[:, :, pl.ds(768 + 512 * b + 256 * q, 256)], tsem.at[b, q]
            )
            for q in (0, 1)
        ]
    def tile_start(i, b):
        @pl.when(i < 4)
        def _():
            for copy in tile_load(act_all, i, b):
                copy.start()
        @pl.when((i >= 4) & (i < 8))
        def _():
            for copy in tile_load(dy_all, i, b):
                copy.start()
    def gu_store(i, b):
        return pltpu.make_async_copy(gub.at[b], gu_o.at[feature(i, b)], gsem.at[0, b])
    def down_store(i, b):
        return pltpu.make_async_copy(downb.at[b], down_o.at[feature(i, b)], gsem.at[1, b])
    for copy in fixed:
        copy.start()
    tile_start(0, 0)
    for copy in fixed:
        copy.wait()

    @pl.loop(0, 8)
    def _(i):
        @pl.when(i == 1)
        def _():
            second(3); third(2)
        @pl.when(i == 3)
        def _(): third(3)
        for b in (0, 1):
            tile_start(i + b, 1 - b)
            forward_out(2 * i + b)
            for copy in tile_load(act_all, i, b):
                copy.wait()
            base = 768 + 512 * b
            @pl.when((i > 0) & (i < 5))
            def _(): gu_store(i, b).wait()
            @pl.when(i > 4)
            def _(): down_store(i, b).wait()
            @pl.when(i < 4)
            def _():
                out = tn(flat(base, 256), flat(0, 256)) + tn(flat(base + 256, 256), flat(256, 256))
                gub[b] = out.astype(bf16)
                gu_store(i, b).start()
            @pl.when(i >= 4)
            def _():
                out = tn(flat(base, 256), flat(512, 128)) + tn(flat(base + 256, 256), flat(640, 128))
                downb[b] = out.astype(bf16)
                down_store(i, b).start()
    for b in (0, 1):
        down_store(7, b).wait()
    me = at(z, x, y)
    for g in (1, 2, 3):
        rz_wait(nearest(z, g))
    @pl.loop(0, rows // 16)
    def _(r):
        q = pl.ds(pl.multiple_of(r * 16, 16), 16)
        out = ic[me, q].astype(f32)
        for g in (1, 2, 3):
            out = out + iz[nearest(z, g), q].astype(f32)
        total[q] = out
    out_store(14, 0).wait()
    out_store(15, 1).wait()

    for s in range(4):
        @pl.when((z < 3) & (s <= z))
        def _(): zcopy(s, 1).wait_send()
        @pl.when((z > 0) & (s >= z))
        def _(): zcopy(s, 0).wait_send()
        x0(s).wait_send(); y1(s).wait_send()
        rx0(s).wait_send(); ry1(s).wait_send()
        for q in (0, 1):
            y0(s, q).wait_send(); x1(s, q).wait_send()
            ry0(s, q).wait_send(); rx1(s, q).wait_send()
            for r in (0, 1):
                for p in (0, 1):
                    side(s, q, r, p).wait_send()
        @pl.when(s != z)
        def _():
            rz(s).wait_send()

def expert_layer(act, deh, dy_all, rank_row, rank_col, gate, wg, wu, wd, sgu, sdt, sd, cid):
    rows, width = act.shape
    cap, hidden = deh.shape[1:]
    h = rows // 2
    f32, bf16 = jnp.float32, jnp.bfloat16
    D = pltpu.SemaphoreType.DMA
    S = jax.ShapeDtypeStruct
    any_ = pl.BlockSpec(memory_space=pl.ANY)
    vm = pl.BlockSpec(memory_space=pltpu.VMEM)
    V = lambda *shape, t=bf16: pltpu.VMEM(shape, t)
    return pl.pallas_call(
        expert_kernel,
        out_shape=[
            S((rows, width), f32), S((32, rows, width), bf16), S((16, cap, width), bf16),
            S((16, cap, hidden), bf16), S((16, cap, hidden), bf16), S((16, cap, hidden), bf16),
            S((32, rows, 128), bf16), S((32, rows, 256), bf16),
            S((16, rows, width), bf16), S((32, rows, width), bf16), S((width, 256), bf16), S((width, 128), bf16),
        ],
        in_specs=[vm, any_, any_, vm, vm, vm] + [any_] * 6,
        out_specs=[vm] + [any_] * 11,
        scratch_shapes=[
            V(*wg.shape), V(*wu.shape), V(*wd.shape), V(*sgu.shape), V(256, width),
            V(16, rows, width), V(16, rows, width), V(8, h, width), V(4, h, width), V(8, h, width), V(4, h, width),
            V(4, rows, width),
            V(2 * cap, hidden, t=f32), V(2 * cap, hidden, t=f32), V(2 * cap, hidden, t=f32),
            V(2 * cap, hidden), V(2 * cap, hidden), V(2 * cap, hidden),
            V(*sd.shape), V(16, 2 * rows, 128, t=f32), V(4, rows, 128), V(4, rows, 256),
            V(2, cap, hidden), V(2, 2, rows, 128), V(2, 2, rows, width), V(2, 256, 256), V(2, 256, 128),
            D((6,)), D((2, 3)), D((2, 7)), D((2, 2)), D((2,)), D, D((2, 2)), D((2, 2)), D((4,)),
            D((4, 2)), D((4,)), D((4,)), D((4,)), D((4, 2)), D((4, 2)), D((4, 2)), D((4, 2)), D((4,)), D((4,)), D((16, 2)), D((16, 2)),
            D((4,)), D((16,)), D((16,)), D((4, 2)), D((4, 2)), D((4,)), D((4,)), D((4, 2)), D((4, 2)), D((4,)), D((4,)),
            D((4,)), D((4,)),
        ],
        compiler_params=pltpu.CompilerParams(collective_id=cid, has_side_effects=True, vmem_limit_bytes=63 << 20),
        name="expert_layer",
    )(act, deh, dy_all, rank_row, rank_col, gate, wg, wu, wd, sgu, sdt, sd)


def norm_back(values, gain, grad):
    width = values.shape[1]
    inv = lax.rsqrt(jnp.sum(values * values, axis=1, keepdims=True) * (1.0 / width) + EPS)
    scaled = grad * gain
    inner = jnp.sum(values * scaled, axis=1, keepdims=True) * (1.0 / width)
    normed = values * inv
    return inv * (scaled - normed * (inv * inner)), grad * normed

def attention_back_kernel(
    part, grad2, x_mid, dy, x_in, gain1, gain2, wq_h, wk_h, wv_h, wo_h, qr, kr, vr, cosine, sine,
    out_half, tok_half, dattn, dq, dk, dv, g1, g2,
    ic, tmp, iy0, ix0, ix1, iy1, izu, izd, wa, wb, wc, dmix, dx2, da1, send1, recv1,
    wsem, ysem, ls, rcs, rcr, ry0s, ry0r, rx0s, rx0r, rx1s, rx1r, ry1s, ry1r, zus, zur, zds, zdr,
):
    f32, bf16 = jnp.float32, jnp.bfloat16
    z, x, y, c = place()
    rows, width = x_mid.shape
    h = 48
    toks = 2 * rows
    heads = qr.shape[1] // HD
    lo, hi = pl.ds(0, h), pl.ds(h, rows - h)
    xn, yn, cn = dev(z, 1 - x, y, c), dev(z, x, 1 - y, c), dev(z, x, y, 1 - c)
    greet(z, x, y, c)

    def at(s, xx, yy): return (s * 2 + xx) * 2 + yy
    def load(s, xx, yy):
        return pltpu.make_async_copy(part.at[blk(s, xx, yy, c)], tmp.at[xx * 2 + yy], ls.at[xx * 2 + yy])
    def cross(s, xx, yy):
        i = at(s, xx, yy)
        return rcopy(part.at[blk(s, xx, yy, 1 - c)], ic.at[i], rcs.at[i], rcr.at[i], cn)
    def ry0(s, xx):
        return rcopy(ic.at[at(s, xx, 1 - y), lo], iy0.at[s * 2 + xx], ry0s.at[s, xx], ry0r.at[s, xx], yn)
    def rx1(s, yy):
        return rcopy(ic.at[at(s, 1 - x, yy), hi], ix1.at[s * 2 + yy], rx1s.at[s, yy], rx1r.at[s, yy], xn)
    def rx0(s):
        return rcopy(ic.at[at(s, 1 - x, y), lo], ix0.at[s], rx0s.at[s], rx0r.at[s], xn)
    def ry1(s):
        return rcopy(ic.at[at(s, x, 1 - y), hi], iy1.at[s], ry1s.at[s], ry1r.at[s], yn)
    def zu(s):
        return rcopy(ic.at[at(s, x, y)], izu.at[s], zus.at[s], zur.at[s], dev(z + 1, x, y, c))
    def zd(s):
        return rcopy(ic.at[at(s, x, y)], izd.at[s], zds.at[s], zdr.at[s], dev(z - 1, x, y, c))
    def add(i, start, count, src, j):
        @pl.loop(0, count // 16)
        def _(r):
            a = pl.ds(pl.multiple_of(start + r * 16, 16), 16)
            b = pl.ds(pl.multiple_of(r * 16, 16), 16)
            ic[i, a] = ic[i, a] + src[j, b]

    four = [(xx, yy) for xx in (0, 1) for yy in (0, 1)]

    def first(g):
        s = nearest(z, g)
        for xx, yy in four:
            load(s, xx, yy).wait(); cross(s, xx, yy).wait_recv()
            add(at(s, xx, yy), 0, rows, tmp, xx * 2 + yy)
            @pl.when(yy != y)
            def _(): ry0(s, xx).start()
            @pl.when(xx != x)
            def _(): rx1(s, yy).start()
        if g > 0:
            for xx, yy in four:
                load(nearest(z, g - 1), xx, yy).start()

    def second(g):
        s = nearest(z, g)
        ry0(s, 1 - x).wait_recv(); add(at(s, 1 - x, y), 0, h, iy0, s * 2 + 1 - x); rx0(s).start()
        rx1(s, 1 - y).wait_recv(); add(at(s, x, 1 - y), h, rows - h, ix1, s * 2 + 1 - y); ry1(s).start()
        ry0(s, x).wait_recv(); add(at(s, x, y), 0, h, iy0, s * 2 + x)
        rx1(s, y).wait_recv(); add(at(s, x, y), h, rows - h, ix1, s * 2 + y)

    def third(g):
        s = nearest(z, g)
        me = at(s, x, y)
        rx0(s).wait_recv(); add(me, 0, h, ix0, s)
        ry1(s).wait_recv(); add(me, h, rows - h, iy1, s)
        @pl.when((s >= z) & (z > 0))
        def _():
            zu(s).wait_recv(); add(me, 0, rows, izu, s)
        @pl.when((s <= z) & (z < 3))
        def _():
            zd(s).wait_recv(); add(me, 0, rows, izd, s)
        @pl.when(s > z)
        def _(): zu(s).start()
        @pl.when(s < z)
        def _(): zd(s).start()

    for g in (3, 2, 1, 0):
        s = nearest(z, g)
        for xx, yy in four:
            cross(s, xx, yy).start()
            if g == 3:
                load(s, xx, yy).start()
    w_out = pltpu.make_async_copy(wo_h, wa, wsem.at[0])
    w_query = pltpu.make_async_copy(wq_h, wb, wsem.at[1])
    w_key = pltpu.make_async_copy(wk_h, wc, wsem.at[2])
    w_value = pltpu.make_async_copy(wv_h, wa, wsem.at[3])
    w_out.start(); w_query.start(); w_key.start()

    g1[...] = jnp.zeros_like(g1)
    g2[...] = jnp.zeros_like(g2)
    @pl.loop(0, rows // 16)
    def _(r):
        q = pl.ds(pl.multiple_of(r * 16, 16), 16)
        back, terms = norm_back(x_mid[q], gain2[...], grad2[q])
        back = back + dy[pl.ds(pl.multiple_of(y * rows + r * 16, 16), 16)].astype(f32)
        dx2[q] = back
        dattn[y, q] = back.astype(bf16)
        g2[...] += jnp.sum(terms, axis=0, keepdims=True)
    attn_swap = rcopy(dattn.at[y], dattn.at[y], ysem.at[0], ysem.at[1], yn)
    attn_swap.start()
    first(3)
    first(2)
    w_out.wait()
    attn_swap.wait_recv()
    full = dattn[...].reshape(toks, width)
    dmix[...] = nn(full, wa[...]).astype(bf16)
    w_value.start()

    scale = HD ** (-0.5)
    def turn_back(values):
        return values * cosine[...] - pltpu.roll(values, HD // 2, 1) * sine[...]
    @pl.loop(0, heads)
    def _(n):
        @pl.when(n == 2)
        def _():
            second(3); first(1)
        @pl.when(n == 5)
        def _():
            second(2); third(3); first(0)
        w = pl.ds(pl.multiple_of(n * HD, HD), HD)
        qh, kh, vh, doh = qr[:, w], kr[:, w], vr[:, w], dmix[:, w]
        scores = nt(qh, kh) * scale
        ahead = lax.broadcasted_iota(jnp.int32, (toks, toks), 0) >= lax.broadcasted_iota(jnp.int32, (toks, toks), 1)
        scores = jnp.where(ahead, scores, -1e30)
        expo = jnp.exp(scores - jnp.max(scores, axis=1, keepdims=True))
        probs = expo * (1.0 / jnp.sum(expo, axis=1, keepdims=True))
        dv[:, w] = lax.dot_general(
            probs.astype(bf16), doh, (((0,), (0,)), ((), ())), preferred_element_type=f32
        ).astype(bf16)
        dprob = nt(doh, vh)
        delta = jnp.sum(probs * dprob, axis=1, keepdims=True)
        ds = (probs * (dprob - delta)).astype(bf16)
        dq[:, w] = turn_back(nn(ds, kh) * scale).astype(bf16)
        dkr = lax.dot_general(ds, qh, (((0,), (0,)), ((), ())), preferred_element_type=f32)
        dk[:, w] = turn_back(dkr * scale).astype(bf16)

    w_query.wait(); w_key.wait(); w_value.wait()
    for n in range(0, width, 512):
        w = pl.ds(n, 512)
        out = nt(dq[...], wb[w, :]) + nt(dk[...], wc[w, :]) + nt(dv[...], wa[w, :])
        da1[0, :, w] = out[:rows]
        da1[1, :, w] = out[rows:]
    @pl.loop(0, rows // 16)
    def _(r):
        q = pl.ds(pl.multiple_of(r * 16, 16), 16)
        send1[q] = da1[1 - y, q].astype(bf16)
    da1_swap = rcopy(send1, recv1, ysem.at[2], ysem.at[3], yn)
    da1_swap.start()
    second(1); third(2)
    da1_swap.wait_recv()
    @pl.loop(0, rows // 16)
    def _(r):
        q = pl.ds(pl.multiple_of(r * 16, 16), 16)
        back, terms = norm_back(
            x_in[pl.ds(pl.multiple_of(y * rows + r * 16, 16), 16)].astype(f32), gain1[...], da1[y, q] + recv1[q].astype(f32)
        )
        tok_half[q] = (back + dx2[q]).astype(bf16)
        g1[...] += jnp.sum(terms, axis=0, keepdims=True)
    second(0); third(1); third(0)
    @pl.loop(0, rows // 16)
    def _(r):
        q = pl.ds(pl.multiple_of(r * 16, 16), 16)
        out_half[q] = (x_mid[q] + ic[at(z, x, y), q].astype(f32)).astype(bf16)
    for swap in (attn_swap, da1_swap):
        swap.wait_send()
    for s in range(4):
        rx0(s).wait_send(); ry1(s).wait_send()
        for q in (0, 1):
            ry0(s, q).wait_send(); rx1(s, q).wait_send()
            for r in (0, 1):
                cross(s, q, r).wait_send()
        @pl.when(s > z)
        def _(): zu(s).wait_send()
        @pl.when(s < z)
        def _(): zd(s).wait_send()

def attention_back(part, grad2, x_mid, dy, x_in, gain1, gain2, weights, qr, kr, vr, cosine, sine, cid):
    rows, width = x_mid.shape
    toks, hw = qr.shape
    h = 48
    f32, bf16 = jnp.float32, jnp.bfloat16
    D = pltpu.SemaphoreType.DMA
    S = jax.ShapeDtypeStruct
    any_ = pl.BlockSpec(memory_space=pl.ANY)
    vm = pl.BlockSpec(memory_space=pltpu.VMEM)
    V = lambda *shape, t=bf16: pltpu.VMEM(shape, t)
    return pl.pallas_call(
        attention_back_kernel,
        out_shape=[
            S((rows, width), bf16), S((rows, width), bf16), S((2, rows, width), bf16),
            S((toks, hw), bf16), S((toks, hw), bf16), S((toks, hw), bf16), S((1, width), f32), S((1, width), f32),
        ],
        in_specs=[any_] + [vm] * 6 + [any_] * 4 + [vm] * 5,
        out_specs=[vm] * 8,
        scratch_shapes=[
            V(16, rows, width), V(4, rows, width), V(8, h, width), V(4, h, width), V(8, rows - h, width), V(4, rows - h, width),
            V(4, rows, width), V(4, rows, width),
            V(width, hw), V(width, hw), V(width, hw), V(toks, hw), V(rows, width, t=f32), V(2, rows, width, t=f32),
            V(rows, width), V(rows, width),
            D((4,)), D((4,)), D((4,)), D((16,)), D((16,)), D((4, 2)), D((4, 2)), D((4,)), D((4,)), D((4, 2)), D((4, 2)), D((4,)), D((4,)),
            D((4,)), D((4,)), D((4,)), D((4,)),
        ],
        compiler_params=pltpu.CompilerParams(collective_id=cid, has_side_effects=True, vmem_limit_bytes=63 << 20),
        name="attention_back",
    )(part, grad2, x_mid, dy, x_in, gain1, gain2, *weights, qr, kr, vr, cosine, sine)

def weight_grad_kernel(
    a1, dattn, dq, dk, dv, mixed, gains, out_half, tok_half,
    oq, ok, ov, oo, og, out_full, tok_full,
    acc, ic, ix, izu, izd, gc, gx, gu, gd, gy, gbuf,
    cs, cr, xs, xr, zus, zur, zds, zdr, gss, gsr, fsem,
):
    f32, bf16 = jnp.float32, jnp.bfloat16
    z, x, y, c = place()
    xn, yn, cn = dev(z, 1 - x, y, c), dev(z, x, 1 - y, c), dev(z, x, y, 1 - c)
    n, depth = 4, acc.shape[2]
    outs = (oq, ok, ov, oo)
    greet(z, x, y, c)
    def pos(s, xx, cc): return (s * 2 + xx) * 2 + cc
    def wc(a, s, xx):
        i = s * 2 + xx
        return rcopy(acc.at[a, pos(s, xx, 1 - c)], ic.at[a, i], cs.at[a, i], cr.at[a, i], cn)
    def wx(a, s):
        return rcopy(acc.at[a, pos(s, 1 - x, c)], ix.at[a, s], xs.at[a, s], xr.at[a, s], xn)
    def zu(a, s):
        return rcopy(acc.at[a, pos(s, x, c)], izu.at[a, s], zus.at[a, s], zur.at[a, s], dev(z + 1, x, y, c))
    def zd(a, s):
        return rcopy(acc.at[a, pos(s, x, c)], izd.at[a, s], zds.at[a, s], zdr.at[a, s], dev(z - 1, x, y, c))
    def add(a, i, src, j):
        @pl.loop(0, depth // 16)
        def _(r):
            b = pl.ds(pl.multiple_of(r * 16, 16), 16)
            acc[a, i, b] = acc[a, i, b] + src[a, j, b]
    def make(g):
        s = nearest(z, g)
        w = pl.ds(pl.multiple_of(s * 4 * depth, 4 * depth), 4 * depth)
        for a, (left, right) in ((3, (dattn, mixed)), (0, (a1, dq)), (1, (a1, dk)), (2, (a1, dv))):
            out = lax.dot_general(left[:, w], right[...], (((0,), (0,)), ((), ())), preferred_element_type=f32).astype(bf16)
            for i in range(4):
                acc[a, s * 4 + i] = out[i * depth:(i + 1) * depth]
            for q in (0, 1):
                wc(a, s, q).start()
    def first(g):
        s = nearest(z, g)
        for a in (3, 0, 1, 2):
            for q in (0, 1):
                wc(a, s, q).wait_recv()
                add(a, pos(s, q, c), ic, s * 2 + q)
            wx(a, s).start()
    def second(g):
        s = nearest(z, g)
        for a in (3, 0, 1, 2):
            wx(a, s).wait_recv(); add(a, pos(s, x, c), ix, s)
            @pl.when((s >= z) & (z > 0))
            def _():
                zu(a, s).wait_recv(); add(a, pos(s, x, c), izu, s)
            @pl.when((s <= z) & (z < 3))
            def _():
                zd(a, s).wait_recv(); add(a, pos(s, x, c), izd, s)
            @pl.when(s > z)
            def _(): zu(a, s).start()
            @pl.when(s < z)
            def _(): zd(a, s).start()
    g_c = rcopy(gains.at[1 - c], gc, gss.at[0], gsr.at[0], cn)
    g_x = rcopy(gbuf.at[1 - x], gx, gss.at[1], gsr.at[1], xn)
    g_u = rcopy(gu.at[1], gu.at[0], gss.at[2], gsr.at[2], dev(z + 1, x, y, c))
    g_d = rcopy(gd.at[1], gd.at[0], gss.at[3], gsr.at[3], dev(z - 1, x, y, c))
    g_y = rcopy(gy.at[0], gy.at[1], gss.at[4], gsr.at[4], yn)
    swaps = [
        rcopy(a, b.at[y], fsem.at[i], fsem.at[i + 2], yn) for i, (a, b) in enumerate(((out_half, out_full), (tok_half, tok_full)))
    ]
    g_c.start()
    make(3); make(2)
    for swap in swaps:
        swap.start()
    out_full[y] = out_half[...]
    tok_full[y] = tok_half[...]
    g_c.wait_recv()
    gbuf[...] = gains[c] + gc[...]
    g_x.start()
    first(3); make(1); first(2); make(0)
    g_x.wait_recv()
    gbuf[x] = gbuf[x] + gx[...]
    second(3)
    gu[1] = gbuf[x]
    gd[1] = gbuf[x]
    @pl.when(z > 0)
    def _():
        g_u.wait_recv()
        gu[1] = gu[1] + gu[0]
    @pl.when(z < 3)
    def _():
        g_u.start()
    first(1)
    second(2)
    @pl.when(z < 3)
    def _():
        g_d.wait_recv()
        gd[1] = gd[1] + gd[0]
    @pl.when(z > 0)
    def _():
        g_d.start()
    first(0)
    second(1)
    gy[0] = gu[1, z] + gd[1, z] - gbuf[x, z]
    g_y.start()
    second(0)
    for a in range(n):
        outs[a][...] = acc[a, pos(z, x, c)].astype(f32)
    g_y.wait_recv()
    og[...] = gy[0] + gy[1]
    for swap in swaps:
        swap.wait()
    g_c.wait_send(); g_x.wait_send(); g_y.wait_send()
    @pl.when(z < 3)
    def _(): g_u.wait_send()
    @pl.when(z > 0)
    def _(): g_d.wait_send()
    for s in range(4):
        for a in range(n):
            for q in (0, 1): wc(a, s, q).wait_send()
            wx(a, s).wait_send()
            @pl.when(s > z)
            def _(): zu(a, s).wait_send()
            @pl.when(s < z)
            def _(): zd(a, s).wait_send()

def weight_grads(a1, dattn, dq, dk, dv, mixed, gains, out_half, tok_half, cid):
    toks, width = a1.shape
    hw = dq.shape[1]
    depth = width // 16
    f32, bf16 = jnp.float32, jnp.bfloat16
    D = pltpu.SemaphoreType.DMA
    S = jax.ShapeDtypeStruct
    vm = pl.BlockSpec(memory_space=pltpu.VMEM)
    V = lambda *shape, t=bf16: pltpu.VMEM(shape, t)
    return pl.pallas_call(
        weight_grad_kernel,
        out_shape=[S((depth, hw), f32)] * 4 + [S((8, 128), f32)] + [S((2,) + out_half.shape, bf16)] * 2,
        in_specs=[vm] * 9,
        out_specs=[vm] * 7,
        scratch_shapes=[
            V(4, 16, depth, hw), V(4, 8, depth, hw), V(4, 4, depth, hw), V(4, 4, depth, hw), V(4, 4, depth, hw),
            V(2, 4, 8, 128, t=f32), V(4, 8, 128, t=f32), V(2, 4, 8, 128, t=f32), V(2, 4, 8, 128, t=f32), V(2, 8, 128, t=f32), V(2, 4, 8, 128, t=f32),
            D((4, 8)), D((4, 8)), D((4, 4)), D((4, 4)), D((4, 4)), D((4, 4)), D((4, 4)), D((4, 4)), D((5,)), D((5,)), D((4,)),
        ],
        compiler_params=pltpu.CompilerParams(collective_id=cid, has_side_effects=True, vmem_limit_bytes=60 << 20),
        name="weight_grads",
    )(a1, dattn, dq, dk, dv, mixed, gains, out_half, tok_half)


def expert_grads_kernel(deg, deu, eh, rows, deo, e_gate, e_up, e_down):
    def tn(left, right):
        return lax.dot_general(left, right, (((0,), (0,)), ((), ())), preferred_element_type=jnp.float32)
    e_gate[...] = tn(deg[...], rows[...])
    e_up[...] = tn(deu[...], rows[...])
    e_down[...] = tn(eh[...], deo[...])


def expert_grads(deg, deu, eh, rows, deo):
    width = rows.shape[1]
    whole = lambda a: pl.BlockSpec(a.shape, lambda i: (0, 0), pipeline_mode=pl.Buffered(1))
    tile = lambda n: pl.BlockSpec((n, 256), lambda i: (0, i))
    hidden = deg.shape[1]
    return pl.pallas_call(
        expert_grads_kernel,
        grid=(width // 256,),
        out_shape=[jax.ShapeDtypeStruct((hidden, width), jnp.float32)] * 3,
        in_specs=[whole(a) for a in (deg, deu, eh)] + [tile(a.shape[0]) for a in (rows, deo)],
        out_specs=[tile(hidden)] * 3,
        compiler_params=pltpu.CompilerParams(vmem_limit_bytes=60 << 20),
        name="expert_grads",
    )(deg, deu, eh, rows, deo)


def attention_kernel(
    x_in, wq_in, wk_in, wv_in, wo_in, gain_in, table_in, dy_in, wd_h, cosine, sine,
    wq_o, wk_o, wv_o, wo_o, dy_all, act1, qr, kr, vr, mixed, x_mid, act2, grow, rank_row, rank_col, gate, deo_o, deh_o,
    gland, tland, inv, wbuf, wob, wd, qa, ka, va, own_attn, send, recv, gm, dyt, deo, deh,
    wsem, lsem, dsem, ssem, ysem, zs, zr, xs, xr, cs, cr, gzs, gzr, gxs, gxr, gys, gyr, gcs, gcr,
):
    f32, bf16 = jnp.float32, jnp.bfloat16
    z, x, y, c = place()
    toks, width = x_in.shape
    rows = toks // 2
    depth, hw = wq_in.shape
    cap, hidden = deh_o.shape[1:]
    xn, yn, cn = dev(z, 1 - x, y, c), dev(z, x, 1 - y, c), dev(z, x, y, 1 - c)
    expert = (z * 2 + x) * 2 + c
    greet(z, x, y, c)
    ins = (gain_in, table_in, wq_in, wk_in, wv_in, wo_in)
    outs = (gland, tland, wq_o, wk_o, wv_o, wo_o)
    n = len(outs)
    def pos(s, xx, cc): return (s * 2 + xx) * 2 + cc
    owns = [pltpu.make_async_copy(ins[a], outs[a].at[expert], lsem.at[a]) for a in range(n)]
    own_rows = pl.ds(pl.multiple_of(y * rows, rows), rows)
    owns.append(pltpu.make_async_copy(dy_in.at[own_rows], dy_all.at[blk(z, x, y, c)], lsem.at[n]))
    for o in owns:
        o.start()
    w_down = pltpu.make_async_copy(wd_h, wd, wsem.at[3])
    w_down.start()

    def wz(a, s, up):
        r = outs[a].at[pos(s, x, c)]
        return rcopy(r, r, zs.at[a, s, up], zr.at[a, s], dev(z + 2 * up - 1, x, y, c))
    def wx(a, s):
        r = outs[a].at[pos(s, x, c)]
        return rcopy(r, r, xs.at[a, s], xr.at[a, s], xn)
    def wc(a, s, xx):
        r = outs[a].at[pos(s, xx, c)]
        return rcopy(r, r, cs.at[a, s * 2 + xx], cr.at[a, s * 2 + xx], cn)
    half = rows - 48
    halves = (pl.ds(0, half), pl.ds(half, rows - half))
    def piece(s, xx, yy, p):
        return dy_all.at[blk(s, xx, yy, c), halves[p]]
    def gz(s, xx, p, up):
        r = piece(s, xx, y, p)
        i = 0 if p == 0 else 1 + xx
        return rcopy(r, r, gzs.at[i, s, up], gzr.at[i, s], dev(z + 2 * up - 1, x, y, c))
    def gx(s, p):
        r = piece(s, x, y, p)
        return rcopy(r, r, gxs.at[p, s], gxr.at[p, s], xn)
    def gy(s, xx, p):
        r = piece(s, xx, y, p)
        return rcopy(r, r, gys.at[p, s, xx], gyr.at[p, s, xx], yn)
    def gc(s, xx, yy, p):
        r = piece(s, xx, yy, p)
        return rcopy(r, r, gcs.at[p, s * 2 + xx, yy], gcr.at[p, s * 2 + xx, yy], cn)

    def column(s):
        for a in range(n):
            wx(a, s).start(); wc(a, s, x).start()
    def middle(g):
        s = nearest(z, g)
        for a in range(n):
            wx(a, s).wait_recv(); wc(a, s, 1 - x).start()
    def gspread(s, xx, p):
        gy(s, xx, p).start(); gc(s, xx, y, p).start()
    def gmiddle(g):
        s = nearest(z, g)
        gx(s, 0).wait_recv()
        gspread(s, 1 - x, 0)
    def glast(g):
        s = nearest(z, g)
        for q in (0, 1):
            for p in (0, 1):
                gy(s, q, p).wait_recv(); gc(s, q, 1 - y, p).start()
    def launch(fn):
        @pl.when(z < 3)
        def _(): fn(1)
        @pl.when(z > 0)
        def _(): fn(0)
    def towards(g):
        s = nearest(z, g)
        up = (s < z).astype(jnp.int32)
        nxt = z + 2 * up - 1
        return s, up, (nxt >= 0) & (nxt <= 3)
    def arrive(g):
        s, up, more = towards(g)
        for a in range(n):
            wz(a, s, up).wait_recv()
            @pl.when(more)
            def _(): wz(a, s, up).start()
        column(s)
    def garrive(g):
        s, up, more = towards(g)
        for xx, p in ((x, 0), (x, 1), (1 - x, 1)):
            gz(s, xx, p, up).wait_recv()
            @pl.when(more)
            def _(): gz(s, xx, p, up).start()
            if p == 0:
                gx(s, 0).start()
            gspread(s, xx, p)

    def project(g):
        s = nearest(z, g)
        for a in range(n):
            for q in (0, 1):
                wc(a, s, q).wait_recv()
        loads = [
            pltpu.make_async_copy(w.at[pl.ds(4 * s, 4)], wbuf.at[i], wsem.at[i])
            for i, w in enumerate((wq_o, wk_o, wv_o))
        ]
        for l in loads:
            l.start()
        for i in range(4):
            at = pl.ds(pl.multiple_of((4 * s + i) * depth, depth), depth)
            two = gland[4 * s + i][0:8].astype(f32)
            grow[:, at] = two
        w = pl.ds(pl.multiple_of(4 * s * depth, 4 * depth), 4 * depth)
        a1 = (x_in[:, w].astype(f32) * inv[...] * grow[0:1, w]).astype(bf16)
        act1[:, w] = a1
        for i, acc in enumerate((qa, ka, va)):
            loads[i].wait()
            out = nn(a1, wbuf[i].reshape(4 * depth, hw))
            if g == 0:
                acc[...] = out
            else:
                acc[...] += out

    def ranks_of(g):
        s = nearest(z, g)
        for i in range(4):
            gm[i:i + 1, :] = tland[4 * s + i, pl.ds(expert, 1), :]
        member = (gm[...] > 0.0).astype(f32).astype(bf16)
        one = lax.broadcasted_iota(jnp.int32, (toks, toks), 0)
        two = lax.broadcasted_iota(jnp.int32, (toks, toks), 1)
        upper = jnp.where(one <= two, 1.0, 0.0).astype(bf16)
        lower = jnp.where(one >= two, 1.0, 0.0).astype(bf16)
        same = jnp.where(one == two, 1.0, 0.0).astype(bf16)
        by_row = jnp.where(gm[...] > 0.0, nn(member, upper) - 1.0, -1.0).astype(jnp.int32)
        by_col = jnp.where(nt(same, member) > 0.5, nt(lower, member) - 1.0, -1.0).astype(jnp.int32)
        for i in range(4):
            rank_row[4 * s + i] = by_row[i:i + 1]
            rank_col[4 * s + i] = by_col[:, i:i + 1]
    def stores(g, xx):
        s = nearest(z, g)
        base = (s * 2 + xx) * 2
        out = []
        for k in (0, 1):
            out.append(pltpu.make_async_copy(deo.at[k], deo_o.at[base + k], ssem.at[k, 0]))
            out.append(pltpu.make_async_copy(deh.at[pl.ds(k * cap, cap)], deh_o.at[base + k], ssem.at[k, 1]))
        return out
    def hidden_grads(g):
        s = nearest(z, g)
        ranks_of(g)
        for xx in (0, 1):
            for yy in (0, 1):
                for p in (0, 1):
                    gc(s, xx, yy, p).wait_recv()
        @pl.loop(0, 2)
        def _(xx):
            base = (s * 2 + xx) * 2
            loads = [pltpu.make_async_copy(dy_all.at[pl.ds(2 * (base + k), 2)], dyt.at[k], dsem.at[k]) for k in (0, 1)]
            for l in loads:
                l.start()
            if g > 0:
                @pl.when(xx == 0)
                def _():
                    for copy in stores(g - 1, 1):
                        copy.wait()
            @pl.when(xx == 1)
            def _():
                for copy in stores(g, 0):
                    copy.wait()
            for k in (0, 1):
                loads[k].wait()
                hit = rank_row[base + k] == lax.broadcasted_iota(jnp.int32, (cap, toks), 0)
                weight = jnp.sum(jnp.where(hit, tland[base + k, pl.ds(expert, 1), :], 0.0), axis=1, keepdims=True)
                gate[base + k] = weight
                pick = jnp.where(hit, 1.0, 0.0).astype(bf16)
                grads = dyt[k].reshape(toks, width)
                for m in range(0, width, 512):
                    deo[k, :, m:m + 512] = (nn(pick, grads[:, m:m + 512]) * weight).astype(bf16)
            deh[...] = nt(deo[...].reshape(2 * cap, width), wd[...])
            for copy in stores(g, xx):
                copy.start()

    for o in owns:
        o.wait()
    gx(z, 1).start()
    launch(lambda up: [wz(a, z, up).start() for a in range(n)])
    column(z)
    launch(lambda up: gz(z, x, 0, up).start())
    launch(lambda up: gz(z, x, 1, up).start())
    gx(z, 0).start()
    gspread(z, x, 0); gspread(z, x, 1)
    @pl.loop(0, toks // 16)
    def _(r):
        q = pl.ds(pl.multiple_of(r * 16, 16), 16)
        v = x_in[q].astype(f32)
        inv[q] = lax.rsqrt(jnp.sum(v * v, axis=1, keepdims=True) * (1.0 / width) + EPS)
    gm[...] = jnp.zeros_like(gm)
    w_down.wait()
    gx(z, 1).wait_recv()
    launch(lambda up: gz(z, 1 - x, 1, up).start())
    gspread(z, 1 - x, 1)
    arrive(1); middle(0); project(0)
    garrive(1); gmiddle(0)
    arrive(2); middle(1); project(1)
    garrive(2); gmiddle(1); glast(0)
    hidden_grads(0)
    arrive(3); middle(2); project(2)
    garrive(3); gmiddle(2); glast(1)
    hidden_grads(1)
    middle(3); project(3)
    w_out = pltpu.make_async_copy(wo_o, wob, wsem.at[3])
    w_out.start()

    scale = HD ** (-0.5)
    def turn(values):
        return values * cosine[...] + pltpu.roll(values, HD // 2, 1) * sine[...]
    @pl.loop(0, hw // HD)
    def _(i):
        @pl.when(i == 4)
        def _(): gmiddle(3)
        w = pl.ds(pl.multiple_of(i * HD, HD), HD)
        qh, kh, vh = turn(qa[:, w]).astype(bf16), turn(ka[:, w]).astype(bf16), va[:, w].astype(bf16)
        qr[:, w] = qh
        kr[:, w] = kh
        vr[:, w] = vh
        scores = nt(qh, kh) * scale
        ahead = lax.broadcasted_iota(jnp.int32, (toks, toks), 0) >= lax.broadcasted_iota(jnp.int32, (toks, toks), 1)
        scores = jnp.where(ahead, scores, -1e30)
        expo = jnp.exp(scores - jnp.max(scores, axis=1, keepdims=True))
        probs = expo * (1.0 / jnp.sum(expo, axis=1, keepdims=True))
        mixed[:, w] = nn(probs.astype(bf16), vh).astype(bf16)
    w_out.wait()
    whole = wob[...].reshape(width, hw)
    other = pl.ds(pl.multiple_of((1 - y) * rows, rows), rows)
    here = pl.ds(pl.multiple_of(y * rows, rows), rows)
    for m in range(0, width, 512):
        send[:, m:m + 512] = nt(mixed[other, :], whole[m:m + 512]).astype(bf16)
    swap = rcopy(send, recv, ysem.at[0], ysem.at[1], yn)
    swap.start()
    for m in range(0, width, 512):
        own_attn[:, m:m + 512] = nt(mixed[here, :], whole[m:m + 512])
    glast(2)
    hidden_grads(2)
    swap.wait_recv()
    @pl.loop(0, rows // 16)
    def _(r):
        q = pl.ds(pl.multiple_of(r * 16, 16), 16)
        at = pl.ds(pl.multiple_of(y * rows + r * 16, 16), 16)
        v = x_in[at].astype(f32) + own_attn[q] + recv[q].astype(f32)
        x_mid[q] = v
        scaled = v * lax.rsqrt(jnp.sum(v * v, axis=1, keepdims=True) * (1.0 / width) + EPS)
        act2[q] = (scaled * grow[1:2]).astype(bf16)
    glast(3)
    hidden_grads(3)
    for copy in stores(3, 1):
        copy.wait()
    swap.wait_send()
    gx(z, 1).wait_send()
    for s in range(4):
        for a in range(n):
            wx(a, s).wait_send()
            for q in (0, 1):
                wc(a, s, q).wait_send()
        gx(s, 0).wait_send()
        for q in (0, 1):
            for p in (0, 1):
                gy(s, q, p).wait_send()
                for r in (0, 1):
                    gc(s, q, r, p).wait_send()
        @pl.when((z < 3) & (s <= z))
        def _():
            for xx, p in ((x, 0), (x, 1), (1 - x, 1)):
                gz(s, xx, p, 1).wait_send()
            for a in range(n):
                wz(a, s, 1).wait_send()
        @pl.when((z > 0) & (s >= z))
        def _():
            for xx, p in ((x, 0), (x, 1), (1 - x, 1)):
                gz(s, xx, p, 0).wait_send()
            for a in range(n):
                wz(a, s, 0).wait_send()

def attention_layer(x_in, weights, gains, table, dy, wd, cosine, sine, cap, cid):
    toks, width = x_in.shape
    depth, hw = weights[0].shape
    rows = toks // 2
    hidden = wd.shape[0]
    n = 6
    f32, bf16, i32 = jnp.float32, jnp.bfloat16, jnp.int32
    D = pltpu.SemaphoreType.DMA
    S = jax.ShapeDtypeStruct
    any_ = pl.BlockSpec(memory_space=pl.ANY)
    vm = pl.BlockSpec(memory_space=pltpu.VMEM)
    V = lambda *shape, t=bf16: pltpu.VMEM(shape, t)
    return pl.pallas_call(
        attention_kernel,
        out_shape=[S((16, depth, hw), bf16)] * 4
        + [S((32, rows, width), bf16), S((toks, width), bf16)]
        + [S((toks, hw), bf16)] * 4
        + [
            S((rows, width), f32), S((rows, width), bf16), S((8, width), f32), S((16, 1, toks), i32), S((16, toks, 1), i32),
            S((16, cap, 1), f32), S((16, cap, width), bf16), S((16, cap, hidden), f32),
        ],
        in_specs=[vm] * 8 + [any_] + [vm] * 2,
        out_specs=[any_] * 5 + [vm] * 11 + [any_] * 2,
        scratch_shapes=[
            V(16, *gains.shape), V(16, *table.shape, t=f32), V(toks, 1, t=f32), V(3, 4, depth, hw), V(16, depth, hw), V(hidden, width),
            V(toks, hw, t=f32), V(toks, hw, t=f32), V(toks, hw, t=f32), V(rows, width, t=f32), V(rows, width), V(rows, width),
            V(8, toks, t=f32), V(2, 2, rows, width), V(2, cap, width), V(2 * cap, hidden, t=f32),
            D((4,)), D((n + 1,)), D((2,)), D((2, 2)), D((2,)),
            D((n, 4, 2)), D((n, 4)), D((n, 4)), D((n, 4)), D((n, 8)), D((n, 8)),
            D((3, 4, 2)), D((3, 4)), D((2, 4)), D((2, 4)), D((2, 4, 2)), D((2, 4, 2)), D((2, 8, 2)), D((2, 8, 2)),
        ],
        compiler_params=pltpu.CompilerParams(collective_id=cid, has_side_effects=True, vmem_limit_bytes=60 << 20),
        name="attention_layer",
    )(x_in, *weights, gains, table, dy, wd, cosine, sine)


def on_device(
    tokens,
    cotangent,
    route_ids,
    route_gates,
    gain_first,
    w_query,
    w_key,
    w_value,
    w_output,
    gain_second,
    shared_gate,
    shared_up,
    shared_down,
    expert_gate,
    expert_up,
    expert_down,
):
    f32, bf16 = jnp.float32, jnp.bfloat16
    rows_dev, width = tokens.shape
    topk = route_ids.shape[1]
    experts = lax.axis_size("dp")
    capacity = rows_dev * topk * 4 // (3 * experts)
    slots = experts * capacity
    positions = jnp.arange(rows_dev, dtype=f32)
    freqs = 10000.0 ** (-2.0 * jnp.arange(HD // 2, dtype=f32) / HD)
    angles = positions[:, None] * freqs[None, :]
    cosine = jnp.concatenate([jnp.cos(angles)] * 2, axis=1)
    sine = jnp.concatenate([-jnp.sin(angles), jnp.sin(angles)], axis=1)
    chosen = route_ids[:, :, None] == jnp.arange(experts, dtype=jnp.int32)[None, None, :]
    table = jnp.sum(jnp.where(chosen, route_gates[:, :, None], 0.0), axis=1)
    gains = jnp.concatenate([gain_first[None], gain_second[None], jnp.zeros((14, gain_first.shape[0]), bf16)])
    exp_gate, exp_up, exp_down = expert_gate[0].T, expert_up[0].T, expert_down[0]

    depth, common_width = shared_gate.shape
    common_dev = common_width // experts
    packed = jnp.stack([shared_gate, shared_up, shared_down])
    packed = packed.reshape(3, depth, experts, common_dev).transpose(2, 0, 1, 3)
    packed = lax.all_to_all(packed, "dp", split_axis=0, concat_axis=0, tiled=True)
    packed = packed.transpose(1, 0, 2, 3).reshape(3, width, common_dev)
    front = capacity - 128
    back = 128 - front - common_dev

    def widen(w):
        return jnp.pad(w, ((0, 0), (front, back)))

    common_gu = jnp.concatenate([widen(packed[0]), widen(packed[1])], axis=1)
    common_down = widen(packed[2])

    (
        query_whole, key_whole, value_whole, output_whole, grad_all, act_one, query_rot, key_rot, value_low, mixed,
        x_mid, act_two, gain_rows, rank_row, rank_col, slot_gate, rows_out_grad, hidden_rows_grad,
    ) = attention_layer(
        tokens, (w_query, w_key, w_value, w_output), gains, table.T, cotangent, exp_down, cosine, sine, capacity, 0
    )
    weights = [w.reshape(width, -1) for w in (query_whole, key_whole, value_whole, output_whole)]

    (
        total_grad, unused_act, rows, hidden_rows, gate_rows_grad, up_rows_grad, unused_hidden, unused_grad, unused_part, ffn,
        gu_grad, down_grad,
    ) = (
        expert_layer(
            act_two, hidden_rows_grad, grad_all, rank_row, rank_col, slot_gate,
            exp_gate, exp_up, exp_down, common_gu, common_down.T[front:], common_down, 1,
        )
    )
    rows = rows.reshape(slots, width)
    rows_out_grad = rows_out_grad.reshape(slots, width)
    hidden_rows = hidden_rows.reshape(slots, -1)
    expert_gate_grad, expert_up_grad, expert_down_grad = expert_grads(
        gate_rows_grad.reshape(slots, -1), up_rows_grad.reshape(slots, -1), hidden_rows, rows, rows_out_grad
    )
    common_w_grad = jnp.concatenate(
        [w[:, front : front + common_dev] for w in (gu_grad[:, :128], gu_grad[:, 128:], down_grad)], axis=1
    )
    common_w_grad = common_w_grad.reshape(experts, depth, 3 * common_dev)
    common_w_grad = lax.all_to_all(common_w_grad, "dp", split_axis=0, concat_axis=0, tiled=True)
    common_w_grad = common_w_grad.reshape(experts, depth, 3, common_dev).transpose(2, 1, 0, 3)
    common_w_grad = common_w_grad.reshape(3, depth, common_width).astype(f32)

    layer_out, tokens_grad, attn_grad, query_grad, key_grad, value_grad, gain_one_grad, gain_two_grad = attention_back(
        ffn,
        total_grad,
        x_mid,
        cotangent,
        tokens,
        gain_rows[0:1],
        gain_rows[1:2],
        weights,
        query_rot,
        key_rot,
        value_low,
        cosine,
        sine,
        2,
    )
    gains = jnp.concatenate([gain_one_grad, gain_two_grad, jnp.zeros((6, width), f32)])
    gains = gains.reshape(8, 4, 2, 2, width // 16).transpose(3, 2, 1, 0, 4)
    query_sum, key_sum, value_sum, output_sum, gain_grads, layer_out, tokens_grad = weight_grads(
        act_one, attn_grad.reshape(rows_dev, width), query_grad, key_grad, value_grad, mixed, gains, layer_out, tokens_grad, 4
    )
    return (
        layer_out.reshape(rows_dev, width),
        tokens_grad.reshape(rows_dev, width),
        gain_grads[0],
        query_sum,
        key_sum,
        value_sum,
        output_sum,
        gain_grads[1],
        common_w_grad[0],
        common_w_grad[1],
        common_w_grad[2],
        expert_gate_grad.T[None],
        expert_up_grad.T[None],
        expert_down_grad[None],
    )


def solution(mesh):
    body = on_device if (mesh.shape["dp"], mesh.shape["tensor"]) == (16, 2) else on_device_plain
    in_specs = (
        P("dp", None),
        P("dp", None),
        P("dp", None),
        P("dp", None),
        P("dp"),
        P("dp", "tensor"),
        P("dp", "tensor"),
        P("dp", "tensor"),
        P("dp", "tensor"),
        P("dp"),
        P("dp", "tensor"),
        P("dp", "tensor"),
        P("dp", "tensor"),
        P("dp", None, "tensor"),
        P("dp", None, "tensor"),
        P("dp", "tensor", None),
    )
    out_specs = (
        P("dp", None),
        P("dp", None),
        P("dp"),
        P("dp", "tensor"),
        P("dp", "tensor"),
        P("dp", "tensor"),
        P("dp", "tensor"),
        P("dp"),
        P("dp", "tensor"),
        P("dp", "tensor"),
        P("dp", "tensor"),
        P("dp", None, "tensor"),
        P("dp", None, "tensor"),
        P("dp", "tensor", None),
    )
    return jax.shard_map(
        body, mesh=mesh, in_specs=in_specs, out_specs=out_specs, check_vma=False
    )
```
